256 devices in a mesh: row: 8 (over z), col: 16 (over y_lo, x, core), head: 2 (over y_hi).
Axes of the slice: x: 4, y: 4 (y_hi: 2, y_lo: 2; y = y_hi * 2 + y_lo), z: 8, core: 2. Of those that a mesh axis runs over, the one named last changes fastest.
Arguments:
- pair_field: bfloat16 [1024, 1024, 128], P('row', 'col'), may hold values from -6 to 6
- ln_gain: float32 [128], replicated, may hold values from 0.25 to 1.75
- w_query: bfloat16 [128, 128], P(None, 'head'), may hold values from -1 to 1
- w_key: bfloat16 [128, 128], P(None, 'head'), may hold values from -1 to 1
- w_value: bfloat16 [128, 128], P(None, 'head'), may hold values from -0.5 to 0.5
- w_gate: bfloat16 [128, 128], P(None, 'head'), may hold values from -0.5 to 0.5
- w_bias: bfloat16 [128, 4], P(None, 'head'), may hold values from -0.5 to 0.5
- w_out: bfloat16 [128, 128], replicated, may hold values from -3 to 3
- tile_mask: int32 [16, 16], replicated, may hold values from 0 to 1, as said below
- type_ids: int32 [1024], replicated, may hold values from 0 to 31, as said below
Outputs:
- pair_update: bfloat16 [1024, 1024, 128], P('row', 'col', 'head')
The draws below stay inside these ranges and needn't reach their ends.
Inputs may be any that keep to these rules, and one draw needn't show every extreme that they name: `tile_mask`: 1 lets a block of 64 query tokens attend to a block of 64 key tokens; diagonal blocks are attended regardless. `type_ids`: 0 marks padding, which is never a key; the first of every 64 tokens is never padding.
All inputs are finite; a program needn't handle non-finite values.
Results may differ from the reference program's by a relative error of at most 0.012.
Values may be sent and summed in bfloat16 or wider, within the bound.
A program may use at most 128 MiB of HBM per device.

```python
import math
import jax
import jax.numpy as jnp
from jax import lax

C = 128
H = 4
D = 32
MB = 64
NTYPES = 32
N = 1024
NB = 16


def draw_pair_field(key, part):
    key = jax.random.fold_in(key, 11)
    first_key = jax.random.fold_in(key, 0)
    field = jnp.clip(jax.random.normal(first_key, (N, N, C), jnp.float32), -6.0, 6.0)
    return field.astype(jnp.bfloat16)


def projection_draw(key, salt):
    key = jax.random.fold_in(key, salt)
    drawn = jnp.clip(jax.random.normal(key, (C, H * D), jnp.float32), -6.0, 6.0) / math.sqrt(C)
    return drawn.astype(jnp.bfloat16)


def draw_w_query(key, part):
    return projection_draw(key, 23)


def draw_w_key(key, part):
    return projection_draw(key, 29)


def draw_tile_mask(key, part):
    key = jax.random.fold_in(key, 37)
    first_key, second_key = jax.random.split(key)
    levels = jax.random.randint(first_key, (NB, 1), 1, 6)
    rolls = jax.random.randint(second_key, (NB, NB), 0, 10)
    return (rolls < levels).astype(jnp.int32)


def draw_type_ids(key, part):
    key = jax.random.fold_in(key, 41)
    first_key, second_key = jax.random.split(key)
    drawn = jnp.maximum(jax.random.randint(first_key, (N,), -8, NTYPES), 0)
    leading = jax.random.randint(second_key, (N,), 1, NTYPES)
    starts = jnp.arange(N, dtype=jnp.int32) % MB == 0
    return jnp.where(starts, leading, drawn).astype(jnp.int32)


def block_levels(stream_key, shape, cuts, least, largest):
    def one(position, blocks):
        steps = jax.random.uniform(jax.random.fold_in(jax.random.fold_in(stream_key, 6), position), (blocks,), jnp.float32, least / len(cuts), largest / len(cuts))
        return jnp.repeat(jnp.exp(steps), shape[position] // blocks).reshape((-1,) + (1,) * (len(shape) - position - 1))

    level = one(*cuts[0])
    for cut in cuts[1:]:
        level = level * one(*cut)
    return level


def bell_draw(rng, dims, deviation, bound, cuts=(), kind=jnp.bfloat16):
    values = jax.random.normal(rng, dims, jnp.float32) * deviation
    if len(cuts) > 0:
        values = block_levels(rng, dims, cuts, -0.22, 0.18) * values
    return jnp.clip(values, min=-bound, max=bound).astype(kind)


def setup_inputs(seed: int = 0) -> dict:
    key_list = jax.random.split(jax.random.key(seed), 11)
    pair_field = draw_pair_field(jax.random.fold_in(key_list[10], 71), 0)
    ln_gain = jnp.clip(1.0 + 0.15 * jax.random.normal(key_list[1], (C,), jnp.float32), 0.25, 1.75)
    w_query = draw_w_query(jax.random.fold_in(key_list[10], 71), 0)
    w_key = draw_w_key(jax.random.fold_in(key_list[10], 71), 0)
    w_value = bell_draw(key_list[4], (C, H * D), C ** -0.5, 0.5, ((1, 2),))
    w_gate = bell_draw(key_list[5], (C, H * D), C ** -0.5, 0.5, ((1, 2),))
    w_bias = bell_draw(key_list[6], (C, H), C ** -0.5, 0.5, ((1, 2),))
    w_out = bell_draw(key_list[7], (H * D, C), 0.5, 3.0)
    tile_mask = draw_tile_mask(jax.random.fold_in(key_list[10], 71), 0)
    type_ids = draw_type_ids(jax.random.fold_in(key_list[10], 71), 0)
    return {"pair_field": pair_field, "ln_gain": ln_gain, "w_query": w_query, "w_key": w_key, "w_value": w_value, "w_gate": w_gate, "w_bias": w_bias, "w_out": w_out, "tile_mask": tile_mask, "type_ids": type_ids}


epsilon = 1e-05
masked_score = -1000000000.0

def layer_norm(field, gain):
    wide = field.astype(jnp.float32)
    centred = wide - lax.optimization_barrier(jnp.mean(wide, axis=-1, keepdims=True))
    spread = lax.optimization_barrier(jnp.mean(centred * centred, axis=-1, keepdims=True))
    return (centred * lax.rsqrt(spread + epsilon) * gain).astype(jnp.bfloat16)

def reference(pair_field, ln_gain, w_query, w_key, w_value, w_gate, w_bias, w_out, tile_mask, type_ids):
    normed = layer_norm(pair_field, ln_gain)
    flat = normed.reshape(N * N, C)

    def project(weight):
        return jnp.dot(flat, weight, preferred_element_type=jnp.float32).reshape(N, N, H, D)
    query = project(w_query).astype(jnp.bfloat16)
    keys = project(w_key).astype(jnp.bfloat16)
    values = project(w_value).astype(jnp.bfloat16)
    gate = project(w_gate)
    bias = jnp.dot(flat, w_bias, preferred_element_type=jnp.float32).astype(jnp.bfloat16).reshape(N, N, H)
    bias_rows = jnp.transpose(bias.astype(jnp.float32), (2, 1, 0))
    block_ids = jnp.arange(N, dtype=jnp.int32) // MB
    contact = jnp.take(jnp.take(tile_mask, block_ids, axis=0), block_ids, axis=1) == 1
    allowed = (contact | (block_ids[:, None] == block_ids[None, :])) & (type_ids != 0)[None, :]
    scale = 1.0 / math.sqrt(D)
    column_step = 8

    def column_block(block_index):
        start = block_index * column_step

        def cut(field):
            return lax.dynamic_slice_in_dim(field, start, column_step, 1)
        query_part = cut(query).astype(jnp.float32)
        key_part = cut(keys).astype(jnp.float32)
        value_part = cut(values).astype(jnp.float32)
        gate_part = cut(gate)
        scores = jnp.einsum('ijhd,kjhd->jhik', query_part, key_part, precision=lax.Precision.HIGHEST) * scale + bias_rows[None]
        scores = jnp.where(allowed[None, None], scores, masked_score)
        row_max = lax.optimization_barrier(jnp.max(scores, axis=-1, keepdims=True))
        exponent = jnp.exp(scores - row_max)
        total_sum = lax.optimization_barrier(jnp.sum(exponent, axis=-1))
        rounded = lax.optimization_barrier(exponent.astype(jnp.bfloat16)).astype(jnp.float32)
        numerator = jnp.einsum('jhik,kjhd->jhid', rounded, value_part, precision=lax.Precision.HIGHEST)
        attention = jnp.transpose(numerator / total_sum[..., None], (2, 0, 1, 3))
        gated_part = (jax.nn.sigmoid(gate_part) * attention).astype(jnp.bfloat16)
        return gated_part.reshape(N, column_step, H * D)
    gated_parts = lax.map(column_block, jnp.arange(N // column_step, dtype=jnp.int32))
    gated = jnp.transpose(gated_parts, (1, 0, 2, 3)).reshape(N * N, H * D)
    mixed = jnp.dot(gated, w_out, preferred_element_type=jnp.float32)
    return mixed.astype(jnp.bfloat16).reshape(N, N, C)
```

```python
import math

import jax
import jax.numpy as jnp
from jax import lax
from jax.experimental import pallas as pl
from jax.experimental.pallas import tpu as pltpu
from jax.sharding import PartitionSpec as P

MESH = pl.DeviceIdType.MESH
F32 = jnp.float32
BF16 = jnp.bfloat16
VMEM = pltpu.VMEM
DMA = pltpu.SemaphoreType.DMA

epsilon = 1e-05
masked_score = -1000000000.0
LOG2E = math.log2(math.e)
SCALE = LOG2E / math.sqrt(32)
SAFE = 64.0
NT = (((1,), (1,)), ((), ()))


def ring(value, size):
    return lax.rem(value + size, size)


def spread_kernel(
    tile_ref, gain_in, wq_ref, wk_ref, wv_ref, wg_ref, wb_in, types_in, w_out_in, mask_in,
    qg_ref, kbd_ref, vbd_ref, bias_ref, bound_ref, mixing_ref, lists_ref,
    half, gain_ref, wb_ref, types_ref, w_out_ref, mask_ref, wide, send, strip, wbuf, wall, flat, bsend, tops,
    load_sem, col_send, col_recv, z_send, z_recv, w_send, w_recv,
    g_send, g_recv, s_send, s_recv, own_sem,
):
    row = lax.axis_index("row")
    col = lax.axis_index("col")
    head = lax.axis_index("head")
    core = lax.rem(col, 2)
    x = lax.rem(lax.div(col, 2), 4)
    y = head * 2 + lax.div(col, 8)

    def place(x_, y_, core_=None):
        return (row, lax.rem(y_, 2) * 8 + x_ * 2 + (core if core_ is None else core_), lax.div(y_, 2))

    def along_z(step):
        return (ring(row + step, 8), col, head)

    partner = place(x, ring(y + 2, 4))
    peers = [along_z(step) for step in range(1, 8)]
    peers += [place(ring(x + 1, 4), y), place(ring(x - 1, 4), y)]
    peers += [place(x, ring(y + 1, 4)), place(x, ring(y - 1, 4)), partner]
    peers += [place(x, y, 1 - core)]
    barrier = pltpu.get_barrier_semaphore()
    for peer in peers:
        pl.semaphore_signal(barrier, inc=1, device_id=peer, device_id_type=MESH)

    loads = [
        (tile_ref.at[:, pl.ds(pl.multiple_of(head * 32, 32), 32), :], half),
        (gain_in, gain_ref), (wb_in, wb_ref), (types_in, types_ref),
    ]
    loads += [
        (ref, wbuf.at[head, pl.ds(kind * 64, 64)]) for kind, ref in enumerate((wq_ref, wk_ref, wv_ref, wg_ref))
    ]
    loads += [(w_out_in, w_out_ref), (mask_in, mask_ref)]
    loads = [pltpu.make_async_copy(src, dst, load_sem.at[n]) for n, (src, dst) in enumerate(loads)]
    for load in loads:
        load.start()
    tops[...] = jnp.zeros_like(tops)
    for load in loads:
        load.wait()
    wbuf[head, 256:272, :] = jnp.concatenate(
        [wb_ref[...].astype(F32), jnp.zeros((14, 128), F32)], axis=0
    ).astype(BF16)

    def widen(block, carry):
        rows = half[pl.ds(block * 8, 8)].astype(F32).reshape(256, 128)
        wide[pl.ds(pl.multiple_of(block * 256, 256), 256), :] = rows
        return carry

    lax.fori_loop(0, 16, widen, 0)
    ones = jnp.ones((128, 128), BF16)
    gain = gain_ref[...]

    def norm_for(target, carry):
        for jj in range(4):
            value = wide[pl.ds(4 * target + jj, 128, stride=32), :]
            mean = jnp.dot(value.astype(BF16), ones, preferred_element_type=F32) * (1.0 / 128)
            centred = value - mean
            squares = (centred * centred).astype(BF16)
            spread = jnp.dot(squares, ones, preferred_element_type=F32) * (1.0 / 128)
            normed = centred * lax.rsqrt(spread + epsilon) * gain
            send[target, jj] = normed.astype(BF16)
        return carry

    lax.fori_loop(0, 4, norm_for, 0, unroll=2)
    pl.semaphore_wait(barrier, len(peers))
    w_copy = pltpu.make_async_remote_copy(
        src_ref=wbuf.at[head], dst_ref=wbuf.at[head], send_sem=w_send, recv_sem=w_recv,
        device_id=partner, device_id_type=MESH,
    )
    w_copy.start()
    lax.fori_loop(4, 8, norm_for, 0, unroll=2)
    pltpu.make_async_remote_copy(
        src_ref=wbuf.at[1 - head], dst_ref=wbuf.at[1 - head], send_sem=w_send, recv_sem=w_recv,
        device_id=partner, device_id_type=MESH,
    ).wait_recv()

    wb = wbuf[0, 256:272, :].astype(F32) + pltpu.roll(wbuf[1, 256:272, :].astype(F32), 2, 0)
    weighted = wb * gain
    wbt = wb.astype(BF16)

    def bias_for(target, carry):
        part = lax.dot_general(wbt, send[target].reshape(512, 128), NT, preferred_element_type=F32)
        for jj in range(4):
            flat[pl.ds(pl.multiple_of((4 * target + jj) * 8, 8), 8), :] = part[0:8, jj * 128:jj * 128 + 128]
        return carry

    lax.fori_loop(0, 8, bias_for, 0, unroll=4)
    living = jnp.broadcast_to(types_ref[pl.ds(row, 1), :] != 0, (32, 128))
    by_head = [
        jnp.where(living, flat[pl.ds(h, 32, stride=8), :] * LOG2E, masked_score) for h in range(4)
    ]
    bsend[0] = jnp.concatenate([b[:, :64] for b in by_head], axis=1).astype(BF16)
    bsend[1] = jnp.concatenate([b[:, 64:] for b in by_head], axis=1).astype(BF16)

    def unit(x_, y_, low, count, core_=None):
        return bias_ref.at[
            lax.rem(y_, 2), x_, core if core_ is None else core_, pl.ds(low, count), lax.div(y_, 2)
        ]

    sent = [w_copy]

    def push(src, dst, send_sem, recv_sem, device):
        copy = pltpu.make_async_remote_copy(
            src_ref=src, dst_ref=dst, send_sem=send_sem, recv_sem=recv_sem,
            device_id=device, device_id_type=MESH,
        )
        copy.start()
        sent.append(copy)

    def arrive(dst, send_sem, recv_sem):
        pltpu.make_async_remote_copy(
            src_ref=dst, dst_ref=dst, send_sem=send_sem, recv_sem=recv_sem,
            device_id=partner, device_id_type=MESH,
        ).wait_recv()

    def chunk(step, low=0, count=2):
        return unit(x, y, 2 * ring(row + step, 8) + low, count)

    def z_push(k, src, dst, step):
        push(src, dst, z_send.at[k], z_recv.at[k], along_z(step))

    def z_arrive(k, dst):
        arrive(dst, z_send.at[k], z_recv.at[k])

    own = pltpu.make_async_copy(bsend, chunk(0), own_sem.at[0])
    own.start()
    for k, step in enumerate((2, -2, 1, -1)):
        z_push(k, bsend, chunk(0), step)

    def strip_rows(step):
        source = ring(row + step, 8)
        return strip.at[:, pl.ds(pl.multiple_of(source * 128, 128), 128), :]

    def col_push(step):
        target = ring(row + step, 8)
        push(send.at[target], strip_rows(0), col_send.at[step], col_recv.at[step], along_z(step))

    own_cols = pltpu.make_async_copy(send.at[row], strip_rows(0), own_sem.at[1])
    own_cols.start()
    col_push(1)
    col_push(7)

    for kind, place_of in enumerate((1, 0, 2, 3)):
        for s in range(2):
            wall[place_of * 128 + s * 64:place_of * 128 + s * 64 + 64, :] = wbuf[s, kind * 64:kind * 64 + 64, :]
    together = (
        lax.div(lax.broadcasted_iota(jnp.int32, (128, 128), 0), 32)
        == lax.div(lax.broadcasted_iota(jnp.int32, (128, 128), 1), 32)
    ).astype(F32).astype(BF16)

    key_head = lax.div(lax.broadcasted_iota(jnp.int32, (128, 128), 0), 32)
    side_of = lax.div(lax.broadcasted_iota(jnp.int32, (128, 128), 1), 64)
    key_here = [(key_head == 2 * n + side_of).astype(F32).astype(BF16) for n in range(2)]
    lane_head = lax.div(lax.broadcasted_iota(jnp.int32, (64, 128), 1), 32)
    value_here = [(lane_head == h).astype(F32).astype(BF16) for h in range(4)]

    def project(step):
        source = ring(row + step, 8)
        rows = pl.ds(pl.multiple_of(source * 128, 128), 128)

        def one(jj, carry):
            value = strip[jj, rows, :]
            keys = lax.dot_general(wall[0:128, :], value, NT, preferred_element_type=F32)
            left = lax.dot_general(value, wall[128:256, :], NT, preferred_element_type=F32)
            right = lax.dot_general(value, wall[256:512, :], NT, preferred_element_type=F32)
            query = left * SCALE
            qg_ref[0, jj, rows, :] = query.astype(BF16)
            qg_ref[1, jj, rows, :] = jax.nn.sigmoid(right[:, 128:]).astype(BF16)
            short = keys.astype(BF16)
            values = right[:, :128].astype(BF16)
            for odd in range(2):
                twice = jnp.concatenate([short[:, odd * 64:odd * 64 + 64]] * 2, axis=1)
                for n in range(2):
                    kbd_ref[jj, 2 * source + odd, :, n * 128:(n + 1) * 128] = twice * key_here[n]
                for h in range(4):
                    vbd_ref[jj, 2 * source + odd, h * 64:(h + 1) * 64, :] = (
                        values[odd * 64:odd * 64 + 64, :] * value_here[h]
                    )
            lengths = jnp.dot((query * query).astype(BF16), together, preferred_element_type=F32)
            tops[0:1, :] = jnp.maximum(tops[0:1, :], jnp.max(lengths, axis=0, keepdims=True))
            lengths = jnp.dot(together, (keys * keys).astype(BF16), preferred_element_type=F32)
            tops[1:2, :] = jnp.maximum(tops[1:2, :], jnp.max(lengths, axis=0, keepdims=True))
            return carry

        lax.fori_loop(0, 4, one, 0, unroll=2)

    def take(step):
        arrive(strip_rows(-step), col_send.at[step], col_recv.at[step])
        project(-step)

    own.wait()
    own_cols.wait()
    for k, step in enumerate((-2, 2, -1, 1)):
        z_arrive(k, chunk(step))
    z_push(4, chunk(-2), chunk(-2), 1)
    z_push(5, chunk(2), chunk(2), -1)
    z_push(6, chunk(-2, 0, 1), chunk(-2, 0, 1), 2)
    z_push(7, chunk(2, 1, 1), chunk(2, 1, 1), -2)
    for step in (2, 6, 3, 5, 4):
        col_push(step)
    project(0)
    z_arrive(4, chunk(-3))
    z_arrive(5, chunk(3))
    z_arrive(6, chunk(4, 0, 1))
    z_arrive(7, chunk(4, 1, 1))

    def make_lists():
        mixing_ref[...] = w_out_ref[...].astype(F32).T.astype(BF16)
        part = mask_ref[...].astype(F32)
        diagonal = lax.broadcasted_iota(jnp.int32, (16, 16), 0) == lax.broadcasted_iota(jnp.int32, (16, 16), 1)
        part = jnp.where((part == 1.0) | diagonal, 1.0, 0.0)
        allowed = jnp.concatenate([part, jnp.zeros((16, 112), F32)], axis=1)
        before = [jnp.zeros((1, 128), F32)]
        for i in range(16):
            before.append(before[-1] + allowed[i:i + 1, :])
        rank = jnp.concatenate(before[:16], axis=0)
        pairs = jnp.broadcast_to(jnp.floor((before[16] + 1.0) * 0.5), (16, 128))
        earlier = (
            lax.broadcasted_iota(jnp.int32, (128, 128), 0) < lax.broadcasted_iota(jnp.int32, (128, 128), 1)
        ).astype(F32).astype(BF16)
        start = jnp.dot(pairs.astype(BF16), earlier, preferred_element_type=F32)
        total = jnp.sum(pairs[0:1, :], axis=1, keepdims=True)
        rank = rank + 2.0 * start
        entry = 2.0 * lax.broadcasted_iota(jnp.int32, (16, 128), 1).astype(F32)
        number = lax.broadcasted_iota(jnp.int32, (16, 128), 0).astype(F32)
        block = jnp.zeros((16, 128), F32)
        picked = [jnp.zeros((16, 128), F32)] * 2
        found = [jnp.zeros((16, 128), F32)] * 2
        for k in range(16):
            at = jnp.broadcast_to(rank[:, k:k + 1], (16, 128))
            here = jnp.broadcast_to(allowed[:, k:k + 1], (16, 128))
            for side in range(2):
                hit = jnp.where(at == entry + side, here, 0.0)
                found[side] = found[side] + hit
                picked[side] = picked[side] + hit * number
                if side == 0:
                    block = block + hit * k
        rows = [jnp.sum(block, axis=0, keepdims=True)]
        for side in range(2):
            missing = 1.0 - jnp.sum(found[side], axis=0, keepdims=True)
            rows.append(jnp.sum(picked[side], axis=0, keepdims=True) + (16.0 + side) * missing)
        rows.append(jnp.broadcast_to(total, (1, 128)))
        rows.append(jnp.zeros((4, 128), F32))
        lists_ref[...] = jnp.concatenate(rows, axis=0).astype(jnp.int32)

    def node(run, a, b):
        return (a, b) if run == 0 else (b, a)

    first = (x, y)
    second = (y, x)

    def shipment(run, index, a, b, low, count, to_a, to_b):
        k = run * 20 + index
        ref = unit(*node(run, a, b), run * 8 + low, count)
        push(ref, ref, g_send.at[k], g_recv.at[k], place(*node(run, to_a, to_b)))

    def receive(run, index, a, b, low, count):
        k = run * 20 + index
        arrive(unit(*node(run, a, b), run * 8 + low, count), g_send.at[k], g_recv.at[k])

    def to_sibling(run, u, v, a, b):
        k = run * 16 + u * 4 + v
        ref = unit(*node(run, a, b), run * 8, 8)
        push(ref, ref, s_send.at[k], s_recv.at[k], place(x, y, 1 - core))

    def across(run, u, a, b):
        shipment(run, 4 + 4 * u, a, b, 0, 8, first[run], ring(b + 1, 4))
        shipment(run, 5 + 4 * u, a, b, 0, 8, first[run], ring(b - 1, 4))

    for run in range(2):
        a, b = first[run], second[run]
        shipment(run, 0, a, b, 0, 8, ring(a + 1, 4), b)
        shipment(run, 1, a, b, 0, 8, ring(a - 1, 4), b)
    for run in range(2):
        a, b = first[run], second[run]
        across(run, 0, a, b)
        to_sibling(run, 0, 0, a, b)
    for run in range(2):
        a, b = first[run], second[run]
        receive(run, 0, ring(a - 1, 4), b, 0, 8)
        shipment(run, 2, ring(a - 1, 4), b, 0, 4, ring(a + 1, 4), b)
        receive(run, 1, ring(a + 1, 4), b, 0, 8)
        shipment(run, 3, ring(a + 1, 4), b, 4, 4, ring(a - 1, 4), b)
    for run in range(2):
        a, b = first[run], second[run]
        across(run, 1, ring(a - 1, 4), b)
        to_sibling(run, 1, 0, ring(a - 1, 4), b)
        across(run, 2, ring(a + 1, 4), b)
        to_sibling(run, 2, 0, ring(a + 1, 4), b)
    for run in range(2):
        a, b = first[run], second[run]
        receive(run, 2, ring(a + 2, 4), b, 0, 4)
        receive(run, 3, ring(a + 2, 4), b, 4, 4)
        across(run, 3, ring(a + 2, 4), b)
        to_sibling(run, 3, 0, ring(a + 2, 4), b)
    take(1)
    take(7)
    for u in range(4):
        for run in range(2):
            a, b = ring(first[run] + (0, -1, 1, 2)[u], 4), second[run]
            receive(run, 4 + 4 * u, a, ring(b - 1, 4), 0, 8)
            shipment(run, 6 + 4 * u, a, ring(b - 1, 4), 0, 4, first[run], ring(b + 1, 4))
            to_sibling(run, u, 1, a, ring(b - 1, 4))
            receive(run, 5 + 4 * u, a, ring(b + 1, 4), 0, 8)
            shipment(run, 7 + 4 * u, a, ring(b + 1, 4), 4, 4, first[run], ring(b - 1, 4))
            to_sibling(run, u, 2, a, ring(b + 1, 4))
        if u == 1:
            make_lists()
        if u == 3:
            take(2)
            take(6)
    for u in range(4):
        for run in range(2):
            a, b = ring(first[run] + (0, -1, 1, 2)[u], 4), second[run]
            receive(run, 6 + 4 * u, a, ring(b + 2, 4), 0, 4)
            receive(run, 7 + 4 * u, a, ring(b + 2, 4), 4, 4)
            to_sibling(run, u, 3, a, ring(b + 2, 4))
    for step in (3, 5, 4):
        take(step)
    bound_ref[0:8, :] = tops[...]
    bound_ref[8:24, :] = jnp.broadcast_to(jnp.sum(weighted * weighted, axis=1, keepdims=True), (16, 128))
    for run in range(2):
        for u in range(4):
            for v in range(4):
                a = ring(first[run] + (0, -1, 1, 2)[u], 4)
                b = ring(second[run] + (0, -1, 1, 2)[v], 4)
                k = run * 16 + u * 4 + v
                arrive(unit(*node(run, a, b), run * 8, 8, 1 - core), s_send.at[k], s_recv.at[k])
    for copy in sent:
        copy.wait_send()


def spread(*operands):
    whole = pl.BlockSpec(memory_space=VMEM)
    return pl.pallas_call(
        spread_kernel,
        out_shape=(
            jax.ShapeDtypeStruct((2, 4, 1024, 128), BF16),
            jax.ShapeDtypeStruct((4, 16, 128, 256), BF16),
            jax.ShapeDtypeStruct((4, 16, 256, 128), BF16),
            jax.ShapeDtypeStruct((2, 4, 2, 16, 2, 32, 256), BF16),
            jax.ShapeDtypeStruct((24, 128), F32),
            jax.ShapeDtypeStruct((128, 128), BF16),
            jax.ShapeDtypeStruct((8, 128), jnp.int32),
        ),
        in_specs=[pl.BlockSpec(memory_space=pltpu.HBM)] * len(operands),
        out_specs=(whole,) * 7,
        scratch_shapes=[
            VMEM((128, 32, 128), BF16),
            VMEM((1, 128), F32),
            VMEM((2, 128), BF16),
            VMEM((8, 128), jnp.int32),
            VMEM((128, 128), BF16),
            VMEM((16, 16), jnp.int32),
            VMEM((4096, 128), F32),
            VMEM((8, 4, 128, 128), BF16),
            VMEM((4, 1024, 128), BF16),
            VMEM((2, 272, 128), BF16),
            VMEM((512, 128), BF16),
            VMEM((256, 128), F32),
            VMEM((2, 32, 256), BF16),
            VMEM((8, 128), F32),
            DMA((10,)), DMA((8,)), DMA((8,)), DMA((8,)), DMA((8,)), DMA, DMA,
            DMA((40,)), DMA((40,)), DMA((32,)), DMA((32,)), DMA((2,)),
        ],
        compiler_params=pltpu.CompilerParams(
            collective_id=0, has_side_effects=True, vmem_limit_bytes=32 * 1024 * 1024
        ),
        name="spread",
    )(*operands)


def attend_kernel(
    lists_ref, qg_ref, kbd, vbd, bias, bound_ref,
    acc0, acc1, acc2, acc3,
    peak,
):
    accs = (acc0, acc1, acc2, acc3)
    for acc in accs:
        acc[...] = jnp.zeros_like(acc)
    same = (
        lax.div(lax.broadcasted_iota(jnp.int32, (256, 128), 0), 64)
        == lax.div(lax.broadcasted_iota(jnp.int32, (256, 128), 1), 32)
    ).astype(F32).astype(BF16)

    reach = jnp.sqrt(jnp.max(bound_ref[0:1, :])) * jnp.sqrt(jnp.max(bound_ref[1:2, :]))
    bias_reach = jnp.sqrt(jnp.max(bound_ref[8:24, :])) * (math.sqrt(128) * LOG2E)
    safe = (reach + bias_reach) * 1.03 <= SAFE

    def query(j, i):
        return qg_ref[0, j, pl.ds(pl.multiple_of(jnp.minimum(i, 15) * 64, 64), 64), :]

    def values_of(j, block):
        return jnp.concatenate([vbd[j, block], same], axis=1)

    total_pairs = lists_ref[3, 0]

    @pl.when(safe)
    def _():
        def step(t, carry):
            work = []
            for side in range(2):
                e = 2 * t + side
                block = lists_ref[0, e]
                ids = (lists_ref[1, e], lists_ref[2, e])
                offset = jnp.concatenate(
                    [bias[jnp.minimum(i, 15), block].astype(F32) for i in ids], axis=0
                )
                work.append((block, ids, offset))
            for j in range(4):
                for block, ids, offset in work:
                    queries = jnp.concatenate([query(j, i) for i in ids], axis=0)
                    score = jnp.dot(queries, kbd[j, block], preferred_element_type=F32)
                    weights = jnp.exp2(score + offset).astype(BF16)
                    total = jnp.dot(weights, values_of(j, block), preferred_element_type=F32)
                    olds = [accs[j][i] for i in ids]
                    for n in range(2):
                        accs[j][ids[n]] = olds[n] + total[n * 64:(n + 1) * 64, :]
            return carry

        lax.fori_loop(0, lax.div(total_pairs + 1, 2), step, 0)

    @pl.when(jnp.logical_not(safe))
    def _():
        peak[...] = jnp.full_like(peak, -1e30)

        def step(n, carry):
            e = lax.div(n, 2)
            block = lists_ref[0, e]
            i = lists_ref[1 + lax.rem(n, 2), e]
            offset = bias[jnp.minimum(i, 15), block].astype(F32)
            for j in range(4):
                score = jnp.dot(query(j, i), kbd[j, block], preferred_element_type=F32) + offset
                old = peak[j, i]
                tops = [
                    jnp.maximum(
                        jnp.max(score[:, h * 64:(h + 1) * 64], axis=1, keepdims=True),
                        old[:, h * 32:h * 32 + 1],
                    )
                    for h in range(4)
                ]
                shift = jnp.concatenate([jnp.broadcast_to(top, (64, 64)) for top in tops], axis=1)
                fresh = jnp.concatenate([jnp.broadcast_to(top, (64, 32)) for top in tops], axis=1)
                decay = jnp.exp2(old - fresh)
                weights = jnp.exp2(score - shift).astype(BF16)
                total = jnp.dot(weights, values_of(j, block), preferred_element_type=F32)
                accs[j][i] = accs[j][i] * jnp.concatenate([decay, decay], axis=1) + total
                peak[j, i] = fresh
            return carry

        lax.fori_loop(0, 2 * total_pairs, step, 0)


def attend(lists, qg, kbd, vbd, bias, bound):
    whole = pl.BlockSpec(memory_space=VMEM)
    return pl.pallas_call(
        attend_kernel,
        out_shape=[jax.ShapeDtypeStruct((18, 64, 256), F32)] * 4,
        in_specs=[pl.BlockSpec(memory_space=pltpu.SMEM)] + [whole] * 5,
        out_specs=[whole] * 4,
        scratch_shapes=[VMEM((4, 18, 64, 128), F32)],
        compiler_params=pltpu.CompilerParams(vmem_limit_bytes=24 * 1024 * 1024),
        name="attend",
    )(lists, qg, kbd, vbd, bias, bound)


def deliver_kernel(
    acc0, acc1, acc2, acc3, qg_ref, mixing_ref, out_ref, update_ref, send_sem, recv_sem, own_sem
):
    row = lax.axis_index("row")
    col = lax.axis_index("col")
    head = lax.axis_index("head")

    def other(flip):
        return (1 - head) if flip else head

    def device(step, flip):
        return (ring(row + step, 8), col, other(flip))

    moves = [(step, flip) for step in (4, 3, 5, 2, 6, 1, 7) for flip in (1, 0)] + [(0, 1)]
    barrier = pltpu.get_barrier_semaphore()
    for step, flip in moves:
        pl.semaphore_signal(barrier, inc=1, device_id=device(step, flip), device_id_type=MESH)

    def spot(step, flip):
        return out_ref.at[pl.ds((other(flip) * 8 + ring(row + step, 8)) * 4, 4)]

    def part(step, flip):
        return update_ref.at[other(flip), ring(row + step, 8)]

    def finish(step):
        target = ring(row + step, 8)
        rows = pl.ds(pl.multiple_of(target * 128, 128), 128)
        for j, acc in enumerate((acc0, acc1, acc2, acc3)):
            sums = acc[pl.ds(target * 2, 2)].reshape(128, 256)
            attention = sums[:, :128] / sums[:, 128:]
            gated = (attention * qg_ref[1, j, rows, :].astype(F32)).astype(BF16)
            update = lax.dot_general(mixing_ref[...], gated, NT, preferred_element_type=F32).astype(BF16)
            update_ref[0, target, j] = update[:64, :]
            update_ref[1, target, j] = update[64:, :]

    copies = []

    def push(step, flip):
        k = flip * 8 + step
        copy = pltpu.make_async_remote_copy(
            src_ref=part(step, flip), dst_ref=spot(0, 0),
            send_sem=send_sem.at[k], recv_sem=recv_sem.at[k],
            device_id=device(step, flip), device_id_type=MESH,
        )
        copy.start()
        copies.append(copy)

    for step in (4, 3, 5, 2, 6, 1, 7, 0):
        finish(step)
        if step == 4:
            pl.semaphore_wait(barrier, len(moves))
        push(step, 1)
        if step > 0:
            push(step, 0)
    own = pltpu.make_async_copy(part(0, 0), spot(0, 0), own_sem)
    own.start()
    own.wait()
    for step, flip in moves:
        k = flip * 8 + step
        pltpu.make_async_remote_copy(
            src_ref=spot(-step, flip), dst_ref=spot(-step, flip),
            send_sem=send_sem.at[k], recv_sem=recv_sem.at[k],
            device_id=device(step, flip), device_id_type=MESH,
        ).wait_recv()
    for copy in copies:
        copy.wait_send()


def deliver(accs, qg, mixing):
    whole = pl.BlockSpec(memory_space=VMEM)
    return pl.pallas_call(
        deliver_kernel,
        out_shape=jax.ShapeDtypeStruct((64, 64, 128), BF16),
        in_specs=[whole] * 6,
        out_specs=whole,
        scratch_shapes=[VMEM((2, 8, 4, 64, 128), BF16), DMA((16,)), DMA((16,)), DMA],
        compiler_params=pltpu.CompilerParams(
            collective_id=1, has_side_effects=True, vmem_limit_bytes=16 * 1024 * 1024
        ),
        name="deliver",
    )(*accs, qg, mixing)


def per_device(
    pair_field, ln_gain, w_query, w_key, w_value, w_gate, w_bias, w_out, tile_mask, type_ids
):
    weights = [w.T for w in (w_query, w_key, w_value, w_gate)]
    weights.append(w_bias.T)
    operands = (pair_field, ln_gain.reshape(1, 128), *weights, type_ids.reshape(8, 128), w_out, tile_mask)
    qg, kbd, vbd, bias, bound, mixing, lists = spread(
        *[pltpu.with_memory_space_constraint(operand, pltpu.HBM) for operand in operands]
    )
    accs = attend(lists, qg, kbd, vbd, bias.reshape(16, 16, 64, 256), bound)
    return jnp.transpose(deliver(accs, qg, mixing), (2, 0, 1))


def solution(mesh):
    return jax.shard_map(
        per_device,
        mesh=mesh,
        in_specs=(
            P("row", "col", None),
            P(),
            P(None, "head"),
            P(None, "head"),
            P(None, "head"),
            P(None, "head"),
            P(None, "head"),
            P(),
            P(),
            P(),
        ),
        out_specs=P("row", "col", "head"),
        check_vma=False,
    )
```

```python
import math

import jax
import jax.numpy as jnp
from jax import lax
from jax.experimental import pallas as pl
from jax.experimental.pallas import tpu as pltpu
from jax.sharding import PartitionSpec as P

MESH = pl.DeviceIdType.MESH
F32 = jnp.float32
BF16 = jnp.bfloat16
VMEM = pltpu.VMEM
DMA = pltpu.SemaphoreType.DMA

epsilon = 1e-05
masked_score = -1000000000.0
LOG2E = math.log2(math.e)
SCALE = LOG2E / math.sqrt(32)
SAFE = 64.0
NT = (((1,), (1,)), ((), ()))


def ring(value, size):
    return lax.rem(value + size, size)


def spread_kernel(
    tile_ref, gain_in, wq_ref, wk_ref, wv_ref, wg_ref, wb_in, types_in, w_out_in, mask_in,
    qg_ref, kbd_ref, vbd_ref, bias_ref, bound_ref, mixing_ref, lists_ref,
    half, gain_ref, wb_ref, types_ref, w_out_ref, mask_ref, wide, send, strip, wbuf, wall, flat, bsend, tops,
    load_sem, col_send, col_recv, z_send, z_recv, w_send, w_recv,
    g_send, g_recv, s_send, s_recv, own_sem,
):
    row = lax.axis_index("row")
    col = lax.axis_index("col")
    head = lax.axis_index("head")
    core = lax.rem(col, 2)
    x = lax.rem(lax.div(col, 2), 4)
    y = head * 2 + lax.div(col, 8)

    def place(x_, y_, core_=None):
        return (row, lax.rem(y_, 2) * 8 + x_ * 2 + (core if core_ is None else core_), lax.div(y_, 2))

    def along_z(step):
        return (ring(row + step, 8), col, head)

    partner = place(x, ring(y + 2, 4))
    peers = [along_z(step) for step in range(1, 8)]
    peers += [place(ring(x + 1, 4), y), place(ring(x - 1, 4), y)]
    peers += [place(x, ring(y + 1, 4)), place(x, ring(y - 1, 4)), partner]
    peers += [place(x, y, 1 - core)]
    barrier = pltpu.get_barrier_semaphore()
    for peer in peers:
        pl.semaphore_signal(barrier, inc=1, device_id=peer, device_id_type=MESH)

    loads = [
        (tile_ref.at[:, pl.ds(pl.multiple_of(head * 32, 32), 32), :], half),
        (gain_in, gain_ref), (wb_in, wb_ref), (types_in, types_ref),
    ]
    loads += [
        (ref, wbuf.at[head, pl.ds(kind * 64, 64)]) for kind, ref in enumerate((wq_ref, wk_ref, wv_ref, wg_ref))
    ]
    loads += [(w_out_in, w_out_ref), (mask_in, mask_ref)]
    loads = [pltpu.make_async_copy(src, dst, load_sem.at[n]) for n, (src, dst) in enumerate(loads)]
    for load in loads:
        load.start()
    tops[...] = jnp.zeros_like(tops)
    for load in loads:
        load.wait()
    wbuf[head, 256:272, :] = jnp.concatenate(
        [wb_ref[...].astype(F32), jnp.zeros((14, 128), F32)], axis=0
    ).astype(BF16)

    def widen(block, carry):
        rows = half[pl.ds(block * 8, 8)].astype(F32).reshape(256, 128)
        wide[pl.ds(pl.multiple_of(block * 256, 256), 256), :] = rows
        return carry

    lax.fori_loop(0, 16, widen, 0)
    ones = jnp.ones((128, 128), BF16)
    gain = gain_ref[...]

    def norm_for(step):
        target = ring(row + step, 8)
        for jj in range(4):
            value = wide[pl.ds(4 * target + jj, 128, stride=32), :]
            mean = jnp.dot(value.astype(BF16), ones, preferred_element_type=F32) * (1.0 / 128)
            centred = value - mean
            squares = (centred * centred).astype(BF16)
            spread = jnp.dot(squares, ones, preferred_element_type=F32) * (1.0 / 128)
            normed = centred * lax.rsqrt(spread + epsilon) * gain
            send[target, jj] = normed.astype(BF16)

    def norm_near(n, carry):
        norm_for(n)
        norm_for(-n)
        return carry

    def norm_far(n, carry):
        norm_for(3 + n)
        norm_for(-3 * (1 - n))
        return carry

    lax.fori_loop(1, 3, norm_near, 0)
    pl.semaphore_wait(barrier, len(peers))
    w_copy = pltpu.make_async_remote_copy(
        src_ref=wbuf.at[head], dst_ref=wbuf.at[head], send_sem=w_send, recv_sem=w_recv,
        device_id=partner, device_id_type=MESH,
    )
    w_copy.start()
    sent = [w_copy]

    def push(src, dst, send_sem, recv_sem, device):
        copy = pltpu.make_async_remote_copy(
            src_ref=src, dst_ref=dst, send_sem=send_sem, recv_sem=recv_sem,
            device_id=device, device_id_type=MESH,
        )
        copy.start()
        sent.append(copy)

    def strip_rows(step):
        source = ring(row + step, 8)
        return strip.at[:, pl.ds(pl.multiple_of(source * 128, 128), 128), :]

    def col_push(step):
        target = ring(row + step, 8)
        push(send.at[target], strip_rows(0), col_send.at[step], col_recv.at[step], along_z(step))

    col_push(1)
    col_push(7)
    lax.fori_loop(0, 2, norm_far, 0)
    pltpu.make_async_remote_copy(
        src_ref=wbuf.at[1 - head], dst_ref=wbuf.at[1 - head], send_sem=w_send, recv_sem=w_recv,
        device_id=partner, device_id_type=MESH,
    ).wait_recv()

    wb = wbuf[0, 256:272, :].astype(F32) + pltpu.roll(wbuf[1, 256:272, :].astype(F32), 2, 0)
    weighted = wb * gain
    wbt = wb.astype(BF16)

    def bias_for(target, carry):
        part = lax.dot_general(wbt, send[target].reshape(512, 128), NT, preferred_element_type=F32)
        for jj in range(4):
            flat[pl.ds(pl.multiple_of((4 * target + jj) * 8, 8), 8), :] = part[0:8, jj * 128:jj * 128 + 128]
        return carry

    lax.fori_loop(0, 8, bias_for, 0, unroll=4)
    living = jnp.broadcast_to(types_ref[pl.ds(row, 1), :] != 0, (32, 128))
    by_head = [
        jnp.where(living, flat[pl.ds(h, 32, stride=8), :] * LOG2E, masked_score) for h in range(4)
    ]
    bsend[0] = jnp.concatenate([b[:, :64] for b in by_head], axis=1).astype(BF16)
    bsend[1] = jnp.concatenate([b[:, 64:] for b in by_head], axis=1).astype(BF16)

    def unit(x_, y_, low, count, core_=None):
        return bias_ref.at[
            lax.rem(y_, 2), x_, core if core_ is None else core_, pl.ds(low, count), lax.div(y_, 2)
        ]

    def arrive(dst, send_sem, recv_sem):
        pltpu.make_async_remote_copy(
            src_ref=dst, dst_ref=dst, send_sem=send_sem, recv_sem=recv_sem,
            device_id=partner, device_id_type=MESH,
        ).wait_recv()

    def chunk(step, low=0, count=2):
        return unit(x, y, 2 * ring(row + step, 8) + low, count)

    def z_push(k, src, dst, step):
        push(src, dst, z_send.at[k], z_recv.at[k], along_z(step))

    def z_arrive(k, dst):
        arrive(dst, z_send.at[k], z_recv.at[k])

    own = pltpu.make_async_copy(bsend, chunk(0), own_sem.at[0])
    own.start()
    for k, step in enumerate((2, -2, 1, -1)):
        z_push(k, bsend, chunk(0), step)

    own_cols = pltpu.make_async_copy(send.at[row], strip_rows(0), own_sem.at[1])
    own_cols.start()

    for kind, place_of in enumerate((1, 0, 2, 3)):
        for s in range(2):
            wall[place_of * 128 + s * 64:place_of * 128 + s * 64 + 64, :] = wbuf[s, kind * 64:kind * 64 + 64, :]
    together = (
        lax.div(lax.broadcasted_iota(jnp.int32, (128, 128), 0), 32)
        == lax.div(lax.broadcasted_iota(jnp.int32, (128, 128), 1), 32)
    ).astype(F32).astype(BF16)

    key_head = lax.div(lax.broadcasted_iota(jnp.int32, (128, 128), 0), 32)
    side_of = lax.div(lax.broadcasted_iota(jnp.int32, (128, 128), 1), 64)
    key_here = [(key_head == 2 * n + side_of).astype(F32).astype(BF16) for n in range(2)]
    lane_head = lax.div(lax.broadcasted_iota(jnp.int32, (64, 128), 1), 32)
    value_here = [(lane_head == h).astype(F32).astype(BF16) for h in range(4)]

    def project(step):
        source = ring(row + step, 8)
        rows = pl.ds(pl.multiple_of(source * 128, 128), 128)

        def one(jj, carry):
            value = strip[jj, rows, :]
            keys = lax.dot_general(wall[0:128, :], value, NT, preferred_element_type=F32)
            left = lax.dot_general(value, wall[128:256, :], NT, preferred_element_type=F32)
            right = lax.dot_general(value, wall[256:512, :], NT, preferred_element_type=F32)
            query = left * SCALE
            qg_ref[0, jj, rows, :] = query.astype(BF16)
            qg_ref[1, jj, rows, :] = jax.nn.sigmoid(right[:, 128:]).astype(BF16)
            short = keys.astype(BF16)
            values = right[:, :128].astype(BF16)
            for odd in range(2):
                twice = jnp.concatenate([short[:, odd * 64:odd * 64 + 64]] * 2, axis=1)
                for n in range(2):
                    kbd_ref[jj, 2 * source + odd, :, n * 128:(n + 1) * 128] = twice * key_here[n]
                for h in range(4):
                    vbd_ref[jj, 2 * source + odd, h * 64:(h + 1) * 64, :] = (
                        values[odd * 64:odd * 64 + 64, :] * value_here[h]
                    )
            lengths = jnp.dot((query * query).astype(BF16), together, preferred_element_type=F32)
            tops[0:1, :] = jnp.maximum(tops[0:1, :], jnp.max(lengths, axis=0, keepdims=True))
            lengths = jnp.dot(together, (keys * keys).astype(BF16), preferred_element_type=F32)
            tops[1:2, :] = jnp.maximum(tops[1:2, :], jnp.max(lengths, axis=0, keepdims=True))
            return carry

        lax.fori_loop(0, 4, one, 0, unroll=2)

    def take(step):
        arrive(strip_rows(-step), col_send.at[step], col_recv.at[step])
        project(-step)

    own.wait()
    own_cols.wait()
    for k, step in enumerate((-2, 2, -1, 1)):
        z_arrive(k, chunk(step))
    z_push(4, chunk(-2), chunk(-2), 1)
    z_push(5, chunk(2), chunk(2), -1)
    z_push(6, chunk(-2, 0, 1), chunk(-2, 0, 1), 2)
    z_push(7, chunk(2, 1, 1), chunk(2, 1, 1), -2)
    project(0)
    z_arrive(4, chunk(-3))
    z_arrive(5, chunk(3))
    z_arrive(6, chunk(4, 0, 1))
    z_arrive(7, chunk(4, 1, 1))

    def make_lists():
        mixing_ref[...] = w_out_ref[...].astype(F32).T.astype(BF16)
        part = mask_ref[...].astype(F32)
        diagonal = lax.broadcasted_iota(jnp.int32, (16, 16), 0) == lax.broadcasted_iota(jnp.int32, (16, 16), 1)
        part = jnp.where((part == 1.0) | diagonal, 1.0, 0.0)
        allowed = jnp.concatenate([part, jnp.zeros((16, 112), F32)], axis=1)
        before = [jnp.zeros((1, 128), F32)]
        for i in range(16):
            before.append(before[-1] + allowed[i:i + 1, :])
        rank = jnp.concatenate(before[:16], axis=0)
        pairs = jnp.broadcast_to(jnp.floor((before[16] + 1.0) * 0.5), (16, 128))
        earlier = (
            lax.broadcasted_iota(jnp.int32, (128, 128), 0) < lax.broadcasted_iota(jnp.int32, (128, 128), 1)
        ).astype(F32).astype(BF16)
        start = jnp.dot(pairs.astype(BF16), earlier, preferred_element_type=F32)
        total = jnp.sum(pairs[0:1, :], axis=1, keepdims=True)
        rank = rank + 2.0 * start
        entry = 2.0 * lax.broadcasted_iota(jnp.int32, (16, 128), 1).astype(F32)
        number = lax.broadcasted_iota(jnp.int32, (16, 128), 0).astype(F32)
        block = jnp.zeros((16, 128), F32)
        picked = [jnp.zeros((16, 128), F32)] * 2
        found = [jnp.zeros((16, 128), F32)] * 2
        for k in range(16):
            at = jnp.broadcast_to(rank[:, k:k + 1], (16, 128))
            here = jnp.broadcast_to(allowed[:, k:k + 1], (16, 128))
            for side in range(2):
                hit = jnp.where(at == entry + side, here, 0.0)
                found[side] = found[side] + hit
                picked[side] = picked[side] + hit * number
                if side == 0:
                    block = block + hit * k
        rows = [jnp.sum(block, axis=0, keepdims=True)]
        for side in range(2):
            missing = 1.0 - jnp.sum(found[side], axis=0, keepdims=True)
            rows.append(jnp.sum(picked[side], axis=0, keepdims=True) + (16.0 + side) * missing)
        rows.append(jnp.broadcast_to(total, (1, 128)))
        rows.append(jnp.zeros((4, 128), F32))
        lists_ref[...] = jnp.concatenate(rows, axis=0).astype(jnp.int32)

    def node(run, a, b):
        return (a, b) if run == 0 else (b, a)

    first = (x, y)
    second = (y, x)

    def shipment(run, index, a, b, low, count, to_a, to_b):
        k = run * 20 + index
        ref = unit(*node(run, a, b), run * 8 + low, count)
        push(ref, ref, g_send.at[k], g_recv.at[k], place(*node(run, to_a, to_b)))

    def receive(run, index, a, b, low, count):
        k = run * 20 + index
        arrive(unit(*node(run, a, b), run * 8 + low, count), g_send.at[k], g_recv.at[k])

    def to_sibling(run, u, v, a, b):
        k = run * 16 + u * 4 + v
        ref = unit(*node(run, a, b), run * 8, 8)
        push(ref, ref, s_send.at[k], s_recv.at[k], place(x, y, 1 - core))

    def across(run, u, a, b):
        shipment(run, 4 + 4 * u, a, b, 0, 8, first[run], ring(b + 1, 4))
        shipment(run, 5 + 4 * u, a, b, 0, 8, first[run], ring(b - 1, 4))

    for run in range(2):
        a, b = first[run], second[run]
        shipment(run, 0, a, b, 0, 8, ring(a + 1, 4), b)
        shipment(run, 1, a, b, 0, 8, ring(a - 1, 4), b)
    for run in range(2):
        a, b = first[run], second[run]
        across(run, 0, a, b)
        to_sibling(run, 0, 0, a, b)
    for step in (2, 6, 3, 5, 4):
        col_push(step)
    for run in range(2):
        a, b = first[run], second[run]
        receive(run, 0, ring(a - 1, 4), b, 0, 8)
        shipment(run, 2, ring(a - 1, 4), b, 0, 4, ring(a + 1, 4), b)
        receive(run, 1, ring(a + 1, 4), b, 0, 8)
        shipment(run, 3, ring(a + 1, 4), b, 4, 4, ring(a - 1, 4), b)
    for run in range(2):
        a, b = first[run], second[run]
        across(run, 1, ring(a - 1, 4), b)
        to_sibling(run, 1, 0, ring(a - 1, 4), b)
        across(run, 2, ring(a + 1, 4), b)
        to_sibling(run, 2, 0, ring(a + 1, 4), b)
    for run in range(2):
        a, b = first[run], second[run]
        receive(run, 2, ring(a + 2, 4), b, 0, 4)
        receive(run, 3, ring(a + 2, 4), b, 4, 4)
        across(run, 3, ring(a + 2, 4), b)
        to_sibling(run, 3, 0, ring(a + 2, 4), b)
    take(1)
    take(7)
    for u in range(4):
        for run in range(2):
            a, b = ring(first[run] + (0, -1, 1, 2)[u], 4), second[run]
            receive(run, 4 + 4 * u, a, ring(b - 1, 4), 0, 8)
            shipment(run, 6 + 4 * u, a, ring(b - 1, 4), 0, 4, first[run], ring(b + 1, 4))
            to_sibling(run, u, 1, a, ring(b - 1, 4))
            receive(run, 5 + 4 * u, a, ring(b + 1, 4), 0, 8)
            shipment(run, 7 + 4 * u, a, ring(b + 1, 4), 4, 4, first[run], ring(b - 1, 4))
            to_sibling(run, u, 2, a, ring(b + 1, 4))
        if u == 1:
            make_lists()
        if u == 3:
            take(2)
            take(6)
    for u in range(4):
        for run in range(2):
            a, b = ring(first[run] + (0, -1, 1, 2)[u], 4), second[run]
            receive(run, 6 + 4 * u, a, ring(b + 2, 4), 0, 4)
            receive(run, 7 + 4 * u, a, ring(b + 2, 4), 4, 4)
            to_sibling(run, u, 3, a, ring(b + 2, 4))
    for step in (3, 5, 4):
        take(step)
    bound_ref[0:8, :] = tops[...]
    bound_ref[8:24, :] = jnp.broadcast_to(jnp.sum(weighted * weighted, axis=1, keepdims=True), (16, 128))
    for run in range(2):
        for u in range(4):
            for v in range(4):
                a = ring(first[run] + (0, -1, 1, 2)[u], 4)
                b = ring(second[run] + (0, -1, 1, 2)[v], 4)
                k = run * 16 + u * 4 + v
                arrive(unit(*node(run, a, b), run * 8, 8, 1 - core), s_send.at[k], s_recv.at[k])
    for copy in sent:
        copy.wait_send()


def spread(*operands):
    whole = pl.BlockSpec(memory_space=VMEM)
    return pl.pallas_call(
        spread_kernel,
        out_shape=(
            jax.ShapeDtypeStruct((2, 4, 1024, 128), BF16),
            jax.ShapeDtypeStruct((4, 16, 128, 256), BF16),
            jax.ShapeDtypeStruct((4, 16, 256, 128), BF16),
            jax.ShapeDtypeStruct((2, 4, 2, 16, 2, 32, 256), BF16),
            jax.ShapeDtypeStruct((24, 128), F32),
            jax.ShapeDtypeStruct((128, 128), BF16),
            jax.ShapeDtypeStruct((8, 128), jnp.int32),
        ),
        in_specs=[pl.BlockSpec(memory_space=pltpu.HBM)] * len(operands),
        out_specs=(whole,) * 7,
        scratch_shapes=[
            VMEM((128, 32, 128), BF16),
            VMEM((1, 128), F32),
            VMEM((2, 128), BF16),
            VMEM((8, 128), jnp.int32),
            VMEM((128, 128), BF16),
            VMEM((16, 16), jnp.int32),
            VMEM((4096, 128), F32),
            VMEM((8, 4, 128, 128), BF16),
            VMEM((4, 1024, 128), BF16),
            VMEM((2, 272, 128), BF16),
            VMEM((512, 128), BF16),
            VMEM((256, 128), F32),
            VMEM((2, 32, 256), BF16),
            VMEM((8, 128), F32),
            DMA((10,)), DMA((8,)), DMA((8,)), DMA((8,)), DMA((8,)), DMA, DMA,
            DMA((40,)), DMA((40,)), DMA((32,)), DMA((32,)), DMA((2,)),
        ],
        compiler_params=pltpu.CompilerParams(
            collective_id=0, has_side_effects=True, vmem_limit_bytes=32 * 1024 * 1024
        ),
        name="spread",
    )(*operands)


def attend_kernel(
    lists_ref, qg_ref, kbd, vbd, bias, bound_ref,
    acc0, acc1, acc2, acc3,
    peak,
):
    accs = (acc0, acc1, acc2, acc3)
    for acc in accs:
        acc[...] = jnp.zeros_like(acc)
    same = (
        lax.div(lax.broadcasted_iota(jnp.int32, (256, 128), 0), 64)
        == lax.div(lax.broadcasted_iota(jnp.int32, (256, 128), 1), 32)
    ).astype(F32).astype(BF16)

    reach = jnp.sqrt(jnp.max(bound_ref[0:1, :])) * jnp.sqrt(jnp.max(bound_ref[1:2, :]))
    bias_reach = jnp.sqrt(jnp.max(bound_ref[8:24, :])) * (math.sqrt(128) * LOG2E)
    safe = (reach + bias_reach) * 1.03 <= SAFE

    def query(j, i):
        return qg_ref[0, j, pl.ds(pl.multiple_of(jnp.minimum(i, 15) * 64, 64), 64), :]

    def values_of(j, block):
        return jnp.concatenate([vbd[j, block], same], axis=1)

    total_pairs = lists_ref[3, 0]

    @pl.when(safe)
    def _():
        def step(t, carry):
            work = []
            for side in range(2):
                e = 2 * t + side
                block = lists_ref[0, e]
                ids = (lists_ref[1, e], lists_ref[2, e])
                offset = jnp.concatenate(
                    [bias[jnp.minimum(i, 15), block].astype(F32) for i in ids], axis=0
                )
                work.append((block, ids, offset))
            for j in range(4):
                for block, ids, offset in work:
                    queries = jnp.concatenate([query(j, i) for i in ids], axis=0)
                    score = jnp.dot(queries, kbd[j, block], preferred_element_type=F32)
                    weights = jnp.exp2(score + offset).astype(BF16)
                    total = jnp.dot(weights, values_of(j, block), preferred_element_type=F32)
                    olds = [accs[j][i] for i in ids]
                    for n in range(2):
                        accs[j][ids[n]] = olds[n] + total[n * 64:(n + 1) * 64, :]
            return carry

        lax.fori_loop(0, lax.div(total_pairs + 1, 2), step, 0)

    @pl.when(jnp.logical_not(safe))
    def _():
        peak[...] = jnp.full_like(peak, -1e30)

        def step(n, carry):
            e = lax.div(n, 2)
            block = lists_ref[0, e]
            i = lists_ref[1 + lax.rem(n, 2), e]
            offset = bias[jnp.minimum(i, 15), block].astype(F32)
            for j in range(4):
                score = jnp.dot(query(j, i), kbd[j, block], preferred_element_type=F32) + offset
                old = peak[j, i]
                tops = [
                    jnp.maximum(
                        jnp.max(score[:, h * 64:(h + 1) * 64], axis=1, keepdims=True),
                        old[:, h * 32:h * 32 + 1],
                    )
                    for h in range(4)
                ]
                shift = jnp.concatenate([jnp.broadcast_to(top, (64, 64)) for top in tops], axis=1)
                fresh = jnp.concatenate([jnp.broadcast_to(top, (64, 32)) for top in tops], axis=1)
                decay = jnp.exp2(old - fresh)
                weights = jnp.exp2(score - shift).astype(BF16)
                total = jnp.dot(weights, values_of(j, block), preferred_element_type=F32)
                accs[j][i] = accs[j][i] * jnp.concatenate([decay, decay], axis=1) + total
                peak[j, i] = fresh
            return carry

        lax.fori_loop(0, 2 * total_pairs, step, 0)


def attend(lists, qg, kbd, vbd, bias, bound):
    whole = pl.BlockSpec(memory_space=VMEM)
    return pl.pallas_call(
        attend_kernel,
        out_shape=[jax.ShapeDtypeStruct((18, 64, 256), F32)] * 4,
        in_specs=[pl.BlockSpec(memory_space=pltpu.SMEM)] + [whole] * 5,
        out_specs=[whole] * 4,
        scratch_shapes=[VMEM((4, 18, 64, 128), F32)],
        compiler_params=pltpu.CompilerParams(vmem_limit_bytes=24 * 1024 * 1024),
        name="attend",
    )(lists, qg, kbd, vbd, bias, bound)


def deliver_kernel(
    acc0, acc1, acc2, acc3, qg_ref, mixing_ref, out_ref, update_ref, send_sem, recv_sem, own_sem
):
    row = lax.axis_index("row")
    col = lax.axis_index("col")
    head = lax.axis_index("head")

    def other(flip):
        return (1 - head) if flip else head

    def device(step, flip):
        return (ring(row + step, 8), col, other(flip))

    moves = [(step, flip) for step in (4, 3, 5, 2, 6, 1, 7) for flip in (1, 0)] + [(0, 1)]
    barrier = pltpu.get_barrier_semaphore()
    for step, flip in moves:
        pl.semaphore_signal(barrier, inc=1, device_id=device(step, flip), device_id_type=MESH)

    def spot(step, flip):
        return out_ref.at[pl.ds((other(flip) * 8 + ring(row + step, 8)) * 4, 4)]

    def part(step, flip):
        return update_ref.at[other(flip), ring(row + step, 8)]

    def finish(step):
        target = ring(row + step, 8)
        rows = pl.ds(pl.multiple_of(target * 128, 128), 128)
        for j, acc in enumerate((acc0, acc1, acc2, acc3)):
            sums = acc[pl.ds(target * 2, 2)].reshape(128, 256)
            attention = sums[:, :128] / sums[:, 128:]
            gated = (attention * qg_ref[1, j, rows, :].astype(F32)).astype(BF16)
            update = lax.dot_general(mixing_ref[...], gated, NT, preferred_element_type=F32).astype(BF16)
            update_ref[0, target, j] = update[:64, :]
            update_ref[1, target, j] = update[64:, :]

    copies = []

    def push(step, flip):
        k = flip * 8 + step
        copy = pltpu.make_async_remote_copy(
            src_ref=part(step, flip), dst_ref=spot(0, 0),
            send_sem=send_sem.at[k], recv_sem=recv_sem.at[k],
            device_id=device(step, flip), device_id_type=MESH,
        )
        copy.start()
        copies.append(copy)

    for step in (4, 3, 5):
        finish(step)
    pl.semaphore_wait(barrier, len(moves))
    for step in (4, 3, 5, 2, 6, 1, 7, 0):
        if step not in (4, 3, 5):
            finish(step)
        push(step, 1)
        if step > 0:
            push(step, 0)
    own = pltpu.make_async_copy(part(0, 0), spot(0, 0), own_sem)
    own.start()
    own.wait()
    for step, flip in moves:
        k = flip * 8 + step
        pltpu.make_async_remote_copy(
            src_ref=spot(-step, flip), dst_ref=spot(-step, flip),
            send_sem=send_sem.at[k], recv_sem=recv_sem.at[k],
            device_id=device(step, flip), device_id_type=MESH,
        ).wait_recv()
    for copy in copies:
        copy.wait_send()


def deliver(accs, qg, mixing):
    whole = pl.BlockSpec(memory_space=VMEM)
    return pl.pallas_call(
        deliver_kernel,
        out_shape=jax.ShapeDtypeStruct((64, 64, 128), BF16),
        in_specs=[whole] * 6,
        out_specs=whole,
        scratch_shapes=[VMEM((2, 8, 4, 64, 128), BF16), DMA((16,)), DMA((16,)), DMA],
        compiler_params=pltpu.CompilerParams(
            collective_id=1, has_side_effects=True, vmem_limit_bytes=16 * 1024 * 1024
        ),
        name="deliver",
    )(*accs, qg, mixing)


def per_device(
    pair_field, ln_gain, w_query, w_key, w_value, w_gate, w_bias, w_out, tile_mask, type_ids
):
    weights = [w.T for w in (w_query, w_key, w_value, w_gate)]
    weights.append(w_bias.T)
    operands = (pair_field, ln_gain.reshape(1, 128), *weights, type_ids.reshape(8, 128), w_out, tile_mask)
    qg, kbd, vbd, bias, bound, mixing, lists = spread(
        *[pltpu.with_memory_space_constraint(operand, pltpu.HBM) for operand in operands]
    )
    accs = attend(lists, qg, kbd, vbd, bias.reshape(16, 16, 64, 256), bound)
    return jnp.transpose(deliver(accs, qg, mixing), (2, 0, 1))


def solution(mesh):
    return jax.shard_map(
        per_device,
        mesh=mesh,
        in_specs=(
            P("row", "col", None),
            P(),
            P(None, "head"),
            P(None, "head"),
            P(None, "head"),
            P(None, "head"),
            P(None, "head"),
            P(),
            P(),
            P(),
        ),
        out_specs=P("row", "col", "head"),
        check_vma=False,
    )
```

```python
import math

import jax
import jax.numpy as jnp
from jax import lax
from jax.experimental import pallas as pl
from jax.experimental.pallas import tpu as pltpu
from jax.sharding import PartitionSpec as P

MESH = pl.DeviceIdType.MESH
F32 = jnp.float32
BF16 = jnp.bfloat16
VMEM = pltpu.VMEM
DMA = pltpu.SemaphoreType.DMA

epsilon = 1e-05
masked_score = -1000000000.0
LOG2E = math.log2(math.e)
SCALE = LOG2E / math.sqrt(32)
SAFE = 64.0
NT = (((1,), (1,)), ((), ()))


def ring(value, size):
    return lax.rem(value + size, size)


def spread_kernel(
    tile_ref, gain_in, wq_ref, wk_ref, wv_ref, wg_ref, wb_in, types_in, w_out_in, mask_in,
    qg_ref, kbd_ref, vbd_ref, bias_ref, bound_ref, mixing_ref, lists_ref,
    half, gain_ref, wb_ref, types_ref, w_out_ref, mask_ref, wide, send, strip, wbuf, wall, flat, bsend, tops,
    load_sem, col_send, col_recv, z_send, z_recv, w_send, w_recv,
    g_send, g_recv, s_send, s_recv, own_sem,
):
    row = lax.axis_index("row")
    col = lax.axis_index("col")
    head = lax.axis_index("head")
    core = lax.rem(col, 2)
    x = lax.rem(lax.div(col, 2), 4)
    y = head * 2 + lax.div(col, 8)

    def place(x_, y_, core_=None):
        return (row, lax.rem(y_, 2) * 8 + x_ * 2 + (core if core_ is None else core_), lax.div(y_, 2))

    def along_z(step):
        return (ring(row + step, 8), col, head)

    partner = place(x, ring(y + 2, 4))
    peers = [along_z(step) for step in range(1, 8)]
    peers += [place(ring(x + 1, 4), y), place(ring(x - 1, 4), y)]
    peers += [place(x, ring(y + 1, 4)), place(x, ring(y - 1, 4)), partner]
    peers += [place(x, y, 1 - core)]
    barrier = pltpu.get_barrier_semaphore()
    for peer in peers:
        pl.semaphore_signal(barrier, inc=1, device_id=peer, device_id_type=MESH)

    loads = [
        (tile_ref.at[:, pl.ds(pl.multiple_of(head * 32, 32), 32), :], half),
        (gain_in, gain_ref), (wb_in, wb_ref), (types_in, types_ref),
    ]
    loads += [
        (ref, wbuf.at[head, pl.ds(kind * 64, 64)]) for kind, ref in enumerate((wq_ref, wk_ref, wv_ref, wg_ref))
    ]
    loads += [(w_out_in, w_out_ref), (mask_in, mask_ref)]
    loads = [pltpu.make_async_copy(src, dst, load_sem.at[n]) for n, (src, dst) in enumerate(loads)]
    for load in loads:
        load.start()
    tops[...] = jnp.zeros_like(tops)
    loads[0].wait()

    def widen(block, carry):
        rows = half[pl.ds(block * 8, 8)].astype(F32).reshape(256, 128)
        wide[pl.ds(pl.multiple_of(block * 256, 256), 256), :] = rows
        return carry

    lax.fori_loop(0, 16, widen, 0)
    ones = jnp.ones((128, 128), BF16)
    loads[1].wait()
    gain = gain_ref[...]

    def norm_for(step):
        target = ring(row + step, 8)
        for jj in range(4):
            value = wide[pl.ds(4 * target + jj, 128, stride=32), :]
            mean = jnp.dot(value.astype(BF16), ones, preferred_element_type=F32) * (1.0 / 128)
            centred = value - mean
            squares = (centred * centred).astype(BF16)
            spread = jnp.dot(squares, ones, preferred_element_type=F32) * (1.0 / 128)
            normed = centred * lax.rsqrt(spread + epsilon) * gain
            send[target, jj] = normed.astype(BF16)

    def norm_near(n, carry):
        norm_for(n)
        norm_for(-n)
        return carry

    def norm_far(n, carry):
        norm_for(3 + n)
        norm_for(-3 * (1 - n))
        return carry

    lax.fori_loop(1, 3, norm_near, 0)
    for load in loads[2:]:
        load.wait()
    wbuf[head, 256:272, :] = jnp.concatenate(
        [wb_ref[...].astype(F32), jnp.zeros((14, 128), F32)], axis=0
    ).astype(BF16)
    pl.semaphore_wait(barrier, len(peers))
    w_copy = pltpu.make_async_remote_copy(
        src_ref=wbuf.at[head], dst_ref=wbuf.at[head], send_sem=w_send, recv_sem=w_recv,
        device_id=partner, device_id_type=MESH,
    )
    w_copy.start()
    sent = [w_copy]

    def push(src, dst, send_sem, recv_sem, device):
        copy = pltpu.make_async_remote_copy(
            src_ref=src, dst_ref=dst, send_sem=send_sem, recv_sem=recv_sem,
            device_id=device, device_id_type=MESH,
        )
        copy.start()
        sent.append(copy)

    def strip_rows(step):
        source = ring(row + step, 8)
        return strip.at[:, pl.ds(pl.multiple_of(source * 128, 128), 128), :]

    def col_push(step):
        target = ring(row + step, 8)
        push(send.at[target], strip_rows(0), col_send.at[step], col_recv.at[step], along_z(step))

    col_push(1)
    col_push(7)
    lax.fori_loop(0, 2, norm_far, 0)
    pltpu.make_async_remote_copy(
        src_ref=wbuf.at[1 - head], dst_ref=wbuf.at[1 - head], send_sem=w_send, recv_sem=w_recv,
        device_id=partner, device_id_type=MESH,
    ).wait_recv()

    wb = wbuf[0, 256:272, :].astype(F32) + pltpu.roll(wbuf[1, 256:272, :].astype(F32), 2, 0)
    weighted = wb * gain
    wbt = wb.astype(BF16)

    def bias_for(target, carry):
        part = lax.dot_general(wbt, send[target].reshape(512, 128), NT, preferred_element_type=F32)
        for jj in range(4):
            flat[pl.ds(pl.multiple_of((4 * target + jj) * 8, 8), 8), :] = part[0:8, jj * 128:jj * 128 + 128]
        return carry

    lax.fori_loop(0, 8, bias_for, 0, unroll=4)
    living = jnp.broadcast_to(types_ref[pl.ds(row, 1), :] != 0, (32, 128))
    by_head = [
        jnp.where(living, flat[pl.ds(h, 32, stride=8), :] * LOG2E, masked_score) for h in range(4)
    ]
    bsend[0] = jnp.concatenate([b[:, :64] for b in by_head], axis=1).astype(BF16)
    bsend[1] = jnp.concatenate([b[:, 64:] for b in by_head], axis=1).astype(BF16)

    def unit(x_, y_, low, count, core_=None):
        return bias_ref.at[
            lax.rem(y_, 2), x_, core if core_ is None else core_, pl.ds(low, count), lax.div(y_, 2)
        ]

    def arrive(dst, send_sem, recv_sem):
        pltpu.make_async_remote_copy(
            src_ref=dst, dst_ref=dst, send_sem=send_sem, recv_sem=recv_sem,
            device_id=partner, device_id_type=MESH,
        ).wait_recv()

    def slot(step):
        return 2 * step - 1 if step > 0 else -2 * step

    def chunk(step, low=0, count=2):
        return unit(x, y, 2 * slot(step) + low, count)

    def z_push(k, src, dst, step):
        push(src, dst, z_send.at[k], z_recv.at[k], along_z(step))

    def z_arrive(k, dst):
        arrive(dst, z_send.at[k], z_recv.at[k])

    own = pltpu.make_async_copy(bsend, chunk(0), own_sem.at[0])
    own.start()
    for k, step in enumerate((2, -2, 1, -1)):
        z_push(k, bsend, chunk(-step), step)

    own_cols = pltpu.make_async_copy(send.at[row], strip_rows(0), own_sem.at[1])
    own_cols.start()

    for kind, place_of in enumerate((1, 0, 2, 3)):
        for s in range(2):
            wall[place_of * 128 + s * 64:place_of * 128 + s * 64 + 64, :] = wbuf[s, kind * 64:kind * 64 + 64, :]
    together = (
        lax.div(lax.broadcasted_iota(jnp.int32, (128, 128), 0), 32)
        == lax.div(lax.broadcasted_iota(jnp.int32, (128, 128), 1), 32)
    ).astype(F32).astype(BF16)

    key_head = lax.div(lax.broadcasted_iota(jnp.int32, (128, 128), 0), 32)
    side_of = lax.div(lax.broadcasted_iota(jnp.int32, (128, 128), 1), 64)
    key_here = [(key_head == 2 * n + side_of).astype(F32).astype(BF16) for n in range(2)]
    lane_head = lax.div(lax.broadcasted_iota(jnp.int32, (64, 128), 1), 32)
    value_here = [(lane_head == h).astype(F32).astype(BF16) for h in range(4)]

    def project(step):
        source = ring(row + step, 8)
        first_block = 2 * slot(step)
        rows = pl.ds(pl.multiple_of(source * 128, 128), 128)

        def one(jj, carry):
            value = strip[jj, rows, :]
            keys = lax.dot_general(wall[0:128, :], value, NT, preferred_element_type=F32)
            left = lax.dot_general(value, wall[128:256, :], NT, preferred_element_type=F32)
            right = lax.dot_general(value, wall[256:512, :], NT, preferred_element_type=F32)
            query = left * SCALE
            qg_ref[0, jj, rows, :] = query.astype(BF16)
            qg_ref[1, jj, rows, :] = jax.nn.sigmoid(right[:, 128:]).astype(BF16)
            short = keys.astype(BF16)
            values = right[:, :128].astype(BF16)
            for odd in range(2):
                twice = jnp.concatenate([short[:, odd * 64:odd * 64 + 64]] * 2, axis=1)
                for n in range(2):
                    kbd_ref[jj, first_block + odd, :, n * 128:(n + 1) * 128] = twice * key_here[n]
                for h in range(4):
                    vbd_ref[jj, first_block + odd, h * 64:(h + 1) * 64, :] = (
                        values[odd * 64:odd * 64 + 64, :] * value_here[h]
                    )
            lengths = jnp.dot((query * query).astype(BF16), together, preferred_element_type=F32)
            tops[0:1, :] = jnp.maximum(tops[0:1, :], jnp.max(lengths, axis=0, keepdims=True))
            lengths = jnp.dot(together, (keys * keys).astype(BF16), preferred_element_type=F32)
            tops[1:2, :] = jnp.maximum(tops[1:2, :], jnp.max(lengths, axis=0, keepdims=True))
            return carry

        lax.fori_loop(0, 4, one, 0, unroll=2)

    def take(step):
        arrive(strip_rows(step), col_send.at[(8 - step) % 8], col_recv.at[(8 - step) % 8])
        project(step)

    own.wait()
    own_cols.wait()
    for k, step in enumerate((-2, 2, -1, 1)):
        z_arrive(k, chunk(step))
    z_push(4, chunk(-2), chunk(-3), 1)
    z_push(5, chunk(2), chunk(3), -1)
    z_push(6, chunk(-2, 0, 1), chunk(4, 0, 1), 2)
    z_push(7, chunk(2, 1, 1), chunk(4, 1, 1), -2)

    def far_bias():
        z_arrive(4, chunk(-3))
        z_arrive(5, chunk(3))
        z_arrive(6, chunk(4, 0, 1))
        z_arrive(7, chunk(4, 1, 1))

    def make_lists():
        mixing_ref[...] = w_out_ref[...].astype(F32).T.astype(BF16)
        part = mask_ref[...].astype(F32)
        place_ = lax.div(lax.broadcasted_iota(jnp.int32, (16, 128), 1), 2)
        away = lax.div(place_ + 1, 2) * (2 * lax.rem(place_, 2) - 1)
        there = 2 * lax.rem(row + away + 8, 8) + lax.rem(lax.broadcasted_iota(jnp.int32, (16, 128), 1), 2)
        inside = lax.broadcasted_iota(jnp.int32, (16, 128), 1) < 16
        turned = (inside & (lax.broadcasted_iota(jnp.int32, (16, 128), 0) == there)).astype(F32).astype(BF16)
        diagonal = lax.broadcasted_iota(jnp.int32, (16, 16), 0) == lax.broadcasted_iota(jnp.int32, (16, 16), 1)
        part = jnp.where((part == 1.0) | diagonal, 1.0, 0.0)
        allowed = jnp.dot(part.astype(BF16), turned, preferred_element_type=F32)
        before = [jnp.zeros((1, 128), F32)]
        for i in range(16):
            before.append(before[-1] + allowed[i:i + 1, :])
        rank = jnp.concatenate(before[:16], axis=0)
        pairs = jnp.broadcast_to(jnp.floor((before[16] + 1.0) * 0.5), (16, 128))
        earlier = (
            lax.broadcasted_iota(jnp.int32, (128, 128), 0) < lax.broadcasted_iota(jnp.int32, (128, 128), 1)
        ).astype(F32).astype(BF16)
        start = jnp.dot(pairs.astype(BF16), earlier, preferred_element_type=F32)
        total = jnp.sum(pairs[0:1, :], axis=1, keepdims=True)
        rank = rank + 2.0 * start
        entry = 2.0 * lax.broadcasted_iota(jnp.int32, (16, 128), 1).astype(F32)
        number = lax.broadcasted_iota(jnp.int32, (16, 128), 0).astype(F32)
        block = jnp.zeros((16, 128), F32)
        picked = [jnp.zeros((16, 128), F32)] * 2
        found = [jnp.zeros((16, 128), F32)] * 2
        for k in range(16):
            at = jnp.broadcast_to(rank[:, k:k + 1], (16, 128))
            here = jnp.broadcast_to(allowed[:, k:k + 1], (16, 128))
            for side in range(2):
                hit = jnp.where(at == entry + side, here, 0.0)
                found[side] = found[side] + hit
                picked[side] = picked[side] + hit * number
                if side == 0:
                    block = block + hit * k
        rows = [jnp.sum(block, axis=0, keepdims=True)]
        for side in range(2):
            missing = 1.0 - jnp.sum(found[side], axis=0, keepdims=True)
            rows.append(jnp.sum(picked[side], axis=0, keepdims=True) + (16.0 + side) * missing)
        rows.append(jnp.broadcast_to(total, (1, 128)))
        rows.append(jnp.zeros((4, 128), F32))
        lists_ref[...] = jnp.concatenate(rows, axis=0).astype(jnp.int32)

    def node(run, a, b):
        return (a, b) if run == 0 else (b, a)

    first = (x, y)
    second = (y, x)

    def shipment(run, index, a, b, low, count, to_a, to_b):
        k = run * 20 + index
        ref = unit(*node(run, a, b), run * 8 + low, count)
        push(ref, ref, g_send.at[k], g_recv.at[k], place(*node(run, to_a, to_b)))

    def receive(run, index, a, b, low, count):
        k = run * 20 + index
        arrive(unit(*node(run, a, b), run * 8 + low, count), g_send.at[k], g_recv.at[k])

    def to_sibling(run, u, v, a, b):
        k = run * 16 + u * 4 + v
        ref = unit(*node(run, a, b), run * 8, 8)
        push(ref, ref, s_send.at[k], s_recv.at[k], place(x, y, 1 - core))

    def across(run, u, a, b):
        shipment(run, 4 + 4 * u, a, b, 0, 8, first[run], ring(b + 1, 4))
        shipment(run, 5 + 4 * u, a, b, 0, 8, first[run], ring(b - 1, 4))

    for run in range(2):
        a, b = first[run], second[run]
        if run == 1:
            project(0)
            far_bias()
        shipment(run, 0, a, b, 0, 8, ring(a + 1, 4), b)
        shipment(run, 1, a, b, 0, 8, ring(a - 1, 4), b)
        across(run, 0, a, b)
        to_sibling(run, 0, 0, a, b)
        if run == 0:
            col_push(2)
            col_push(6)
    for step in (3, 5, 4):
        col_push(step)
    for run in range(2):
        a, b = first[run], second[run]
        receive(run, 0, ring(a - 1, 4), b, 0, 8)
        shipment(run, 2, ring(a - 1, 4), b, 0, 4, ring(a + 1, 4), b)
        receive(run, 1, ring(a + 1, 4), b, 0, 8)
        shipment(run, 3, ring(a + 1, 4), b, 4, 4, ring(a - 1, 4), b)
    for run in range(2):
        a, b = first[run], second[run]
        across(run, 1, ring(a - 1, 4), b)
        to_sibling(run, 1, 0, ring(a - 1, 4), b)
        across(run, 2, ring(a + 1, 4), b)
        to_sibling(run, 2, 0, ring(a + 1, 4), b)
    for run in range(2):
        a, b = first[run], second[run]
        receive(run, 2, ring(a + 2, 4), b, 0, 4)
        receive(run, 3, ring(a + 2, 4), b, 4, 4)
        across(run, 3, ring(a + 2, 4), b)
        to_sibling(run, 3, 0, ring(a + 2, 4), b)
    take(1)
    take(-1)
    for u in range(4):
        for run in range(2):
            a, b = ring(first[run] + (0, -1, 1, 2)[u], 4), second[run]
            receive(run, 4 + 4 * u, a, ring(b - 1, 4), 0, 8)
            shipment(run, 6 + 4 * u, a, ring(b - 1, 4), 0, 4, first[run], ring(b + 1, 4))
            to_sibling(run, u, 1, a, ring(b - 1, 4))
            receive(run, 5 + 4 * u, a, ring(b + 1, 4), 0, 8)
            shipment(run, 7 + 4 * u, a, ring(b + 1, 4), 4, 4, first[run], ring(b - 1, 4))
            to_sibling(run, u, 2, a, ring(b + 1, 4))
        if u == 1:
            make_lists()
        if u == 3:
            take(2)
            take(-2)
    for u in range(4):
        for run in range(2):
            a, b = ring(first[run] + (0, -1, 1, 2)[u], 4), second[run]
            receive(run, 6 + 4 * u, a, ring(b + 2, 4), 0, 4)
            receive(run, 7 + 4 * u, a, ring(b + 2, 4), 4, 4)
            to_sibling(run, u, 3, a, ring(b + 2, 4))
        if u >= 2:
            take((3, -3)[u - 2])
    take(4)
    bound_ref[0:8, :] = tops[...]
    bound_ref[8:24, :] = jnp.broadcast_to(jnp.sum(weighted * weighted, axis=1, keepdims=True), (16, 128))
    for run in range(2):
        for u in range(4):
            for v in range(4):
                a = ring(first[run] + (0, -1, 1, 2)[u], 4)
                b = ring(second[run] + (0, -1, 1, 2)[v], 4)
                k = run * 16 + u * 4 + v
                arrive(unit(*node(run, a, b), run * 8, 8, 1 - core), s_send.at[k], s_recv.at[k])
    for copy in sent:
        copy.wait_send()


def spread(*operands):
    whole = pl.BlockSpec(memory_space=VMEM)
    return pl.pallas_call(
        spread_kernel,
        out_shape=(
            jax.ShapeDtypeStruct((2, 4, 1024, 128), BF16),
            jax.ShapeDtypeStruct((4, 16, 128, 256), BF16),
            jax.ShapeDtypeStruct((4, 16, 256, 128), BF16),
            jax.ShapeDtypeStruct((2, 4, 2, 16, 2, 32, 256), BF16),
            jax.ShapeDtypeStruct((24, 128), F32),
            jax.ShapeDtypeStruct((128, 128), BF16),
            jax.ShapeDtypeStruct((8, 128), jnp.int32),
        ),
        in_specs=[pl.BlockSpec(memory_space=pltpu.HBM)] * len(operands),
        out_specs=(whole,) * 7,
        scratch_shapes=[
            VMEM((128, 32, 128), BF16),
            VMEM((1, 128), F32),
            VMEM((2, 128), BF16),
            VMEM((8, 128), jnp.int32),
            VMEM((128, 128), BF16),
            VMEM((16, 16), jnp.int32),
            VMEM((4096, 128), F32),
            VMEM((8, 4, 128, 128), BF16),
            VMEM((4, 1024, 128), BF16),
            VMEM((2, 272, 128), BF16),
            VMEM((512, 128), BF16),
            VMEM((256, 128), F32),
            VMEM((2, 32, 256), BF16),
            VMEM((8, 128), F32),
            DMA((10,)), DMA((8,)), DMA((8,)), DMA((8,)), DMA((8,)), DMA, DMA,
            DMA((40,)), DMA((40,)), DMA((32,)), DMA((32,)), DMA((2,)),
        ],
        compiler_params=pltpu.CompilerParams(
            collective_id=0, has_side_effects=True, vmem_limit_bytes=32 * 1024 * 1024
        ),
        name="spread",
    )(*operands)


def attend_kernel(
    lists_ref, qg_ref, kbd, vbd, bias, bound_ref,
    acc0, acc1, acc2, acc3,
    peak,
):
    accs = (acc0, acc1, acc2, acc3)
    for acc in accs:
        acc[...] = jnp.zeros_like(acc)
    same = (
        lax.div(lax.broadcasted_iota(jnp.int32, (256, 128), 0), 64)
        == lax.div(lax.broadcasted_iota(jnp.int32, (256, 128), 1), 32)
    ).astype(F32).astype(BF16)

    reach = jnp.sqrt(jnp.max(bound_ref[0:1, :])) * jnp.sqrt(jnp.max(bound_ref[1:2, :]))
    bias_reach = jnp.sqrt(jnp.max(bound_ref[8:24, :])) * (math.sqrt(128) * LOG2E)
    safe = (reach + bias_reach) * 1.03 <= SAFE

    def query(j, i):
        return qg_ref[0, j, pl.ds(pl.multiple_of(jnp.minimum(i, 15) * 64, 64), 64), :]

    def values_of(j, block):
        return jnp.concatenate([vbd[j, block], same], axis=1)

    total_pairs = lists_ref[3, 0]

    @pl.when(safe)
    def _():
        def step(t, carry):
            work = []
            for side in range(2):
                e = 2 * t + side
                block = lists_ref[0, e]
                ids = (lists_ref[1, e], lists_ref[2, e])
                offset = jnp.concatenate(
                    [bias[jnp.minimum(i, 15), block].astype(F32) for i in ids], axis=0
                )
                work.append((block, ids, offset))
            for j in range(4):
                for block, ids, offset in work:
                    queries = jnp.concatenate([query(j, i) for i in ids], axis=0)
                    score = jnp.dot(queries, kbd[j, block], preferred_element_type=F32)
                    weights = jnp.exp2(score + offset).astype(BF16)
                    total = jnp.dot(weights, values_of(j, block), preferred_element_type=F32)
                    olds = [accs[j][i] for i in ids]
                    for n in range(2):
                        accs[j][ids[n]] = olds[n] + total[n * 64:(n + 1) * 64, :]
            return carry

        lax.fori_loop(0, lax.div(total_pairs + 1, 2), step, 0)

    @pl.when(jnp.logical_not(safe))
    def _():
        peak[...] = jnp.full_like(peak, -1e30)

        def step(n, carry):
            e = lax.div(n, 2)
            block = lists_ref[0, e]
            i = lists_ref[1 + lax.rem(n, 2), e]
            offset = bias[jnp.minimum(i, 15), block].astype(F32)
            for j in range(4):
                score = jnp.dot(query(j, i), kbd[j, block], preferred_element_type=F32) + offset
                old = peak[j, i]
                tops = [
                    jnp.maximum(
                        jnp.max(score[:, h * 64:(h + 1) * 64], axis=1, keepdims=True),
                        old[:, h * 32:h * 32 + 1],
                    )
                    for h in range(4)
                ]
                shift = jnp.concatenate([jnp.broadcast_to(top, (64, 64)) for top in tops], axis=1)
                fresh = jnp.concatenate([jnp.broadcast_to(top, (64, 32)) for top in tops], axis=1)
                decay = jnp.exp2(old - fresh)
                weights = jnp.exp2(score - shift).astype(BF16)
                total = jnp.dot(weights, values_of(j, block), preferred_element_type=F32)
                accs[j][i] = accs[j][i] * jnp.concatenate([decay, decay], axis=1) + total
                peak[j, i] = fresh
            return carry

        lax.fori_loop(0, 2 * total_pairs, step, 0)


def attend(lists, qg, kbd, vbd, bias, bound):
    whole = pl.BlockSpec(memory_space=VMEM)
    return pl.pallas_call(
        attend_kernel,
        out_shape=[jax.ShapeDtypeStruct((18, 64, 256), F32)] * 4,
        in_specs=[pl.BlockSpec(memory_space=pltpu.SMEM)] + [whole] * 5,
        out_specs=[whole] * 4,
        scratch_shapes=[VMEM((4, 18, 64, 128), F32)],
        compiler_params=pltpu.CompilerParams(vmem_limit_bytes=24 * 1024 * 1024),
        name="attend",
    )(lists, qg, kbd, vbd, bias, bound)


def deliver_kernel(
    acc0, acc1, acc2, acc3, qg_ref, mixing_ref, out_ref, update_ref, send_sem, recv_sem, own_sem
):
    row = lax.axis_index("row")
    col = lax.axis_index("col")
    head = lax.axis_index("head")

    def other(flip):
        return (1 - head) if flip else head

    def device(step, flip):
        return (ring(row + step, 8), col, other(flip))

    moves = [(step, flip) for step in (4, 3, 5, 2, 6, 1, 7) for flip in (1, 0)] + [(0, 1)]
    barrier = pltpu.get_barrier_semaphore()
    for step, flip in moves:
        pl.semaphore_signal(barrier, inc=1, device_id=device(step, flip), device_id_type=MESH)

    def spot(step, flip):
        return out_ref.at[pl.ds((other(flip) * 8 + ring(row + step, 8)) * 4, 4)]

    def part(step, flip):
        return update_ref.at[other(flip), ring(row + step, 8)]

    def finish(step):
        target = ring(row + step, 8)
        rows = pl.ds(pl.multiple_of(target * 128, 128), 128)
        for j, acc in enumerate((acc0, acc1, acc2, acc3)):
            sums = acc[pl.ds(target * 2, 2)].reshape(128, 256)
            attention = sums[:, :128] / sums[:, 128:]
            gated = (attention * qg_ref[1, j, rows, :].astype(F32)).astype(BF16)
            update = lax.dot_general(mixing_ref[...], gated, NT, preferred_element_type=F32).astype(BF16)
            update_ref[0, target, j] = update[:64, :]
            update_ref[1, target, j] = update[64:, :]

    copies = []

    def push(step, flip):
        k = flip * 8 + step
        copy = pltpu.make_async_remote_copy(
            src_ref=part(step, flip), dst_ref=spot(0, 0),
            send_sem=send_sem.at[k], recv_sem=recv_sem.at[k],
            device_id=device(step, flip), device_id_type=MESH,
        )
        copy.start()
        copies.append(copy)

    for step in (4, 3, 5):
        finish(step)
    pl.semaphore_wait(barrier, len(moves))
    for step in (4, 3, 5, 2, 6, 1, 7, 0):
        if step not in (4, 3, 5):
            finish(step)
        push(step, 1)
        if step > 0:
            push(step, 0)
    own = pltpu.make_async_copy(part(0, 0), spot(0, 0), own_sem)
    own.start()
    own.wait()
    for step, flip in moves:
        k = flip * 8 + step
        pltpu.make_async_remote_copy(
            src_ref=spot(-step, flip), dst_ref=spot(-step, flip),
            send_sem=send_sem.at[k], recv_sem=recv_sem.at[k],
            device_id=device(step, flip), device_id_type=MESH,
        ).wait_recv()
    for copy in copies:
        copy.wait_send()


def deliver(accs, qg, mixing):
    whole = pl.BlockSpec(memory_space=VMEM)
    return pl.pallas_call(
        deliver_kernel,
        out_shape=jax.ShapeDtypeStruct((64, 64, 128), BF16),
        in_specs=[whole] * 6,
        out_specs=whole,
        scratch_shapes=[VMEM((2, 8, 4, 64, 128), BF16), DMA((16,)), DMA((16,)), DMA],
        compiler_params=pltpu.CompilerParams(
            collective_id=1, has_side_effects=True, vmem_limit_bytes=16 * 1024 * 1024
        ),
        name="deliver",
    )(*accs, qg, mixing)


def per_device(
    pair_field, ln_gain, w_query, w_key, w_value, w_gate, w_bias, w_out, tile_mask, type_ids
):
    weights = [w.T for w in (w_query, w_key, w_value, w_gate)]
    weights.append(w_bias.T)
    operands = (pair_field, ln_gain.reshape(1, 128), *weights, type_ids.reshape(8, 128), w_out, tile_mask)
    qg, kbd, vbd, bias, bound, mixing, lists = spread(
        *[pltpu.with_memory_space_constraint(operand, pltpu.HBM) for operand in operands]
    )
    accs = attend(lists, qg, kbd, vbd, bias.reshape(16, 16, 64, 256), bound)
    return jnp.transpose(deliver(accs, qg, mixing), (2, 0, 1))


def solution(mesh):
    return jax.shard_map(
        per_device,
        mesh=mesh,
        in_specs=(
            P("row", "col", None),
            P(),
            P(None, "head"),
            P(None, "head"),
            P(None, "head"),
            P(None, "head"),
            P(None, "head"),
            P(),
            P(),
            P(),
        ),
        out_specs=P("row", "col", "head"),
        check_vma=False,
    )
```

```python
import math

import jax
import jax.numpy as jnp
from jax import lax
from jax.experimental import pallas as pl
from jax.experimental.pallas import tpu as pltpu
from jax.sharding import PartitionSpec as P

MESH = pl.DeviceIdType.MESH
F32 = jnp.float32
BF16 = jnp.bfloat16
VMEM = pltpu.VMEM
DMA = pltpu.SemaphoreType.DMA

epsilon = 1e-05
masked_score = -1000000000.0
LOG2E = math.log2(math.e)
SCALE = LOG2E / math.sqrt(32)
SAFE = 64.0
NT = (((1,), (1,)), ((), ()))


def ring(value, size):
    return lax.rem(value + size, size)


def spread_kernel(
    tile_ref, gain_in, wq_ref, wk_ref, wv_ref, wg_ref, wb_in, types_in, w_out_in, mask_in,
    qg_ref, kbd_ref, vbd_ref, bias_ref, bound_ref, mixing_ref, lists_ref,
    half, gain_ref, wb_ref, types_ref, w_out_ref, mask_ref, wide, send, strip, wbuf, wall, flat, bsend, tops,
    load_sem, col_send, col_recv, z_send, z_recv, w_send, w_recv,
    g_send, g_recv, s_send, s_recv, own_sem,
):
    row = lax.axis_index("row")
    col = lax.axis_index("col")
    head = lax.axis_index("head")
    core = lax.rem(col, 2)
    x = lax.rem(lax.div(col, 2), 4)
    y = head * 2 + lax.div(col, 8)

    def place(x_, y_, core_=None):
        return (row, lax.rem(y_, 2) * 8 + x_ * 2 + (core if core_ is None else core_), lax.div(y_, 2))

    def along_z(step):
        return (ring(row + step, 8), col, head)

    partner = place(x, ring(y + 2, 4))
    peers = [along_z(step) for step in range(1, 8)]
    peers += [place(ring(x + 1, 4), y), place(ring(x - 1, 4), y)]
    peers += [place(x, ring(y + 1, 4)), place(x, ring(y - 1, 4)), partner]
    peers += [place(x, y, 1 - core)]
    barrier = pltpu.get_barrier_semaphore()
    for peer in peers:
        pl.semaphore_signal(barrier, inc=1, device_id=peer, device_id_type=MESH)

    loads = [
        (tile_ref.at[:, pl.ds(pl.multiple_of(head * 32, 32), 32), :], half),
        (gain_in, gain_ref), (wb_in, wb_ref), (types_in, types_ref),
    ]
    loads += [
        (ref, wbuf.at[head, pl.ds(kind * 64, 64)]) for kind, ref in enumerate((wq_ref, wk_ref, wv_ref, wg_ref))
    ]
    loads += [(w_out_in, w_out_ref), (mask_in, mask_ref)]
    loads = [pltpu.make_async_copy(src, dst, load_sem.at[n]) for n, (src, dst) in enumerate(loads)]
    for load in loads:
        load.start()
    tops[...] = jnp.zeros_like(tops)
    loads[0].wait()

    def widen(block, carry):
        rows = half[pl.ds(block * 8, 8)].astype(F32).reshape(256, 128)
        wide[pl.ds(pl.multiple_of(block * 256, 256), 256), :] = rows
        return carry

    lax.fori_loop(0, 16, widen, 0)
    ones = jnp.ones((128, 128), BF16)
    loads[1].wait()
    gain = gain_ref[...]

    def norm_for(step):
        target = ring(row + step, 8)
        for jj in range(4):
            value = wide[pl.ds(4 * target + jj, 128, stride=32), :]
            mean = jnp.dot(value.astype(BF16), ones, preferred_element_type=F32) * (1.0 / 128)
            centred = value - mean
            squares = (centred * centred).astype(BF16)
            spread = jnp.dot(squares, ones, preferred_element_type=F32) * (1.0 / 128)
            normed = centred * lax.rsqrt(spread + epsilon) * gain
            send[target, jj] = normed.astype(BF16)

    def norm_near(n, carry):
        norm_for(n)
        norm_for(-n)
        return carry

    def norm_far(n, carry):
        norm_for(3 + n)
        norm_for(-3 * (1 - n))
        return carry

    lax.fori_loop(1, 3, norm_near, 0)
    for load in loads[2:]:
        load.wait()
    wbuf[head, 256:272, :] = jnp.concatenate(
        [wb_ref[...].astype(F32), jnp.zeros((14, 128), F32)], axis=0
    ).astype(BF16)
    pl.semaphore_wait(barrier, len(peers))
    w_copy = pltpu.make_async_remote_copy(
        src_ref=wbuf.at[head], dst_ref=wbuf.at[head], send_sem=w_send, recv_sem=w_recv,
        device_id=partner, device_id_type=MESH,
    )
    w_copy.start()
    sent = [w_copy]

    def push(src, dst, send_sem, recv_sem, device):
        copy = pltpu.make_async_remote_copy(
            src_ref=src, dst_ref=dst, send_sem=send_sem, recv_sem=recv_sem,
            device_id=device, device_id_type=MESH,
        )
        copy.start()
        sent.append(copy)

    def strip_rows(step):
        source = ring(row + step, 8)
        return strip.at[:, pl.ds(pl.multiple_of(source * 128, 128), 128), :]

    def col_push(step):
        target = ring(row + step, 8)
        push(send.at[target], strip_rows(0), col_send.at[step], col_recv.at[step], along_z(step))

    col_push(1)
    col_push(7)
    lax.fori_loop(0, 2, norm_far, 0)
    pltpu.make_async_remote_copy(
        src_ref=wbuf.at[1 - head], dst_ref=wbuf.at[1 - head], send_sem=w_send, recv_sem=w_recv,
        device_id=partner, device_id_type=MESH,
    ).wait_recv()

    wb = wbuf[0, 256:272, :].astype(F32) + pltpu.roll(wbuf[1, 256:272, :].astype(F32), 2, 0)
    weighted = wb * gain
    wbt = wb.astype(BF16)

    def bias_for(target, carry):
        part = lax.dot_general(wbt, send[target].reshape(512, 128), NT, preferred_element_type=F32)
        for jj in range(4):
            flat[pl.ds(pl.multiple_of((4 * target + jj) * 8, 8), 8), :] = part[0:8, jj * 128:jj * 128 + 128]
        return carry

    lax.fori_loop(0, 8, bias_for, 0, unroll=4)
    living = jnp.broadcast_to(types_ref[pl.ds(row, 1), :] != 0, (32, 128))
    by_head = [
        jnp.where(living, flat[pl.ds(h, 32, stride=8), :] * LOG2E, masked_score) for h in range(4)
    ]
    bsend[0] = jnp.concatenate([b[:, :64] for b in by_head], axis=1).astype(BF16)
    bsend[1] = jnp.concatenate([b[:, 64:] for b in by_head], axis=1).astype(BF16)

    def unit(x_, y_, low, count, core_=None):
        return bias_ref.at[
            low // 8, lax.rem(y_, 2), x_, core if core_ is None else core_, lax.div(y_, 2), pl.ds(low % 8, count)
        ]

    def arrive(dst, send_sem, recv_sem):
        pltpu.make_async_remote_copy(
            src_ref=dst, dst_ref=dst, send_sem=send_sem, recv_sem=recv_sem,
            device_id=partner, device_id_type=MESH,
        ).wait_recv()

    def slot(step):
        return 2 * step - 1 if step > 0 else -2 * step

    def chunk(step, low=0, count=2):
        return unit(x, y, 2 * slot(step) + low, count)

    def z_push(k, src, dst, step):
        push(src, dst, z_send.at[k], z_recv.at[k], along_z(step))

    def z_arrive(k, dst):
        arrive(dst, z_send.at[k], z_recv.at[k])

    own = pltpu.make_async_copy(bsend, chunk(0), own_sem.at[0])
    own.start()
    for k, step in enumerate((2, -2, 1, -1)):
        z_push(k, bsend, chunk(-step), step)

    own_cols = pltpu.make_async_copy(send.at[row], strip_rows(0), own_sem.at[1])
    own_cols.start()

    for kind, place_of in enumerate((1, 0, 2, 3)):
        for s in range(2):
            wall[place_of * 128 + s * 64:place_of * 128 + s * 64 + 64, :] = wbuf[s, kind * 64:kind * 64 + 64, :]
    together = (
        lax.div(lax.broadcasted_iota(jnp.int32, (128, 128), 0), 32)
        == lax.div(lax.broadcasted_iota(jnp.int32, (128, 128), 1), 32)
    ).astype(F32).astype(BF16)

    key_head = lax.div(lax.broadcasted_iota(jnp.int32, (128, 128), 0), 32)
    side_of = lax.div(lax.broadcasted_iota(jnp.int32, (128, 128), 1), 64)
    key_here = [(key_head == 2 * n + side_of).astype(F32).astype(BF16) for n in range(2)]
    lane_head = lax.div(lax.broadcasted_iota(jnp.int32, (64, 128), 1), 32)
    value_here = [(lane_head == h).astype(F32).astype(BF16) for h in range(4)]

    def project(step):
        source = ring(row + step, 8)
        first_block = 2 * slot(step)
        rows = pl.ds(pl.multiple_of(source * 128, 128), 128)

        def one(jj, carry):
            value = strip[jj, rows, :]
            keys = lax.dot_general(wall[0:128, :], value, NT, preferred_element_type=F32)
            left = lax.dot_general(value, wall[128:256, :], NT, preferred_element_type=F32)
            right = lax.dot_general(value, wall[256:512, :], NT, preferred_element_type=F32)
            query = left * SCALE
            qg_ref[0, jj, rows, :] = query.astype(BF16)
            qg_ref[1, jj, rows, :] = jax.nn.sigmoid(right[:, 128:]).astype(BF16)
            short = keys.astype(BF16)
            values = right[:, :128].astype(BF16)
            for odd in range(2):
                twice = jnp.concatenate([short[:, odd * 64:odd * 64 + 64]] * 2, axis=1)
                for n in range(2):
                    kbd_ref[jj, first_block + odd, :, n * 128:(n + 1) * 128] = twice * key_here[n]
                for h in range(4):
                    vbd_ref[jj, first_block + odd, h * 64:(h + 1) * 64, :] = (
                        values[odd * 64:odd * 64 + 64, :] * value_here[h]
                    )
            lengths = jnp.dot((query * query).astype(BF16), together, preferred_element_type=F32)
            tops[0:1, :] = jnp.maximum(tops[0:1, :], jnp.max(lengths, axis=0, keepdims=True))
            lengths = jnp.dot(together, (keys * keys).astype(BF16), preferred_element_type=F32)
            tops[1:2, :] = jnp.maximum(tops[1:2, :], jnp.max(lengths, axis=0, keepdims=True))
            return carry

        lax.fori_loop(0, 4, one, 0, unroll=2)

    def take(step):
        arrive(strip_rows(step), col_send.at[(8 - step) % 8], col_recv.at[(8 - step) % 8])
        project(step)

    own.wait()
    own_cols.wait()
    for k, step in enumerate((-2, 2, -1, 1)):
        z_arrive(k, chunk(step))
    z_push(4, chunk(-2), chunk(-3), 1)
    z_push(5, chunk(2), chunk(3), -1)
    z_push(6, chunk(-2, 0, 1), chunk(4, 0, 1), 2)
    z_push(7, chunk(2, 1, 1), chunk(4, 1, 1), -2)

    def far_bias():
        z_arrive(4, chunk(-3))
        z_arrive(5, chunk(3))
        z_arrive(6, chunk(4, 0, 1))
        z_arrive(7, chunk(4, 1, 1))

    def make_lists():
        mixing_ref[...] = w_out_ref[...].astype(F32).T.astype(BF16)
        part = mask_ref[...].astype(F32)
        place_ = lax.div(lax.broadcasted_iota(jnp.int32, (16, 128), 1), 2)
        away = lax.div(place_ + 1, 2) * (2 * lax.rem(place_, 2) - 1)
        there = 2 * lax.rem(row + away + 8, 8) + lax.rem(lax.broadcasted_iota(jnp.int32, (16, 128), 1), 2)
        inside = lax.broadcasted_iota(jnp.int32, (16, 128), 1) < 16
        turned = (inside & (lax.broadcasted_iota(jnp.int32, (16, 128), 0) == there)).astype(F32).astype(BF16)
        diagonal = lax.broadcasted_iota(jnp.int32, (16, 16), 0) == lax.broadcasted_iota(jnp.int32, (16, 16), 1)
        part = jnp.where((part == 1.0) | diagonal, 1.0, 0.0)
        allowed = jnp.dot(part.astype(BF16), turned, preferred_element_type=F32)
        before = [jnp.zeros((1, 128), F32)]
        for i in range(16):
            before.append(before[-1] + allowed[i:i + 1, :])
        rank = jnp.concatenate(before[:16], axis=0)
        pairs = jnp.broadcast_to(jnp.floor((before[16] + 1.0) * 0.5), (16, 128))
        earlier = (
            lax.broadcasted_iota(jnp.int32, (128, 128), 0) < lax.broadcasted_iota(jnp.int32, (128, 128), 1)
        ).astype(F32).astype(BF16)
        start = jnp.dot(pairs.astype(BF16), earlier, preferred_element_type=F32)
        total = jnp.sum(pairs[0:1, :], axis=1, keepdims=True)
        rank = rank + 2.0 * start
        entry = 2.0 * lax.broadcasted_iota(jnp.int32, (16, 128), 1).astype(F32)
        number = lax.broadcasted_iota(jnp.int32, (16, 128), 0).astype(F32)
        block = jnp.zeros((16, 128), F32)
        picked = [jnp.zeros((16, 128), F32)] * 2
        found = [jnp.zeros((16, 128), F32)] * 2
        for k in range(16):
            at = jnp.broadcast_to(rank[:, k:k + 1], (16, 128))
            here = jnp.broadcast_to(allowed[:, k:k + 1], (16, 128))
            for side in range(2):
                hit = jnp.where(at == entry + side, here, 0.0)
                found[side] = found[side] + hit
                picked[side] = picked[side] + hit * number
                if side == 0:
                    block = block + hit * k
        rows = [jnp.sum(block, axis=0, keepdims=True)]
        for side in range(2):
            missing = 1.0 - jnp.sum(found[side], axis=0, keepdims=True)
            rows.append(jnp.sum(picked[side], axis=0, keepdims=True) + (16.0 + side) * missing)
        rows.append(jnp.broadcast_to(total, (1, 128)))
        rows.append(jnp.zeros((4, 128), F32))
        lists_ref[...] = jnp.concatenate(rows, axis=0).astype(jnp.int32)

    def node(run, a, b):
        return (a, b) if run == 0 else (b, a)

    first = (x, y)
    second = (y, x)

    def shipment(run, index, a, b, low, count, to_a, to_b):
        k = run * 20 + index
        ref = unit(*node(run, a, b), run * 8 + low, count)
        push(ref, ref, g_send.at[k], g_recv.at[k], place(*node(run, to_a, to_b)))

    def receive(run, index, a, b, low, count):
        k = run * 20 + index
        arrive(unit(*node(run, a, b), run * 8 + low, count), g_send.at[k], g_recv.at[k])

    def to_sibling(run, u, v, a, b):
        k = run * 16 + u * 4 + v
        ref = unit(*node(run, a, b), run * 8, 8)
        push(ref, ref, s_send.at[k], s_recv.at[k], place(x, y, 1 - core))

    def across(run, u, a, b):
        shipment(run, 4 + 4 * u, a, b, 0, 8, first[run], ring(b + 1, 4))
        shipment(run, 5 + 4 * u, a, b, 0, 8, first[run], ring(b - 1, 4))

    for run in range(2):
        a, b = first[run], second[run]
        if run == 1:
            project(0)
            far_bias()
        shipment(run, 0, a, b, 0, 8, ring(a + 1, 4), b)
        shipment(run, 1, a, b, 0, 8, ring(a - 1, 4), b)
        across(run, 0, a, b)
        to_sibling(run, 0, 0, a, b)
        if run == 0:
            col_push(2)
            col_push(6)
    for step in (3, 5, 4):
        col_push(step)
    for run in range(2):
        a, b = first[run], second[run]
        receive(run, 0, ring(a - 1, 4), b, 0, 8)
        shipment(run, 2, ring(a - 1, 4), b, 0, 4, ring(a + 1, 4), b)
        receive(run, 1, ring(a + 1, 4), b, 0, 8)
        shipment(run, 3, ring(a + 1, 4), b, 4, 4, ring(a - 1, 4), b)
    for run in range(2):
        a, b = first[run], second[run]
        across(run, 1, ring(a - 1, 4), b)
        to_sibling(run, 1, 0, ring(a - 1, 4), b)
        across(run, 2, ring(a + 1, 4), b)
        to_sibling(run, 2, 0, ring(a + 1, 4), b)
    for run in range(2):
        a, b = first[run], second[run]
        receive(run, 2, ring(a + 2, 4), b, 0, 4)
        receive(run, 3, ring(a + 2, 4), b, 4, 4)
        across(run, 3, ring(a + 2, 4), b)
        to_sibling(run, 3, 0, ring(a + 2, 4), b)
    take(1)
    take(-1)
    for u in range(4):
        for run in range(2):
            a, b = ring(first[run] + (0, -1, 1, 2)[u], 4), second[run]
            receive(run, 4 + 4 * u, a, ring(b - 1, 4), 0, 8)
            shipment(run, 6 + 4 * u, a, ring(b - 1, 4), 0, 4, first[run], ring(b + 1, 4))
            to_sibling(run, u, 1, a, ring(b - 1, 4))
            receive(run, 5 + 4 * u, a, ring(b + 1, 4), 0, 8)
            shipment(run, 7 + 4 * u, a, ring(b + 1, 4), 4, 4, first[run], ring(b - 1, 4))
            to_sibling(run, u, 2, a, ring(b + 1, 4))
        if u == 1:
            make_lists()
        if u == 3:
            take(2)
            take(-2)
    for u in range(4):
        for run in range(2):
            a, b = ring(first[run] + (0, -1, 1, 2)[u], 4), second[run]
            receive(run, 6 + 4 * u, a, ring(b + 2, 4), 0, 4)
            receive(run, 7 + 4 * u, a, ring(b + 2, 4), 4, 4)
            to_sibling(run, u, 3, a, ring(b + 2, 4))
        if u >= 2:
            take((3, -3)[u - 2])
    take(4)
    bound_ref[0:8, :] = tops[...]
    bound_ref[8:24, :] = jnp.broadcast_to(jnp.sum(weighted * weighted, axis=1, keepdims=True), (16, 128))
    for run in range(2):
        for u in range(4):
            for v in range(4):
                a = ring(first[run] + (0, -1, 1, 2)[u], 4)
                b = ring(second[run] + (0, -1, 1, 2)[v], 4)
                k = run * 16 + u * 4 + v
                arrive(unit(*node(run, a, b), run * 8, 8, 1 - core), s_send.at[k], s_recv.at[k])
    for copy in sent:
        copy.wait_send()


def spread(*operands):
    whole = pl.BlockSpec(memory_space=VMEM)
    return pl.pallas_call(
        spread_kernel,
        out_shape=(
            jax.ShapeDtypeStruct((2, 4, 1024, 128), BF16),
            jax.ShapeDtypeStruct((4, 16, 128, 256), BF16),
            jax.ShapeDtypeStruct((4, 16, 256, 128), BF16),
            jax.ShapeDtypeStruct((2, 2, 4, 2, 2, 8, 32, 256), BF16),
            jax.ShapeDtypeStruct((24, 128), F32),
            jax.ShapeDtypeStruct((128, 128), BF16),
            jax.ShapeDtypeStruct((8, 128), jnp.int32),
        ),
        in_specs=[pl.BlockSpec(memory_space=pltpu.HBM)] * len(operands),
        out_specs=(whole,) * 7,
        scratch_shapes=[
            VMEM((128, 32, 128), BF16),
            VMEM((1, 128), F32),
            VMEM((2, 128), BF16),
            VMEM((8, 128), jnp.int32),
            VMEM((128, 128), BF16),
            VMEM((16, 16), jnp.int32),
            VMEM((4096, 128), F32),
            VMEM((8, 4, 128, 128), BF16),
            VMEM((4, 1024, 128), BF16),
            VMEM((2, 272, 128), BF16),
            VMEM((512, 128), BF16),
            VMEM((256, 128), F32),
            VMEM((2, 32, 256), BF16),
            VMEM((8, 128), F32),
            DMA((10,)), DMA((8,)), DMA((8,)), DMA((8,)), DMA((8,)), DMA, DMA,
            DMA((40,)), DMA((40,)), DMA((32,)), DMA((32,)), DMA((2,)),
        ],
        compiler_params=pltpu.CompilerParams(
            collective_id=0, has_side_effects=True, vmem_limit_bytes=32 * 1024 * 1024
        ),
        name="spread",
    )(*operands)


def attend_kernel(
    lists_ref, qg_ref, kbd, vbd, bias, bound_ref,
    acc0, acc1, acc2, acc3,
    peak,
):
    accs = (acc0, acc1, acc2, acc3)
    for acc in accs:
        acc[...] = jnp.zeros_like(acc)
    same = (
        lax.div(lax.broadcasted_iota(jnp.int32, (256, 128), 0), 64)
        == lax.div(lax.broadcasted_iota(jnp.int32, (256, 128), 1), 32)
    ).astype(F32).astype(BF16)

    reach = jnp.sqrt(jnp.max(bound_ref[0:1, :])) * jnp.sqrt(jnp.max(bound_ref[1:2, :]))
    bias_reach = jnp.sqrt(jnp.max(bound_ref[8:24, :])) * (math.sqrt(128) * LOG2E)
    safe = (reach + bias_reach) * 1.03 <= SAFE

    def query(j, i):
        return qg_ref[0, j, pl.ds(pl.multiple_of(jnp.minimum(i, 15) * 64, 64), 64), :]

    def values_of(j, block):
        return jnp.concatenate([vbd[j, block], same], axis=1)

    def offset_of(i, block):
        at = (lax.div(block, 8), jnp.minimum(i, 15))
        n = lax.rem(block, 8)
        return [bias[at[0], at[1], half, n].astype(F32) for half in range(2)]

    total_pairs = lists_ref[3, 0]

    @pl.when(safe)
    def _():
        def step(t, carry):
            work = []
            for side in range(2):
                e = 2 * t + side
                block = lists_ref[0, e]
                ids = (lists_ref[1, e], lists_ref[2, e])
                offset = jnp.concatenate(offset_of(ids[0], block) + offset_of(ids[1], block), axis=0)
                work.append((block, ids, offset))
            for j in range(4):
                for block, ids, offset in work:
                    queries = jnp.concatenate([query(j, i) for i in ids], axis=0)
                    score = jnp.dot(queries, kbd[j, block], preferred_element_type=F32)
                    weights = jnp.exp2(score + offset).astype(BF16)
                    total = jnp.dot(weights, values_of(j, block), preferred_element_type=F32)
                    olds = [accs[j][i] for i in ids]
                    for n in range(2):
                        accs[j][ids[n]] = olds[n] + total[n * 64:(n + 1) * 64, :]
            return carry

        lax.fori_loop(0, lax.div(total_pairs + 1, 2), step, 0)

    @pl.when(jnp.logical_not(safe))
    def _():
        peak[...] = jnp.full_like(peak, -1e30)

        def step(n, carry):
            e = lax.div(n, 2)
            block = lists_ref[0, e]
            i = lists_ref[1 + lax.rem(n, 2), e]
            offset = jnp.concatenate(offset_of(i, block), axis=0)
            for j in range(4):
                score = jnp.dot(query(j, i), kbd[j, block], preferred_element_type=F32) + offset
                old = peak[j, i]
                tops = [
                    jnp.maximum(
                        jnp.max(score[:, h * 64:(h + 1) * 64], axis=1, keepdims=True),
                        old[:, h * 32:h * 32 + 1],
                    )
                    for h in range(4)
                ]
                shift = jnp.concatenate([jnp.broadcast_to(top, (64, 64)) for top in tops], axis=1)
                fresh = jnp.concatenate([jnp.broadcast_to(top, (64, 32)) for top in tops], axis=1)
                decay = jnp.exp2(old - fresh)
                weights = jnp.exp2(score - shift).astype(BF16)
                total = jnp.dot(weights, values_of(j, block), preferred_element_type=F32)
                accs[j][i] = accs[j][i] * jnp.concatenate([decay, decay], axis=1) + total
                peak[j, i] = fresh
            return carry

        lax.fori_loop(0, 2 * total_pairs, step, 0)


def attend(lists, qg, kbd, vbd, bias, bound):
    whole = pl.BlockSpec(memory_space=VMEM)
    return pl.pallas_call(
        attend_kernel,
        out_shape=[jax.ShapeDtypeStruct((18, 64, 256), F32)] * 4,
        in_specs=[pl.BlockSpec(memory_space=pltpu.SMEM)] + [whole] * 5,
        out_specs=[whole] * 4,
        scratch_shapes=[VMEM((4, 18, 64, 128), F32)],
        compiler_params=pltpu.CompilerParams(vmem_limit_bytes=24 * 1024 * 1024),
        name="attend",
    )(lists, qg, kbd, vbd, bias, bound)


def deliver_kernel(
    acc0, acc1, acc2, acc3, qg_ref, mixing_ref, out_ref, update_ref, send_sem, recv_sem, own_sem
):
    row = lax.axis_index("row")
    col = lax.axis_index("col")
    head = lax.axis_index("head")

    def other(flip):
        return (1 - head) if flip else head

    def device(step, flip):
        return (ring(row + step, 8), col, other(flip))

    moves = [(step, flip) for step in (4, 3, 5, 2, 6, 1, 7) for flip in (1, 0)] + [(0, 1)]
    barrier = pltpu.get_barrier_semaphore()
    for step, flip in moves:
        pl.semaphore_signal(barrier, inc=1, device_id=device(step, flip), device_id_type=MESH)

    def spot(step, flip):
        return out_ref.at[pl.ds((other(flip) * 8 + ring(row + step, 8)) * 4, 4)]

    def part(step, flip):
        return update_ref.at[other(flip), ring(row + step, 8)]

    def finish(step):
        target = ring(row + step, 8)
        rows = pl.ds(pl.multiple_of(target * 128, 128), 128)
        for j, acc in enumerate((acc0, acc1, acc2, acc3)):
            sums = acc[pl.ds(target * 2, 2)].reshape(128, 256)
            attention = sums[:, :128] / sums[:, 128:]
            gated = (attention * qg_ref[1, j, rows, :].astype(F32)).astype(BF16)
            update = lax.dot_general(mixing_ref[...], gated, NT, preferred_element_type=F32).astype(BF16)
            update_ref[0, target, j] = update[:64, :]
            update_ref[1, target, j] = update[64:, :]

    copies = []

    def push(step, flip):
        k = flip * 8 + step
        copy = pltpu.make_async_remote_copy(
            src_ref=part(step, flip), dst_ref=spot(0, 0),
            send_sem=send_sem.at[k], recv_sem=recv_sem.at[k],
            device_id=device(step, flip), device_id_type=MESH,
        )
        copy.start()
        copies.append(copy)

    for step in (4, 3, 5):
        finish(step)
    pl.semaphore_wait(barrier, len(moves))
    for step in (4, 3, 5, 2, 6, 1, 7, 0):
        if step not in (4, 3, 5):
            finish(step)
        push(step, 1)
        if step > 0:
            push(step, 0)
    own = pltpu.make_async_copy(part(0, 0), spot(0, 0), own_sem)
    own.start()
    own.wait()
    for step, flip in moves:
        k = flip * 8 + step
        pltpu.make_async_remote_copy(
            src_ref=spot(-step, flip), dst_ref=spot(-step, flip),
            send_sem=send_sem.at[k], recv_sem=recv_sem.at[k],
            device_id=device(step, flip), device_id_type=MESH,
        ).wait_recv()
    for copy in copies:
        copy.wait_send()


def deliver(accs, qg, mixing):
    whole = pl.BlockSpec(memory_space=VMEM)
    return pl.pallas_call(
        deliver_kernel,
        out_shape=jax.ShapeDtypeStruct((64, 64, 128), BF16),
        in_specs=[whole] * 6,
        out_specs=whole,
        scratch_shapes=[VMEM((2, 8, 4, 64, 128), BF16), DMA((16,)), DMA((16,)), DMA],
        compiler_params=pltpu.CompilerParams(
            collective_id=1, has_side_effects=True, vmem_limit_bytes=16 * 1024 * 1024
        ),
        name="deliver",
    )(*accs, qg, mixing)


def per_device(
    pair_field, ln_gain, w_query, w_key, w_value, w_gate, w_bias, w_out, tile_mask, type_ids
):
    weights = [w.T for w in (w_query, w_key, w_value, w_gate)]
    weights.append(w_bias.T)
    operands = (pair_field, ln_gain.reshape(1, 128), *weights, type_ids.reshape(8, 128), w_out, tile_mask)
    qg, kbd, vbd, bias, bound, mixing, lists = spread(
        *[pltpu.with_memory_space_constraint(operand, pltpu.HBM) for operand in operands]
    )
    accs = attend(lists, qg, kbd, vbd, bias.reshape(2, 16, 2, 8, 32, 256), bound)
    return jnp.transpose(deliver(accs, qg, mixing), (2, 0, 1))


def solution(mesh):
    return jax.shard_map(
        per_device,
        mesh=mesh,
        in_specs=(
            P("row", "col", None),
            P(),
            P(None, "head"),
            P(None, "head"),
            P(None, "head"),
            P(None, "head"),
            P(None, "head"),
            P(),
            P(),
            P(),
        ),
        out_specs=P("row", "col", "head"),
        check_vma=False,
    )
```

```python
import math

import jax
import jax.numpy as jnp
from jax import lax
from jax.experimental import pallas as pl
from jax.experimental.pallas import tpu as pltpu
from jax.sharding import PartitionSpec as P

MESH = pl.DeviceIdType.MESH
F32 = jnp.float32
BF16 = jnp.bfloat16
VMEM = pltpu.VMEM
DMA = pltpu.SemaphoreType.DMA

epsilon = 1e-05
masked_score = -1000000000.0
LOG2E = math.log2(math.e)
SCALE = LOG2E / math.sqrt(32)
SAFE = 64.0
NT = (((1,), (1,)), ((), ()))


def ring(value, size):
    return lax.rem(value + size, size)


def spread_kernel(
    tile_ref, gain_in, wq_ref, wk_ref, wv_ref, wg_ref, wb_in, types_in, w_out_in, mask_in,
    qg_ref, kbd_ref, vbd_ref, bias_ref, bound_ref, mixing_ref, lists_ref,
    half, gain_ref, wb_ref, types_ref, w_out_ref, mask_ref, wide, send, strip, wbuf, wall, flat, bsend, tops,
    load_sem, col_send, col_recv, z_send, z_recv, w_send, w_recv,
    g_send, g_recv, s_send, s_recv, own_sem,
):
    row = lax.axis_index("row")
    col = lax.axis_index("col")
    head = lax.axis_index("head")
    core = lax.rem(col, 2)
    x = lax.rem(lax.div(col, 2), 4)
    y = head * 2 + lax.div(col, 8)

    def place(x_, y_, core_=None):
        return (row, lax.rem(y_, 2) * 8 + x_ * 2 + (core if core_ is None else core_), lax.div(y_, 2))

    def along_z(step):
        return (ring(row + step, 8), col, head)

    partner = place(x, ring(y + 2, 4))
    peers = [along_z(step) for step in range(1, 8)]
    peers += [place(ring(x + 1, 4), y), place(ring(x - 1, 4), y)]
    peers += [place(x, ring(y + 1, 4)), place(x, ring(y - 1, 4)), partner]
    peers += [place(x, y, 1 - core)]
    barrier = pltpu.get_barrier_semaphore()
    for peer in peers:
        pl.semaphore_signal(barrier, inc=1, device_id=peer, device_id_type=MESH)

    loads = [
        (tile_ref.at[:, pl.ds(pl.multiple_of(head * 32, 32), 32), :], half),
        (gain_in, gain_ref), (wb_in, wb_ref), (types_in, types_ref),
    ]
    loads += [
        (ref, wbuf.at[head, pl.ds(kind * 64, 64)]) for kind, ref in enumerate((wq_ref, wk_ref, wv_ref, wg_ref))
    ]
    loads += [(w_out_in, w_out_ref), (mask_in, mask_ref)]
    loads = [pltpu.make_async_copy(src, dst, load_sem.at[n]) for n, (src, dst) in enumerate(loads)]
    for load in loads:
        load.start()
    tops[...] = jnp.zeros_like(tops)
    loads[0].wait()

    def widen(block, carry):
        rows = half[pl.ds(block * 8, 8)].astype(F32).reshape(256, 128)
        wide[pl.ds(pl.multiple_of(block * 256, 256), 256), :] = rows
        return carry

    lax.fori_loop(0, 16, widen, 0)
    ones = jnp.ones((128, 128), BF16)
    loads[1].wait()
    gain = gain_ref[...]

    def norm_for(step):
        target = ring(row + step, 8)
        for jj in range(4):
            value = wide[pl.ds(4 * target + jj, 128, stride=32), :]
            mean = jnp.dot(value.astype(BF16), ones, preferred_element_type=F32) * (1.0 / 128)
            centred = value - mean
            squares = (centred * centred).astype(BF16)
            spread = jnp.dot(squares, ones, preferred_element_type=F32) * (1.0 / 128)
            normed = centred * lax.rsqrt(spread + epsilon) * gain
            send[target, jj] = normed.astype(BF16)

    def norm_near(n, carry):
        norm_for(n)
        norm_for(-n)
        return carry

    def norm_far(n, carry):
        norm_for(3 + n)
        norm_for(-3 * (1 - n))
        return carry

    lax.fori_loop(1, 3, norm_near, 0)
    for load in loads[2:]:
        load.wait()
    wbuf[head, 256:272, :] = jnp.concatenate(
        [wb_ref[...].astype(F32), jnp.zeros((14, 128), F32)], axis=0
    ).astype(BF16)
    pl.semaphore_wait(barrier, len(peers))
    w_copy = pltpu.make_async_remote_copy(
        src_ref=wbuf.at[head], dst_ref=wbuf.at[head], send_sem=w_send, recv_sem=w_recv,
        device_id=partner, device_id_type=MESH,
    )
    w_copy.start()
    sent = [w_copy]

    def push(src, dst, send_sem, recv_sem, device):
        copy = pltpu.make_async_remote_copy(
            src_ref=src, dst_ref=dst, send_sem=send_sem, recv_sem=recv_sem,
            device_id=device, device_id_type=MESH,
        )
        copy.start()
        sent.append(copy)

    def strip_rows(step, core_=None):
        source = ring(row + step, 8)
        return strip.at[
            core if core_ is None else core_, :, pl.ds(pl.multiple_of(source * 128, 128), 128), :
        ]

    def col_push(step):
        target = ring(row + step, 8)
        push(send.at[target], strip_rows(0), col_send.at[step], col_recv.at[step], along_z(step))

    col_push(1)
    col_push(7)
    lax.fori_loop(0, 2, norm_far, 0)
    pltpu.make_async_remote_copy(
        src_ref=wbuf.at[1 - head], dst_ref=wbuf.at[1 - head], send_sem=w_send, recv_sem=w_recv,
        device_id=partner, device_id_type=MESH,
    ).wait_recv()

    wb = wbuf[0, 256:272, :].astype(F32) + pltpu.roll(wbuf[1, 256:272, :].astype(F32), 2, 0)
    weighted = wb * gain
    wbt = wb.astype(BF16)

    def bias_for(target, carry):
        part = lax.dot_general(wbt, send[target].reshape(512, 128), NT, preferred_element_type=F32)
        for jj in range(4):
            flat[pl.ds(pl.multiple_of((4 * target + jj) * 8, 8), 8), :] = part[0:8, jj * 128:jj * 128 + 128]
        return carry

    lax.fori_loop(0, 8, bias_for, 0, unroll=4)
    living = jnp.broadcast_to(types_ref[pl.ds(row, 1), :] != 0, (32, 128))
    by_head = [
        jnp.where(living, flat[pl.ds(h, 32, stride=8), :] * LOG2E, masked_score) for h in range(4)
    ]
    bsend[0] = jnp.concatenate([b[:, :64] for b in by_head], axis=1).astype(BF16)
    bsend[1] = jnp.concatenate([b[:, 64:] for b in by_head], axis=1).astype(BF16)

    def unit(x_, y_, low, count):
        return bias_ref.at[low // 8, lax.rem(y_, 2), x_, lax.div(y_, 2), pl.ds(low % 8, count)]

    def arrive(dst, send_sem, recv_sem):
        pltpu.make_async_remote_copy(
            src_ref=dst, dst_ref=dst, send_sem=send_sem, recv_sem=recv_sem,
            device_id=partner, device_id_type=MESH,
        ).wait_recv()

    def slot(step):
        return 2 * step - 1 if step > 0 else -2 * step

    def chunk(step, low=0, count=2):
        return unit(x, y, 2 * slot(step) + low, count)

    def z_push(k, src, dst, step):
        push(src, dst, z_send.at[k], z_recv.at[k], along_z(step))

    def z_arrive(k, dst):
        arrive(dst, z_send.at[k], z_recv.at[k])

    own = pltpu.make_async_copy(bsend, chunk(0), own_sem.at[0])
    own.start()
    for k, step in enumerate((2, -2, 1, -1)):
        z_push(k, bsend, chunk(-step), step)

    own_cols = pltpu.make_async_copy(send.at[row], strip_rows(0), own_sem.at[1])
    own_cols.start()

    for kind, place_of in enumerate((2, 0, 1, 3)):
        for s in range(2):
            wall[place_of * 128 + s * 64:place_of * 128 + s * 64 + 64, :] = wbuf[s, kind * 64:kind * 64 + 64, :]
    together = (
        lax.div(lax.broadcasted_iota(jnp.int32, (128, 128), 0), 32)
        == lax.div(lax.broadcasted_iota(jnp.int32, (128, 128), 1), 32)
    ).astype(F32).astype(BF16)

    key_head = lax.div(lax.broadcasted_iota(jnp.int32, (128, 128), 0), 32)
    side_of = lax.div(lax.broadcasted_iota(jnp.int32, (128, 128), 1), 64)
    key_here = [(key_head == 2 * n + side_of).astype(F32).astype(BF16) for n in range(2)]
    lane_head = lax.div(lax.broadcasted_iota(jnp.int32, (64, 128), 1), 32)
    value_here = [(lane_head == h).astype(F32).astype(BF16) for h in range(4)]

    def project(core_, step):
        source = ring(row + step, 8)
        first_block = 2 * slot(step)
        rows = pl.ds(pl.multiple_of(source * 128, 128), 128)
        own_rows = pl.ds(pl.multiple_of(source * 128 + core * 64, 64), 64)
        into = pl.ds(pl.multiple_of(source * 64, 64), 64)

        def one(jj, carry):
            m = core_ * 4 + jj
            value = strip[core_, jj, rows, :]
            keys = lax.dot_general(wall[0:128, :], value, NT, preferred_element_type=F32)
            values = lax.dot_general(value, wall[128:256, :], NT, preferred_element_type=F32).astype(BF16)
            both = lax.dot_general(strip[core_, jj, own_rows, :], wall[256:512, :], NT, preferred_element_type=F32)
            query = both[:, :128] * SCALE
            qg_ref[0, m, into, :] = query.astype(BF16)
            qg_ref[1, m, into, :] = jax.nn.sigmoid(both[:, 128:]).astype(BF16)
            short = keys.astype(BF16)
            for odd in range(2):
                twice = jnp.concatenate([short[:, odd * 64:odd * 64 + 64]] * 2, axis=1)
                for n in range(2):
                    kbd_ref[m, first_block + odd, :, n * 128:(n + 1) * 128] = twice * key_here[n]
                for h in range(4):
                    vbd_ref[m, first_block + odd, h * 64:(h + 1) * 64, :] = (
                        values[odd * 64:odd * 64 + 64, :] * value_here[h]
                    )
            lengths = jnp.dot((query * query).astype(BF16), together, preferred_element_type=F32)
            tops[0:1, :] = jnp.maximum(tops[0:1, :], jnp.max(lengths, axis=0, keepdims=True))
            lengths = jnp.dot(together, (keys * keys).astype(BF16), preferred_element_type=F32)
            tops[1:2, :] = jnp.maximum(tops[1:2, :], jnp.max(lengths, axis=0, keepdims=True))
            return carry

        lax.fori_loop(0, 4, one, 0, unroll=2)

    def share(step):
        k = step % 8
        push(strip_rows(step), strip_rows(step), s_send.at[k], s_recv.at[k], place(x, y, 1 - core))

    def take(step):
        arrive(strip_rows(step), col_send.at[(8 - step) % 8], col_recv.at[(8 - step) % 8])
        share(step)
        project(core, step)

    def take_shared(step):
        k = step % 8
        arrive(strip_rows(step, 1 - core), s_send.at[k], s_recv.at[k])
        project(1 - core, step)

    own_cols.wait()
    share(0)
    own.wait()
    for k, step in enumerate((-2, 2, -1, 1)):
        z_arrive(k, chunk(step))
    z_push(4, chunk(-2), chunk(-3), 1)
    z_push(5, chunk(2), chunk(3), -1)
    z_push(6, chunk(-2, 0, 1), chunk(4, 0, 1), 2)
    z_push(7, chunk(2, 1, 1), chunk(4, 1, 1), -2)
    for step in (2, 6, 3, 5, 4):
        col_push(step)

    def far_bias():
        z_arrive(4, chunk(-3))
        z_arrive(5, chunk(3))
        z_arrive(6, chunk(4, 0, 1))
        z_arrive(7, chunk(4, 1, 1))

    def make_lists():
        mixing_ref[...] = w_out_ref[...].astype(F32).T.astype(BF16)
        part = mask_ref[...].astype(F32)
        place_ = lax.div(lax.broadcasted_iota(jnp.int32, (16, 128), 1), 2)
        away = lax.div(place_ + 1, 2) * (2 * lax.rem(place_, 2) - 1)
        there = 2 * lax.rem(row + away + 8, 8) + lax.rem(lax.broadcasted_iota(jnp.int32, (16, 128), 1), 2)
        inside = lax.broadcasted_iota(jnp.int32, (16, 128), 1) < 16
        turned = (inside & (lax.broadcasted_iota(jnp.int32, (16, 128), 0) == there)).astype(F32).astype(BF16)
        diagonal = lax.broadcasted_iota(jnp.int32, (16, 16), 0) == lax.broadcasted_iota(jnp.int32, (16, 16), 1)
        part = jnp.where((part == 1.0) | diagonal, 1.0, 0.0)
        wanted = lax.broadcasted_iota(jnp.int32, (16, 16), 0)
        mine = (wanted < 8) & (lax.broadcasted_iota(jnp.int32, (16, 16), 1) == 2 * wanted + core)
        part = jnp.dot(mine.astype(F32).astype(BF16), part.astype(BF16), preferred_element_type=F32)
        allowed = jnp.dot(part.astype(BF16), turned, preferred_element_type=F32)
        before = [jnp.zeros((1, 128), F32)]
        for i in range(16):
            before.append(before[-1] + allowed[i:i + 1, :])
        rank = jnp.concatenate(before[:16], axis=0)
        pairs = jnp.broadcast_to(jnp.floor((before[16] + 1.0) * 0.5), (16, 128))
        earlier = (
            lax.broadcasted_iota(jnp.int32, (128, 128), 0) < lax.broadcasted_iota(jnp.int32, (128, 128), 1)
        ).astype(F32).astype(BF16)
        start = jnp.dot(pairs.astype(BF16), earlier, preferred_element_type=F32)
        total = jnp.sum(pairs[0:1, :], axis=1, keepdims=True)
        rank = rank + 2.0 * start
        entry = 2.0 * lax.broadcasted_iota(jnp.int32, (16, 128), 1).astype(F32)
        number = lax.broadcasted_iota(jnp.int32, (16, 128), 0).astype(F32)
        block = jnp.zeros((16, 128), F32)
        picked = [jnp.zeros((16, 128), F32)] * 2
        found = [jnp.zeros((16, 128), F32)] * 2
        for k in range(16):
            at = jnp.broadcast_to(rank[:, k:k + 1], (16, 128))
            here = jnp.broadcast_to(allowed[:, k:k + 1], (16, 128))
            for side in range(2):
                hit = jnp.where(at == entry + side, here, 0.0)
                found[side] = found[side] + hit
                picked[side] = picked[side] + hit * number
                if side == 0:
                    block = block + hit * k
        rows = [jnp.sum(block, axis=0, keepdims=True)]
        for side in range(2):
            missing = 1.0 - jnp.sum(found[side], axis=0, keepdims=True)
            rows.append(jnp.sum(picked[side], axis=0, keepdims=True) + (8.0 + side) * missing)
        rows.append(jnp.broadcast_to(total, (1, 128)))
        rows.append(jnp.zeros((4, 128), F32))
        lists_ref[...] = jnp.concatenate(rows, axis=0).astype(jnp.int32)

    def node(run, a, b):
        return (a, b) if run == 0 else (b, a)

    first = (x, y)
    second = (y, x)

    def shipment(run, index, a, b, low, count, to_a, to_b):
        k = run * 20 + index
        ref = unit(*node(run, a, b), run * 8 + low, count)
        push(ref, ref, g_send.at[k], g_recv.at[k], place(*node(run, to_a, to_b)))

    def receive(run, index, a, b, low, count):
        k = run * 20 + index
        arrive(unit(*node(run, a, b), run * 8 + low, count), g_send.at[k], g_recv.at[k])

    def across(run, u, a, b):
        shipment(run, 4 + 4 * u, a, b, 0, 8, first[run], ring(b + 1, 4))
        shipment(run, 5 + 4 * u, a, b, 0, 8, first[run], ring(b - 1, 4))

    for run in range(2):
        a, b = first[run], second[run]
        if run == 1:
            project(core, 0)
            far_bias()
        shipment(run, 0, a, b, 0, 8, ring(a + 1, 4), b)
        shipment(run, 1, a, b, 0, 8, ring(a - 1, 4), b)
        across(run, 0, a, b)
    for run in range(2):
        a, b = first[run], second[run]
        receive(run, 0, ring(a - 1, 4), b, 0, 8)
        shipment(run, 2, ring(a - 1, 4), b, 0, 4, ring(a + 1, 4), b)
        receive(run, 1, ring(a + 1, 4), b, 0, 8)
        shipment(run, 3, ring(a + 1, 4), b, 4, 4, ring(a - 1, 4), b)
    for run in range(2):
        a, b = first[run], second[run]
        across(run, 1, ring(a - 1, 4), b)
        across(run, 2, ring(a + 1, 4), b)
    for run in range(2):
        a, b = first[run], second[run]
        receive(run, 2, ring(a + 2, 4), b, 0, 4)
        receive(run, 3, ring(a + 2, 4), b, 4, 4)
        across(run, 3, ring(a + 2, 4), b)
    take(1)
    take(-1)
    take_shared(0)
    for u in range(4):
        for run in range(2):
            a, b = ring(first[run] + (0, -1, 1, 2)[u], 4), second[run]
            receive(run, 4 + 4 * u, a, ring(b - 1, 4), 0, 8)
            shipment(run, 6 + 4 * u, a, ring(b - 1, 4), 0, 4, first[run], ring(b + 1, 4))
            receive(run, 5 + 4 * u, a, ring(b + 1, 4), 0, 8)
            shipment(run, 7 + 4 * u, a, ring(b + 1, 4), 4, 4, first[run], ring(b - 1, 4))
        if u == 1:
            make_lists()
            take_shared(1)
        if u == 2:
            take_shared(-1)
            take(2)
        if u == 3:
            take(-2)
            take(3)
            take(-3)
            take_shared(2)
    for u in range(4):
        for run in range(2):
            a, b = ring(first[run] + (0, -1, 1, 2)[u], 4), second[run]
            receive(run, 6 + 4 * u, a, ring(b + 2, 4), 0, 4)
            receive(run, 7 + 4 * u, a, ring(b + 2, 4), 4, 4)
        if u == 0:
            take(4)
        if u == 1:
            take_shared(-2)
        if u == 2:
            take_shared(3)
    take_shared(-3)
    take_shared(4)
    bound_ref[0:8, :] = tops[...]
    bound_ref[8:24, :] = jnp.broadcast_to(jnp.sum(weighted * weighted, axis=1, keepdims=True), (16, 128))
    for copy in sent:
        copy.wait_send()


def spread(*operands):
    whole = pl.BlockSpec(memory_space=VMEM)
    return pl.pallas_call(
        spread_kernel,
        out_shape=(
            jax.ShapeDtypeStruct((2, 8, 512, 128), BF16),
            jax.ShapeDtypeStruct((8, 16, 128, 256), BF16),
            jax.ShapeDtypeStruct((8, 16, 256, 128), BF16),
            jax.ShapeDtypeStruct((2, 2, 4, 2, 8, 32, 256), BF16),
            jax.ShapeDtypeStruct((24, 128), F32),
            jax.ShapeDtypeStruct((128, 128), BF16),
            jax.ShapeDtypeStruct((8, 128), jnp.int32),
        ),
        in_specs=[pl.BlockSpec(memory_space=pltpu.HBM)] * len(operands),
        out_specs=(whole,) * 7,
        scratch_shapes=[
            VMEM((128, 32, 128), BF16),
            VMEM((1, 128), F32),
            VMEM((2, 128), BF16),
            VMEM((8, 128), jnp.int32),
            VMEM((128, 128), BF16),
            VMEM((16, 16), jnp.int32),
            VMEM((4096, 128), F32),
            VMEM((8, 4, 128, 128), BF16),
            VMEM((2, 4, 1024, 128), BF16),
            VMEM((2, 272, 128), BF16),
            VMEM((512, 128), BF16),
            VMEM((256, 128), F32),
            VMEM((2, 32, 256), BF16),
            VMEM((8, 128), F32),
            DMA((10,)), DMA((8,)), DMA((8,)), DMA((8,)), DMA((8,)), DMA, DMA,
            DMA((40,)), DMA((40,)), DMA((8,)), DMA((8,)), DMA((2,)),
        ],
        compiler_params=pltpu.CompilerParams(
            collective_id=0, has_side_effects=True, vmem_limit_bytes=20 * 1024 * 1024
        ),
        name="spread",
    )(*operands)


def attend_kernel(
    lists_ref, qg_ref, kbd, vbd, bias, bound_ref, *accs_and_peak
):
    *accs, peak = accs_and_peak
    for acc in accs:
        acc[...] = jnp.zeros_like(acc)
    same = (
        lax.div(lax.broadcasted_iota(jnp.int32, (256, 128), 0), 64)
        == lax.div(lax.broadcasted_iota(jnp.int32, (256, 128), 1), 32)
    ).astype(F32).astype(BF16)

    reach = jnp.sqrt(jnp.max(bound_ref[0:1, :])) * jnp.sqrt(jnp.max(bound_ref[1:2, :]))
    bias_reach = jnp.sqrt(jnp.max(bound_ref[8:24, :])) * (math.sqrt(128) * LOG2E)
    safe = (reach + bias_reach) * 1.03 <= SAFE

    def query(j, i):
        return qg_ref[0, j, pl.ds(pl.multiple_of(jnp.minimum(i, 7) * 64, 64), 64), :]

    def values_of(j, block):
        return jnp.concatenate([vbd[j, block], same], axis=1)

    def offset_of(i, block):
        at = (lax.div(block, 8), jnp.minimum(i, 7))
        n = lax.rem(block, 8)
        return [bias[at[0], at[1], half, n].astype(F32) for half in range(2)]

    total_pairs = lists_ref[3, 0]

    @pl.when(safe)
    def _():
        def step(t, carry):
            work = []
            for side in range(2):
                e = 2 * t + side
                block = lists_ref[0, e]
                ids = (lists_ref[1, e], lists_ref[2, e])
                offset = jnp.concatenate(offset_of(ids[0], block) + offset_of(ids[1], block), axis=0)
                work.append((block, ids, offset))
            for j in range(8):
                for block, ids, offset in work:
                    queries = jnp.concatenate([query(j, i) for i in ids], axis=0)
                    score = jnp.dot(queries, kbd[j, block], preferred_element_type=F32)
                    weights = jnp.exp2(score + offset).astype(BF16)
                    total = jnp.dot(weights, values_of(j, block), preferred_element_type=F32)
                    olds = [accs[j][i] for i in ids]
                    for n in range(2):
                        accs[j][ids[n]] = olds[n] + total[n * 64:(n + 1) * 64, :]
            return carry

        lax.fori_loop(0, lax.div(total_pairs + 1, 2), step, 0)

    @pl.when(jnp.logical_not(safe))
    def _():
        peak[...] = jnp.full_like(peak, -1e30)

        def step(n, carry):
            e = lax.div(n, 2)
            block = lists_ref[0, e]
            i = lists_ref[1 + lax.rem(n, 2), e]
            offset = jnp.concatenate(offset_of(i, block), axis=0)
            for j in range(8):
                score = jnp.dot(query(j, i), kbd[j, block], preferred_element_type=F32) + offset
                old = peak[j, i]
                tops = [
                    jnp.maximum(
                        jnp.max(score[:, h * 64:(h + 1) * 64], axis=1, keepdims=True),
                        old[:, h * 32:h * 32 + 1],
                    )
                    for h in range(4)
                ]
                shift = jnp.concatenate([jnp.broadcast_to(top, (64, 64)) for top in tops], axis=1)
                fresh = jnp.concatenate([jnp.broadcast_to(top, (64, 32)) for top in tops], axis=1)
                decay = jnp.exp2(old - fresh)
                weights = jnp.exp2(score - shift).astype(BF16)
                total = jnp.dot(weights, values_of(j, block), preferred_element_type=F32)
                accs[j][i] = accs[j][i] * jnp.concatenate([decay, decay], axis=1) + total
                peak[j, i] = fresh
            return carry

        lax.fori_loop(0, 2 * total_pairs, step, 0)


def attend(lists, qg, kbd, vbd, bias, bound):
    whole = pl.BlockSpec(memory_space=VMEM)
    return pl.pallas_call(
        attend_kernel,
        out_shape=[jax.ShapeDtypeStruct((10, 64, 256), F32)] * 8,
        in_specs=[pl.BlockSpec(memory_space=pltpu.SMEM)] + [whole] * 5,
        out_specs=[whole] * 8,
        scratch_shapes=[VMEM((8, 10, 64, 128), F32)],
        compiler_params=pltpu.CompilerParams(vmem_limit_bytes=16 * 1024 * 1024),
        name="attend",
    )(lists, qg, kbd, vbd, bias, bound)


def deliver_kernel(*refs):
    accs = refs[:8]
    qg_ref, mixing_ref, out_ref, update_ref, landed, send_sem, recv_sem, own_sem = refs[8:]
    row = lax.axis_index("row")
    col = lax.axis_index("col")
    head = lax.axis_index("head")
    core = lax.rem(col, 2)

    def device(step, flip, cross):
        return (
            ring(row + step, 8),
            col + 1 - 2 * core if cross else col,
            (1 - head) if flip else head,
        )

    def from_(step, flip, cross):
        there = device(step, flip, cross)
        return landed.at[(1 - core) if cross else core, there[2] * 8 + there[0]]

    def part(step, flip, cross):
        there = device(step, flip, cross)
        return update_ref.at[there[2], there[0], (1 - core) if cross else core]

    steps = (4, 3, 5, 2, 6, 1, 7, 0)
    kinds = ((1, 0), (1, 1), (0, 0), (0, 1))
    moves = [(step, flip, cross) for step in steps for flip, cross in kinds if step or flip or cross]
    barrier = pltpu.get_barrier_semaphore()
    for move in moves:
        pl.semaphore_signal(barrier, inc=1, device_id=device(*move), device_id_type=MESH)

    def finish(step):
        target = ring(row + step, 8)
        rows = pl.ds(pl.multiple_of(target * 64, 64), 64)
        for core_ in range(2):
            for pair in range(2):
                gated = []
                for m in (core_ * 4 + 2 * pair, core_ * 4 + 2 * pair + 1):
                    sums = accs[m][target]
                    attention = sums[:, :128] / sums[:, 128:]
                    gated.append((attention * qg_ref[1, m, rows, :].astype(F32)).astype(BF16))
                gated = jnp.concatenate(gated, axis=0)
                update = lax.dot_general(mixing_ref[...], gated, NT, preferred_element_type=F32).astype(BF16)
                update_ref[0, target, core_, pair] = update[:64, :]
                update_ref[1, target, core_, pair] = update[64:, :]

    copies = []

    def push(step, flip, cross):
        k = (flip * 2 + cross) * 8 + step
        copy = pltpu.make_async_remote_copy(
            src_ref=part(step, flip, cross), dst_ref=from_(0, 0, 0),
            send_sem=send_sem.at[k], recv_sem=recv_sem.at[k],
            device_id=device(step, flip, cross), device_id_type=MESH,
        )
        copy.start()
        copies.append(copy)

    def arrive(step, flip, cross):
        k = (flip * 2 + cross) * 8 + step
        ref = from_(-step, flip, cross)
        pltpu.make_async_remote_copy(
            src_ref=ref, dst_ref=ref, send_sem=send_sem.at[k], recv_sem=recv_sem.at[k],
            device_id=device(0, 0, 1), device_id_type=MESH,
        ).wait_recv()

    for step in (4, 3, 5):
        finish(step)
    pl.semaphore_wait(barrier, len(moves))
    for step in steps:
        if step not in (4, 3, 5):
            finish(step)
        for flip, cross in kinds:
            if step or flip or cross:
                push(step, flip, cross)
    own = pltpu.make_async_copy(part(0, 0, 0), from_(0, 0, 0), own_sem)
    own.start()

    def join(step, flip):
        source = ((1 - head) if flip else head) * 8 + ring(row - step, 8)
        for pair in range(2):
            low = landed[0, source, pair]
            high = landed[1, source, pair]
            out_ref[source * 4 + pair * 2] = jnp.concatenate([low[:, :64], high[:, :64]], axis=1)
            out_ref[source * 4 + pair * 2 + 1] = jnp.concatenate([low[:, 64:], high[:, 64:]], axis=1)

    own.wait()
    arrive(0, 0, 1)
    join(0, 0)
    arrive(0, 1, 0)
    arrive(0, 1, 1)
    join(0, 1)
    for step in (1, 7, 2, 6, 3, 5, 4):
        for flip in range(2):
            arrive(step, flip, 0)
            arrive(step, flip, 1)
            join(step, flip)
    for copy in copies:
        copy.wait_send()


def deliver(accs, qg, mixing):
    whole = pl.BlockSpec(memory_space=VMEM)
    return pl.pallas_call(
        deliver_kernel,
        out_shape=jax.ShapeDtypeStruct((64, 64, 128), BF16),
        in_specs=[whole] * 10,
        out_specs=whole,
        scratch_shapes=[
            VMEM((2, 8, 2, 2, 64, 128), BF16),
            VMEM((2, 16, 2, 64, 128), BF16),
            DMA((32,)), DMA((32,)), DMA,
        ],
        compiler_params=pltpu.CompilerParams(
            collective_id=1, has_side_effects=True, vmem_limit_bytes=16 * 1024 * 1024
        ),
        name="deliver",
    )(*accs, qg, mixing)


def per_device(
    pair_field, ln_gain, w_query, w_key, w_value, w_gate, w_bias, w_out, tile_mask, type_ids
):
    weights = [w.T for w in (w_query, w_key, w_value, w_gate)]
    weights.append(w_bias.T)
    operands = (pair_field, ln_gain.reshape(1, 128), *weights, type_ids.reshape(8, 128), w_out, tile_mask)
    qg, kbd, vbd, bias, bound, mixing, lists = spread(
        *[pltpu.with_memory_space_constraint(operand, pltpu.HBM) for operand in operands]
    )
    accs = attend(lists, qg, kbd, vbd, bias.reshape(2, 8, 2, 8, 32, 256), bound)
    return jnp.transpose(deliver(accs, qg, mixing), (2, 0, 1))


def solution(mesh):
    return jax.shard_map(
        per_device,
        mesh=mesh,
        in_specs=(
            P("row", "col", None),
            P(),
            P(None, "head"),
            P(None, "head"),
            P(None, "head"),
            P(None, "head"),
            P(None, "head"),
            P(),
            P(),
            P(),
        ),
        out_specs=P("row", "col", "head"),
        check_vma=False,
    )
```

```python
import math

import jax
import jax.numpy as jnp
from jax import lax
from jax.experimental import pallas as pl
from jax.experimental.pallas import tpu as pltpu
from jax.sharding import PartitionSpec as P

MESH = pl.DeviceIdType.MESH
F32 = jnp.float32
BF16 = jnp.bfloat16
VMEM = pltpu.VMEM
DMA = pltpu.SemaphoreType.DMA

epsilon = 1e-05
masked_score = -1000000000.0
LOG2E = math.log2(math.e)
SCALE = LOG2E / math.sqrt(32)
SAFE = 64.0
NT = (((1,), (1,)), ((), ()))


def ring(value, size):
    return lax.rem(value + size, size)


def spread_kernel(
    tile_ref, gain_in, wq_ref, wk_ref, wv_ref, wg_ref, wb_in, types_in, w_out_in, mask_in,
    qg_ref, kbd_ref, vbd_ref, bias_ref, bound_ref, mixing_ref, lists_ref,
    half, gain_ref, wb_ref, types_ref, w_out_ref, mask_ref, wide, send, strip, wbuf, wall, flat, bsend, tops,
    load_sem, col_send, col_recv, z_send, z_recv, w_send, w_recv,
    g_send, g_recv, s_send, s_recv, own_sem,
):
    row = lax.axis_index("row")
    col = lax.axis_index("col")
    head = lax.axis_index("head")
    core = lax.rem(col, 2)
    x = lax.rem(lax.div(col, 2), 4)
    y = head * 2 + lax.div(col, 8)

    def place(x_, y_, core_=None):
        return (row, lax.rem(y_, 2) * 8 + x_ * 2 + (core if core_ is None else core_), lax.div(y_, 2))

    def along_z(step):
        return (ring(row + step, 8), col, head)

    partner = place(x, ring(y + 2, 4))
    peers = [along_z(step) for step in range(1, 8)]
    peers += [place(ring(x + 1, 4), y), place(ring(x - 1, 4), y)]
    peers += [place(x, ring(y + 1, 4)), place(x, ring(y - 1, 4)), partner]
    peers += [place(x, y, 1 - core)]
    barrier = pltpu.get_barrier_semaphore()
    for peer in peers:
        pl.semaphore_signal(barrier, inc=1, device_id=peer, device_id_type=MESH)

    loads = [
        (tile_ref.at[:, pl.ds(pl.multiple_of(head * 32, 32), 32), :], half),
        (gain_in, gain_ref), (wb_in, wb_ref), (types_in, types_ref),
    ]
    loads += [
        (ref, wbuf.at[head, pl.ds(kind * 64, 64)]) for kind, ref in enumerate((wq_ref, wk_ref, wv_ref, wg_ref))
    ]
    loads += [(w_out_in, w_out_ref), (mask_in, mask_ref)]
    loads = [pltpu.make_async_copy(src, dst, load_sem.at[n]) for n, (src, dst) in enumerate(loads)]
    for load in loads:
        load.start()
    tops[...] = jnp.zeros_like(tops)
    loads[0].wait()

    def widen(block, carry):
        rows = half[pl.ds(block * 8, 8)].astype(F32).reshape(256, 128)
        wide[pl.ds(pl.multiple_of(block * 256, 256), 256), :] = rows
        return carry

    lax.fori_loop(0, 16, widen, 0)
    ones = jnp.ones((128, 128), BF16)
    loads[1].wait()
    gain = gain_ref[...]

    def norm_for(step):
        target = ring(row + step, 8)
        for jj in range(4):
            value = wide[pl.ds(4 * target + jj, 128, stride=32), :]
            mean = jnp.dot(value.astype(BF16), ones, preferred_element_type=F32) * (1.0 / 128)
            centred = value - mean
            squares = (centred * centred).astype(BF16)
            spread = jnp.dot(squares, ones, preferred_element_type=F32) * (1.0 / 128)
            normed = centred * lax.rsqrt(spread + epsilon) * gain
            send[target, jj] = normed.astype(BF16)

    def norm_near(n, carry):
        norm_for(n)
        norm_for(-n)
        return carry

    def norm_far(n, carry):
        norm_for(3 + n)
        norm_for(-3 * (1 - n))
        return carry

    lax.fori_loop(1, 3, norm_near, 0)
    for load in loads[2:]:
        load.wait()
    wbuf[head, 256:272, :] = jnp.concatenate(
        [wb_ref[...].astype(F32), jnp.zeros((14, 128), F32)], axis=0
    ).astype(BF16)
    pl.semaphore_wait(barrier, len(peers))
    w_copy = pltpu.make_async_remote_copy(
        src_ref=wbuf.at[head], dst_ref=wbuf.at[head], send_sem=w_send, recv_sem=w_recv,
        device_id=partner, device_id_type=MESH,
    )
    w_copy.start()
    sent = [w_copy]

    def push(src, dst, send_sem, recv_sem, device):
        copy = pltpu.make_async_remote_copy(
            src_ref=src, dst_ref=dst, send_sem=send_sem, recv_sem=recv_sem,
            device_id=device, device_id_type=MESH,
        )
        copy.start()
        sent.append(copy)

    def strip_rows(step):
        source = ring(row + step, 8)
        return strip.at[:, pl.ds(pl.multiple_of(source * 128, 128), 128), :]

    def col_push(step):
        target = ring(row + step, 8)
        push(send.at[target], strip_rows(0), col_send.at[step], col_recv.at[step], along_z(step))

    col_push(1)
    col_push(7)
    lax.fori_loop(0, 2, norm_far, 0)
    pltpu.make_async_remote_copy(
        src_ref=wbuf.at[1 - head], dst_ref=wbuf.at[1 - head], send_sem=w_send, recv_sem=w_recv,
        device_id=partner, device_id_type=MESH,
    ).wait_recv()

    wb = wbuf[0, 256:272, :].astype(F32) + pltpu.roll(wbuf[1, 256:272, :].astype(F32), 2, 0)
    weighted = wb * gain
    wbt = wb.astype(BF16)

    def bias_for(target, carry):
        part = lax.dot_general(wbt, send[target].reshape(512, 128), NT, preferred_element_type=F32)
        for jj in range(4):
            flat[pl.ds(pl.multiple_of((4 * target + jj) * 8, 8), 8), :] = part[0:8, jj * 128:jj * 128 + 128]
        return carry

    lax.fori_loop(0, 8, bias_for, 0, unroll=4)
    living = jnp.broadcast_to(types_ref[pl.ds(row, 1), :] != 0, (32, 128))
    by_head = [
        jnp.where(living, flat[pl.ds(h, 32, stride=8), :] * LOG2E, masked_score) for h in range(4)
    ]
    bsend[0] = jnp.concatenate([b[:, :64] for b in by_head], axis=1).astype(BF16)
    bsend[1] = jnp.concatenate([b[:, 64:] for b in by_head], axis=1).astype(BF16)

    def unit(x_, y_, low, count, core_=None):
        return bias_ref.at[
            low // 8, lax.rem(y_, 2), x_, core if core_ is None else core_, lax.div(y_, 2), pl.ds(low % 8, count)
        ]

    def arrive(dst, send_sem, recv_sem):
        pltpu.make_async_remote_copy(
            src_ref=dst, dst_ref=dst, send_sem=send_sem, recv_sem=recv_sem,
            device_id=partner, device_id_type=MESH,
        ).wait_recv()

    def slot(step):
        return 2 * step - 1 if step > 0 else -2 * step

    def chunk(step, low=0, count=2):
        return unit(x, y, 2 * slot(step) + low, count)

    def z_push(k, src, dst, step):
        push(src, dst, z_send.at[k], z_recv.at[k], along_z(step))

    def z_arrive(k, dst):
        arrive(dst, z_send.at[k], z_recv.at[k])

    own = pltpu.make_async_copy(bsend, chunk(0), own_sem.at[0])
    own.start()
    for k, step in enumerate((2, -2, 1, -1)):
        z_push(k, bsend, chunk(-step), step)

    own_cols = pltpu.make_async_copy(send.at[row], strip_rows(0), own_sem.at[1])
    own_cols.start()

    for kind, place_of in enumerate((1, 0, 2, 3)):
        for s in range(2):
            wall[place_of * 128 + s * 64:place_of * 128 + s * 64 + 64, :] = wbuf[s, kind * 64:kind * 64 + 64, :]
    together = (
        lax.div(lax.broadcasted_iota(jnp.int32, (128, 128), 0), 32)
        == lax.div(lax.broadcasted_iota(jnp.int32, (128, 128), 1), 32)
    ).astype(F32).astype(BF16)

    key_head = lax.div(lax.broadcasted_iota(jnp.int32, (128, 128), 0), 32)
    side_of = lax.div(lax.broadcasted_iota(jnp.int32, (128, 128), 1), 64)
    key_here = [(key_head == 2 * n + side_of).astype(F32).astype(BF16) for n in range(2)]
    lane_head = lax.div(lax.broadcasted_iota(jnp.int32, (64, 128), 1), 32)
    value_here = [(lane_head == h).astype(F32).astype(BF16) for h in range(4)]

    def project(step):
        source = ring(row + step, 8)
        first_block = 2 * slot(step)
        rows = pl.ds(pl.multiple_of(source * 128, 128), 128)

        def one(jj, carry):
            value = strip[jj, rows, :]
            keys = lax.dot_general(wall[0:128, :], value, NT, preferred_element_type=F32)
            left = lax.dot_general(value, wall[128:256, :], NT, preferred_element_type=F32)
            right = lax.dot_general(value, wall[256:512, :], NT, preferred_element_type=F32)
            query = left * SCALE
            qg_ref[0, jj, rows, :] = query.astype(BF16)
            qg_ref[1, jj, rows, :] = jax.nn.sigmoid(right[:, 128:]).astype(BF16)
            short = keys.astype(BF16)
            values = right[:, :128].astype(BF16)
            for odd in range(2):
                twice = jnp.concatenate([short[:, odd * 64:odd * 64 + 64]] * 2, axis=1)
                for n in range(2):
                    kbd_ref[jj, first_block + odd, :, n * 128:(n + 1) * 128] = twice * key_here[n]
                for h in range(4):
                    vbd_ref[jj, first_block + odd, h * 64:(h + 1) * 64, :] = (
                        values[odd * 64:odd * 64 + 64, :] * value_here[h]
                    )
            lengths = jnp.dot((query * query).astype(BF16), together, preferred_element_type=F32)
            tops[0:1, :] = jnp.maximum(tops[0:1, :], jnp.max(lengths, axis=0, keepdims=True))
            lengths = jnp.dot(together, (keys * keys).astype(BF16), preferred_element_type=F32)
            tops[1:2, :] = jnp.maximum(tops[1:2, :], jnp.max(lengths, axis=0, keepdims=True))
            return carry

        lax.fori_loop(0, 4, one, 0, unroll=True)

    def take(step):
        arrive(strip_rows(step), col_send.at[(8 - step) % 8], col_recv.at[(8 - step) % 8])
        project(step)

    def make_lists():
        mixing_ref[...] = w_out_ref[...].astype(F32).T.astype(BF16)
        part = mask_ref[...].astype(F32)
        place_ = lax.div(lax.broadcasted_iota(jnp.int32, (16, 128), 1), 2)
        away = lax.div(place_ + 1, 2) * (2 * lax.rem(place_, 2) - 1)
        there = 2 * lax.rem(row + away + 8, 8) + lax.rem(lax.broadcasted_iota(jnp.int32, (16, 128), 1), 2)
        inside = lax.broadcasted_iota(jnp.int32, (16, 128), 1) < 16
        turned = (inside & (lax.broadcasted_iota(jnp.int32, (16, 128), 0) == there)).astype(F32).astype(BF16)
        diagonal = lax.broadcasted_iota(jnp.int32, (16, 16), 0) == lax.broadcasted_iota(jnp.int32, (16, 16), 1)
        part = jnp.where((part == 1.0) | diagonal, 1.0, 0.0)
        allowed = jnp.dot(part.astype(BF16), turned, preferred_element_type=F32)
        before = [jnp.zeros((1, 128), F32)]
        for i in range(16):
            before.append(before[-1] + allowed[i:i + 1, :])
        rank = jnp.concatenate(before[:16], axis=0)
        pairs = jnp.broadcast_to(jnp.floor((before[16] + 1.0) * 0.5), (16, 128))
        earlier = (
            lax.broadcasted_iota(jnp.int32, (128, 128), 0) < lax.broadcasted_iota(jnp.int32, (128, 128), 1)
        ).astype(F32).astype(BF16)
        start = jnp.dot(pairs.astype(BF16), earlier, preferred_element_type=F32)
        total = jnp.sum(pairs[0:1, :], axis=1, keepdims=True)
        rank = rank + 2.0 * start
        entry = 2.0 * lax.broadcasted_iota(jnp.int32, (16, 128), 1).astype(F32)
        number = lax.broadcasted_iota(jnp.int32, (16, 128), 0).astype(F32)
        block = jnp.zeros((16, 128), F32)
        picked = [jnp.zeros((16, 128), F32)] * 2
        found = [jnp.zeros((16, 128), F32)] * 2
        for k in range(16):
            at = jnp.broadcast_to(rank[:, k:k + 1], (16, 128))
            here = jnp.broadcast_to(allowed[:, k:k + 1], (16, 128))
            for side in range(2):
                hit = jnp.where(at == entry + side, here, 0.0)
                found[side] = found[side] + hit
                picked[side] = picked[side] + hit * number
                if side == 0:
                    block = block + hit * k
        rows = [jnp.sum(block, axis=0, keepdims=True)]
        for side in range(2):
            missing = 1.0 - jnp.sum(found[side], axis=0, keepdims=True)
            rows.append(jnp.sum(picked[side], axis=0, keepdims=True) + (16.0 + side) * missing)
        rows.append(jnp.broadcast_to(total, (1, 128)))
        rows.append(jnp.zeros((4, 128), F32))
        lists_ref[...] = jnp.concatenate(rows, axis=0).astype(jnp.int32)

    own_cols.wait()
    project(0)
    make_lists()
    own.wait()
    for k, step in enumerate((-2, 2, -1, 1)):
        z_arrive(k, chunk(step))
    z_push(4, chunk(-2), chunk(-3), 1)
    z_push(5, chunk(2), chunk(3), -1)
    z_push(6, chunk(-2, 0, 1), chunk(4, 0, 1), 2)
    z_push(7, chunk(2, 1, 1), chunk(4, 1, 1), -2)

    def far_bias():
        z_arrive(4, chunk(-3))
        z_arrive(5, chunk(3))
        z_arrive(6, chunk(4, 0, 1))
        z_arrive(7, chunk(4, 1, 1))

    def node(run, a, b):
        return (a, b) if run == 0 else (b, a)

    first = (x, y)
    second = (y, x)

    def shipment(run, index, a, b, low, count, to_a, to_b):
        k = run * 20 + index
        ref = unit(*node(run, a, b), run * 8 + low, count)
        push(ref, ref, g_send.at[k], g_recv.at[k], place(*node(run, to_a, to_b)))

    def receive(run, index, a, b, low, count):
        k = run * 20 + index
        arrive(unit(*node(run, a, b), run * 8 + low, count), g_send.at[k], g_recv.at[k])

    def to_sibling(run, u, v, a, b):
        k = run * 16 + u * 4 + v
        ref = unit(*node(run, a, b), run * 8, 8)
        push(ref, ref, s_send.at[k], s_recv.at[k], place(x, y, 1 - core))

    def across(run, u, a, b):
        shipment(run, 4 + 4 * u, a, b, 0, 8, first[run], ring(b + 1, 4))
        shipment(run, 5 + 4 * u, a, b, 0, 8, first[run], ring(b - 1, 4))

    for run in range(2):
        a, b = first[run], second[run]
        if run == 1:
            take(1)
            take(-1)
            far_bias()
        shipment(run, 0, a, b, 0, 8, ring(a + 1, 4), b)
        shipment(run, 1, a, b, 0, 8, ring(a - 1, 4), b)
        across(run, 0, a, b)
        to_sibling(run, 0, 0, a, b)
        if run == 0:
            col_push(2)
            col_push(6)
    for step in (3, 5, 4):
        col_push(step)
    for run in range(2):
        a, b = first[run], second[run]
        receive(run, 0, ring(a - 1, 4), b, 0, 8)
        shipment(run, 2, ring(a - 1, 4), b, 0, 4, ring(a + 1, 4), b)
        receive(run, 1, ring(a + 1, 4), b, 0, 8)
        shipment(run, 3, ring(a + 1, 4), b, 4, 4, ring(a - 1, 4), b)
    for run in range(2):
        a, b = first[run], second[run]
        across(run, 1, ring(a - 1, 4), b)
        to_sibling(run, 1, 0, ring(a - 1, 4), b)
        across(run, 2, ring(a + 1, 4), b)
        to_sibling(run, 2, 0, ring(a + 1, 4), b)
    for run in range(2):
        a, b = first[run], second[run]
        receive(run, 2, ring(a + 2, 4), b, 0, 4)
        receive(run, 3, ring(a + 2, 4), b, 4, 4)
        across(run, 3, ring(a + 2, 4), b)
        to_sibling(run, 3, 0, ring(a + 2, 4), b)
    take(2)
    for u in range(4):
        for run in range(2):
            a, b = ring(first[run] + (0, -1, 1, 2)[u], 4), second[run]
            receive(run, 4 + 4 * u, a, ring(b - 1, 4), 0, 8)
            shipment(run, 6 + 4 * u, a, ring(b - 1, 4), 0, 4, first[run], ring(b + 1, 4))
            to_sibling(run, u, 1, a, ring(b - 1, 4))
            receive(run, 5 + 4 * u, a, ring(b + 1, 4), 0, 8)
            shipment(run, 7 + 4 * u, a, ring(b + 1, 4), 4, 4, first[run], ring(b - 1, 4))
            to_sibling(run, u, 2, a, ring(b + 1, 4))
        if u == 1:
            take(-2)
        if u == 3:
            take(3)
    for u in range(4):
        for run in range(2):
            a, b = ring(first[run] + (0, -1, 1, 2)[u], 4), second[run]
            receive(run, 6 + 4 * u, a, ring(b + 2, 4), 0, 4)
            receive(run, 7 + 4 * u, a, ring(b + 2, 4), 4, 4)
            to_sibling(run, u, 3, a, ring(b + 2, 4))
        if u == 3:
            take(-3)
    take(4)
    bound_ref[0:8, :] = tops[...]
    bound_ref[8:24, :] = jnp.broadcast_to(jnp.sum(weighted * weighted, axis=1, keepdims=True), (16, 128))
    for run in range(2):
        for u in range(4):
            for v in range(4):
                a = ring(first[run] + (0, -1, 1, 2)[u], 4)
                b = ring(second[run] + (0, -1, 1, 2)[v], 4)
                k = run * 16 + u * 4 + v
                arrive(unit(*node(run, a, b), run * 8, 8, 1 - core), s_send.at[k], s_recv.at[k])
    for copy in sent:
        copy.wait_send()


def spread(*operands):
    whole = pl.BlockSpec(memory_space=VMEM)
    return pl.pallas_call(
        spread_kernel,
        out_shape=(
            jax.ShapeDtypeStruct((2, 4, 1024, 128), BF16),
            jax.ShapeDtypeStruct((4, 16, 128, 256), BF16),
            jax.ShapeDtypeStruct((4, 16, 256, 128), BF16),
            jax.ShapeDtypeStruct((2, 2, 4, 2, 2, 8, 32, 256), BF16),
            jax.ShapeDtypeStruct((24, 128), F32),
            jax.ShapeDtypeStruct((128, 128), BF16),
            jax.ShapeDtypeStruct((8, 128), jnp.int32),
        ),
        in_specs=[pl.BlockSpec(memory_space=pltpu.HBM)] * len(operands),
        out_specs=(whole,) * 7,
        scratch_shapes=[
            VMEM((128, 32, 128), BF16),
            VMEM((1, 128), F32),
            VMEM((2, 128), BF16),
            VMEM((8, 128), jnp.int32),
            VMEM((128, 128), BF16),
            VMEM((16, 16), jnp.int32),
            VMEM((4096, 128), F32),
            VMEM((8, 4, 128, 128), BF16),
            VMEM((4, 1024, 128), BF16),
            VMEM((2, 272, 128), BF16),
            VMEM((512, 128), BF16),
            VMEM((256, 128), F32),
            VMEM((2, 32, 256), BF16),
            VMEM((8, 128), F32),
            DMA((10,)), DMA((8,)), DMA((8,)), DMA((8,)), DMA((8,)), DMA, DMA,
            DMA((40,)), DMA((40,)), DMA((32,)), DMA((32,)), DMA((2,)),
        ],
        compiler_params=pltpu.CompilerParams(
            collective_id=0, has_side_effects=True, vmem_limit_bytes=32 * 1024 * 1024
        ),
        name="spread",
    )(*operands)


def attend_kernel(
    lists_ref, qg_ref, kbd, vbd, bias, bound_ref, mixing_ref,
    update_ref,
    acc0, acc1, acc2, acc3, peak,
):
    accs = (acc0, acc1, acc2, acc3)
    for acc in accs:
        acc[...] = jnp.zeros_like(acc)
    same = (
        lax.div(lax.broadcasted_iota(jnp.int32, (256, 128), 0), 64)
        == lax.div(lax.broadcasted_iota(jnp.int32, (256, 128), 1), 32)
    ).astype(F32).astype(BF16)

    reach = jnp.sqrt(jnp.max(bound_ref[0:1, :])) * jnp.sqrt(jnp.max(bound_ref[1:2, :]))
    bias_reach = jnp.sqrt(jnp.max(bound_ref[8:24, :])) * (math.sqrt(128) * LOG2E)
    safe = (reach + bias_reach) * 1.03 <= SAFE

    def query(j, i):
        return qg_ref[0, j, pl.ds(pl.multiple_of(jnp.minimum(i, 15) * 64, 64), 64), :]

    def values_of(j, block):
        return jnp.concatenate([vbd[j, block], same], axis=1)

    def offset_of(i, block):
        at = (lax.div(block, 8), jnp.minimum(i, 15))
        n = lax.rem(block, 8)
        return [bias[at[0], at[1], half, n].astype(F32) for half in range(2)]

    total_pairs = lists_ref[3, 0]

    @pl.when(safe)
    def _():
        def step(t, carry):
            work = []
            for side in range(2):
                e = 2 * t + side
                block = lists_ref[0, e]
                ids = (lists_ref[1, e], lists_ref[2, e])
                offset = jnp.concatenate(offset_of(ids[0], block) + offset_of(ids[1], block), axis=0)
                work.append((block, ids, offset))
            for j in range(4):
                for block, ids, offset in work:
                    queries = jnp.concatenate([query(j, i) for i in ids], axis=0)
                    score = jnp.dot(queries, kbd[j, block], preferred_element_type=F32)
                    weights = jnp.exp2(score + offset).astype(BF16)
                    total = jnp.dot(weights, values_of(j, block), preferred_element_type=F32)
                    olds = [accs[j][i] for i in ids]
                    for n in range(2):
                        accs[j][ids[n]] = olds[n] + total[n * 64:(n + 1) * 64, :]
            return carry

        lax.fori_loop(0, lax.div(total_pairs + 1, 2), step, 0)

    @pl.when(jnp.logical_not(safe))
    def _():
        peak[...] = jnp.full_like(peak, -1e30)

        def step(n, carry):
            e = lax.div(n, 2)
            block = lists_ref[0, e]
            i = lists_ref[1 + lax.rem(n, 2), e]
            offset = jnp.concatenate(offset_of(i, block), axis=0)
            for j in range(4):
                score = jnp.dot(query(j, i), kbd[j, block], preferred_element_type=F32) + offset
                old = peak[j, i]
                tops = [
                    jnp.maximum(
                        jnp.max(score[:, h * 64:(h + 1) * 64], axis=1, keepdims=True),
                        old[:, h * 32:h * 32 + 1],
                    )
                    for h in range(4)
                ]
                shift = jnp.concatenate([jnp.broadcast_to(top, (64, 64)) for top in tops], axis=1)
                fresh = jnp.concatenate([jnp.broadcast_to(top, (64, 32)) for top in tops], axis=1)
                decay = jnp.exp2(old - fresh)
                weights = jnp.exp2(score - shift).astype(BF16)
                total = jnp.dot(weights, values_of(j, block), preferred_element_type=F32)
                accs[j][i] = accs[j][i] * jnp.concatenate([decay, decay], axis=1) + total
                peak[j, i] = fresh
            return carry

        lax.fori_loop(0, 2 * total_pairs, step, 0)

    def finish(target, carry):
        rows = pl.ds(pl.multiple_of(target * 128, 128), 128)
        for j in range(4):
            sums = accs[j][pl.ds(target * 2, 2)].reshape(128, 256)
            attention = sums[:, :128] / sums[:, 128:]
            gated = (attention * qg_ref[1, j, rows, :].astype(F32)).astype(BF16)
            update = lax.dot_general(mixing_ref[...], gated, NT, preferred_element_type=F32).astype(BF16)
            update_ref[0, target, j] = update[:64, :]
            update_ref[1, target, j] = update[64:, :]
        return carry

    lax.fori_loop(0, 8, finish, 0, unroll=2)


def attend(lists, qg, kbd, vbd, bias, bound, mixing):
    whole = pl.BlockSpec(memory_space=VMEM)
    return pl.pallas_call(
        attend_kernel,
        out_shape=jax.ShapeDtypeStruct((2, 8, 4, 64, 128), BF16),
        in_specs=[pl.BlockSpec(memory_space=pltpu.SMEM)] + [whole] * 6,
        out_specs=whole,
        scratch_shapes=[VMEM((18, 64, 256), F32)] * 4 + [VMEM((4, 18, 64, 128), F32)],
        compiler_params=pltpu.CompilerParams(vmem_limit_bytes=24 * 1024 * 1024),
        name="attend",
    )(lists, qg, kbd, vbd, bias, bound, mixing)


def deliver_kernel(update_ref, out_ref, send_sem, recv_sem, own_sem):
    row = lax.axis_index("row")
    col = lax.axis_index("col")
    head = lax.axis_index("head")

    def other(flip):
        return (1 - head) if flip else head

    def device(step, flip):
        return (ring(row + step, 8), col, other(flip))

    moves = [(step, flip) for step in (4, 3, 5, 2, 6, 1, 7) for flip in (1, 0)] + [(0, 1)]
    barrier = pltpu.get_barrier_semaphore()
    for step, flip in moves:
        pl.semaphore_signal(barrier, inc=1, device_id=device(step, flip), device_id_type=MESH)

    def spot(step, flip):
        return out_ref.at[pl.ds((other(flip) * 8 + ring(row + step, 8)) * 4, 4)]

    def part(step, flip):
        return update_ref.at[other(flip), ring(row + step, 8)]

    own = pltpu.make_async_copy(part(0, 0), spot(0, 0), own_sem)
    own.start()
    pl.semaphore_wait(barrier, len(moves))
    copies = []
    for step, flip in moves:
        k = flip * 8 + step
        copy = pltpu.make_async_remote_copy(
            src_ref=part(step, flip), dst_ref=spot(0, 0),
            send_sem=send_sem.at[k], recv_sem=recv_sem.at[k],
            device_id=device(step, flip), device_id_type=MESH,
        )
        copy.start()
        copies.append(copy)
    own.wait()
    for step, flip in moves:
        k = flip * 8 + step
        pltpu.make_async_remote_copy(
            src_ref=spot(-step, flip), dst_ref=spot(-step, flip),
            send_sem=send_sem.at[k], recv_sem=recv_sem.at[k],
            device_id=device(step, flip), device_id_type=MESH,
        ).wait_recv()
    for copy in copies:
        copy.wait_send()


def deliver(update):
    whole = pl.BlockSpec(memory_space=VMEM)
    return pl.pallas_call(
        deliver_kernel,
        out_shape=jax.ShapeDtypeStruct((64, 64, 128), BF16),
        in_specs=[whole],
        out_specs=whole,
        scratch_shapes=[DMA((16,)), DMA((16,)), DMA],
        compiler_params=pltpu.CompilerParams(
            collective_id=1, has_side_effects=True, vmem_limit_bytes=16 * 1024 * 1024
        ),
        name="deliver",
    )(update)


def per_device(
    pair_field, ln_gain, w_query, w_key, w_value, w_gate, w_bias, w_out, tile_mask, type_ids
):
    weights = [w.T for w in (w_query, w_key, w_value, w_gate)]
    weights.append(w_bias.T)
    operands = (pair_field, ln_gain.reshape(1, 128), *weights, type_ids.reshape(8, 128), w_out, tile_mask)
    qg, kbd, vbd, bias, bound, mixing, lists = spread(
        *[pltpu.with_memory_space_constraint(operand, pltpu.HBM) for operand in operands]
    )
    update = attend(lists, qg, kbd, vbd, bias.reshape(2, 16, 2, 8, 32, 256), bound, mixing)
    return jnp.transpose(deliver(update), (2, 0, 1))


def solution(mesh):
    return jax.shard_map(
        per_device,
        mesh=mesh,
        in_specs=(
            P("row", "col", None),
            P(),
            P(None, "head"),
            P(None, "head"),
            P(None, "head"),
            P(None, "head"),
            P(None, "head"),
            P(),
            P(),
            P(),
        ),
        out_specs=P("row", "col", "head"),
        check_vma=False,
    )
```

```python
import math

import jax
import jax.numpy as jnp
from jax import lax
from jax.experimental import pallas as pl
from jax.experimental.pallas import tpu as pltpu
from jax.sharding import PartitionSpec as P

MESH = pl.DeviceIdType.MESH
F32 = jnp.float32
BF16 = jnp.bfloat16
VMEM = pltpu.VMEM
DMA = pltpu.SemaphoreType.DMA

epsilon = 1e-05
masked_score = -1000000000.0
LOG2E = math.log2(math.e)
SCALE = LOG2E / math.sqrt(32)
SAFE = 64.0
NT = (((1,), (1,)), ((), ()))


def ring(value, size):
    return lax.rem(value + size, size)


def spread_kernel(
    tile_ref, gain_in, wq_ref, wk_ref, wv_ref, wg_ref, wb_in, types_in, w_out_in, mask_in,
    qg_ref, kbd_ref, vbd_ref, bias_ref, bound_ref, mixing_ref, lists_ref,
    half, gain_ref, wb_ref, types_ref, w_out_ref, mask_ref, wide, send, strip, wbuf, wall, flat, bsend, tops,
    load_sem, col_send, col_recv, z_send, z_recv, w_send, w_recv,
    g_send, g_recv, s_send, s_recv, own_sem,
):
    row = lax.axis_index("row")
    col = lax.axis_index("col")
    head = lax.axis_index("head")
    core = lax.rem(col, 2)
    x = lax.rem(lax.div(col, 2), 4)
    y = head * 2 + lax.div(col, 8)

    def place(x_, y_, core_=None):
        return (row, lax.rem(y_, 2) * 8 + x_ * 2 + (core if core_ is None else core_), lax.div(y_, 2))

    def along_z(step):
        return (ring(row + step, 8), col, head)

    partner = place(x, ring(y + 2, 4))
    peers = [along_z(step) for step in range(1, 8)]
    peers += [place(ring(x + 1, 4), y), place(ring(x - 1, 4), y)]
    peers += [place(x, ring(y + 1, 4)), place(x, ring(y - 1, 4)), partner]
    peers += [place(x, y, 1 - core)]
    barrier = pltpu.get_barrier_semaphore()
    for peer in peers:
        pl.semaphore_signal(barrier, inc=1, device_id=peer, device_id_type=MESH)

    loads = [
        (tile_ref.at[:, pl.ds(pl.multiple_of(head * 32, 32), 32), :], half),
        (gain_in, gain_ref), (wb_in, wb_ref), (types_in, types_ref),
    ]
    loads += [
        (ref, wbuf.at[head, pl.ds(kind * 64, 64)]) for kind, ref in enumerate((wq_ref, wk_ref, wv_ref, wg_ref))
    ]
    loads += [(w_out_in, w_out_ref), (mask_in, mask_ref)]
    loads = [pltpu.make_async_copy(src, dst, load_sem.at[n]) for n, (src, dst) in enumerate(loads)]
    for load in loads:
        load.start()
    tops[...] = jnp.zeros_like(tops)
    loads[0].wait()

    def widen(block, carry):
        rows = half[pl.ds(block * 8, 8)].astype(F32).reshape(256, 128)
        wide[pl.ds(pl.multiple_of(block * 256, 256), 256), :] = rows
        return carry

    lax.fori_loop(0, 16, widen, 0)
    ones = jnp.ones((128, 128), BF16)
    loads[1].wait()
    gain = gain_ref[...]

    def norm_for(step):
        target = ring(row + step, 8)
        for jj in range(4):
            value = wide[pl.ds(4 * target + jj, 128, stride=32), :]
            mean = jnp.dot(value.astype(BF16), ones, preferred_element_type=F32) * (1.0 / 128)
            centred = value - mean
            squares = (centred * centred).astype(BF16)
            spread = jnp.dot(squares, ones, preferred_element_type=F32) * (1.0 / 128)
            normed = centred * lax.rsqrt(spread + epsilon) * gain
            send[target, jj] = normed.astype(BF16)

    def norm_near(n, carry):
        norm_for(n)
        norm_for(-n)
        return carry

    def norm_far(n, carry):
        norm_for(3 + n)
        norm_for(-3 * (1 - n))
        return carry

    lax.fori_loop(1, 3, norm_near, 0)
    for load in loads[2:]:
        load.wait()
    wbuf[head, 256:272, :] = jnp.concatenate(
        [wb_ref[...].astype(F32), jnp.zeros((14, 128), F32)], axis=0
    ).astype(BF16)
    pl.semaphore_wait(barrier, len(peers))
    w_copy = pltpu.make_async_remote_copy(
        src_ref=wbuf.at[head], dst_ref=wbuf.at[head], send_sem=w_send, recv_sem=w_recv,
        device_id=partner, device_id_type=MESH,
    )
    w_copy.start()
    sent = [w_copy]

    def push(src, dst, send_sem, recv_sem, device):
        copy = pltpu.make_async_remote_copy(
            src_ref=src, dst_ref=dst, send_sem=send_sem, recv_sem=recv_sem,
            device_id=device, device_id_type=MESH,
        )
        copy.start()
        sent.append(copy)

    def strip_rows(step):
        source = ring(row + step, 8)
        return strip.at[:, pl.ds(pl.multiple_of(source * 128, 128), 128), :]

    def col_push(step):
        target = ring(row + step, 8)
        push(send.at[target], strip_rows(0), col_send.at[step], col_recv.at[step], along_z(step))

    col_push(1)
    col_push(7)
    lax.fori_loop(0, 2, norm_far, 0)
    pltpu.make_async_remote_copy(
        src_ref=wbuf.at[1 - head], dst_ref=wbuf.at[1 - head], send_sem=w_send, recv_sem=w_recv,
        device_id=partner, device_id_type=MESH,
    ).wait_recv()

    wb = wbuf[0, 256:272, :].astype(F32) + pltpu.roll(wbuf[1, 256:272, :].astype(F32), 2, 0)
    weighted = wb * gain
    wbt = wb.astype(BF16)

    def bias_for(target, carry):
        part = lax.dot_general(wbt, send[target].reshape(512, 128), NT, preferred_element_type=F32)
        for jj in range(4):
            flat[pl.ds(pl.multiple_of((4 * target + jj) * 8, 8), 8), :] = part[0:8, jj * 128:jj * 128 + 128]
        return carry

    lax.fori_loop(0, 8, bias_for, 0, unroll=4)
    living = jnp.broadcast_to(types_ref[pl.ds(row, 1), :] != 0, (32, 128))
    by_head = [
        jnp.where(living, flat[pl.ds(h, 32, stride=8), :] * LOG2E, masked_score) for h in range(4)
    ]
    bsend[0] = jnp.concatenate([b[:, :64] for b in by_head], axis=1).astype(BF16)
    bsend[1] = jnp.concatenate([b[:, 64:] for b in by_head], axis=1).astype(BF16)

    def unit(x_, y_, run, low, count, core_=None):
        return bias_ref.at[
            run, lax.rem(y_, 2), x_, core if core_ is None else core_, lax.div(y_, 2), pl.ds(low, count)
        ]

    def arrive(dst, send_sem, recv_sem):
        pltpu.make_async_remote_copy(
            src_ref=dst, dst_ref=dst, send_sem=send_sem, recv_sem=recv_sem,
            device_id=partner, device_id_type=MESH,
        ).wait_recv()

    def slot(step):
        return 2 * step - 1 if step > 0 else -2 * step

    spans = ((0, 2, 5), (5, 7, 8))

    def chunk(step, low=0, count=2):
        return bias_ref.at[pl.ds(low, count), lax.rem(y, 2), x, core, lax.div(y, 2), slot(step)]

    def z_push(k, src, dst, step):
        push(src, dst, z_send.at[k], z_recv.at[k], along_z(step))

    def z_arrive(k, dst):
        arrive(dst, z_send.at[k], z_recv.at[k])

    own = pltpu.make_async_copy(bsend, chunk(0), own_sem.at[0])
    own.start()
    for k, step in enumerate((2, -2, 1, -1)):
        z_push(k, bsend, chunk(-step), step)

    own_cols = pltpu.make_async_copy(send.at[row], strip_rows(0), own_sem.at[1])
    own_cols.start()

    for kind, place_of in enumerate((1, 0, 2, 3)):
        for s in range(2):
            wall[place_of * 128 + s * 64:place_of * 128 + s * 64 + 64, :] = wbuf[s, kind * 64:kind * 64 + 64, :]
    together = (
        lax.div(lax.broadcasted_iota(jnp.int32, (128, 128), 0), 32)
        == lax.div(lax.broadcasted_iota(jnp.int32, (128, 128), 1), 32)
    ).astype(F32).astype(BF16)

    key_head = lax.div(lax.broadcasted_iota(jnp.int32, (128, 128), 0), 32)
    side_of = lax.div(lax.broadcasted_iota(jnp.int32, (128, 128), 1), 64)
    key_here = [(key_head == 2 * n + side_of).astype(F32).astype(BF16) for n in range(2)]
    lane_head = lax.div(lax.broadcasted_iota(jnp.int32, (64, 128), 1), 32)
    value_here = [(lane_head == h).astype(F32).astype(BF16) for h in range(4)]

    def project(step):
        source = ring(row + step, 8)
        first_block = 2 * slot(step)
        rows = pl.ds(pl.multiple_of(source * 128, 128), 128)

        def one(jj, carry):
            value = strip[jj, rows, :]
            keys = lax.dot_general(wall[0:128, :], value, NT, preferred_element_type=F32)
            left = lax.dot_general(value, wall[128:256, :], NT, preferred_element_type=F32)
            right = lax.dot_general(value, wall[256:512, :], NT, preferred_element_type=F32)
            query = left * SCALE
            qg_ref[0, jj, rows, :] = query.astype(BF16)
            qg_ref[1, jj, rows, :] = jax.nn.sigmoid(right[:, 128:]).astype(BF16)
            short = keys.astype(BF16)
            values = right[:, :128].astype(BF16)
            for odd in range(2):
                twice = jnp.concatenate([short[:, odd * 64:odd * 64 + 64]] * 2, axis=1)
                for n in range(2):
                    kbd_ref[jj, first_block + odd, :, n * 128:(n + 1) * 128] = twice * key_here[n]
                for h in range(4):
                    vbd_ref[jj, first_block + odd, h * 64:(h + 1) * 64, :] = (
                        values[odd * 64:odd * 64 + 64, :] * value_here[h]
                    )
            lengths = jnp.dot((query * query).astype(BF16), together, preferred_element_type=F32)
            tops[0:1, :] = jnp.maximum(tops[0:1, :], jnp.max(lengths, axis=0, keepdims=True))
            lengths = jnp.dot(together, (keys * keys).astype(BF16), preferred_element_type=F32)
            tops[1:2, :] = jnp.maximum(tops[1:2, :], jnp.max(lengths, axis=0, keepdims=True))
            return carry

        lax.fori_loop(0, 4, one, 0, unroll=True)

    def take(step):
        arrive(strip_rows(step), col_send.at[(8 - step) % 8], col_recv.at[(8 - step) % 8])
        project(step)

    def make_lists():
        mixing_ref[...] = w_out_ref[...].astype(F32).T.astype(BF16)
        part = mask_ref[...].astype(F32)
        place_ = lax.div(lax.broadcasted_iota(jnp.int32, (16, 128), 1), 2)
        away = lax.div(place_ + 1, 2) * (2 * lax.rem(place_, 2) - 1)
        there = 2 * lax.rem(row + away + 8, 8) + lax.rem(lax.broadcasted_iota(jnp.int32, (16, 128), 1), 2)
        inside = lax.broadcasted_iota(jnp.int32, (16, 128), 1) < 16
        turned = (inside & (lax.broadcasted_iota(jnp.int32, (16, 128), 0) == there)).astype(F32).astype(BF16)
        diagonal = lax.broadcasted_iota(jnp.int32, (16, 16), 0) == lax.broadcasted_iota(jnp.int32, (16, 16), 1)
        part = jnp.where((part == 1.0) | diagonal, 1.0, 0.0)
        allowed = jnp.dot(part.astype(BF16), turned, preferred_element_type=F32)
        before = [jnp.zeros((1, 128), F32)]
        for i in range(16):
            before.append(before[-1] + allowed[i:i + 1, :])
        rank = jnp.concatenate(before[:16], axis=0)
        pairs = jnp.broadcast_to(jnp.floor((before[16] + 1.0) * 0.5), (16, 128))
        earlier = (
            lax.broadcasted_iota(jnp.int32, (128, 128), 0) < lax.broadcasted_iota(jnp.int32, (128, 128), 1)
        ).astype(F32).astype(BF16)
        start = jnp.dot(pairs.astype(BF16), earlier, preferred_element_type=F32)
        total = jnp.sum(pairs[0:1, :], axis=1, keepdims=True)
        rank = rank + 2.0 * start
        entry = 2.0 * lax.broadcasted_iota(jnp.int32, (16, 128), 1).astype(F32)
        number = lax.broadcasted_iota(jnp.int32, (16, 128), 0).astype(F32)
        block = jnp.zeros((16, 128), F32)
        picked = [jnp.zeros((16, 128), F32)] * 2
        found = [jnp.zeros((16, 128), F32)] * 2
        for k in range(16):
            at = jnp.broadcast_to(rank[:, k:k + 1], (16, 128))
            here = jnp.broadcast_to(allowed[:, k:k + 1], (16, 128))
            for side in range(2):
                hit = jnp.where(at == entry + side, here, 0.0)
                found[side] = found[side] + hit
                picked[side] = picked[side] + hit * number
                if side == 0:
                    block = block + hit * k
        rows = [jnp.sum(block, axis=0, keepdims=True)]
        for side in range(2):
            missing = 1.0 - jnp.sum(found[side], axis=0, keepdims=True)
            rows.append(jnp.sum(picked[side], axis=0, keepdims=True) + (16.0 + side) * missing)
        rows.append(jnp.broadcast_to(total, (1, 128)))
        rows.append(jnp.zeros((4, 128), F32))
        lists_ref[...] = jnp.concatenate(rows, axis=0).astype(jnp.int32)

    own_cols.wait()
    project(0)
    make_lists()
    own.wait()
    for k, step in enumerate((-2, 2, -1, 1)):
        z_arrive(k, chunk(step))
    z_push(4, chunk(-2), chunk(-3), 1)
    z_push(5, chunk(2), chunk(3), -1)
    z_push(6, chunk(-2, 0, 1), chunk(4, 0, 1), 2)
    z_push(7, chunk(2, 1, 1), chunk(4, 1, 1), -2)

    def far_bias():
        z_arrive(4, chunk(-3))
        z_arrive(5, chunk(3))
        z_arrive(6, chunk(4, 0, 1))
        z_arrive(7, chunk(4, 1, 1))

    def node(run, a, b):
        return (a, b) if run == 0 else (b, a)

    first = (x, y)
    second = (y, x)

    def whole_of(span):
        return span[0], span[2] - span[0]

    def halves_of(span):
        return (span[0], span[1] - span[0]), (span[1], span[2] - span[1])

    def shipment(far, run, index, a, b, rows, to_a, to_b):
        k = far * 40 + run * 20 + index
        ref = unit(*node(run, a, b), run, *rows)
        push(ref, ref, g_send.at[k], g_recv.at[k], place(*node(run, to_a, to_b)))

    def receive(far, run, index, a, b, rows):
        k = far * 40 + run * 20 + index
        arrive(unit(*node(run, a, b), run, *rows), g_send.at[k], g_recv.at[k])

    def to_sibling(run, u, v):
        k = run * 16 + u * 4 + v
        a, b = ring(first[run] + (0, -1, 1, 2)[u], 4), ring(second[run] + (0, -1, 1, 2)[v], 4)
        ref = unit(*node(run, a, b), run, 0, 8)
        push(ref, ref, s_send.at[k], s_recv.at[k], place(x, y, 1 - core))

    def begin(far, run):
        a, b, rows = first[run], second[run], whole_of(spans[far])
        shipment(far, run, 0, a, b, rows, ring(a + 1, 4), b)
        shipment(far, run, 1, a, b, rows, ring(a - 1, 4), b)

    def across(far, run, u):
        a, b, rows = ring(first[run] + (0, -1, 1, 2)[u], 4), second[run], whole_of(spans[far])
        shipment(far, run, 4 + 4 * u, a, b, rows, first[run], ring(b + 1, 4))
        shipment(far, run, 5 + 4 * u, a, b, rows, first[run], ring(b - 1, 4))

    def pass_first(far, run):
        a, b, rows = first[run], second[run], whole_of(spans[far])
        low, high = halves_of(spans[far])
        receive(far, run, 0, ring(a - 1, 4), b, rows)
        shipment(far, run, 2, ring(a - 1, 4), b, low, ring(a + 1, 4), b)
        receive(far, run, 1, ring(a + 1, 4), b, rows)
        shipment(far, run, 3, ring(a + 1, 4), b, high, ring(a - 1, 4), b)

    def end_first(far, run):
        a, b = ring(first[run] + 2, 4), second[run]
        low, high = halves_of(spans[far])
        receive(far, run, 2, a, b, low)
        receive(far, run, 3, a, b, high)

    def pass_second(far, run, u):
        a, b, rows = ring(first[run] + (0, -1, 1, 2)[u], 4), second[run], whole_of(spans[far])
        low, high = halves_of(spans[far])
        receive(far, run, 4 + 4 * u, a, ring(b - 1, 4), rows)
        shipment(far, run, 6 + 4 * u, a, ring(b - 1, 4), low, first[run], ring(b + 1, 4))
        receive(far, run, 5 + 4 * u, a, ring(b + 1, 4), rows)
        shipment(far, run, 7 + 4 * u, a, ring(b + 1, 4), high, first[run], ring(b - 1, 4))

    def end_second(far, run, u):
        a, b = ring(first[run] + (0, -1, 1, 2)[u], 4), ring(second[run] + 2, 4)
        low, high = halves_of(spans[far])
        receive(far, run, 6 + 4 * u, a, b, low)
        receive(far, run, 7 + 4 * u, a, b, high)

    for run in range(2):
        begin(0, run)
    for run in range(2):
        across(0, run, 0)
    for step in (2, 6, 3, 5, 4):
        col_push(step)
    take(1)
    take(-1)
    far_bias()
    for run in range(2):
        begin(1, run)
    for run in range(2):
        across(1, run, 0)
    for run in range(2):
        to_sibling(run, 0, 0)
    for far in range(2):
        for run in range(2):
            pass_first(far, run)
        for run in range(2):
            across(far, run, 1)
            across(far, run, 2)
    for run in range(2):
        to_sibling(run, 1, 0)
        to_sibling(run, 2, 0)
    for far in range(2):
        for run in range(2):
            end_first(far, run)
            across(far, run, 3)
    for run in range(2):
        to_sibling(run, 3, 0)
    take(2)
    for u in range(4):
        for far in range(2):
            for run in range(2):
                pass_second(far, run, u)
        for run in range(2):
            to_sibling(run, u, 1)
            to_sibling(run, u, 2)
        if u == 1:
            take(-2)
        if u == 3:
            take(3)
    for u in range(4):
        for run in range(2):
            for far in range(2):
                end_second(far, run, u)
            to_sibling(run, u, 3)
        if u == 2:
            take(-3)
    take(4)
    bound_ref[0:8, :] = tops[...]
    bound_ref[8:24, :] = jnp.broadcast_to(jnp.sum(weighted * weighted, axis=1, keepdims=True), (16, 128))
    for run in range(2):
        for u in range(4):
            for v in range(4):
                a = ring(first[run] + (0, -1, 1, 2)[u], 4)
                b = ring(second[run] + (0, -1, 1, 2)[v], 4)
                k = run * 16 + u * 4 + v
                arrive(unit(*node(run, a, b), run, 0, 8, 1 - core), s_send.at[k], s_recv.at[k])
    for copy in sent:
        copy.wait_send()


def spread(*operands):
    whole = pl.BlockSpec(memory_space=VMEM)
    return pl.pallas_call(
        spread_kernel,
        out_shape=(
            jax.ShapeDtypeStruct((2, 4, 1024, 128), BF16),
            jax.ShapeDtypeStruct((4, 16, 128, 256), BF16),
            jax.ShapeDtypeStruct((4, 16, 256, 128), BF16),
            jax.ShapeDtypeStruct((2, 2, 4, 2, 2, 8, 32, 256), BF16),
            jax.ShapeDtypeStruct((24, 128), F32),
            jax.ShapeDtypeStruct((128, 128), BF16),
            jax.ShapeDtypeStruct((8, 128), jnp.int32),
        ),
        in_specs=[pl.BlockSpec(memory_space=pltpu.HBM)] * len(operands),
        out_specs=(whole,) * 7,
        scratch_shapes=[
            VMEM((128, 32, 128), BF16),
            VMEM((1, 128), F32),
            VMEM((2, 128), BF16),
            VMEM((8, 128), jnp.int32),
            VMEM((128, 128), BF16),
            VMEM((16, 16), jnp.int32),
            VMEM((4096, 128), F32),
            VMEM((8, 4, 128, 128), BF16),
            VMEM((4, 1024, 128), BF16),
            VMEM((2, 272, 128), BF16),
            VMEM((512, 128), BF16),
            VMEM((256, 128), F32),
            VMEM((2, 32, 256), BF16),
            VMEM((8, 128), F32),
            DMA((10,)), DMA((8,)), DMA((8,)), DMA((8,)), DMA((8,)), DMA, DMA,
            DMA((80,)), DMA((80,)), DMA((32,)), DMA((32,)), DMA((2,)),
        ],
        compiler_params=pltpu.CompilerParams(
            collective_id=0, has_side_effects=True, vmem_limit_bytes=32 * 1024 * 1024
        ),
        name="spread",
    )(*operands)


def attend_kernel(
    lists_ref, qg_ref, kbd, vbd, bias, bound_ref,
    acc0, acc1, acc2, acc3,
    peak,
):
    accs = (acc0, acc1, acc2, acc3)
    for acc in accs:
        acc[...] = jnp.zeros_like(acc)
    same = (
        lax.div(lax.broadcasted_iota(jnp.int32, (256, 128), 0), 64)
        == lax.div(lax.broadcasted_iota(jnp.int32, (256, 128), 1), 32)
    ).astype(F32).astype(BF16)

    reach = jnp.sqrt(jnp.max(bound_ref[0:1, :])) * jnp.sqrt(jnp.max(bound_ref[1:2, :]))
    bias_reach = jnp.sqrt(jnp.max(bound_ref[8:24, :])) * (math.sqrt(128) * LOG2E)
    safe = (reach + bias_reach) * 1.03 <= SAFE

    def query(j, i):
        return qg_ref[0, j, pl.ds(pl.multiple_of(jnp.minimum(i, 15) * 64, 64), 64), :]

    def values_of(j, block):
        return jnp.concatenate([vbd[j, block], same], axis=1)

    def offset_of(i, block):
        at = (lax.rem(block, 2), jnp.minimum(i, 15))
        n = lax.div(block, 2)
        return [bias[at[0], at[1], half, n].astype(F32) for half in range(2)]

    total_pairs = lists_ref[3, 0]

    @pl.when(safe)
    def _():
        def step(t, carry):
            work = []
            for side in range(2):
                e = 2 * t + side
                block = lists_ref[0, e]
                ids = (lists_ref[1, e], lists_ref[2, e])
                offset = jnp.concatenate(offset_of(ids[0], block) + offset_of(ids[1], block), axis=0)
                work.append((block, ids, offset))
            for j in range(4):
                for block, ids, offset in work:
                    queries = jnp.concatenate([query(j, i) for i in ids], axis=0)
                    score = jnp.dot(queries, kbd[j, block], preferred_element_type=F32)
                    weights = jnp.exp2(score + offset).astype(BF16)
                    total = jnp.dot(weights, values_of(j, block), preferred_element_type=F32)
                    olds = [accs[j][i] for i in ids]
                    for n in range(2):
                        accs[j][ids[n]] = olds[n] + total[n * 64:(n + 1) * 64, :]
            return carry

        lax.fori_loop(0, lax.div(total_pairs + 1, 2), step, 0)

    @pl.when(jnp.logical_not(safe))
    def _():
        peak[...] = jnp.full_like(peak, -1e30)

        def step(n, carry):
            e = lax.div(n, 2)
            block = lists_ref[0, e]
            i = lists_ref[1 + lax.rem(n, 2), e]
            offset = jnp.concatenate(offset_of(i, block), axis=0)
            for j in range(4):
                score = jnp.dot(query(j, i), kbd[j, block], preferred_element_type=F32) + offset
                old = peak[j, i]
                tops = [
                    jnp.maximum(
                        jnp.max(score[:, h * 64:(h + 1) * 64], axis=1, keepdims=True),
                        old[:, h * 32:h * 32 + 1],
                    )
                    for h in range(4)
                ]
                shift = jnp.concatenate([jnp.broadcast_to(top, (64, 64)) for top in tops], axis=1)
                fresh = jnp.concatenate([jnp.broadcast_to(top, (64, 32)) for top in tops], axis=1)
                decay = jnp.exp2(old - fresh)
                weights = jnp.exp2(score - shift).astype(BF16)
                total = jnp.dot(weights, values_of(j, block), preferred_element_type=F32)
                accs[j][i] = accs[j][i] * jnp.concatenate([decay, decay], axis=1) + total
                peak[j, i] = fresh
            return carry

        lax.fori_loop(0, 2 * total_pairs, step, 0)


def attend(lists, qg, kbd, vbd, bias, bound):
    whole = pl.BlockSpec(memory_space=VMEM)
    return pl.pallas_call(
        attend_kernel,
        out_shape=[jax.ShapeDtypeStruct((18, 64, 256), F32)] * 4,
        in_specs=[pl.BlockSpec(memory_space=pltpu.SMEM)] + [whole] * 5,
        out_specs=[whole] * 4,
        scratch_shapes=[VMEM((4, 18, 64, 128), F32)],
        compiler_params=pltpu.CompilerParams(vmem_limit_bytes=24 * 1024 * 1024),
        name="attend",
    )(lists, qg, kbd, vbd, bias, bound)


def deliver_kernel(
    acc0, acc1, acc2, acc3, qg_ref, mixing_ref, out_ref, update_ref, send_sem, recv_sem, own_sem
):
    row = lax.axis_index("row")
    col = lax.axis_index("col")
    head = lax.axis_index("head")

    def other(flip):
        return (1 - head) if flip else head

    def device(step, flip):
        return (ring(row + step, 8), col, other(flip))

    moves = [(step, flip) for step in (4, 3, 5, 2, 6, 1, 7) for flip in (1, 0)] + [(0, 1)]
    barrier = pltpu.get_barrier_semaphore()
    for step, flip in moves:
        pl.semaphore_signal(barrier, inc=1, device_id=device(step, flip), device_id_type=MESH)

    def spot(step, flip):
        return out_ref.at[pl.ds((other(flip) * 8 + ring(row + step, 8)) * 4, 4)]

    def part(step, flip):
        return update_ref.at[other(flip), ring(row + step, 8)]

    def finish(step):
        target = ring(row + step, 8)
        rows = pl.ds(pl.multiple_of(target * 128, 128), 128)
        for j, acc in enumerate((acc0, acc1, acc2, acc3)):
            sums = acc[pl.ds(target * 2, 2)].reshape(128, 256)
            attention = sums[:, :128] / sums[:, 128:]
            gated = (attention * qg_ref[1, j, rows, :].astype(F32)).astype(BF16)
            update = lax.dot_general(mixing_ref[...], gated, NT, preferred_element_type=F32).astype(BF16)
            update_ref[0, target, j] = update[:64, :]
            update_ref[1, target, j] = update[64:, :]

    copies = []

    def push(step, flip):
        k = flip * 8 + step
        copy = pltpu.make_async_remote_copy(
            src_ref=part(step, flip), dst_ref=spot(0, 0),
            send_sem=send_sem.at[k], recv_sem=recv_sem.at[k],
            device_id=device(step, flip), device_id_type=MESH,
        )
        copy.start()
        copies.append(copy)

    for step in (4, 3, 5):
        finish(step)
    pl.semaphore_wait(barrier, len(moves))
    for step in (4, 3, 5, 2, 6, 1, 7, 0):
        if step not in (4, 3, 5):
            finish(step)
        push(step, 1)
        if step > 0:
            push(step, 0)
    own = pltpu.make_async_copy(part(0, 0), spot(0, 0), own_sem)
    own.start()
    own.wait()
    for step, flip in moves:
        k = flip * 8 + step
        pltpu.make_async_remote_copy(
            src_ref=spot(-step, flip), dst_ref=spot(-step, flip),
            send_sem=send_sem.at[k], recv_sem=recv_sem.at[k],
            device_id=device(step, flip), device_id_type=MESH,
        ).wait_recv()
    for copy in copies:
        copy.wait_send()


def deliver(accs, qg, mixing):
    whole = pl.BlockSpec(memory_space=VMEM)
    return pl.pallas_call(
        deliver_kernel,
        out_shape=jax.ShapeDtypeStruct((64, 64, 128), BF16),
        in_specs=[whole] * 6,
        out_specs=whole,
        scratch_shapes=[VMEM((2, 8, 4, 64, 128), BF16), DMA((16,)), DMA((16,)), DMA],
        compiler_params=pltpu.CompilerParams(
            collective_id=1, has_side_effects=True, vmem_limit_bytes=16 * 1024 * 1024
        ),
        name="deliver",
    )(*accs, qg, mixing)


def per_device(
    pair_field, ln_gain, w_query, w_key, w_value, w_gate, w_bias, w_out, tile_mask, type_ids
):
    weights = [w.T for w in (w_query, w_key, w_value, w_gate)]
    weights.append(w_bias.T)
    operands = (pair_field, ln_gain.reshape(1, 128), *weights, type_ids.reshape(8, 128), w_out, tile_mask)
    qg, kbd, vbd, bias, bound, mixing, lists = spread(
        *[pltpu.with_memory_space_constraint(operand, pltpu.HBM) for operand in operands]
    )
    accs = attend(lists, qg, kbd, vbd, bias.reshape(2, 16, 2, 8, 32, 256), bound)
    return jnp.transpose(deliver(accs, qg, mixing), (2, 0, 1))


def solution(mesh):
    return jax.shard_map(
        per_device,
        mesh=mesh,
        in_specs=(
            P("row", "col", None),
            P(),
            P(None, "head"),
            P(None, "head"),
            P(None, "head"),
            P(None, "head"),
            P(None, "head"),
            P(),
            P(),
            P(),
        ),
        out_specs=P("row", "col", "head"),
        check_vma=False,
    )
```

```python
import math

import jax
import jax.numpy as jnp
from jax import lax
from jax.experimental import pallas as pl
from jax.experimental.pallas import tpu as pltpu
from jax.sharding import PartitionSpec as P

MESH = pl.DeviceIdType.MESH
F32 = jnp.float32
BF16 = jnp.bfloat16
VMEM = pltpu.VMEM
DMA = pltpu.SemaphoreType.DMA

epsilon = 1e-05
masked_score = -1000000000.0
LOG2E = math.log2(math.e)
SCALE = LOG2E / math.sqrt(32)
SAFE = 64.0
NT = (((1,), (1,)), ((), ()))


def ring(value, size):
    return lax.rem(value + size, size)


def spread_kernel(
    tile_ref, gain_in, wq_ref, wk_ref, wv_ref, wg_ref, wb_in, types_in, w_out_in, mask_in,
    qg_ref, kbd_ref, vbd_ref, bias_ref, bound_ref, mixing_ref, lists_ref,
    half, gain_ref, wb_ref, types_ref, w_out_ref, mask_ref, wide, send, strip, wbuf, wall, flat, bsend, tops,
    load_sem, col_send, col_recv, z_send, z_recv, w_send, w_recv,
    g_send, g_recv, s_send, s_recv, own_sem,
):
    row = lax.axis_index("row")
    col = lax.axis_index("col")
    head = lax.axis_index("head")
    core = lax.rem(col, 2)
    x = lax.rem(lax.div(col, 2), 4)
    y = head * 2 + lax.div(col, 8)

    def place(x_, y_, core_=None):
        return (row, lax.rem(y_, 2) * 8 + x_ * 2 + (core if core_ is None else core_), lax.div(y_, 2))

    def along_z(step):
        return (ring(row + step, 8), col, head)

    partner = place(x, ring(y + 2, 4))
    peers = [along_z(step) for step in range(1, 8)]
    peers += [place(ring(x + 1, 4), y), place(ring(x - 1, 4), y)]
    peers += [place(x, ring(y + 1, 4)), place(x, ring(y - 1, 4)), partner]
    peers += [place(x, y, 1 - core)]
    barrier = pltpu.get_barrier_semaphore()
    for peer in peers:
        pl.semaphore_signal(barrier, inc=1, device_id=peer, device_id_type=MESH)

    loads = [
        (tile_ref.at[:, pl.ds(pl.multiple_of(head * 32, 32), 32), :], half),
        (gain_in, gain_ref), (wb_in, wb_ref), (types_in, types_ref),
    ]
    loads += [
        (ref, wbuf.at[head, pl.ds(kind * 64, 64)]) for kind, ref in enumerate((wq_ref, wk_ref, wv_ref, wg_ref))
    ]
    loads += [(w_out_in, w_out_ref), (mask_in, mask_ref)]
    loads = [pltpu.make_async_copy(src, dst, load_sem.at[n]) for n, (src, dst) in enumerate(loads)]
    for load in loads:
        load.start()
    tops[...] = jnp.zeros_like(tops)
    loads[0].wait()

    def widen(block, carry):
        rows = half[pl.ds(block * 8, 8)].astype(F32).reshape(256, 128)
        wide[pl.ds(pl.multiple_of(block * 256, 256), 256), :] = rows
        return carry

    lax.fori_loop(0, 16, widen, 0)
    ones = jnp.ones((128, 128), BF16)
    loads[1].wait()
    gain = gain_ref[...]

    def norm_for(step):
        target = ring(row + step, 8)
        for jj in range(4):
            value = wide[pl.ds(4 * target + jj, 128, stride=32), :]
            mean = jnp.dot(value.astype(BF16), ones, preferred_element_type=F32) * (1.0 / 128)
            centred = value - mean
            squares = (centred * centred).astype(BF16)
            spread = jnp.dot(squares, ones, preferred_element_type=F32) * (1.0 / 128)
            normed = centred * lax.rsqrt(spread + epsilon) * gain
            send[target, jj] = normed.astype(BF16)

    def norm_near(n, carry):
        norm_for(n)
        norm_for(-n)
        return carry

    def norm_far(n, carry):
        norm_for(3 + n)
        norm_for(-3 * (1 - n))
        return carry

    lax.fori_loop(1, 3, norm_near, 0)
    for load in loads[2:]:
        load.wait()
    wbuf[head, 256:272, :] = jnp.concatenate(
        [wb_ref[...].astype(F32), jnp.zeros((14, 128), F32)], axis=0
    ).astype(BF16)
    pl.semaphore_wait(barrier, len(peers))
    w_copy = pltpu.make_async_remote_copy(
        src_ref=wbuf.at[head], dst_ref=wbuf.at[head], send_sem=w_send, recv_sem=w_recv,
        device_id=partner, device_id_type=MESH,
    )
    w_copy.start()
    sent = [w_copy]

    def push(src, dst, send_sem, recv_sem, device):
        copy = pltpu.make_async_remote_copy(
            src_ref=src, dst_ref=dst, send_sem=send_sem, recv_sem=recv_sem,
            device_id=device, device_id_type=MESH,
        )
        copy.start()
        sent.append(copy)

    def strip_rows(step):
        source = ring(row + step, 8)
        return strip.at[:, pl.ds(pl.multiple_of(source * 128, 128), 128), :]

    def col_push(step):
        target = ring(row + step, 8)
        push(send.at[target], strip_rows(0), col_send.at[step], col_recv.at[step], along_z(step))

    col_push(1)
    col_push(7)
    lax.fori_loop(0, 2, norm_far, 0)
    pltpu.make_async_remote_copy(
        src_ref=wbuf.at[1 - head], dst_ref=wbuf.at[1 - head], send_sem=w_send, recv_sem=w_recv,
        device_id=partner, device_id_type=MESH,
    ).wait_recv()

    wb = wbuf[0, 256:272, :].astype(F32) + pltpu.roll(wbuf[1, 256:272, :].astype(F32), 2, 0)
    weighted = wb * gain
    wbt = wb.astype(BF16)

    def bias_for(target, carry):
        part = lax.dot_general(wbt, send[target].reshape(512, 128), NT, preferred_element_type=F32)
        for jj in range(4):
            flat[pl.ds(pl.multiple_of((4 * target + jj) * 8, 8), 8), :] = part[0:8, jj * 128:jj * 128 + 128]
        return carry

    lax.fori_loop(0, 8, bias_for, 0, unroll=4)
    living = jnp.broadcast_to(types_ref[pl.ds(row, 1), :] != 0, (32, 128))
    by_head = [
        jnp.where(living, flat[pl.ds(h, 32, stride=8), :] * LOG2E, masked_score) for h in range(4)
    ]
    bsend[0] = jnp.concatenate([b[:, :64] for b in by_head], axis=1).astype(BF16)
    bsend[1] = jnp.concatenate([b[:, 64:] for b in by_head], axis=1).astype(BF16)

    def unit(x_, y_, run, low, count, core_=None):
        return bias_ref.at[
            run, lax.rem(y_, 2), x_, core if core_ is None else core_, lax.div(y_, 2), pl.ds(low, count)
        ]

    def arrive(dst, send_sem, recv_sem):
        pltpu.make_async_remote_copy(
            src_ref=dst, dst_ref=dst, send_sem=send_sem, recv_sem=recv_sem,
            device_id=partner, device_id_type=MESH,
        ).wait_recv()

    def slot(step):
        return 2 * step - 1 if step > 0 else -2 * step

    spans = ((0, 2, 5), (5, 7, 8))

    def chunk(step, low=0, count=2):
        return bias_ref.at[pl.ds(low, count), lax.rem(y, 2), x, core, lax.div(y, 2), slot(step)]

    def z_push(k, src, dst, step):
        push(src, dst, z_send.at[k], z_recv.at[k], along_z(step))

    def z_arrive(k, dst):
        arrive(dst, z_send.at[k], z_recv.at[k])

    own = pltpu.make_async_copy(bsend, chunk(0), own_sem.at[0])
    own.start()
    for k, step in enumerate((2, -2, 1, -1)):
        z_push(k, bsend, chunk(-step), step)

    own_cols = pltpu.make_async_copy(send.at[row], strip_rows(0), own_sem.at[1])
    own_cols.start()

    for kind, place_of in enumerate((1, 0, 2, 3)):
        for s in range(2):
            wall[place_of * 128 + s * 64:place_of * 128 + s * 64 + 64, :] = wbuf[s, kind * 64:kind * 64 + 64, :]
    together = (
        lax.div(lax.broadcasted_iota(jnp.int32, (128, 128), 0), 32)
        == lax.div(lax.broadcasted_iota(jnp.int32, (128, 128), 1), 32)
    ).astype(F32).astype(BF16)

    key_head = lax.div(lax.broadcasted_iota(jnp.int32, (128, 128), 0), 32)
    side_of = lax.div(lax.broadcasted_iota(jnp.int32, (128, 128), 1), 64)
    key_here = [(key_head == 2 * n + side_of).astype(F32).astype(BF16) for n in range(2)]
    lane_head = lax.div(lax.broadcasted_iota(jnp.int32, (64, 128), 1), 32)
    value_here = [(lane_head == h).astype(F32).astype(BF16) for h in range(4)]

    def project(step):
        source = ring(row + step, 8)
        first_block = 2 * slot(step)
        rows = pl.ds(pl.multiple_of(source * 128, 128), 128)

        def one(jj, carry):
            value = strip[jj, rows, :]
            keys = lax.dot_general(wall[0:128, :], value, NT, preferred_element_type=F32)
            left = lax.dot_general(value, wall[128:256, :], NT, preferred_element_type=F32)
            right = lax.dot_general(value, wall[256:512, :], NT, preferred_element_type=F32)
            query = left * SCALE
            qg_ref[0, jj, rows, :] = query.astype(BF16)
            qg_ref[1, jj, rows, :] = jax.nn.sigmoid(right[:, 128:]).astype(BF16)
            short = keys.astype(BF16)
            values = right[:, :128].astype(BF16)
            for odd in range(2):
                twice = jnp.concatenate([short[:, odd * 64:odd * 64 + 64]] * 2, axis=1)
                for n in range(2):
                    kbd_ref[jj, first_block + odd, :, n * 128:(n + 1) * 128] = twice * key_here[n]
                for h in range(4):
                    vbd_ref[jj, first_block + odd, h * 64:(h + 1) * 64, :] = (
                        values[odd * 64:odd * 64 + 64, :] * value_here[h]
                    )
            lengths = jnp.dot((query * query).astype(BF16), together, preferred_element_type=F32)
            tops[0:1, :] = jnp.maximum(tops[0:1, :], jnp.max(lengths, axis=0, keepdims=True))
            lengths = jnp.dot(together, (keys * keys).astype(BF16), preferred_element_type=F32)
            tops[1:2, :] = jnp.maximum(tops[1:2, :], jnp.max(lengths, axis=0, keepdims=True))
            return carry

        lax.fori_loop(0, 4, one, 0, unroll=True)

    def take(step):
        arrive(strip_rows(step), col_send.at[(8 - step) % 8], col_recv.at[(8 - step) % 8])
        project(step)

    def make_lists():
        mixing_ref[...] = w_out_ref[...].astype(F32).T.astype(BF16)
        part = mask_ref[...].astype(F32)
        place_ = lax.div(lax.broadcasted_iota(jnp.int32, (16, 128), 1), 2)
        away = lax.div(place_ + 1, 2) * (2 * lax.rem(place_, 2) - 1)
        there = 2 * lax.rem(row + away + 8, 8) + lax.rem(lax.broadcasted_iota(jnp.int32, (16, 128), 1), 2)
        inside = lax.broadcasted_iota(jnp.int32, (16, 128), 1) < 16
        turned = (inside & (lax.broadcasted_iota(jnp.int32, (16, 128), 0) == there)).astype(F32).astype(BF16)
        diagonal = lax.broadcasted_iota(jnp.int32, (16, 16), 0) == lax.broadcasted_iota(jnp.int32, (16, 16), 1)
        part = jnp.where((part == 1.0) | diagonal, 1.0, 0.0)
        allowed = jnp.dot(part.astype(BF16), turned, preferred_element_type=F32)
        before = [jnp.zeros((1, 128), F32)]
        for i in range(16):
            before.append(before[-1] + allowed[i:i + 1, :])
        rank = jnp.concatenate(before[:16], axis=0)
        pairs = jnp.broadcast_to(jnp.floor((before[16] + 1.0) * 0.5), (16, 128))
        earlier = (
            lax.broadcasted_iota(jnp.int32, (128, 128), 0) < lax.broadcasted_iota(jnp.int32, (128, 128), 1)
        ).astype(F32).astype(BF16)
        start = jnp.dot(pairs.astype(BF16), earlier, preferred_element_type=F32)
        total = jnp.sum(pairs[0:1, :], axis=1, keepdims=True)
        rank = rank + 2.0 * start
        entry = 2.0 * lax.broadcasted_iota(jnp.int32, (16, 128), 1).astype(F32)
        number = lax.broadcasted_iota(jnp.int32, (16, 128), 0).astype(F32)
        block = jnp.zeros((16, 128), F32)
        picked = [jnp.zeros((16, 128), F32)] * 2
        found = [jnp.zeros((16, 128), F32)] * 2
        for k in range(16):
            at = jnp.broadcast_to(rank[:, k:k + 1], (16, 128))
            here = jnp.broadcast_to(allowed[:, k:k + 1], (16, 128))
            for side in range(2):
                hit = jnp.where(at == entry + side, here, 0.0)
                found[side] = found[side] + hit
                picked[side] = picked[side] + hit * number
                if side == 0:
                    block = block + hit * k
        rows = [jnp.sum(block, axis=0, keepdims=True)]
        for side in range(2):
            missing = 1.0 - jnp.sum(found[side], axis=0, keepdims=True)
            rows.append(jnp.sum(picked[side], axis=0, keepdims=True) + (16.0 + side) * missing)
        rows.append(jnp.broadcast_to(total, (1, 128)))
        rows.append(jnp.zeros((4, 128), F32))
        lists_ref[...] = jnp.concatenate(rows, axis=0).astype(jnp.int32)

    own_cols.wait()
    project(0)
    make_lists()
    own.wait()
    for k, step in enumerate((-2, 2, -1, 1)):
        z_arrive(k, chunk(step))
    z_push(4, chunk(-2), chunk(-3), 1)
    z_push(5, chunk(2), chunk(3), -1)
    z_push(6, chunk(-2, 0, 1), chunk(4, 0, 1), 2)
    z_push(7, chunk(2, 1, 1), chunk(4, 1, 1), -2)

    def far_bias():
        z_arrive(4, chunk(-3))
        z_arrive(5, chunk(3))
        z_arrive(6, chunk(4, 0, 1))
        z_arrive(7, chunk(4, 1, 1))

    def node(run, a, b):
        return (a, b) if run == 0 else (b, a)

    first = (x, y)
    second = (y, x)

    def whole_of(span):
        return span[0], span[2] - span[0]

    def halves_of(span):
        return (span[0], span[1] - span[0]), (span[1], span[2] - span[1])

    def shipment(far, run, index, a, b, rows, to_a, to_b):
        k = far * 40 + run * 20 + index
        ref = unit(*node(run, a, b), run, *rows)
        push(ref, ref, g_send.at[k], g_recv.at[k], place(*node(run, to_a, to_b)))

    def receive(far, run, index, a, b, rows):
        k = far * 40 + run * 20 + index
        arrive(unit(*node(run, a, b), run, *rows), g_send.at[k], g_recv.at[k])

    def to_sibling(run, u, v):
        k = run * 16 + u * 4 + v
        a, b = ring(first[run] + (0, -1, 1, 2)[u], 4), ring(second[run] + (0, -1, 1, 2)[v], 4)
        ref = unit(*node(run, a, b), run, 0, 8)
        push(ref, ref, s_send.at[k], s_recv.at[k], place(x, y, 1 - core))

    def begin(far, run):
        a, b, rows = first[run], second[run], whole_of(spans[far])
        shipment(far, run, 0, a, b, rows, ring(a + 1, 4), b)
        shipment(far, run, 1, a, b, rows, ring(a - 1, 4), b)

    def across(far, run, u):
        a, b, rows = ring(first[run] + (0, -1, 1, 2)[u], 4), second[run], whole_of(spans[far])
        shipment(far, run, 4 + 4 * u, a, b, rows, first[run], ring(b + 1, 4))
        shipment(far, run, 5 + 4 * u, a, b, rows, first[run], ring(b - 1, 4))

    def pass_first(far, run):
        a, b, rows = first[run], second[run], whole_of(spans[far])
        low, high = halves_of(spans[far])
        receive(far, run, 0, ring(a - 1, 4), b, rows)
        shipment(far, run, 2, ring(a - 1, 4), b, low, ring(a + 1, 4), b)
        receive(far, run, 1, ring(a + 1, 4), b, rows)
        shipment(far, run, 3, ring(a + 1, 4), b, high, ring(a - 1, 4), b)

    def end_first(far, run):
        a, b = ring(first[run] + 2, 4), second[run]
        low, high = halves_of(spans[far])
        receive(far, run, 2, a, b, low)
        receive(far, run, 3, a, b, high)

    def pass_second(far, run, u):
        a, b, rows = ring(first[run] + (0, -1, 1, 2)[u], 4), second[run], whole_of(spans[far])
        low, high = halves_of(spans[far])
        receive(far, run, 4 + 4 * u, a, ring(b - 1, 4), rows)
        shipment(far, run, 6 + 4 * u, a, ring(b - 1, 4), low, first[run], ring(b + 1, 4))
        receive(far, run, 5 + 4 * u, a, ring(b + 1, 4), rows)
        shipment(far, run, 7 + 4 * u, a, ring(b + 1, 4), high, first[run], ring(b - 1, 4))

    def end_second(far, run, u):
        a, b = ring(first[run] + (0, -1, 1, 2)[u], 4), ring(second[run] + 2, 4)
        low, high = halves_of(spans[far])
        receive(far, run, 6 + 4 * u, a, b, low)
        receive(far, run, 7 + 4 * u, a, b, high)

    for run in range(2):
        begin(0, run)
    for run in range(2):
        across(0, run, 0)
    for step in (2, 6, 3, 5, 4):
        col_push(step)
    take(1)
    take(-1)
    far_bias()
    for run in range(2):
        begin(1, run)
    for run in range(2):
        across(1, run, 0)
    for run in range(2):
        to_sibling(run, 0, 0)
    for far in range(2):
        for run in range(2):
            pass_first(far, run)
        for run in range(2):
            across(far, run, 1)
            across(far, run, 2)
    for run in range(2):
        to_sibling(run, 1, 0)
        to_sibling(run, 2, 0)
    for far in range(2):
        for run in range(2):
            end_first(far, run)
            across(far, run, 3)
    for run in range(2):
        to_sibling(run, 3, 0)
    take(2)
    for u in range(4):
        for far in range(2):
            for run in range(2):
                pass_second(far, run, u)
        for run in range(2):
            to_sibling(run, u, 1)
            to_sibling(run, u, 2)
        if u == 1:
            take(-2)
        if u == 3:
            take(3)
    for u in range(4):
        for run in range(2):
            for far in range(2):
                end_second(far, run, u)
            to_sibling(run, u, 3)
        if u == 2:
            take(-3)
    take(4)
    bound_ref[0:8, :] = tops[...]
    bound_ref[8:24, :] = jnp.broadcast_to(jnp.sum(weighted * weighted, axis=1, keepdims=True), (16, 128))
    for run in range(2):
        for u in range(4):
            for v in range(4):
                a = ring(first[run] + (0, -1, 1, 2)[u], 4)
                b = ring(second[run] + (0, -1, 1, 2)[v], 4)
                k = run * 16 + u * 4 + v
                arrive(unit(*node(run, a, b), run, 0, 8, 1 - core), s_send.at[k], s_recv.at[k])
    for copy in sent:
        copy.wait_send()


def spread(*operands):
    whole = pl.BlockSpec(memory_space=VMEM)
    return pl.pallas_call(
        spread_kernel,
        out_shape=(
            jax.ShapeDtypeStruct((2, 4, 1024, 128), BF16),
            jax.ShapeDtypeStruct((4, 16, 128, 256), BF16),
            jax.ShapeDtypeStruct((4, 16, 256, 128), BF16),
            jax.ShapeDtypeStruct((2, 2, 4, 2, 2, 8, 32, 256), BF16),
            jax.ShapeDtypeStruct((24, 128), F32),
            jax.ShapeDtypeStruct((128, 128), BF16),
            jax.ShapeDtypeStruct((8, 128), jnp.int32),
        ),
        in_specs=[pl.BlockSpec(memory_space=pltpu.HBM)] * len(operands),
        out_specs=(whole,) * 7,
        scratch_shapes=[
            VMEM((128, 32, 128), BF16),
            VMEM((1, 128), F32),
            VMEM((2, 128), BF16),
            VMEM((8, 128), jnp.int32),
            VMEM((128, 128), BF16),
            VMEM((16, 16), jnp.int32),
            VMEM((4096, 128), F32),
            VMEM((8, 4, 128, 128), BF16),
            VMEM((4, 1024, 128), BF16),
            VMEM((2, 272, 128), BF16),
            VMEM((512, 128), BF16),
            VMEM((256, 128), F32),
            VMEM((2, 32, 256), BF16),
            VMEM((8, 128), F32),
            DMA((10,)), DMA((8,)), DMA((8,)), DMA((8,)), DMA((8,)), DMA, DMA,
            DMA((80,)), DMA((80,)), DMA((32,)), DMA((32,)), DMA((2,)),
        ],
        compiler_params=pltpu.CompilerParams(
            collective_id=0, has_side_effects=True, vmem_limit_bytes=32 * 1024 * 1024
        ),
        name="spread",
    )(*operands)


def attend_kernel(
    lists_ref, qg_ref, kbd, vbd, bias, bound_ref,
    acc0, acc1, acc2, acc3,
    peak,
):
    accs = (acc0, acc1, acc2, acc3)
    for acc in accs:
        acc[...] = jnp.zeros_like(acc)
    same = (
        lax.div(lax.broadcasted_iota(jnp.int32, (256, 128), 0), 64)
        == lax.div(lax.broadcasted_iota(jnp.int32, (256, 128), 1), 32)
    ).astype(F32).astype(BF16)

    reach = jnp.sqrt(jnp.max(bound_ref[0:1, :])) * jnp.sqrt(jnp.max(bound_ref[1:2, :]))
    bias_reach = jnp.sqrt(jnp.max(bound_ref[8:24, :])) * (math.sqrt(128) * LOG2E)
    safe = (reach + bias_reach) * 1.03 <= SAFE

    def query(j, i):
        return qg_ref[0, j, pl.ds(pl.multiple_of(jnp.minimum(i, 15) * 64, 64), 64), :]

    def values_of(j, block):
        return jnp.concatenate([vbd[j, block], same], axis=1)

    def offset_of(i, block):
        at = (lax.rem(block, 2), jnp.minimum(i, 15))
        n = lax.div(block, 2)
        return [bias[at[0], at[1], half, n].astype(F32) for half in range(2)]

    total_pairs = lists_ref[3, 0]

    @pl.when(safe)
    def _():
        def step(t, carry):
            work = []
            for side in range(2):
                e = 2 * t + side
                block = lists_ref[0, e]
                ids = (lists_ref[1, e], lists_ref[2, e])
                offset = jnp.concatenate(offset_of(ids[0], block) + offset_of(ids[1], block), axis=0)
                work.append((block, ids, offset))
            for j in range(4):
                for block, ids, offset in work:
                    queries = jnp.concatenate([query(j, i) for i in ids], axis=0)
                    score = jnp.dot(queries, kbd[j, block], preferred_element_type=F32)
                    weights = jnp.exp2(score + offset).astype(BF16)
                    total = jnp.dot(weights, values_of(j, block), preferred_element_type=F32)
                    olds = [accs[j][i] for i in ids]
                    for n in range(2):
                        accs[j][ids[n]] = olds[n] + total[n * 64:(n + 1) * 64, :]
            return carry

        lax.fori_loop(0, lax.div(total_pairs + 1, 2), step, 0)

    @pl.when(jnp.logical_not(safe))
    def _():
        peak[...] = jnp.full_like(peak, -1e30)

        def step(n, carry):
            e = lax.div(n, 2)
            block = lists_ref[0, e]
            i = lists_ref[1 + lax.rem(n, 2), e]
            offset = jnp.concatenate(offset_of(i, block), axis=0)
            for j in range(4):
                score = jnp.dot(query(j, i), kbd[j, block], preferred_element_type=F32) + offset
                old = peak[j, i]
                tops = [
                    jnp.maximum(
                        jnp.max(score[:, h * 64:(h + 1) * 64], axis=1, keepdims=True),
                        old[:, h * 32:h * 32 + 1],
                    )
                    for h in range(4)
                ]
                shift = jnp.concatenate([jnp.broadcast_to(top, (64, 64)) for top in tops], axis=1)
                fresh = jnp.concatenate([jnp.broadcast_to(top, (64, 32)) for top in tops], axis=1)
                decay = jnp.exp2(old - fresh)
                weights = jnp.exp2(score - shift).astype(BF16)
                total = jnp.dot(weights, values_of(j, block), preferred_element_type=F32)
                accs[j][i] = accs[j][i] * jnp.concatenate([decay, decay], axis=1) + total
                peak[j, i] = fresh
            return carry

        lax.fori_loop(0, 2 * total_pairs, step, 0)


def attend(lists, qg, kbd, vbd, bias, bound):
    whole = pl.BlockSpec(memory_space=VMEM)
    return pl.pallas_call(
        attend_kernel,
        out_shape=[jax.ShapeDtypeStruct((18, 64, 256), F32)] * 4,
        in_specs=[pl.BlockSpec(memory_space=pltpu.SMEM)] + [whole] * 5,
        out_specs=[whole] * 4,
        scratch_shapes=[VMEM((4, 18, 64, 128), F32)],
        compiler_params=pltpu.CompilerParams(vmem_limit_bytes=24 * 1024 * 1024),
        name="attend",
    )(lists, qg, kbd, vbd, bias, bound)


def deliver_kernel(
    acc0, acc1, acc2, acc3, qg_ref, mixing_ref, out_ref,
    update_ref, relay, send_sem, recv_sem, own_sem,
):
    row = lax.axis_index("row")
    col = lax.axis_index("col")
    head = lax.axis_index("head")

    def other(flip):
        return (1 - head) if flip else head

    def device(step, flip):
        return (ring(row + step, 8), col, other(flip))

    steps = (4, 3, 5, 2, 6, 1, 7, 0)
    partner = device(0, 1)
    peers = [partner] + [device(step, 0) for step in steps if step]
    barrier = pltpu.get_barrier_semaphore()
    for peer in peers:
        pl.semaphore_signal(barrier, inc=1, device_id=peer, device_id_type=MESH)

    def spot(step, flip):
        return out_ref.at[pl.ds((other(flip) * 8 + ring(row + step, 8)) * 4, 4)]

    def part(step, flip):
        return update_ref.at[other(flip), ring(row + step, 8)]

    def finish(step):
        target = ring(row + step, 8)
        rows = pl.ds(pl.multiple_of(target * 128, 128), 128)
        for j, acc in enumerate((acc0, acc1, acc2, acc3)):
            sums = acc[pl.ds(target * 2, 2)].reshape(128, 256)
            attention = sums[:, :128] / sums[:, 128:]
            gated = (attention * qg_ref[1, j, rows, :].astype(F32)).astype(BF16)
            update = lax.dot_general(mixing_ref[...], gated, NT, preferred_element_type=F32).astype(BF16)
            update_ref[0, target, j] = update[:64, :]
            update_ref[1, target, j] = update[64:, :]

    copies = []

    def push(k, src, dst, target):
        copy = pltpu.make_async_remote_copy(
            src_ref=src, dst_ref=dst, send_sem=send_sem.at[k], recv_sem=recv_sem.at[k],
            device_id=target, device_id_type=MESH,
        )
        copy.start()
        copies.append(copy)

    def arrive(k, ref):
        pltpu.make_async_remote_copy(
            src_ref=ref, dst_ref=ref, send_sem=send_sem.at[k], recv_sem=recv_sem.at[k],
            device_id=partner, device_id_type=MESH,
        ).wait_recv()

    for step in (4, 3, 5):
        finish(step)
    pl.semaphore_wait(barrier, len(peers))
    for step in steps:
        if step not in (4, 3, 5):
            finish(step)
        if step:
            push(step, part(step, 1), relay.at[step - 1], partner)
            push(8 + step, part(step, 0), spot(0, 0), device(step, 0))
        else:
            push(0, part(0, 1), spot(0, 0), partner)
    own = pltpu.make_async_copy(part(0, 0), spot(0, 0), own_sem)
    own.start()
    for step in steps[:-1]:
        arrive(step, relay.at[step - 1])
        push(16 + step, relay.at[step - 1], spot(0, 1), device(step, 0))
    own.wait()
    arrive(0, spot(0, 1))
    for step in steps[:-1]:
        arrive(8 + step, spot(-step, 0))
    for step in steps[:-1]:
        arrive(16 + step, spot(-step, 1))
    for copy in copies:
        copy.wait_send()


def deliver(accs, qg, mixing):
    whole = pl.BlockSpec(memory_space=VMEM)
    return pl.pallas_call(
        deliver_kernel,
        out_shape=jax.ShapeDtypeStruct((64, 64, 128), BF16),
        in_specs=[whole] * 6,
        out_specs=whole,
        scratch_shapes=[VMEM((2, 8, 4, 64, 128), BF16), VMEM((7, 4, 64, 128), BF16), DMA((24,)), DMA((24,)), DMA],
        compiler_params=pltpu.CompilerParams(
            collective_id=1, has_side_effects=True, vmem_limit_bytes=16 * 1024 * 1024
        ),
        name="deliver",
    )(*accs, qg, mixing)


def per_device(
    pair_field, ln_gain, w_query, w_key, w_value, w_gate, w_bias, w_out, tile_mask, type_ids
):
    weights = [w.T for w in (w_query, w_key, w_value, w_gate)]
    weights.append(w_bias.T)
    operands = (pair_field, ln_gain.reshape(1, 128), *weights, type_ids.reshape(8, 128), w_out, tile_mask)
    qg, kbd, vbd, bias, bound, mixing, lists = spread(
        *[pltpu.with_memory_space_constraint(operand, pltpu.HBM) for operand in operands]
    )
    accs = attend(lists, qg, kbd, vbd, bias.reshape(2, 16, 2, 8, 32, 256), bound)
    return jnp.transpose(deliver(accs, qg, mixing), (2, 0, 1))


def solution(mesh):
    return jax.shard_map(
        per_device,
        mesh=mesh,
        in_specs=(
            P("row", "col", None),
            P(),
            P(None, "head"),
            P(None, "head"),
            P(None, "head"),
            P(None, "head"),
            P(None, "head"),
            P(),
            P(),
            P(),
        ),
        out_specs=P("row", "col", "head"),
        check_vma=False,
    )
```

```python
import math

import jax
import jax.numpy as jnp
from jax import lax
from jax.experimental import pallas as pl
from jax.experimental.pallas import tpu as pltpu
from jax.sharding import PartitionSpec as P

MESH = pl.DeviceIdType.MESH
F32 = jnp.float32
BF16 = jnp.bfloat16
VMEM = pltpu.VMEM
DMA = pltpu.SemaphoreType.DMA

epsilon = 1e-05
masked_score = -1000000000.0
LOG2E = math.log2(math.e)
SCALE = LOG2E / math.sqrt(32)
SAFE = 64.0
NT = (((1,), (1,)), ((), ()))


def ring(value, size):
    return lax.rem(value + size, size)


def spread_kernel(
    tile_ref, gain_in, wq_ref, wk_ref, wv_ref, wg_ref, wb_in, types_in, w_out_in, mask_in,
    qg_ref, kbd_ref, vbd_ref, bias_ref, bound_ref, mixing_ref, lists_ref,
    half, gain_ref, wb_ref, types_ref, w_out_ref, mask_ref, wide, send, strip, wbuf, wall, flat, bsend, tops,
    load_sem, col_send, col_recv, z_send, z_recv, w_send, w_recv,
    g_send, g_recv, s_send, s_recv, own_sem,
):
    row = lax.axis_index("row")
    col = lax.axis_index("col")
    head = lax.axis_index("head")
    core = lax.rem(col, 2)
    x = lax.rem(lax.div(col, 2), 4)
    y = head * 2 + lax.div(col, 8)

    def place(x_, y_, core_=None):
        return (row, lax.rem(y_, 2) * 8 + x_ * 2 + (core if core_ is None else core_), lax.div(y_, 2))

    def along_z(step):
        return (ring(row + step, 8), col, head)

    partner = place(x, ring(y + 2, 4))
    peers = [along_z(step) for step in range(1, 8)]
    peers += [place(ring(x + 1, 4), y), place(ring(x - 1, 4), y)]
    peers += [place(x, ring(y + 1, 4)), place(x, ring(y - 1, 4)), partner]
    peers += [place(x, y, 1 - core)]
    barrier = pltpu.get_barrier_semaphore()
    for peer in peers:
        pl.semaphore_signal(barrier, inc=1, device_id=peer, device_id_type=MESH)

    loads = [
        (tile_ref.at[:, pl.ds(pl.multiple_of(head * 32, 32), 32), :], half),
        (gain_in, gain_ref), (wb_in, wb_ref), (types_in, types_ref),
    ]
    loads += [
        (ref, wbuf.at[head, pl.ds(kind * 64, 64)]) for kind, ref in enumerate((wq_ref, wk_ref, wv_ref, wg_ref))
    ]
    loads += [(w_out_in, w_out_ref), (mask_in, mask_ref)]
    loads = [pltpu.make_async_copy(src, dst, load_sem.at[n]) for n, (src, dst) in enumerate(loads)]
    for load in loads:
        load.start()
    tops[...] = jnp.zeros_like(tops)
    loads[0].wait()

    def widen(block, carry):
        rows = half[pl.ds(block * 8, 8)].astype(F32).reshape(256, 128)
        wide[pl.ds(pl.multiple_of(block * 256, 256), 256), :] = rows
        return carry

    lax.fori_loop(0, 16, widen, 0)
    ones = jnp.ones((128, 128), BF16)
    loads[1].wait()
    gain = gain_ref[...]

    def norm_for(step):
        target = ring(row + step, 8)
        for jj in range(4):
            value = wide[pl.ds(4 * target + jj, 128, stride=32), :]
            mean = jnp.dot(value.astype(BF16), ones, preferred_element_type=F32) * (1.0 / 128)
            centred = value - mean
            squares = (centred * centred).astype(BF16)
            spread = jnp.dot(squares, ones, preferred_element_type=F32) * (1.0 / 128)
            normed = centred * lax.rsqrt(spread + epsilon) * gain
            send[target, jj] = normed.astype(BF16)

    def norm_near(n, carry):
        norm_for(n)
        norm_for(-n)
        return carry

    def norm_far(n, carry):
        norm_for(3 + n)
        norm_for(-3 * (1 - n))
        return carry

    lax.fori_loop(1, 3, norm_near, 0)
    for load in loads[2:]:
        load.wait()
    wbuf[head, 256:272, :] = jnp.concatenate(
        [wb_ref[...].astype(F32), jnp.zeros((14, 128), F32)], axis=0
    ).astype(BF16)
    pl.semaphore_wait(barrier, len(peers))
    w_copy = pltpu.make_async_remote_copy(
        src_ref=wbuf.at[head], dst_ref=wbuf.at[head], send_sem=w_send, recv_sem=w_recv,
        device_id=partner, device_id_type=MESH,
    )
    w_copy.start()
    sent = [w_copy]

    def push(src, dst, send_sem, recv_sem, device):
        copy = pltpu.make_async_remote_copy(
            src_ref=src, dst_ref=dst, send_sem=send_sem, recv_sem=recv_sem,
            device_id=device, device_id_type=MESH,
        )
        copy.start()
        sent.append(copy)

    def strip_rows(step):
        source = ring(row + step, 8)
        return strip.at[:, pl.ds(pl.multiple_of(source * 128, 128), 128), :]

    def col_push(step):
        target = ring(row + step, 8)
        push(send.at[target], strip_rows(0), col_send.at[step], col_recv.at[step], along_z(step))

    col_push(1)
    col_push(7)
    lax.fori_loop(0, 2, norm_far, 0)
    pltpu.make_async_remote_copy(
        src_ref=wbuf.at[1 - head], dst_ref=wbuf.at[1 - head], send_sem=w_send, recv_sem=w_recv,
        device_id=partner, device_id_type=MESH,
    ).wait_recv()

    wb = wbuf[0, 256:272, :].astype(F32) + pltpu.roll(wbuf[1, 256:272, :].astype(F32), 2, 0)
    weighted = wb * gain
    wbt = wb.astype(BF16)

    def bias_for(target, carry):
        part = lax.dot_general(wbt, send[target].reshape(512, 128), NT, preferred_element_type=F32)
        for jj in range(4):
            flat[pl.ds(pl.multiple_of((4 * target + jj) * 8, 8), 8), :] = part[0:8, jj * 128:jj * 128 + 128]
        return carry

    lax.fori_loop(0, 8, bias_for, 0, unroll=4)
    living = jnp.broadcast_to(types_ref[pl.ds(row, 1), :] != 0, (32, 128))
    by_head = [
        jnp.where(living, flat[pl.ds(h, 32, stride=8), :] * LOG2E, masked_score) for h in range(4)
    ]
    bsend[0] = jnp.concatenate([b[:, :64] for b in by_head], axis=1).astype(BF16)
    bsend[1] = jnp.concatenate([b[:, 64:] for b in by_head], axis=1).astype(BF16)

    def unit(x_, y_, run, low, count, core_=None):
        return bias_ref.at[
            run, lax.rem(y_, 2), x_, core if core_ is None else core_, lax.div(y_, 2), pl.ds(low, count)
        ]

    def arrive(dst, send_sem, recv_sem):
        pltpu.make_async_remote_copy(
            src_ref=dst, dst_ref=dst, send_sem=send_sem, recv_sem=recv_sem,
            device_id=partner, device_id_type=MESH,
        ).wait_recv()

    def slot(step):
        return 2 * step - 1 if step > 0 else -2 * step

    spans = ((0, 2, 5), (5, 7, 8))

    def chunk(step, low=0, count=2):
        return bias_ref.at[pl.ds(low, count), lax.rem(y, 2), x, core, lax.div(y, 2), slot(step)]

    def z_push(k, src, dst, step):
        push(src, dst, z_send.at[k], z_recv.at[k], along_z(step))

    def z_arrive(k, dst):
        arrive(dst, z_send.at[k], z_recv.at[k])

    own = pltpu.make_async_copy(bsend, chunk(0), own_sem.at[0])
    own.start()
    for k, step in enumerate((2, -2, 1, -1)):
        z_push(k, bsend, chunk(-step), step)

    own_cols = pltpu.make_async_copy(send.at[row], strip_rows(0), own_sem.at[1])
    own_cols.start()

    for kind, place_of in enumerate((1, 0, 2, 3)):
        for s in range(2):
            wall[place_of * 128 + s * 64:place_of * 128 + s * 64 + 64, :] = wbuf[s, kind * 64:kind * 64 + 64, :]
    together = (
        lax.div(lax.broadcasted_iota(jnp.int32, (128, 128), 0), 32)
        == lax.div(lax.broadcasted_iota(jnp.int32, (128, 128), 1), 32)
    ).astype(F32).astype(BF16)

    key_head = lax.div(lax.broadcasted_iota(jnp.int32, (128, 128), 0), 32)
    side_of = lax.div(lax.broadcasted_iota(jnp.int32, (128, 128), 1), 64)
    key_here = [(key_head == 2 * n + side_of).astype(F32).astype(BF16) for n in range(2)]
    lane_head = lax.div(lax.broadcasted_iota(jnp.int32, (64, 128), 1), 32)
    value_here = [(lane_head == h).astype(F32).astype(BF16) for h in range(4)]

    def project(step):
        source = ring(row + step, 8)
        first_block = 2 * slot(step)
        rows = pl.ds(pl.multiple_of(source * 128, 128), 128)

        def one(jj, carry):
            value = strip[jj, rows, :]
            keys = lax.dot_general(wall[0:128, :], value, NT, preferred_element_type=F32)
            left = lax.dot_general(value, wall[128:256, :], NT, preferred_element_type=F32)
            right = lax.dot_general(value, wall[256:512, :], NT, preferred_element_type=F32)
            query = left * SCALE
            qg_ref[0, jj, rows, :] = query.astype(BF16)
            qg_ref[1, jj, rows, :] = jax.nn.sigmoid(right[:, 128:]).astype(BF16)
            short = keys.astype(BF16)
            values = right[:, :128].astype(BF16)
            for odd in range(2):
                twice = jnp.concatenate([short[:, odd * 64:odd * 64 + 64]] * 2, axis=1)
                for n in range(2):
                    kbd_ref[jj, first_block + odd, :, n * 128:(n + 1) * 128] = twice * key_here[n]
                for h in range(4):
                    vbd_ref[jj, first_block + odd, h * 64:(h + 1) * 64, :] = (
                        values[odd * 64:odd * 64 + 64, :] * value_here[h]
                    )
            lengths = jnp.dot((query * query).astype(BF16), together, preferred_element_type=F32)
            tops[0:1, :] = jnp.maximum(tops[0:1, :], jnp.max(lengths, axis=0, keepdims=True))
            lengths = jnp.dot(together, (keys * keys).astype(BF16), preferred_element_type=F32)
            tops[1:2, :] = jnp.maximum(tops[1:2, :], jnp.max(lengths, axis=0, keepdims=True))
            return carry

        lax.fori_loop(0, 4, one, 0, unroll=True)

    def take(step):
        arrive(strip_rows(step), col_send.at[(8 - step) % 8], col_recv.at[(8 - step) % 8])
        project(step)

    def make_lists():
        mixing_ref[...] = w_out_ref[...].astype(F32).T.astype(BF16)
        part = mask_ref[...].astype(F32)
        place_ = lax.div(lax.broadcasted_iota(jnp.int32, (16, 128), 1), 2)
        away = lax.div(place_ + 1, 2) * (2 * lax.rem(place_, 2) - 1)
        there = 2 * lax.rem(row + away + 8, 8) + lax.rem(lax.broadcasted_iota(jnp.int32, (16, 128), 1), 2)
        inside = lax.broadcasted_iota(jnp.int32, (16, 128), 1) < 16
        turned = (inside & (lax.broadcasted_iota(jnp.int32, (16, 128), 0) == there)).astype(F32).astype(BF16)
        diagonal = lax.broadcasted_iota(jnp.int32, (16, 16), 0) == lax.broadcasted_iota(jnp.int32, (16, 16), 1)
        part = jnp.where((part == 1.0) | diagonal, 1.0, 0.0)
        allowed = jnp.dot(part.astype(BF16), turned, preferred_element_type=F32)
        before = [jnp.zeros((1, 128), F32)]
        for i in range(16):
            before.append(before[-1] + allowed[i:i + 1, :])
        rank = jnp.concatenate(before[:16], axis=0)
        pairs = jnp.broadcast_to(jnp.floor((before[16] + 1.0) * 0.5), (16, 128))
        earlier = (
            lax.broadcasted_iota(jnp.int32, (128, 128), 0) < lax.broadcasted_iota(jnp.int32, (128, 128), 1)
        ).astype(F32).astype(BF16)
        start = jnp.dot(pairs.astype(BF16), earlier, preferred_element_type=F32)
        total = jnp.sum(pairs[0:1, :], axis=1, keepdims=True)
        rank = rank + 2.0 * start
        entry = 2.0 * lax.broadcasted_iota(jnp.int32, (16, 128), 1).astype(F32)
        number = lax.broadcasted_iota(jnp.int32, (16, 128), 0).astype(F32)
        block = jnp.zeros((16, 128), F32)
        picked = [jnp.zeros((16, 128), F32)] * 2
        found = [jnp.zeros((16, 128), F32)] * 2
        for k in range(16):
            at = jnp.broadcast_to(rank[:, k:k + 1], (16, 128))
            here = jnp.broadcast_to(allowed[:, k:k + 1], (16, 128))
            for side in range(2):
                hit = jnp.where(at == entry + side, here, 0.0)
                found[side] = found[side] + hit
                picked[side] = picked[side] + hit * number
                if side == 0:
                    block = block + hit * k
        rows = [jnp.sum(block, axis=0, keepdims=True)]
        for side in range(2):
            missing = 1.0 - jnp.sum(found[side], axis=0, keepdims=True)
            rows.append(jnp.sum(picked[side], axis=0, keepdims=True) + (16.0 + side) * missing)
        rows.append(jnp.broadcast_to(total, (1, 128)))
        rows.append(jnp.zeros((4, 128), F32))
        lists_ref[...] = jnp.concatenate(rows, axis=0).astype(jnp.int32)

    own_cols.wait()
    project(0)
    make_lists()
    own.wait()
    for k, step in enumerate((-2, 2, -1, 1)):
        z_arrive(k, chunk(step))
    z_push(4, chunk(-2), chunk(-3), 1)
    z_push(5, chunk(2), chunk(3), -1)
    z_push(6, chunk(-2, 0, 1), chunk(4, 0, 1), 2)
    z_push(7, chunk(2, 1, 1), chunk(4, 1, 1), -2)

    def far_bias():
        z_arrive(4, chunk(-3))
        z_arrive(5, chunk(3))
        z_arrive(6, chunk(4, 0, 1))
        z_arrive(7, chunk(4, 1, 1))

    def node(run, a, b):
        return (a, b) if run == 0 else (b, a)

    first = (x, y)
    second = (y, x)

    def whole_of(span):
        return span[0], span[2] - span[0]

    def halves_of(span):
        return (span[0], span[1] - span[0]), (span[1], span[2] - span[1])

    def shipment(far, run, index, a, b, rows, to_a, to_b):
        k = far * 40 + run * 20 + index
        ref = unit(*node(run, a, b), run, *rows)
        push(ref, ref, g_send.at[k], g_recv.at[k], place(*node(run, to_a, to_b)))

    def receive(far, run, index, a, b, rows):
        k = far * 40 + run * 20 + index
        arrive(unit(*node(run, a, b), run, *rows), g_send.at[k], g_recv.at[k])

    def to_sibling(run, u, v):
        k = run * 16 + u * 4 + v
        a, b = ring(first[run] + (0, -1, 1, 2)[u], 4), ring(second[run] + (0, -1, 1, 2)[v], 4)
        ref = unit(*node(run, a, b), run, 0, 8)
        push(ref, ref, s_send.at[k], s_recv.at[k], place(x, y, 1 - core))

    def begin(far, run):
        a, b, rows = first[run], second[run], whole_of(spans[far])
        shipment(far, run, 0, a, b, rows, ring(a + 1, 4), b)
        shipment(far, run, 1, a, b, rows, ring(a - 1, 4), b)

    def across(far, run, u):
        a, b, rows = ring(first[run] + (0, -1, 1, 2)[u], 4), second[run], whole_of(spans[far])
        shipment(far, run, 4 + 4 * u, a, b, rows, first[run], ring(b + 1, 4))
        shipment(far, run, 5 + 4 * u, a, b, rows, first[run], ring(b - 1, 4))

    def pass_first(far, run):
        a, b, rows = first[run], second[run], whole_of(spans[far])
        low, high = halves_of(spans[far])
        receive(far, run, 0, ring(a - 1, 4), b, rows)
        shipment(far, run, 2, ring(a - 1, 4), b, low, ring(a + 1, 4), b)
        receive(far, run, 1, ring(a + 1, 4), b, rows)
        shipment(far, run, 3, ring(a + 1, 4), b, high, ring(a - 1, 4), b)

    def end_first(far, run):
        a, b = ring(first[run] + 2, 4), second[run]
        low, high = halves_of(spans[far])
        receive(far, run, 2, a, b, low)
        receive(far, run, 3, a, b, high)

    def pass_second(far, run, u):
        a, b, rows = ring(first[run] + (0, -1, 1, 2)[u], 4), second[run], whole_of(spans[far])
        low, high = halves_of(spans[far])
        receive(far, run, 4 + 4 * u, a, ring(b - 1, 4), rows)
        shipment(far, run, 6 + 4 * u, a, ring(b - 1, 4), low, first[run], ring(b + 1, 4))
        receive(far, run, 5 + 4 * u, a, ring(b + 1, 4), rows)
        shipment(far, run, 7 + 4 * u, a, ring(b + 1, 4), high, first[run], ring(b - 1, 4))

    def end_second(far, run, u):
        a, b = ring(first[run] + (0, -1, 1, 2)[u], 4), ring(second[run] + 2, 4)
        low, high = halves_of(spans[far])
        receive(far, run, 6 + 4 * u, a, b, low)
        receive(far, run, 7 + 4 * u, a, b, high)

    for run in range(2):
        begin(0, run)
    for run in range(2):
        across(0, run, 0)
    for step in (2, 6, 3, 5, 4):
        col_push(step)
    take(1)
    take(-1)
    far_bias()
    for run in range(2):
        begin(1, run)
    for run in range(2):
        across(1, run, 0)
    for run in range(2):
        to_sibling(run, 0, 0)
    for far in range(2):
        for run in range(2):
            pass_first(far, run)
        for run in range(2):
            across(far, run, 1)
            across(far, run, 2)
    for run in range(2):
        to_sibling(run, 1, 0)
        to_sibling(run, 2, 0)
    for far in range(2):
        for run in range(2):
            end_first(far, run)
            across(far, run, 3)
    for run in range(2):
        to_sibling(run, 3, 0)
    take(2)
    for u in range(4):
        for far in range(2):
            for run in range(2):
                pass_second(far, run, u)
        for run in range(2):
            to_sibling(run, u, 1)
            to_sibling(run, u, 2)
        if u == 1:
            take(-2)
        if u == 3:
            take(3)
    for u in range(4):
        for run in range(2):
            for far in range(2):
                end_second(far, run, u)
            to_sibling(run, u, 3)
        if u == 2:
            take(-3)
    take(4)
    bound_ref[0:8, :] = tops[...]
    bound_ref[8:24, :] = jnp.broadcast_to(jnp.sum(weighted * weighted, axis=1, keepdims=True), (16, 128))
    for run in range(2):
        for u in range(4):
            for v in range(4):
                a = ring(first[run] + (0, -1, 1, 2)[u], 4)
                b = ring(second[run] + (0, -1, 1, 2)[v], 4)
                k = run * 16 + u * 4 + v
                arrive(unit(*node(run, a, b), run, 0, 8, 1 - core), s_send.at[k], s_recv.at[k])
    for copy in sent:
        copy.wait_send()


def spread(*operands):
    whole = pl.BlockSpec(memory_space=VMEM)
    return pl.pallas_call(
        spread_kernel,
        out_shape=(
            jax.ShapeDtypeStruct((2, 4, 1024, 128), BF16),
            jax.ShapeDtypeStruct((4, 16, 128, 256), BF16),
            jax.ShapeDtypeStruct((4, 16, 256, 128), BF16),
            jax.ShapeDtypeStruct((2, 2, 4, 2, 2, 8, 32, 256), BF16),
            jax.ShapeDtypeStruct((24, 128), F32),
            jax.ShapeDtypeStruct((128, 128), BF16),
            jax.ShapeDtypeStruct((8, 128), jnp.int32),
        ),
        in_specs=[pl.BlockSpec(memory_space=pltpu.HBM)] * len(operands),
        out_specs=(whole,) * 7,
        scratch_shapes=[
            VMEM((128, 32, 128), BF16),
            VMEM((1, 128), F32),
            VMEM((2, 128), BF16),
            VMEM((8, 128), jnp.int32),
            VMEM((128, 128), BF16),
            VMEM((16, 16), jnp.int32),
            VMEM((4096, 128), F32),
            VMEM((8, 4, 128, 128), BF16),
            VMEM((4, 1024, 128), BF16),
            VMEM((2, 272, 128), BF16),
            VMEM((512, 128), BF16),
            VMEM((256, 128), F32),
            VMEM((2, 32, 256), BF16),
            VMEM((8, 128), F32),
            DMA((10,)), DMA((8,)), DMA((8,)), DMA((8,)), DMA((8,)), DMA, DMA,
            DMA((80,)), DMA((80,)), DMA((32,)), DMA((32,)), DMA((2,)),
        ],
        compiler_params=pltpu.CompilerParams(
            collective_id=0, has_side_effects=True, vmem_limit_bytes=32 * 1024 * 1024
        ),
        name="spread",
    )(*operands)


def attend_kernel(
    lists_ref, qg_ref, kbd, vbd, bias, bound_ref,
    acc0, acc1, acc2, acc3,
    peak,
):
    accs = (acc0, acc1, acc2, acc3)
    for acc in accs:
        acc[...] = jnp.zeros_like(acc)
    same = (
        lax.div(lax.broadcasted_iota(jnp.int32, (256, 128), 0), 64)
        == lax.div(lax.broadcasted_iota(jnp.int32, (256, 128), 1), 32)
    ).astype(F32).astype(BF16)

    reach = jnp.sqrt(jnp.max(bound_ref[0:1, :])) * jnp.sqrt(jnp.max(bound_ref[1:2, :]))
    bias_reach = jnp.sqrt(jnp.max(bound_ref[8:24, :])) * (math.sqrt(128) * LOG2E)
    safe = (reach + bias_reach) * 1.03 <= SAFE

    def query(j, i):
        return qg_ref[0, j, pl.ds(pl.multiple_of(jnp.minimum(i, 15) * 64, 64), 64), :]

    def values_of(j, block):
        return jnp.concatenate([vbd[j, block], same], axis=1)

    def offset_of(i, block):
        at = (lax.rem(block, 2), jnp.minimum(i, 15))
        n = lax.div(block, 2)
        return [bias[at[0], at[1], half, n].astype(F32) for half in range(2)]

    total_pairs = lists_ref[3, 0]

    @pl.when(safe)
    def _():
        def step(t, carry):
            work = []
            for side in range(2):
                e = 2 * t + side
                block = lists_ref[0, e]
                ids = (lists_ref[1, e], lists_ref[2, e])
                offset = jnp.concatenate(offset_of(ids[0], block) + offset_of(ids[1], block), axis=0)
                work.append((block, ids, offset))
            for j in range(4):
                for block, ids, offset in work:
                    queries = jnp.concatenate([query(j, i) for i in ids], axis=0)
                    score = jnp.dot(queries, kbd[j, block], preferred_element_type=F32)
                    weights = jnp.exp2(score + offset).astype(BF16)
                    total = jnp.dot(weights, values_of(j, block), preferred_element_type=F32)
                    olds = [accs[j][i] for i in ids]
                    for n in range(2):
                        accs[j][ids[n]] = olds[n] + total[n * 64:(n + 1) * 64, :]
            return carry

        lax.fori_loop(0, lax.div(total_pairs + 1, 2), step, 0)

    @pl.when(jnp.logical_not(safe))
    def _():
        peak[...] = jnp.full_like(peak, -1e30)

        def step(n, carry):
            e = lax.div(n, 2)
            block = lists_ref[0, e]
            i = lists_ref[1 + lax.rem(n, 2), e]
            offset = jnp.concatenate(offset_of(i, block), axis=0)
            for j in range(4):
                score = jnp.dot(query(j, i), kbd[j, block], preferred_element_type=F32) + offset
                old = peak[j, i]
                tops = [
                    jnp.maximum(
                        jnp.max(score[:, h * 64:(h + 1) * 64], axis=1, keepdims=True),
                        old[:, h * 32:h * 32 + 1],
                    )
                    for h in range(4)
                ]
                shift = jnp.concatenate([jnp.broadcast_to(top, (64, 64)) for top in tops], axis=1)
                fresh = jnp.concatenate([jnp.broadcast_to(top, (64, 32)) for top in tops], axis=1)
                decay = jnp.exp2(old - fresh)
                weights = jnp.exp2(score - shift).astype(BF16)
                total = jnp.dot(weights, values_of(j, block), preferred_element_type=F32)
                accs[j][i] = accs[j][i] * jnp.concatenate([decay, decay], axis=1) + total
                peak[j, i] = fresh
            return carry

        lax.fori_loop(0, 2 * total_pairs, step, 0)


def attend(lists, qg, kbd, vbd, bias, bound):
    whole = pl.BlockSpec(memory_space=VMEM)
    return pl.pallas_call(
        attend_kernel,
        out_shape=[jax.ShapeDtypeStruct((18, 64, 256), F32)] * 4,
        in_specs=[pl.BlockSpec(memory_space=pltpu.SMEM)] + [whole] * 5,
        out_specs=[whole] * 4,
        scratch_shapes=[VMEM((4, 18, 64, 128), F32)],
        compiler_params=pltpu.CompilerParams(vmem_limit_bytes=24 * 1024 * 1024),
        name="attend",
    )(lists, qg, kbd, vbd, bias, bound)


def deliver_kernel(
    acc0, acc1, acc2, acc3, qg_ref, mixing_ref, out_ref,
    update_ref, relay, midway, send_sem, recv_sem, own_sem,
):
    row = lax.axis_index("row")
    col = lax.axis_index("col")
    head = lax.axis_index("head")

    def other(flip):
        return (1 - head) if flip else head

    def device(step, flip):
        return (ring(row + step, 8), col, other(flip))

    steps = (4, 3, 5, 2, 6, 1, 7, 0)
    partner = device(0, 1)
    peers = [partner] + [device(step, 0) for step in steps if step]
    barrier = pltpu.get_barrier_semaphore()
    for peer in peers:
        pl.semaphore_signal(barrier, inc=1, device_id=peer, device_id_type=MESH)

    def spot(step, flip, low=0, count=4):
        return out_ref.at[pl.ds((other(flip) * 8 + ring(row + step, 8)) * 4 + low, count)]

    def part(step, flip):
        return update_ref.at[other(flip), ring(row + step, 8)]

    def finish(step):
        target = ring(row + step, 8)
        rows = pl.ds(pl.multiple_of(target * 128, 128), 128)
        for j, acc in enumerate((acc0, acc1, acc2, acc3)):
            sums = acc[pl.ds(target * 2, 2)].reshape(128, 256)
            attention = sums[:, :128] / sums[:, 128:]
            gated = (attention * qg_ref[1, j, rows, :].astype(F32)).astype(BF16)
            update = lax.dot_general(mixing_ref[...], gated, NT, preferred_element_type=F32).astype(BF16)
            update_ref[0, target, j] = update[:64, :]
            update_ref[1, target, j] = update[64:, :]

    copies = []

    def push(k, src, dst, target):
        copy = pltpu.make_async_remote_copy(
            src_ref=src, dst_ref=dst, send_sem=send_sem.at[k], recv_sem=recv_sem.at[k],
            device_id=target, device_id_type=MESH,
        )
        copy.start()
        copies.append(copy)

    def arrive(k, ref):
        pltpu.make_async_remote_copy(
            src_ref=ref, dst_ref=ref, send_sem=send_sem.at[k], recv_sem=recv_sem.at[k],
            device_id=partner, device_id_type=MESH,
        ).wait_recv()

    ways = (2, -2)

    def half_way(flip, src):
        for way in range(2):
            n = 2 * flip + way
            push(24 + n, src.at[pl.ds(2 * way, 2)], midway.at[n], device(ways[way], 0))

    def pass_on(flip):
        for way in range(2):
            n = 2 * flip + way
            arrive(24 + n, midway.at[n])
            push(28 + n, midway.at[n], spot(-ways[way], flip, 2 * way, 2), device(ways[way], 0))

    for step in (4, 3, 5):
        finish(step)
    pl.semaphore_wait(barrier, len(peers))
    for step in steps:
        if step not in (4, 3, 5):
            finish(step)
        if step:
            push(step, part(step, 1), relay.at[step - 1], partner)
        else:
            push(0, part(0, 1), spot(0, 0), partner)
        if step == 4:
            half_way(0, part(4, 0))
        elif step:
            push(8 + step, part(step, 0), spot(0, 0), device(step, 0))
    pass_on(0)
    own = pltpu.make_async_copy(part(0, 0), spot(0, 0), own_sem)
    own.start()
    for step in steps[:-1]:
        arrive(step, relay.at[step - 1])
        if step == 4:
            half_way(1, relay.at[3])
        else:
            push(16 + step, relay.at[step - 1], spot(0, 1), device(step, 0))
        if step == 2:
            pass_on(1)
    own.wait()
    arrive(0, spot(0, 1))
    for flip in range(2):
        for step in steps[1:-1]:
            arrive(8 + flip * 8 + step, spot(-step, flip))
        for way in range(2):
            arrive(28 + 2 * flip + way, spot(4, flip, 2 * way, 2))
    for copy in copies:
        copy.wait_send()


def deliver(accs, qg, mixing):
    whole = pl.BlockSpec(memory_space=VMEM)
    return pl.pallas_call(
        deliver_kernel,
        out_shape=jax.ShapeDtypeStruct((64, 64, 128), BF16),
        in_specs=[whole] * 6,
        out_specs=whole,
        scratch_shapes=[
            VMEM((2, 8, 4, 64, 128), BF16), VMEM((7, 4, 64, 128), BF16),
            VMEM((4, 2, 64, 128), BF16), DMA((32,)), DMA((32,)), DMA,
        ],
        compiler_params=pltpu.CompilerParams(
            collective_id=1, has_side_effects=True, vmem_limit_bytes=16 * 1024 * 1024
        ),
        name="deliver",
    )(*accs, qg, mixing)


def per_device(
    pair_field, ln_gain, w_query, w_key, w_value, w_gate, w_bias, w_out, tile_mask, type_ids
):
    weights = [w.T for w in (w_query, w_key, w_value, w_gate)]
    weights.append(w_bias.T)
    operands = (pair_field, ln_gain.reshape(1, 128), *weights, type_ids.reshape(8, 128), w_out, tile_mask)
    qg, kbd, vbd, bias, bound, mixing, lists = spread(
        *[pltpu.with_memory_space_constraint(operand, pltpu.HBM) for operand in operands]
    )
    accs = attend(lists, qg, kbd, vbd, bias.reshape(2, 16, 2, 8, 32, 256), bound)
    return jnp.transpose(deliver(accs, qg, mixing), (2, 0, 1))


def solution(mesh):
    return jax.shard_map(
        per_device,
        mesh=mesh,
        in_specs=(
            P("row", "col", None),
            P(),
            P(None, "head"),
            P(None, "head"),
            P(None, "head"),
            P(None, "head"),
            P(None, "head"),
            P(),
            P(),
            P(),
        ),
        out_specs=P("row", "col", "head"),
        check_vma=False,
    )
```

```python
import math

import jax
import jax.numpy as jnp
from jax import lax
from jax.experimental import pallas as pl
from jax.experimental.pallas import tpu as pltpu
from jax.sharding import PartitionSpec as P

MESH = pl.DeviceIdType.MESH
F32 = jnp.float32
BF16 = jnp.bfloat16
VMEM = pltpu.VMEM
DMA = pltpu.SemaphoreType.DMA

epsilon = 1e-05
masked_score = -1000000000.0
LOG2E = math.log2(math.e)
SCALE = LOG2E / math.sqrt(32)
SAFE = 64.0
NT = (((1,), (1,)), ((), ()))


def ring(value, size):
    return lax.rem(value + size, size)


def spread_kernel(
    tile_ref, gain_in, wq_ref, wk_ref, wv_ref, wg_ref, wb_in, types_in, w_out_in, mask_in,
    qg_ref, kbd_ref, vbd_ref, bias_ref, bound_ref, mixing_ref, lists_ref,
    half, gain_ref, wb_ref, types_ref, w_out_ref, mask_ref, wide, send, strip, wbuf, wall, flat, bsend, tops,
    load_sem, col_send, col_recv, z_send, z_recv, w_send, w_recv,
    g_send, g_recv, s_send, s_recv, own_sem,
):
    row = lax.axis_index("row")
    col = lax.axis_index("col")
    head = lax.axis_index("head")
    core = lax.rem(col, 2)
    x = lax.rem(lax.div(col, 2), 4)
    y = head * 2 + lax.div(col, 8)

    def place(x_, y_, core_=None):
        return (row, lax.rem(y_, 2) * 8 + x_ * 2 + (core if core_ is None else core_), lax.div(y_, 2))

    def along_z(step):
        return (ring(row + step, 8), col, head)

    partner = place(x, ring(y + 2, 4))
    peers = [along_z(step) for step in range(1, 8)]
    peers += [place(ring(x + 1, 4), y), place(ring(x - 1, 4), y)]
    peers += [place(x, ring(y + 1, 4)), place(x, ring(y - 1, 4)), partner]
    peers += [place(x, y, 1 - core)]
    barrier = pltpu.get_barrier_semaphore()
    for peer in peers:
        pl.semaphore_signal(barrier, inc=1, device_id=peer, device_id_type=MESH)

    loads = [
        (tile_ref.at[:, pl.ds(pl.multiple_of(head * 32, 32), 32), :], half),
        (gain_in, gain_ref), (wb_in, wb_ref), (types_in, types_ref),
    ]
    loads += [
        (ref, wbuf.at[head, pl.ds(kind * 64, 64)]) for kind, ref in enumerate((wq_ref, wk_ref, wv_ref, wg_ref))
    ]
    loads += [(w_out_in, w_out_ref), (mask_in, mask_ref)]
    loads = [pltpu.make_async_copy(src, dst, load_sem.at[n]) for n, (src, dst) in enumerate(loads)]
    for load in loads:
        load.start()
    tops[...] = jnp.zeros_like(tops)
    for load in loads[1:]:
        load.wait()
    wbuf[head, 256:272, :] = jnp.concatenate(
        [wb_ref[...].astype(F32), jnp.zeros((14, 128), F32)], axis=0
    ).astype(BF16)
    pl.semaphore_wait(barrier, len(peers))
    w_copy = pltpu.make_async_remote_copy(
        src_ref=wbuf.at[head], dst_ref=wbuf.at[head], send_sem=w_send, recv_sem=w_recv,
        device_id=partner, device_id_type=MESH,
    )
    w_copy.start()
    loads[0].wait()

    def widen(block, carry):
        rows = half[pl.ds(block * 8, 8)].astype(F32).reshape(256, 128)
        wide[pl.ds(pl.multiple_of(block * 256, 256), 256), :] = rows
        return carry

    lax.fori_loop(0, 16, widen, 0)
    ones = jnp.ones((128, 128), BF16)
    gain = gain_ref[...]

    def norm_for(step):
        target = ring(row + step, 8)
        for jj in range(4):
            value = wide[pl.ds(4 * target + jj, 128, stride=32), :]
            mean = jnp.dot(value.astype(BF16), ones, preferred_element_type=F32) * (1.0 / 128)
            centred = value - mean
            squares = (centred * centred).astype(BF16)
            spread = jnp.dot(squares, ones, preferred_element_type=F32) * (1.0 / 128)
            normed = centred * lax.rsqrt(spread + epsilon) * gain
            send[target, jj] = normed.astype(BF16)

    def norm_near(n, carry):
        norm_for(n)
        norm_for(-n)
        return carry

    lax.fori_loop(1, 3, norm_near, 0)
    sent = [w_copy]

    def push(src, dst, send_sem, recv_sem, device):
        copy = pltpu.make_async_remote_copy(
            src_ref=src, dst_ref=dst, send_sem=send_sem, recv_sem=recv_sem,
            device_id=device, device_id_type=MESH,
        )
        copy.start()
        sent.append(copy)

    def strip_rows(step):
        source = ring(row + step, 8)
        return strip.at[:, pl.ds(pl.multiple_of(source * 128, 128), 128), :]

    def col_push(step):
        target = ring(row + step, 8)
        push(send.at[target], strip_rows(0), col_send.at[step], col_recv.at[step], along_z(step))

    col_push(1)
    col_push(7)
    pltpu.make_async_remote_copy(
        src_ref=wbuf.at[1 - head], dst_ref=wbuf.at[1 - head], send_sem=w_send, recv_sem=w_recv,
        device_id=partner, device_id_type=MESH,
    ).wait_recv()

    wb = wbuf[0, 256:272, :].astype(F32) + pltpu.roll(wbuf[1, 256:272, :].astype(F32), 2, 0)
    weighted = wb * gain
    wbt = wb.astype(BF16)

    def bias_for(step):
        target = ring(row + step, 8)
        part = lax.dot_general(wbt, send[target].reshape(512, 128), NT, preferred_element_type=F32)
        for jj in range(4):
            flat[pl.ds(pl.multiple_of((4 * target + jj) * 8, 8), 8), :] = part[0:8, jj * 128:jj * 128 + 128]

    def norm_far(n, carry):
        far = (3 + n, -3 * (1 - n))
        near = (1 + n, -1 - n)
        for step in far:
            norm_for(step)
        for step in near + far:
            bias_for(step)
        return carry

    lax.fori_loop(0, 2, norm_far, 0)
    living = jnp.broadcast_to(types_ref[pl.ds(row, 1), :] != 0, (32, 128))
    by_head = [
        jnp.where(living, flat[pl.ds(h, 32, stride=8), :] * LOG2E, masked_score) for h in range(4)
    ]
    bsend[0] = jnp.concatenate([b[:, :64] for b in by_head], axis=1).astype(BF16)
    bsend[1] = jnp.concatenate([b[:, 64:] for b in by_head], axis=1).astype(BF16)

    def unit(x_, y_, run, low, count, core_=None):
        return bias_ref.at[
            run, lax.rem(y_, 2), x_, core if core_ is None else core_, lax.div(y_, 2), pl.ds(low, count)
        ]

    def arrive(dst, send_sem, recv_sem):
        pltpu.make_async_remote_copy(
            src_ref=dst, dst_ref=dst, send_sem=send_sem, recv_sem=recv_sem,
            device_id=partner, device_id_type=MESH,
        ).wait_recv()

    def slot(step):
        return 2 * step - 1 if step > 0 else -2 * step

    spans = ((0, 2, 5), (5, 7, 8))

    def chunk(step, low=0, count=2):
        return bias_ref.at[pl.ds(low, count), lax.rem(y, 2), x, core, lax.div(y, 2), slot(step)]

    def z_push(k, src, dst, step):
        push(src, dst, z_send.at[k], z_recv.at[k], along_z(step))

    def z_arrive(k, dst):
        arrive(dst, z_send.at[k], z_recv.at[k])

    own = pltpu.make_async_copy(bsend, chunk(0), own_sem.at[0])
    own.start()
    for k, step in enumerate((2, -2, 1, -1)):
        z_push(k, bsend, chunk(-step), step)

    own_cols = pltpu.make_async_copy(send.at[row], strip_rows(0), own_sem.at[1])
    own_cols.start()

    for kind, place_of in enumerate((1, 0, 2, 3)):
        for s in range(2):
            wall[place_of * 128 + s * 64:place_of * 128 + s * 64 + 64, :] = wbuf[s, kind * 64:kind * 64 + 64, :]
    together = (
        lax.div(lax.broadcasted_iota(jnp.int32, (128, 128), 0), 32)
        == lax.div(lax.broadcasted_iota(jnp.int32, (128, 128), 1), 32)
    ).astype(F32).astype(BF16)

    key_head = lax.div(lax.broadcasted_iota(jnp.int32, (128, 128), 0), 32)
    side_of = lax.div(lax.broadcasted_iota(jnp.int32, (128, 128), 1), 64)
    key_here = [(key_head == 2 * n + side_of).astype(F32).astype(BF16) for n in range(2)]
    lane_head = lax.div(lax.broadcasted_iota(jnp.int32, (64, 128), 1), 32)
    value_here = [(lane_head == h).astype(F32).astype(BF16) for h in range(4)]

    def project(step):
        source = ring(row + step, 8)
        first_block = 2 * slot(step)
        rows = pl.ds(pl.multiple_of(source * 128, 128), 128)

        def one(jj, carry):
            value = strip[jj, rows, :]
            keys = lax.dot_general(wall[0:128, :], value, NT, preferred_element_type=F32)
            left = lax.dot_general(value, wall[128:256, :], NT, preferred_element_type=F32)
            right = lax.dot_general(value, wall[256:512, :], NT, preferred_element_type=F32)
            query = left * SCALE
            qg_ref[0, jj, rows, :] = query.astype(BF16)
            qg_ref[1, jj, rows, :] = jax.nn.sigmoid(right[:, 128:]).astype(BF16)
            short = keys.astype(BF16)
            values = right[:, :128].astype(BF16)
            for odd in range(2):
                twice = jnp.concatenate([short[:, odd * 64:odd * 64 + 64]] * 2, axis=1)
                for n in range(2):
                    kbd_ref[jj, first_block + odd, :, n * 128:(n + 1) * 128] = twice * key_here[n]
                for h in range(4):
                    vbd_ref[jj, first_block + odd, h * 64:(h + 1) * 64, :] = (
                        values[odd * 64:odd * 64 + 64, :] * value_here[h]
                    )
            lengths = jnp.dot((query * query).astype(BF16), together, preferred_element_type=F32)
            tops[0:1, :] = jnp.maximum(tops[0:1, :], jnp.max(lengths, axis=0, keepdims=True))
            lengths = jnp.dot(together, (keys * keys).astype(BF16), preferred_element_type=F32)
            tops[1:2, :] = jnp.maximum(tops[1:2, :], jnp.max(lengths, axis=0, keepdims=True))
            return carry

        lax.fori_loop(0, 4, one, 0, unroll=True)

    def take(step):
        arrive(strip_rows(step), col_send.at[(8 - step) % 8], col_recv.at[(8 - step) % 8])
        project(step)

    def make_lists():
        mixing_ref[...] = w_out_ref[...].astype(F32).T.astype(BF16)
        part = mask_ref[...].astype(F32)
        place_ = lax.div(lax.broadcasted_iota(jnp.int32, (16, 128), 1), 2)
        away = lax.div(place_ + 1, 2) * (2 * lax.rem(place_, 2) - 1)
        there = 2 * lax.rem(row + away + 8, 8) + lax.rem(lax.broadcasted_iota(jnp.int32, (16, 128), 1), 2)
        inside = lax.broadcasted_iota(jnp.int32, (16, 128), 1) < 16
        turned = (inside & (lax.broadcasted_iota(jnp.int32, (16, 128), 0) == there)).astype(F32).astype(BF16)
        diagonal = lax.broadcasted_iota(jnp.int32, (16, 16), 0) == lax.broadcasted_iota(jnp.int32, (16, 16), 1)
        part = jnp.where((part == 1.0) | diagonal, 1.0, 0.0)
        allowed = jnp.dot(part.astype(BF16), turned, preferred_element_type=F32)
        before = [jnp.zeros((1, 128), F32)]
        for i in range(16):
            before.append(before[-1] + allowed[i:i + 1, :])
        rank = jnp.concatenate(before[:16], axis=0)
        pairs = jnp.broadcast_to(jnp.floor(before[16] * 0.5), (16, 128))
        single = jnp.broadcast_to(before[16], (16, 128)) - 2.0 * pairs
        alone = allowed * jnp.where(rank == 2.0 * pairs, 1.0, 0.0)
        allowed = allowed - alone
        earlier = (
            lax.broadcasted_iota(jnp.int32, (128, 128), 0) < lax.broadcasted_iota(jnp.int32, (128, 128), 1)
        ).astype(F32).astype(BF16)
        start = jnp.dot(pairs.astype(BF16), earlier, preferred_element_type=F32)
        total = jnp.sum(pairs[0:1, :], axis=1, keepdims=True)
        single_start = jnp.dot(single.astype(BF16), earlier, preferred_element_type=F32)
        singles = jnp.sum(single[0:1, :], axis=1, keepdims=True)
        rank = rank + 2.0 * start
        entry = 2.0 * lax.broadcasted_iota(jnp.int32, (16, 128), 1).astype(F32)
        number = lax.broadcasted_iota(jnp.int32, (16, 128), 0).astype(F32)
        block = jnp.zeros((16, 128), F32)
        single_block = jnp.zeros((16, 128), F32)
        single_picked = jnp.zeros((16, 128), F32)
        single_found = jnp.zeros((16, 128), F32)
        picked = [jnp.zeros((16, 128), F32)] * 2
        found = [jnp.zeros((16, 128), F32)] * 2
        for k in range(16):
            at = jnp.broadcast_to(rank[:, k:k + 1], (16, 128))
            here = jnp.broadcast_to(allowed[:, k:k + 1], (16, 128))
            for side in range(2):
                hit = jnp.where(at == entry + side, here, 0.0)
                found[side] = found[side] + hit
                picked[side] = picked[side] + hit * number
                if side == 0:
                    block = block + hit * k
            at = jnp.broadcast_to(single_start[:, k:k + 1], (16, 128))
            here = jnp.broadcast_to(alone[:, k:k + 1], (16, 128))
            hit = jnp.where(2.0 * at == entry, here, 0.0)
            single_found = single_found + hit
            single_picked = single_picked + hit * number
            single_block = single_block + hit * k
        rows = [jnp.sum(block, axis=0, keepdims=True)]
        for side in range(2):
            missing = 1.0 - jnp.sum(found[side], axis=0, keepdims=True)
            rows.append(jnp.sum(picked[side], axis=0, keepdims=True) + (16.0 + side) * missing)
        rows.append(jnp.broadcast_to(total, (1, 128)))
        missing = 1.0 - jnp.sum(single_found, axis=0, keepdims=True)
        rows.append(jnp.sum(single_block, axis=0, keepdims=True))
        rows.append(jnp.sum(single_picked, axis=0, keepdims=True) + 16.0 * missing)
        rows.append(jnp.broadcast_to(singles, (1, 128)))
        rows.append(jnp.zeros((1, 128), F32))
        lists_ref[...] = jnp.concatenate(rows, axis=0).astype(jnp.int32)

    own_cols.wait()
    project(0)
    make_lists()
    own.wait()
    for k, step in enumerate((-2, 2, -1, 1)):
        z_arrive(k, chunk(step))
    z_push(4, chunk(-2), chunk(-3), 1)
    z_push(5, chunk(2), chunk(3), -1)
    z_push(6, chunk(-2, 0, 1), chunk(4, 0, 1), 2)
    z_push(7, chunk(2, 1, 1), chunk(4, 1, 1), -2)

    def far_bias():
        z_arrive(4, chunk(-3))
        z_arrive(5, chunk(3))
        z_arrive(6, chunk(4, 0, 1))
        z_arrive(7, chunk(4, 1, 1))

    def node(run, a, b):
        return (a, b) if run == 0 else (b, a)

    first = (x, y)
    second = (y, x)

    def whole_of(span):
        return span[0], span[2] - span[0]

    def halves_of(span):
        return (span[0], span[1] - span[0]), (span[1], span[2] - span[1])

    def shipment(far, run, index, a, b, rows, to_a, to_b):
        k = far * 40 + run * 20 + index
        ref = unit(*node(run, a, b), run, *rows)
        push(ref, ref, g_send.at[k], g_recv.at[k], place(*node(run, to_a, to_b)))

    def receive(far, run, index, a, b, rows):
        k = far * 40 + run * 20 + index
        arrive(unit(*node(run, a, b), run, *rows), g_send.at[k], g_recv.at[k])

    def to_sibling(run, u, v):
        k = run * 16 + u * 4 + v
        a, b = ring(first[run] + (0, -1, 1, 2)[u], 4), ring(second[run] + (0, -1, 1, 2)[v], 4)
        ref = unit(*node(run, a, b), run, 0, 8)
        push(ref, ref, s_send.at[k], s_recv.at[k], place(x, y, 1 - core))

    def begin(far, run):
        a, b, rows = first[run], second[run], whole_of(spans[far])
        shipment(far, run, 0, a, b, rows, ring(a + 1, 4), b)
        shipment(far, run, 1, a, b, rows, ring(a - 1, 4), b)

    def across(far, run, u):
        a, b, rows = ring(first[run] + (0, -1, 1, 2)[u], 4), second[run], whole_of(spans[far])
        shipment(far, run, 4 + 4 * u, a, b, rows, first[run], ring(b + 1, 4))
        shipment(far, run, 5 + 4 * u, a, b, rows, first[run], ring(b - 1, 4))

    def pass_first(far, run):
        a, b, rows = first[run], second[run], whole_of(spans[far])
        low, high = halves_of(spans[far])
        receive(far, run, 0, ring(a - 1, 4), b, rows)
        shipment(far, run, 2, ring(a - 1, 4), b, low, ring(a + 1, 4), b)
        receive(far, run, 1, ring(a + 1, 4), b, rows)
        shipment(far, run, 3, ring(a + 1, 4), b, high, ring(a - 1, 4), b)

    def end_first(far, run):
        a, b = ring(first[run] + 2, 4), second[run]
        low, high = halves_of(spans[far])
        receive(far, run, 2, a, b, low)
        receive(far, run, 3, a, b, high)

    def pass_second(far, run, u):
        a, b, rows = ring(first[run] + (0, -1, 1, 2)[u], 4), second[run], whole_of(spans[far])
        low, high = halves_of(spans[far])
        receive(far, run, 4 + 4 * u, a, ring(b - 1, 4), rows)
        shipment(far, run, 6 + 4 * u, a, ring(b - 1, 4), low, first[run], ring(b + 1, 4))
        receive(far, run, 5 + 4 * u, a, ring(b + 1, 4), rows)
        shipment(far, run, 7 + 4 * u, a, ring(b + 1, 4), high, first[run], ring(b - 1, 4))

    def end_second(far, run, u):
        a, b = ring(first[run] + (0, -1, 1, 2)[u], 4), ring(second[run] + 2, 4)
        low, high = halves_of(spans[far])
        receive(far, run, 6 + 4 * u, a, b, low)
        receive(far, run, 7 + 4 * u, a, b, high)

    for run in range(2):
        begin(0, run)
    for run in range(2):
        across(0, run, 0)
    for step in (2, 6, 3, 5, 4):
        col_push(step)
    take(1)
    take(-1)
    far_bias()
    for run in range(2):
        begin(1, run)
    for run in range(2):
        across(1, run, 0)
    for run in range(2):
        to_sibling(run, 0, 0)
    for far in range(2):
        for run in range(2):
            pass_first(far, run)
        for run in range(2):
            across(far, run, 1)
            across(far, run, 2)
    for run in range(2):
        to_sibling(run, 1, 0)
        to_sibling(run, 2, 0)
    for far in range(2):
        for run in range(2):
            end_first(far, run)
            across(far, run, 3)
    for run in range(2):
        to_sibling(run, 3, 0)
    take(2)
    for u in range(4):
        for far in range(2):
            for run in range(2):
                pass_second(far, run, u)
        for run in range(2):
            to_sibling(run, u, 1)
            to_sibling(run, u, 2)
        if u == 1:
            take(-2)
        if u == 3:
            take(3)
    for u in range(4):
        for run in range(2):
            for far in range(2):
                end_second(far, run, u)
            to_sibling(run, u, 3)
        if u == 2:
            take(-3)
    take(4)
    bound_ref[0:8, :] = tops[...]
    bound_ref[8:24, :] = jnp.broadcast_to(jnp.sum(weighted * weighted, axis=1, keepdims=True), (16, 128))
    for run in range(2):
        for u in range(4):
            for v in range(4):
                a = ring(first[run] + (0, -1, 1, 2)[u], 4)
                b = ring(second[run] + (0, -1, 1, 2)[v], 4)
                k = run * 16 + u * 4 + v
                arrive(unit(*node(run, a, b), run, 0, 8, 1 - core), s_send.at[k], s_recv.at[k])
    for copy in sent:
        copy.wait_send()


def spread(*operands):
    whole = pl.BlockSpec(memory_space=VMEM)
    return pl.pallas_call(
        spread_kernel,
        out_shape=(
            jax.ShapeDtypeStruct((2, 4, 1024, 128), BF16),
            jax.ShapeDtypeStruct((4, 16, 128, 256), BF16),
            jax.ShapeDtypeStruct((4, 16, 256, 128), BF16),
            jax.ShapeDtypeStruct((2, 2, 4, 2, 2, 8, 32, 256), BF16),
            jax.ShapeDtypeStruct((24, 128), F32),
            jax.ShapeDtypeStruct((128, 128), BF16),
            jax.ShapeDtypeStruct((8, 128), jnp.int32),
        ),
        in_specs=[pl.BlockSpec(memory_space=pltpu.HBM)] * len(operands),
        out_specs=(whole,) * 7,
        scratch_shapes=[
            VMEM((128, 32, 128), BF16),
            VMEM((1, 128), F32),
            VMEM((2, 128), BF16),
            VMEM((8, 128), jnp.int32),
            VMEM((128, 128), BF16),
            VMEM((16, 16), jnp.int32),
            VMEM((4096, 128), F32),
            VMEM((8, 4, 128, 128), BF16),
            VMEM((4, 1024, 128), BF16),
            VMEM((2, 272, 128), BF16),
            VMEM((512, 128), BF16),
            VMEM((256, 128), F32),
            VMEM((2, 32, 256), BF16),
            VMEM((8, 128), F32),
            DMA((10,)), DMA((8,)), DMA((8,)), DMA((8,)), DMA((8,)), DMA, DMA,
            DMA((80,)), DMA((80,)), DMA((32,)), DMA((32,)), DMA((2,)),
        ],
        compiler_params=pltpu.CompilerParams(
            collective_id=0, has_side_effects=True, vmem_limit_bytes=32 * 1024 * 1024
        ),
        name="spread",
    )(*operands)


def attend_kernel(
    lists_ref, qg_ref, kbd, vbd, bias, bound_ref,
    acc0, acc1, acc2, acc3,
    peak,
):
    accs = (acc0, acc1, acc2, acc3)
    for acc in accs:
        acc[...] = jnp.zeros_like(acc)
    same = (
        lax.div(lax.broadcasted_iota(jnp.int32, (256, 128), 0), 64)
        == lax.div(lax.broadcasted_iota(jnp.int32, (256, 128), 1), 32)
    ).astype(F32).astype(BF16)

    reach = jnp.sqrt(jnp.max(bound_ref[0:1, :])) * jnp.sqrt(jnp.max(bound_ref[1:2, :]))
    bias_reach = jnp.sqrt(jnp.max(bound_ref[8:24, :])) * (math.sqrt(128) * LOG2E)
    safe = (reach + bias_reach) * 1.03 <= SAFE

    def query(j, i):
        return qg_ref[0, j, pl.ds(pl.multiple_of(jnp.minimum(i, 15) * 64, 64), 64), :]

    def values_of(j, block):
        return jnp.concatenate([vbd[j, block], same], axis=1)

    def offset_of(i, block):
        at = (lax.rem(block, 2), jnp.minimum(i, 15))
        n = lax.div(block, 2)
        return [bias[at[0], at[1], half, n].astype(F32) for half in range(2)]

    total_pairs = lists_ref[3, 0]

    @pl.when(safe)
    def _():
        def step(t, carry):
            work = []
            for side in range(2):
                e = 2 * t + side
                block = lists_ref[0, e]
                ids = (lists_ref[1, e], lists_ref[2, e])
                offset = jnp.concatenate(offset_of(ids[0], block) + offset_of(ids[1], block), axis=0)
                work.append((block, ids, offset))
            for j in range(4):
                for block, ids, offset in work:
                    queries = jnp.concatenate([query(j, i) for i in ids], axis=0)
                    score = jnp.dot(queries, kbd[j, block], preferred_element_type=F32)
                    weights = jnp.exp2(score + offset).astype(BF16)
                    total = jnp.dot(weights, values_of(j, block), preferred_element_type=F32)
                    olds = [accs[j][i] for i in ids]
                    for n in range(2):
                        accs[j][ids[n]] = olds[n] + total[n * 64:(n + 1) * 64, :]
            return carry

        def single_step(t, carry):
            for j in range(4):
                for side in range(4):
                    e = 4 * t + side
                    block = lists_ref[4, e]
                    i = lists_ref[5, e]
                    offset = jnp.concatenate(offset_of(i, block), axis=0)
                    score = jnp.dot(query(j, i), kbd[j, block], preferred_element_type=F32)
                    weights = jnp.exp2(score + offset).astype(BF16)
                    total = jnp.dot(weights, values_of(j, block), preferred_element_type=F32)
                    accs[j][i] = accs[j][i] + total
            return carry

        lax.fori_loop(0, lax.div(total_pairs + 1, 2), step, 0)
        lax.fori_loop(0, lax.div(lists_ref[6, 0] + 3, 4), single_step, 0)

    @pl.when(jnp.logical_not(safe))
    def _():
        peak[...] = jnp.full_like(peak, -1e30)

        def step(n, carry):
            e = jnp.where(n < 2 * total_pairs, lax.div(n, 2), n - 2 * total_pairs)
            line = jnp.where(n < 2 * total_pairs, lax.rem(n, 2), 4)
            block = lists_ref[jnp.where(line == 4, 4, 0), e]
            i = lists_ref[1 + line, e]
            offset = jnp.concatenate(offset_of(i, block), axis=0)
            for j in range(4):
                score = jnp.dot(query(j, i), kbd[j, block], preferred_element_type=F32) + offset
                old = peak[j, i]
                tops = [
                    jnp.maximum(
                        jnp.max(score[:, h * 64:(h + 1) * 64], axis=1, keepdims=True),
                        old[:, h * 32:h * 32 + 1],
                    )
                    for h in range(4)
                ]
                shift = jnp.concatenate([jnp.broadcast_to(top, (64, 64)) for top in tops], axis=1)
                fresh = jnp.concatenate([jnp.broadcast_to(top, (64, 32)) for top in tops], axis=1)
                decay = jnp.exp2(old - fresh)
                weights = jnp.exp2(score - shift).astype(BF16)
                total = jnp.dot(weights, values_of(j, block), preferred_element_type=F32)
                accs[j][i] = accs[j][i] * jnp.concatenate([decay, decay], axis=1) + total
                peak[j, i] = fresh
            return carry

        lax.fori_loop(0, 2 * total_pairs + lists_ref[6, 0], step, 0)


def attend(lists, qg, kbd, vbd, bias, bound):
    whole = pl.BlockSpec(memory_space=VMEM)
    return pl.pallas_call(
        attend_kernel,
        out_shape=[jax.ShapeDtypeStruct((18, 64, 256), F32)] * 4,
        in_specs=[pl.BlockSpec(memory_space=pltpu.SMEM)] + [whole] * 5,
        out_specs=[whole] * 4,
        scratch_shapes=[VMEM((4, 18, 64, 128), F32)],
        compiler_params=pltpu.CompilerParams(vmem_limit_bytes=24 * 1024 * 1024),
        name="attend",
    )(lists, qg, kbd, vbd, bias, bound)


def deliver_kernel(
    acc0, acc1, acc2, acc3, qg_ref, mixing_ref, out_ref,
    update_ref, relay, send_sem, recv_sem, own_sem,
):
    row = lax.axis_index("row")
    col = lax.axis_index("col")
    head = lax.axis_index("head")

    def other(flip):
        return (1 - head) if flip else head

    def device(step, flip):
        return (ring(row + step, 8), col, other(flip))

    steps = (4, 3, 5, 2, 6, 1, 7, 0)
    partner = device(0, 1)
    peers = [partner] + [device(step, 0) for step in steps if step]
    barrier = pltpu.get_barrier_semaphore()
    for peer in peers:
        pl.semaphore_signal(barrier, inc=1, device_id=peer, device_id_type=MESH)

    def spot(step, flip):
        return out_ref.at[pl.ds((other(flip) * 8 + ring(row + step, 8)) * 4, 4)]

    def part(step, flip):
        return update_ref.at[other(flip), ring(row + step, 8)]

    def finish(step):
        target = ring(row + step, 8)
        rows = pl.ds(pl.multiple_of(target * 128, 128), 128)
        for j, acc in enumerate((acc0, acc1, acc2, acc3)):
            sums = acc[pl.ds(target * 2, 2)].reshape(128, 256)
            attention = sums[:, :128] / sums[:, 128:]
            gated = (attention * qg_ref[1, j, rows, :].astype(F32)).astype(BF16)
            update = lax.dot_general(mixing_ref[...], gated, NT, preferred_element_type=F32).astype(BF16)
            update_ref[0, target, j] = update[:64, :]
            update_ref[1, target, j] = update[64:, :]

    copies = []

    def push(k, src, dst, target):
        copy = pltpu.make_async_remote_copy(
            src_ref=src, dst_ref=dst, send_sem=send_sem.at[k], recv_sem=recv_sem.at[k],
            device_id=target, device_id_type=MESH,
        )
        copy.start()
        copies.append(copy)

    def arrive(k, ref):
        pltpu.make_async_remote_copy(
            src_ref=ref, dst_ref=ref, send_sem=send_sem.at[k], recv_sem=recv_sem.at[k],
            device_id=partner, device_id_type=MESH,
        ).wait_recv()

    for step in (4, 3, 5):
        finish(step)
    pl.semaphore_wait(barrier, len(peers))
    for step in steps:
        if step not in (4, 3, 5):
            finish(step)
        if step:
            push(step, part(step, 1), relay.at[step - 1], partner)
            push(8 + step, part(step, 0), spot(0, 0), device(step, 0))
        else:
            push(0, part(0, 1), spot(0, 0), partner)
    own = pltpu.make_async_copy(part(0, 0), spot(0, 0), own_sem)
    own.start()
    for step in steps[:-1]:
        arrive(step, relay.at[step - 1])
        push(16 + step, relay.at[step - 1], spot(0, 1), device(step, 0))
    own.wait()
    arrive(0, spot(0, 1))
    for step in steps[:-1]:
        arrive(8 + step, spot(-step, 0))
    for step in steps[:-1]:
        arrive(16 + step, spot(-step, 1))
    for copy in copies:
        copy.wait_send()


def deliver(accs, qg, mixing):
    whole = pl.BlockSpec(memory_space=VMEM)
    return pl.pallas_call(
        deliver_kernel,
        out_shape=jax.ShapeDtypeStruct((64, 64, 128), BF16),
        in_specs=[whole] * 6,
        out_specs=whole,
        scratch_shapes=[VMEM((2, 8, 4, 64, 128), BF16), VMEM((7, 4, 64, 128), BF16), DMA((24,)), DMA((24,)), DMA],
        compiler_params=pltpu.CompilerParams(
            collective_id=1, has_side_effects=True, vmem_limit_bytes=16 * 1024 * 1024
        ),
        name="deliver",
    )(*accs, qg, mixing)


def per_device(
    pair_field, ln_gain, w_query, w_key, w_value, w_gate, w_bias, w_out, tile_mask, type_ids
):
    weights = [w.T for w in (w_query, w_key, w_value, w_gate)]
    weights.append(w_bias.T)
    operands = (pair_field, ln_gain.reshape(1, 128), *weights, type_ids.reshape(8, 128), w_out, tile_mask)
    qg, kbd, vbd, bias, bound, mixing, lists = spread(
        *[pltpu.with_memory_space_constraint(operand, pltpu.HBM) for operand in operands]
    )
    accs = attend(lists, qg, kbd, vbd, bias.reshape(2, 16, 2, 8, 32, 256), bound)
    return jnp.transpose(deliver(accs, qg, mixing), (2, 0, 1))


def solution(mesh):
    return jax.shard_map(
        per_device,
        mesh=mesh,
        in_specs=(
            P("row", "col", None),
            P(),
            P(None, "head"),
            P(None, "head"),
            P(None, "head"),
            P(None, "head"),
            P(None, "head"),
            P(),
            P(),
            P(),
        ),
        out_specs=P("row", "col", "head"),
        check_vma=False,
    )
```

```python
import math

import jax
import jax.numpy as jnp
from jax import lax
from jax.experimental import pallas as pl
from jax.experimental.pallas import tpu as pltpu
from jax.sharding import PartitionSpec as P

MESH = pl.DeviceIdType.MESH
F32 = jnp.float32
BF16 = jnp.bfloat16
VMEM = pltpu.VMEM
DMA = pltpu.SemaphoreType.DMA

epsilon = 1e-05
masked_score = -1000000000.0
LOG2E = math.log2(math.e)
SCALE = LOG2E / math.sqrt(32)
SAFE = 64.0
NT = (((1,), (1,)), ((), ()))


def ring(value, size):
    return lax.rem(value + size, size)


def spread_kernel(
    tile_ref, gain_in, wq_ref, wk_ref, wv_ref, wg_ref, wb_in, types_in, w_out_in, mask_in,
    qg_ref, kbd_ref, vbd_ref, bias_ref, bound_ref, mixing_ref, lists_ref,
    half, gain_ref, wb_ref, types_ref, w_out_ref, mask_ref, wide, send, strip, wbuf, wall, flat, bsend, tops,
    load_sem, col_send, col_recv, z_send, z_recv, w_send, w_recv,
    g_send, g_recv, s_send, s_recv, own_sem,
):
    row = lax.axis_index("row")
    col = lax.axis_index("col")
    head = lax.axis_index("head")
    core = lax.rem(col, 2)
    x = lax.rem(lax.div(col, 2), 4)
    y = head * 2 + lax.div(col, 8)

    def place(x_, y_, core_=None):
        return (row, lax.rem(y_, 2) * 8 + x_ * 2 + (core if core_ is None else core_), lax.div(y_, 2))

    def along_z(step):
        return (ring(row + step, 8), col, head)

    partner = place(x, ring(y + 2, 4))
    peers = [along_z(step) for step in range(1, 8)]
    peers += [place(ring(x + 1, 4), y), place(ring(x - 1, 4), y)]
    peers += [place(x, ring(y + 1, 4)), place(x, ring(y - 1, 4)), partner]
    peers += [place(x, y, 1 - core)]
    barrier = pltpu.get_barrier_semaphore()
    for peer in peers:
        pl.semaphore_signal(barrier, inc=1, device_id=peer, device_id_type=MESH)

    loads = [
        (tile_ref.at[:, pl.ds(pl.multiple_of(head * 32, 32), 32), :], half),
        (gain_in, gain_ref), (wb_in, wb_ref), (types_in, types_ref),
    ]
    loads += [
        (ref, wbuf.at[head, pl.ds(kind * 64, 64)]) for kind, ref in enumerate((wq_ref, wk_ref, wv_ref, wg_ref))
    ]
    loads += [(w_out_in, w_out_ref), (mask_in, mask_ref)]
    loads = [pltpu.make_async_copy(src, dst, load_sem.at[n]) for n, (src, dst) in enumerate(loads)]
    for load in loads:
        load.start()
    tops[...] = jnp.zeros_like(tops)
    loads[0].wait()

    def widen(block, carry):
        rows = half[pl.ds(block * 8, 8)].astype(F32).reshape(256, 128)
        wide[pl.ds(pl.multiple_of(block * 256, 256), 256), :] = rows
        return carry

    lax.fori_loop(0, 16, widen, 0)
    ones = jnp.ones((128, 128), BF16)
    loads[1].wait()
    gain = gain_ref[...]

    def norm_for(step):
        target = ring(row + step, 8)
        for jj in range(4):
            value = wide[pl.ds(4 * target + jj, 128, stride=32), :]
            mean = jnp.dot(value.astype(BF16), ones, preferred_element_type=F32) * (1.0 / 128)
            centred = value - mean
            squares = (centred * centred).astype(BF16)
            spread = jnp.dot(squares, ones, preferred_element_type=F32) * (1.0 / 128)
            normed = centred * lax.rsqrt(spread + epsilon) * gain
            send[target, jj] = normed.astype(BF16)

    def norm_near(n, carry):
        norm_for(n)
        norm_for(-n)
        return carry

    def norm_far(n, carry):
        norm_for(3 + n)
        norm_for(-3 * (1 - n))
        return carry

    lax.fori_loop(1, 3, norm_near, 0)
    for load in loads[2:]:
        load.wait()
    wbuf[head, 256:272, :] = jnp.concatenate(
        [wb_ref[...].astype(F32), jnp.zeros((14, 128), F32)], axis=0
    ).astype(BF16)
    pl.semaphore_wait(barrier, len(peers))
    w_copy = pltpu.make_async_remote_copy(
        src_ref=wbuf.at[head], dst_ref=wbuf.at[head], send_sem=w_send, recv_sem=w_recv,
        device_id=partner, device_id_type=MESH,
    )
    w_copy.start()
    sent = [w_copy]

    def push(src, dst, send_sem, recv_sem, device):
        copy = pltpu.make_async_remote_copy(
            src_ref=src, dst_ref=dst, send_sem=send_sem, recv_sem=recv_sem,
            device_id=device, device_id_type=MESH,
        )
        copy.start()
        sent.append(copy)

    def strip_rows(step):
        source = ring(row + step, 8)
        return strip.at[:, pl.ds(pl.multiple_of(source * 128, 128), 128), :]

    def col_push(step):
        target = ring(row + step, 8)
        push(send.at[target], strip_rows(0), col_send.at[step], col_recv.at[step], along_z(step))

    col_push(1)
    col_push(7)
    lax.fori_loop(0, 2, norm_far, 0)
    pltpu.make_async_remote_copy(
        src_ref=wbuf.at[1 - head], dst_ref=wbuf.at[1 - head], send_sem=w_send, recv_sem=w_recv,
        device_id=partner, device_id_type=MESH,
    ).wait_recv()

    wb = wbuf[0, 256:272, :].astype(F32) + pltpu.roll(wbuf[1, 256:272, :].astype(F32), 2, 0)
    weighted = wb * gain
    wbt = wb.astype(BF16)

    def bias_for(target, carry):
        part = lax.dot_general(wbt, send[target].reshape(512, 128), NT, preferred_element_type=F32)
        for jj in range(4):
            flat[pl.ds(pl.multiple_of((4 * target + jj) * 8, 8), 8), :] = part[0:8, jj * 128:jj * 128 + 128]
        return carry

    lax.fori_loop(0, 8, bias_for, 0, unroll=4)
    living = jnp.broadcast_to(types_ref[pl.ds(row, 1), :] != 0, (32, 128))
    by_head = [
        jnp.where(living, flat[pl.ds(h, 32, stride=8), :] * LOG2E, masked_score) for h in range(4)
    ]
    bsend[0] = jnp.concatenate([b[:, :64] for b in by_head], axis=1).astype(BF16)
    bsend[1] = jnp.concatenate([b[:, 64:] for b in by_head], axis=1).astype(BF16)

    def unit(x_, y_, run, low, count, core_=None):
        return bias_ref.at[
            run, lax.rem(y_, 2), x_, core if core_ is None else core_, lax.div(y_, 2), pl.ds(low, count)
        ]

    def arrive(dst, send_sem, recv_sem):
        pltpu.make_async_remote_copy(
            src_ref=dst, dst_ref=dst, send_sem=send_sem, recv_sem=recv_sem,
            device_id=partner, device_id_type=MESH,
        ).wait_recv()

    def slot(step):
        return 2 * step - 1 if step > 0 else -2 * step

    spans = ((0, 2, 5), (5, 7, 8))

    def chunk(step, low=0, count=2):
        return bias_ref.at[pl.ds(low, count), lax.rem(y, 2), x, core, lax.div(y, 2), slot(step)]

    def z_push(k, src, dst, step):
        push(src, dst, z_send.at[k], z_recv.at[k], along_z(step))

    def z_arrive(k, dst):
        arrive(dst, z_send.at[k], z_recv.at[k])

    own = pltpu.make_async_copy(bsend, chunk(0), own_sem.at[0])
    own.start()
    for k, step in enumerate((2, -2, 1, -1)):
        z_push(k, bsend, chunk(-step), step)

    own_cols = pltpu.make_async_copy(send.at[row], strip_rows(0), own_sem.at[1])
    own_cols.start()

    for kind, place_of in enumerate((1, 0, 2, 3)):
        for s in range(2):
            wall[place_of * 128 + s * 64:place_of * 128 + s * 64 + 64, :] = wbuf[s, kind * 64:kind * 64 + 64, :]
    together = (
        lax.div(lax.broadcasted_iota(jnp.int32, (128, 128), 0), 32)
        == lax.div(lax.broadcasted_iota(jnp.int32, (128, 128), 1), 32)
    ).astype(F32).astype(BF16)

    key_head = lax.div(lax.broadcasted_iota(jnp.int32, (128, 128), 0), 32)
    side_of = lax.div(lax.broadcasted_iota(jnp.int32, (128, 128), 1), 64)
    key_here = [(key_head == 2 * n + side_of).astype(F32).astype(BF16) for n in range(2)]
    lane_head = lax.div(lax.broadcasted_iota(jnp.int32, (64, 128), 1), 32)
    value_here = [(lane_head == h).astype(F32).astype(BF16) for h in range(4)]

    def project(step):
        source = ring(row + step, 8)
        first_block = 2 * slot(step)
        rows = pl.ds(pl.multiple_of(source * 128, 128), 128)

        def one(jj, carry):
            value = strip[jj, rows, :]
            keys = lax.dot_general(wall[0:128, :], value, NT, preferred_element_type=F32)
            left = lax.dot_general(value, wall[128:256, :], NT, preferred_element_type=F32)
            right = lax.dot_general(value, wall[256:512, :], NT, preferred_element_type=F32)
            query = left * SCALE
            qg_ref[0, jj, rows, :] = query.astype(BF16)
            qg_ref[1, jj, rows, :] = jax.nn.sigmoid(right[:, 128:]).astype(BF16)
            short = keys.astype(BF16)
            values = right[:, :128].astype(BF16)
            for odd in range(2):
                twice = jnp.concatenate([short[:, odd * 64:odd * 64 + 64]] * 2, axis=1)
                for n in range(2):
                    kbd_ref[jj, first_block + odd, :, n * 128:(n + 1) * 128] = twice * key_here[n]
                for h in range(4):
                    vbd_ref[jj, first_block + odd, h * 64:(h + 1) * 64, :] = (
                        values[odd * 64:odd * 64 + 64, :] * value_here[h]
                    )
            lengths = jnp.dot((query * query).astype(BF16), together, preferred_element_type=F32)
            tops[0:1, :] = jnp.maximum(tops[0:1, :], jnp.max(lengths, axis=0, keepdims=True))
            lengths = jnp.dot(together, (keys * keys).astype(BF16), preferred_element_type=F32)
            tops[1:2, :] = jnp.maximum(tops[1:2, :], jnp.max(lengths, axis=0, keepdims=True))
            return carry

        lax.fori_loop(0, 4, one, 0, unroll=True)

    def take(step):
        arrive(strip_rows(step), col_send.at[(8 - step) % 8], col_recv.at[(8 - step) % 8])
        project(step)

    def make_lists():
        mixing_ref[...] = w_out_ref[...].astype(F32).T.astype(BF16)
        part = mask_ref[...].astype(F32)
        place_ = lax.div(lax.broadcasted_iota(jnp.int32, (16, 128), 1), 2)
        away = lax.div(place_ + 1, 2) * (2 * lax.rem(place_, 2) - 1)
        there = 2 * lax.rem(row + away + 8, 8) + lax.rem(lax.broadcasted_iota(jnp.int32, (16, 128), 1), 2)
        inside = lax.broadcasted_iota(jnp.int32, (16, 128), 1) < 16
        turned = (inside & (lax.broadcasted_iota(jnp.int32, (16, 128), 0) == there)).astype(F32).astype(BF16)
        diagonal = lax.broadcasted_iota(jnp.int32, (16, 16), 0) == lax.broadcasted_iota(jnp.int32, (16, 16), 1)
        part = jnp.where((part == 1.0) | diagonal, 1.0, 0.0)
        allowed = jnp.dot(part.astype(BF16), turned, preferred_element_type=F32)
        before = [jnp.zeros((1, 128), F32)]
        for i in range(16):
            before.append(before[-1] + allowed[i:i + 1, :])
        rank = jnp.concatenate(before[:16], axis=0)
        pairs = jnp.broadcast_to(jnp.floor(before[16] * 0.5), (16, 128))
        single = jnp.broadcast_to(before[16], (16, 128)) - 2.0 * pairs
        alone = allowed * jnp.where(rank == 2.0 * pairs, 1.0, 0.0)
        allowed = allowed - alone
        earlier = (
            lax.broadcasted_iota(jnp.int32, (128, 128), 0) < lax.broadcasted_iota(jnp.int32, (128, 128), 1)
        ).astype(F32).astype(BF16)
        start = jnp.dot(pairs.astype(BF16), earlier, preferred_element_type=F32)
        total = jnp.sum(pairs[0:1, :], axis=1, keepdims=True)
        single_start = jnp.dot(single.astype(BF16), earlier, preferred_element_type=F32)
        singles = jnp.sum(single[0:1, :], axis=1, keepdims=True)
        rank = rank + 2.0 * start
        entry = 2.0 * lax.broadcasted_iota(jnp.int32, (16, 128), 1).astype(F32)
        number = lax.broadcasted_iota(jnp.int32, (16, 128), 0).astype(F32)
        block = jnp.zeros((16, 128), F32)
        single_block = jnp.zeros((16, 128), F32)
        single_picked = jnp.zeros((16, 128), F32)
        single_found = jnp.zeros((16, 128), F32)
        picked = [jnp.zeros((16, 128), F32)] * 2
        found = [jnp.zeros((16, 128), F32)] * 2
        for k in range(16):
            at = jnp.broadcast_to(rank[:, k:k + 1], (16, 128))
            here = jnp.broadcast_to(allowed[:, k:k + 1], (16, 128))
            for side in range(2):
                hit = jnp.where(at == entry + side, here, 0.0)
                found[side] = found[side] + hit
                picked[side] = picked[side] + hit * number
                if side == 0:
                    block = block + hit * k
            at = jnp.broadcast_to(single_start[:, k:k + 1], (16, 128))
            here = jnp.broadcast_to(alone[:, k:k + 1], (16, 128))
            hit = jnp.where(2.0 * at == entry, here, 0.0)
            single_found = single_found + hit
            single_picked = single_picked + hit * number
            single_block = single_block + hit * k
        rows = [jnp.sum(block, axis=0, keepdims=True)]
        for side in range(2):
            missing = 1.0 - jnp.sum(found[side], axis=0, keepdims=True)
            rows.append(jnp.sum(picked[side], axis=0, keepdims=True) + (16.0 + side) * missing)
        rows.append(jnp.broadcast_to(total, (1, 128)))
        missing = 1.0 - jnp.sum(single_found, axis=0, keepdims=True)
        rows.append(jnp.sum(single_block, axis=0, keepdims=True))
        rows.append(jnp.sum(single_picked, axis=0, keepdims=True) + 16.0 * missing)
        rows.append(jnp.broadcast_to(singles, (1, 128)))
        rows.append(jnp.zeros((1, 128), F32))
        lists_ref[...] = jnp.concatenate(rows, axis=0).astype(jnp.int32)

    own_cols.wait()
    project(0)
    make_lists()
    own.wait()
    for k, step in enumerate((-2, 2, -1, 1)):
        z_arrive(k, chunk(step))
    z_push(4, chunk(-2), chunk(-3), 1)
    z_push(5, chunk(2), chunk(3), -1)
    z_push(6, chunk(-2, 0, 1), chunk(4, 0, 1), 2)
    z_push(7, chunk(2, 1, 1), chunk(4, 1, 1), -2)

    def far_bias():
        z_arrive(4, chunk(-3))
        z_arrive(5, chunk(3))
        z_arrive(6, chunk(4, 0, 1))
        z_arrive(7, chunk(4, 1, 1))

    def node(run, a, b):
        return (a, b) if run == 0 else (b, a)

    first = (x, y)
    second = (y, x)

    def whole_of(span):
        return span[0], span[2] - span[0]

    def halves_of(span):
        return (span[0], span[1] - span[0]), (span[1], span[2] - span[1])

    def shipment(far, run, index, a, b, rows, to_a, to_b):
        k = far * 40 + run * 20 + index
        ref = unit(*node(run, a, b), run, *rows)
        push(ref, ref, g_send.at[k], g_recv.at[k], place(*node(run, to_a, to_b)))

    def receive(far, run, index, a, b, rows):
        k = far * 40 + run * 20 + index
        arrive(unit(*node(run, a, b), run, *rows), g_send.at[k], g_recv.at[k])

    def to_sibling(run, u, v):
        k = run * 16 + u * 4 + v
        a, b = ring(first[run] + (0, -1, 1, 2)[u], 4), ring(second[run] + (0, -1, 1, 2)[v], 4)
        ref = unit(*node(run, a, b), run, 0, 8)
        push(ref, ref, s_send.at[k], s_recv.at[k], place(x, y, 1 - core))

    def begin(far, run):
        a, b, rows = first[run], second[run], whole_of(spans[far])
        shipment(far, run, 0, a, b, rows, ring(a + 1, 4), b)
        shipment(far, run, 1, a, b, rows, ring(a - 1, 4), b)

    def across(far, run, u):
        a, b, rows = ring(first[run] + (0, -1, 1, 2)[u], 4), second[run], whole_of(spans[far])
        shipment(far, run, 4 + 4 * u, a, b, rows, first[run], ring(b + 1, 4))
        shipment(far, run, 5 + 4 * u, a, b, rows, first[run], ring(b - 1, 4))

    def pass_first(far, run):
        a, b, rows = first[run], second[run], whole_of(spans[far])
        low, high = halves_of(spans[far])
        receive(far, run, 0, ring(a - 1, 4), b, rows)
        shipment(far, run, 2, ring(a - 1, 4), b, low, ring(a + 1, 4), b)
        receive(far, run, 1, ring(a + 1, 4), b, rows)
        shipment(far, run, 3, ring(a + 1, 4), b, high, ring(a - 1, 4), b)

    def end_first(far, run):
        a, b = ring(first[run] + 2, 4), second[run]
        low, high = halves_of(spans[far])
        receive(far, run, 2, a, b, low)
        receive(far, run, 3, a, b, high)

    def pass_second(far, run, u):
        a, b, rows = ring(first[run] + (0, -1, 1, 2)[u], 4), second[run], whole_of(spans[far])
        low, high = halves_of(spans[far])
        receive(far, run, 4 + 4 * u, a, ring(b - 1, 4), rows)
        shipment(far, run, 6 + 4 * u, a, ring(b - 1, 4), low, first[run], ring(b + 1, 4))
        receive(far, run, 5 + 4 * u, a, ring(b + 1, 4), rows)
        shipment(far, run, 7 + 4 * u, a, ring(b + 1, 4), high, first[run], ring(b - 1, 4))

    def end_second(far, run, u):
        a, b = ring(first[run] + (0, -1, 1, 2)[u], 4), ring(second[run] + 2, 4)
        low, high = halves_of(spans[far])
        receive(far, run, 6 + 4 * u, a, b, low)
        receive(far, run, 7 + 4 * u, a, b, high)

    for run in range(2):
        begin(0, run)
    for run in range(2):
        across(0, run, 0)
    for step in (2, 6, 3, 5, 4):
        col_push(step)
    take(1)
    take(-1)
    far_bias()
    for run in range(2):
        begin(1, run)
    for run in range(2):
        across(1, run, 0)
    for run in range(2):
        to_sibling(run, 0, 0)
    for far in range(2):
        for run in range(2):
            pass_first(far, run)
        for run in range(2):
            across(far, run, 1)
            across(far, run, 2)
    for run in range(2):
        to_sibling(run, 1, 0)
        to_sibling(run, 2, 0)
    for far in range(2):
        for run in range(2):
            end_first(far, run)
            across(far, run, 3)
    for run in range(2):
        to_sibling(run, 3, 0)
    take(2)
    for u in range(4):
        for far in range(2):
            for run in range(2):
                pass_second(far, run, u)
        for run in range(2):
            to_sibling(run, u, 1)
            to_sibling(run, u, 2)
        if u == 1:
            take(-2)
        if u == 3:
            take(3)
    for u in range(4):
        for run in range(2):
            for far in range(2):
                end_second(far, run, u)
            to_sibling(run, u, 3)
        if u == 2:
            take(-3)
    take(4)
    bound_ref[0:8, :] = tops[...]
    bound_ref[8:24, :] = jnp.broadcast_to(jnp.sum(weighted * weighted, axis=1, keepdims=True), (16, 128))
    for run in range(2):
        for u in range(4):
            for v in range(4):
                a = ring(first[run] + (0, -1, 1, 2)[u], 4)
                b = ring(second[run] + (0, -1, 1, 2)[v], 4)
                k = run * 16 + u * 4 + v
                arrive(unit(*node(run, a, b), run, 0, 8, 1 - core), s_send.at[k], s_recv.at[k])
    for copy in sent:
        copy.wait_send()


def spread(*operands):
    whole = pl.BlockSpec(memory_space=VMEM)
    return pl.pallas_call(
        spread_kernel,
        out_shape=(
            jax.ShapeDtypeStruct((2, 4, 1024, 128), BF16),
            jax.ShapeDtypeStruct((4, 16, 128, 256), BF16),
            jax.ShapeDtypeStruct((4, 16, 256, 128), BF16),
            jax.ShapeDtypeStruct((2, 2, 4, 2, 2, 8, 32, 256), BF16),
            jax.ShapeDtypeStruct((24, 128), F32),
            jax.ShapeDtypeStruct((128, 128), BF16),
            jax.ShapeDtypeStruct((8, 128), jnp.int32),
        ),
        in_specs=[pl.BlockSpec(memory_space=pltpu.HBM)] * len(operands),
        out_specs=(whole,) * 7,
        scratch_shapes=[
            VMEM((128, 32, 128), BF16),
            VMEM((1, 128), F32),
            VMEM((2, 128), BF16),
            VMEM((8, 128), jnp.int32),
            VMEM((128, 128), BF16),
            VMEM((16, 16), jnp.int32),
            VMEM((4096, 128), F32),
            VMEM((8, 4, 128, 128), BF16),
            VMEM((4, 1024, 128), BF16),
            VMEM((2, 272, 128), BF16),
            VMEM((512, 128), BF16),
            VMEM((256, 128), F32),
            VMEM((2, 32, 256), BF16),
            VMEM((8, 128), F32),
            DMA((10,)), DMA((8,)), DMA((8,)), DMA((8,)), DMA((8,)), DMA, DMA,
            DMA((80,)), DMA((80,)), DMA((32,)), DMA((32,)), DMA((2,)),
        ],
        compiler_params=pltpu.CompilerParams(
            collective_id=0, has_side_effects=True, vmem_limit_bytes=32 * 1024 * 1024
        ),
        name="spread",
    )(*operands)


def attend_kernel(
    lists_ref, qg_ref, kbd, vbd, bias, bound_ref,
    acc0, acc1, acc2, acc3,
    peak,
):
    accs = (acc0, acc1, acc2, acc3)
    for acc in accs:
        acc[...] = jnp.zeros_like(acc)
    same = (
        lax.div(lax.broadcasted_iota(jnp.int32, (256, 128), 0), 64)
        == lax.div(lax.broadcasted_iota(jnp.int32, (256, 128), 1), 32)
    ).astype(F32).astype(BF16)

    reach = jnp.sqrt(jnp.max(bound_ref[0:1, :])) * jnp.sqrt(jnp.max(bound_ref[1:2, :]))
    bias_reach = jnp.sqrt(jnp.max(bound_ref[8:24, :])) * (math.sqrt(128) * LOG2E)
    safe = (reach + bias_reach) * 1.03 <= SAFE

    def query(j, i):
        return qg_ref[0, j, pl.ds(pl.multiple_of(jnp.minimum(i, 15) * 64, 64), 64), :]

    def values_of(j, block):
        return jnp.concatenate([vbd[j, block], same], axis=1)

    def offset_of(i, block):
        at = (lax.rem(block, 2), jnp.minimum(i, 15))
        n = lax.div(block, 2)
        return [bias[at[0], at[1], half, n].astype(F32) for half in range(2)]

    total_pairs = lists_ref[3, 0]

    @pl.when(safe)
    def _():
        def pairs_from(first, count):
            work = []
            for side in range(count):
                e = first + side
                block = lists_ref[0, e]
                ids = (lists_ref[1, e], lists_ref[2, e])
                offset = jnp.concatenate(offset_of(ids[0], block) + offset_of(ids[1], block), axis=0)
                work.append((block, ids, offset))
            for j in range(4):
                for block, ids, offset in work:
                    queries = jnp.concatenate([query(j, i) for i in ids], axis=0)
                    score = jnp.dot(queries, kbd[j, block], preferred_element_type=F32)
                    weights = jnp.exp2(score + offset).astype(BF16)
                    total = jnp.dot(weights, values_of(j, block), preferred_element_type=F32)
                    olds = [accs[j][i] for i in ids]
                    for n in range(2):
                        accs[j][ids[n]] = olds[n] + total[n * 64:(n + 1) * 64, :]

        def four_step(t, carry):
            pairs_from(4 * t, 4)
            return carry

        def two_step(t, carry):
            pairs_from(2 * t, 2)
            return carry

        def single_step(t, carry):
            for j in range(4):
                for side in range(4):
                    e = 4 * t + side
                    block = lists_ref[4, e]
                    i = lists_ref[5, e]
                    offset = jnp.concatenate(offset_of(i, block), axis=0)
                    score = jnp.dot(query(j, i), kbd[j, block], preferred_element_type=F32)
                    weights = jnp.exp2(score + offset).astype(BF16)
                    total = jnp.dot(weights, values_of(j, block), preferred_element_type=F32)
                    accs[j][i] = accs[j][i] + total
            return carry

        fours = lax.div(total_pairs, 4)
        lax.fori_loop(0, fours, four_step, 0)
        lax.fori_loop(2 * fours, lax.div(total_pairs + 1, 2), two_step, 0)
        lax.fori_loop(0, lax.div(lists_ref[6, 0] + 3, 4), single_step, 0)

    @pl.when(jnp.logical_not(safe))
    def _():
        peak[...] = jnp.full_like(peak, -1e30)

        def step(n, carry):
            e = jnp.where(n < 2 * total_pairs, lax.div(n, 2), n - 2 * total_pairs)
            line = jnp.where(n < 2 * total_pairs, lax.rem(n, 2), 4)
            block = lists_ref[jnp.where(line == 4, 4, 0), e]
            i = lists_ref[1 + line, e]
            offset = jnp.concatenate(offset_of(i, block), axis=0)
            for j in range(4):
                score = jnp.dot(query(j, i), kbd[j, block], preferred_element_type=F32) + offset
                old = peak[j, i]
                tops = [
                    jnp.maximum(
                        jnp.max(score[:, h * 64:(h + 1) * 64], axis=1, keepdims=True),
                        old[:, h * 32:h * 32 + 1],
                    )
                    for h in range(4)
                ]
                shift = jnp.concatenate([jnp.broadcast_to(top, (64, 64)) for top in tops], axis=1)
                fresh = jnp.concatenate([jnp.broadcast_to(top, (64, 32)) for top in tops], axis=1)
                decay = jnp.exp2(old - fresh)
                weights = jnp.exp2(score - shift).astype(BF16)
                total = jnp.dot(weights, values_of(j, block), preferred_element_type=F32)
                accs[j][i] = accs[j][i] * jnp.concatenate([decay, decay], axis=1) + total
                peak[j, i] = fresh
            return carry

        lax.fori_loop(0, 2 * total_pairs + lists_ref[6, 0], step, 0)


def attend(lists, qg, kbd, vbd, bias, bound):
    whole = pl.BlockSpec(memory_space=VMEM)
    return pl.pallas_call(
        attend_kernel,
        out_shape=[jax.ShapeDtypeStruct((18, 64, 256), F32)] * 4,
        in_specs=[pl.BlockSpec(memory_space=pltpu.SMEM)] + [whole] * 5,
        out_specs=[whole] * 4,
        scratch_shapes=[VMEM((4, 18, 64, 128), F32)],
        compiler_params=pltpu.CompilerParams(vmem_limit_bytes=24 * 1024 * 1024),
        name="attend",
    )(lists, qg, kbd, vbd, bias, bound)


def deliver_kernel(
    acc0, acc1, acc2, acc3, qg_ref, mixing_ref, out_ref,
    update_ref, relay, send_sem, recv_sem, own_sem,
):
    row = lax.axis_index("row")
    col = lax.axis_index("col")
    head = lax.axis_index("head")

    def other(flip):
        return (1 - head) if flip else head

    def device(step, flip):
        return (ring(row + step, 8), col, other(flip))

    steps = (4, 3, 5, 2, 6, 1, 7, 0)
    partner = device(0, 1)
    peers = [partner] + [device(step, 0) for step in steps if step]
    barrier = pltpu.get_barrier_semaphore()
    for peer in peers:
        pl.semaphore_signal(barrier, inc=1, device_id=peer, device_id_type=MESH)

    def spot(step, flip):
        return out_ref.at[pl.ds((other(flip) * 8 + ring(row + step, 8)) * 4, 4)]

    def part(step, flip):
        return update_ref.at[other(flip), ring(row + step, 8)]

    def finish(step):
        target = ring(row + step, 8)
        rows = pl.ds(pl.multiple_of(target * 128, 128), 128)
        for j, acc in enumerate((acc0, acc1, acc2, acc3)):
            sums = acc[pl.ds(target * 2, 2)].reshape(128, 256)
            attention = sums[:, :128] / sums[:, 128:]
            gated = (attention * qg_ref[1, j, rows, :].astype(F32)).astype(BF16)
            update = lax.dot_general(mixing_ref[...], gated, NT, preferred_element_type=F32).astype(BF16)
            update_ref[0, target, j] = update[:64, :]
            update_ref[1, target, j] = update[64:, :]

    copies = []

    def push(k, src, dst, target):
        copy = pltpu.make_async_remote_copy(
            src_ref=src, dst_ref=dst, send_sem=send_sem.at[k], recv_sem=recv_sem.at[k],
            device_id=target, device_id_type=MESH,
        )
        copy.start()
        copies.append(copy)

    def arrive(k, ref):
        pltpu.make_async_remote_copy(
            src_ref=ref, dst_ref=ref, send_sem=send_sem.at[k], recv_sem=recv_sem.at[k],
            device_id=partner, device_id_type=MESH,
        ).wait_recv()

    for step in (4, 3, 5):
        finish(step)
    pl.semaphore_wait(barrier, len(peers))
    for step in steps:
        if step not in (4, 3, 5):
            finish(step)
        if step:
            push(step, part(step, 1), relay.at[step - 1], partner)
            push(8 + step, part(step, 0), spot(0, 0), device(step, 0))
        else:
            push(0, part(0, 1), spot(0, 0), partner)
    own = pltpu.make_async_copy(part(0, 0), spot(0, 0), own_sem)
    own.start()
    for step in steps[:-1]:
        arrive(step, relay.at[step - 1])
        push(16 + step, relay.at[step - 1], spot(0, 1), device(step, 0))
    own.wait()
    arrive(0, spot(0, 1))
    for step in steps[:-1]:
        arrive(8 + step, spot(-step, 0))
    for step in steps[:-1]:
        arrive(16 + step, spot(-step, 1))
    for copy in copies:
        copy.wait_send()


def deliver(accs, qg, mixing):
    whole = pl.BlockSpec(memory_space=VMEM)
    return pl.pallas_call(
        deliver_kernel,
        out_shape=jax.ShapeDtypeStruct((64, 64, 128), BF16),
        in_specs=[whole] * 6,
        out_specs=whole,
        scratch_shapes=[VMEM((2, 8, 4, 64, 128), BF16), VMEM((7, 4, 64, 128), BF16), DMA((24,)), DMA((24,)), DMA],
        compiler_params=pltpu.CompilerParams(
            collective_id=1, has_side_effects=True, vmem_limit_bytes=16 * 1024 * 1024
        ),
        name="deliver",
    )(*accs, qg, mixing)


def per_device(
    pair_field, ln_gain, w_query, w_key, w_value, w_gate, w_bias, w_out, tile_mask, type_ids
):
    weights = [w.T for w in (w_query, w_key, w_value, w_gate)]
    weights.append(w_bias.T)
    operands = (pair_field, ln_gain.reshape(1, 128), *weights, type_ids.reshape(8, 128), w_out, tile_mask)
    qg, kbd, vbd, bias, bound, mixing, lists = spread(
        *[pltpu.with_memory_space_constraint(operand, pltpu.HBM) for operand in operands]
    )
    accs = attend(lists, qg, kbd, vbd, bias.reshape(2, 16, 2, 8, 32, 256), bound)
    return jnp.transpose(deliver(accs, qg, mixing), (2, 0, 1))


def solution(mesh):
    return jax.shard_map(
        per_device,
        mesh=mesh,
        in_specs=(
            P("row", "col", None),
            P(),
            P(None, "head"),
            P(None, "head"),
            P(None, "head"),
            P(None, "head"),
            P(None, "head"),
            P(),
            P(),
            P(),
        ),
        out_specs=P("row", "col", "head"),
        check_vma=False,
    )
```

```python
import math

import jax
import jax.numpy as jnp
from jax import lax
from jax.experimental import pallas as pl
from jax.experimental.pallas import tpu as pltpu
from jax.sharding import PartitionSpec as P

MESH = pl.DeviceIdType.MESH
F32 = jnp.float32
BF16 = jnp.bfloat16
VMEM = pltpu.VMEM
DMA = pltpu.SemaphoreType.DMA

epsilon = 1e-05
masked_score = -1000000000.0
LOG2E = math.log2(math.e)
SCALE = LOG2E / math.sqrt(32)
SAFE = 64.0
NT = (((1,), (1,)), ((), ()))


def ring(value, size):
    return lax.rem(value + size, size)


def spread_kernel(
    tile_ref, gain_in, wq_ref, wk_ref, wv_ref, wg_ref, wb_in, types_in, w_out_in, mask_in,
    qg_ref, kbd_ref, vbd_ref, bias_ref, bound_ref, mixing_ref, lists_ref,
    half, gain_ref, wb_ref, types_ref, w_out_ref, mask_ref, wide, send, strip, wbuf, wall, flat, bsend, tops,
    load_sem, col_send, col_recv, z_send, z_recv, w_send, w_recv,
    g_send, g_recv, s_send, s_recv, own_sem,
):
    row = lax.axis_index("row")
    col = lax.axis_index("col")
    head = lax.axis_index("head")
    core = lax.rem(col, 2)
    x = lax.rem(lax.div(col, 2), 4)
    y = head * 2 + lax.div(col, 8)

    def place(x_, y_, core_=None):
        return (row, lax.rem(y_, 2) * 8 + x_ * 2 + (core if core_ is None else core_), lax.div(y_, 2))

    def along_z(step):
        return (ring(row + step, 8), col, head)

    partner = place(x, ring(y + 2, 4))
    peers = [along_z(step) for step in range(1, 8)]
    peers += [place(ring(x + 1, 4), y), place(ring(x - 1, 4), y)]
    peers += [place(x, ring(y + 1, 4)), place(x, ring(y - 1, 4)), partner]
    peers += [place(x, y, 1 - core)]
    barrier = pltpu.get_barrier_semaphore()
    for peer in peers:
        pl.semaphore_signal(barrier, inc=1, device_id=peer, device_id_type=MESH)

    loads = [
        (tile_ref.at[:, pl.ds(pl.multiple_of(head * 32, 32), 32), :], half),
        (gain_in, gain_ref), (wb_in, wb_ref), (types_in, types_ref),
    ]
    loads += [
        (ref, wbuf.at[head, pl.ds(kind * 64, 64)]) for kind, ref in enumerate((wq_ref, wk_ref, wv_ref, wg_ref))
    ]
    loads += [(w_out_in, w_out_ref), (mask_in, mask_ref)]
    loads = [pltpu.make_async_copy(src, dst, load_sem.at[n]) for n, (src, dst) in enumerate(loads)]
    for load in loads:
        load.start()
    tops[...] = jnp.zeros_like(tops)
    loads[0].wait()

    def widen(block, carry):
        rows = half[pl.ds(block * 8, 8)].astype(F32).reshape(256, 128)
        wide[pl.ds(pl.multiple_of(block * 256, 256), 256), :] = rows
        return carry

    lax.fori_loop(0, 16, widen, 0)
    ones = jnp.ones((128, 128), BF16)
    loads[1].wait()
    gain = gain_ref[...]

    def norm_for(step):
        target = ring(row + step, 8)
        for jj in range(4):
            value = wide[pl.ds(4 * target + jj, 128, stride=32), :]
            mean = jnp.dot(value.astype(BF16), ones, preferred_element_type=F32) * (1.0 / 128)
            centred = value - mean
            squares = (centred * centred).astype(BF16)
            spread = jnp.dot(squares, ones, preferred_element_type=F32) * (1.0 / 128)
            normed = centred * lax.rsqrt(spread + epsilon) * gain
            send[target, jj] = normed.astype(BF16)

    def norm_near(n, carry):
        norm_for(n)
        norm_for(-n)
        return carry

    def norm_far(n, carry):
        norm_for(3 + n)
        norm_for(-3 * (1 - n))
        return carry

    lax.fori_loop(1, 3, norm_near, 0)
    for load in loads[2:]:
        load.wait()
    wbuf[head, 256:272, :] = jnp.concatenate(
        [wb_ref[...].astype(F32), jnp.zeros((14, 128), F32)], axis=0
    ).astype(BF16)
    pl.semaphore_wait(barrier, len(peers))
    w_copy = pltpu.make_async_remote_copy(
        src_ref=wbuf.at[head], dst_ref=wbuf.at[head], send_sem=w_send, recv_sem=w_recv,
        device_id=partner, device_id_type=MESH,
    )
    w_copy.start()
    sent = [w_copy]

    def push(src, dst, send_sem, recv_sem, device):
        copy = pltpu.make_async_remote_copy(
            src_ref=src, dst_ref=dst, send_sem=send_sem, recv_sem=recv_sem,
            device_id=device, device_id_type=MESH,
        )
        copy.start()
        sent.append(copy)

    def strip_rows(step):
        source = ring(row + step, 8)
        return strip.at[:, pl.ds(pl.multiple_of(source * 128, 128), 128), :]

    def col_push(step):
        target = ring(row + step, 8)
        push(send.at[target], strip_rows(0), col_send.at[step], col_recv.at[step], along_z(step))

    col_push(1)
    col_push(7)
    lax.fori_loop(0, 2, norm_far, 0)
    pltpu.make_async_remote_copy(
        src_ref=wbuf.at[1 - head], dst_ref=wbuf.at[1 - head], send_sem=w_send, recv_sem=w_recv,
        device_id=partner, device_id_type=MESH,
    ).wait_recv()

    wb = wbuf[0, 256:272, :].astype(F32) + pltpu.roll(wbuf[1, 256:272, :].astype(F32), 2, 0)
    weighted = wb * gain
    wbt = wb.astype(BF16)

    def bias_for(target, carry):
        part = lax.dot_general(wbt, send[target].reshape(512, 128), NT, preferred_element_type=F32)
        for jj in range(4):
            flat[pl.ds(pl.multiple_of((4 * target + jj) * 8, 8), 8), :] = part[0:8, jj * 128:jj * 128 + 128]
        return carry

    lax.fori_loop(0, 8, bias_for, 0, unroll=4)
    living = jnp.broadcast_to(types_ref[pl.ds(row, 1), :] != 0, (32, 128))
    by_head = [
        jnp.where(living, flat[pl.ds(h, 32, stride=8), :] * LOG2E, masked_score) for h in range(4)
    ]
    bsend[0] = jnp.concatenate([b[:, :64] for b in by_head], axis=1).astype(BF16)
    bsend[1] = jnp.concatenate([b[:, 64:] for b in by_head], axis=1).astype(BF16)

    def unit(x_, y_, run, low, count, core_=None):
        return bias_ref.at[
            run, lax.rem(y_, 2), x_, core if core_ is None else core_, lax.div(y_, 2), pl.ds(low, count)
        ]

    def arrive(dst, send_sem, recv_sem):
        pltpu.make_async_remote_copy(
            src_ref=dst, dst_ref=dst, send_sem=send_sem, recv_sem=recv_sem,
            device_id=partner, device_id_type=MESH,
        ).wait_recv()

    def slot(step):
        return 2 * step - 1 if step > 0 else -2 * step

    spans = ((0, 2, 5), (5, 7, 8))

    def chunk(step, low=0, count=2):
        return bias_ref.at[pl.ds(low, count), lax.rem(y, 2), x, core, lax.div(y, 2), slot(step)]

    def z_push(k, src, dst, step):
        push(src, dst, z_send.at[k], z_recv.at[k], along_z(step))

    def z_arrive(k, dst):
        arrive(dst, z_send.at[k], z_recv.at[k])

    own = pltpu.make_async_copy(bsend, chunk(0), own_sem.at[0])
    own.start()
    for k, step in enumerate((2, -2, 1, -1)):
        z_push(k, bsend, chunk(-step), step)

    own_cols = pltpu.make_async_copy(send.at[row], strip_rows(0), own_sem.at[1])
    own_cols.start()

    for kind, place_of in enumerate((1, 0, 2, 3)):
        for s in range(2):
            wall[place_of * 128 + s * 64:place_of * 128 + s * 64 + 64, :] = wbuf[s, kind * 64:kind * 64 + 64, :]
    together = (
        lax.div(lax.broadcasted_iota(jnp.int32, (128, 128), 0), 32)
        == lax.div(lax.broadcasted_iota(jnp.int32, (128, 128), 1), 32)
    ).astype(F32).astype(BF16)

    key_head = lax.div(lax.broadcasted_iota(jnp.int32, (128, 128), 0), 32)
    side_of = lax.div(lax.broadcasted_iota(jnp.int32, (128, 128), 1), 64)
    key_here = [(key_head == 2 * n + side_of).astype(F32).astype(BF16) for n in range(2)]
    lane_head = lax.div(lax.broadcasted_iota(jnp.int32, (64, 128), 1), 32)
    value_here = [(lane_head == h).astype(F32).astype(BF16) for h in range(4)]

    def project(step):
        source = ring(row + step, 8)
        first_block = 2 * slot(step)
        rows = pl.ds(pl.multiple_of(source * 128, 128), 128)

        def one(jj, carry):
            value = strip[jj, rows, :]
            keys = lax.dot_general(wall[0:128, :], value, NT, preferred_element_type=F32)
            left = lax.dot_general(value, wall[128:256, :], NT, preferred_element_type=F32)
            right = lax.dot_general(value, wall[256:512, :], NT, preferred_element_type=F32)
            query = left * SCALE
            qg_ref[0, jj, rows, :] = query.astype(BF16)
            qg_ref[1, jj, rows, :] = jax.nn.sigmoid(right[:, 128:]).astype(BF16)
            short = keys.astype(BF16)
            values = right[:, :128].astype(BF16)
            for odd in range(2):
                twice = jnp.concatenate([short[:, odd * 64:odd * 64 + 64]] * 2, axis=1)
                for n in range(2):
                    kbd_ref[jj, first_block + odd, :, n * 128:(n + 1) * 128] = twice * key_here[n]
                for h in range(4):
                    vbd_ref[jj, first_block + odd, h * 64:(h + 1) * 64, :] = (
                        values[odd * 64:odd * 64 + 64, :] * value_here[h]
                    )
            lengths = jnp.dot((query * query).astype(BF16), together, preferred_element_type=F32)
            tops[0:1, :] = jnp.maximum(tops[0:1, :], jnp.max(lengths, axis=0, keepdims=True))
            lengths = jnp.dot(together, (keys * keys).astype(BF16), preferred_element_type=F32)
            tops[1:2, :] = jnp.maximum(tops[1:2, :], jnp.max(lengths, axis=0, keepdims=True))
            return carry

        lax.fori_loop(0, 4, one, 0, unroll=True)

    def take(step):
        arrive(strip_rows(step), col_send.at[(8 - step) % 8], col_recv.at[(8 - step) % 8])
        project(step)

    def make_lists():
        mixing_ref[...] = w_out_ref[...].astype(F32).T.astype(BF16)
        part = mask_ref[...].astype(F32)
        place_ = lax.div(lax.broadcasted_iota(jnp.int32, (16, 128), 1), 2)
        away = lax.div(place_ + 1, 2) * (2 * lax.rem(place_, 2) - 1)
        there = 2 * lax.rem(row + away + 8, 8) + lax.rem(lax.broadcasted_iota(jnp.int32, (16, 128), 1), 2)
        inside = lax.broadcasted_iota(jnp.int32, (16, 128), 1) < 16
        turned = (inside & (lax.broadcasted_iota(jnp.int32, (16, 128), 0) == there)).astype(F32).astype(BF16)
        diagonal = lax.broadcasted_iota(jnp.int32, (16, 16), 0) == lax.broadcasted_iota(jnp.int32, (16, 16), 1)
        part = jnp.where((part == 1.0) | diagonal, 1.0, 0.0)
        allowed = jnp.dot(part.astype(BF16), turned, preferred_element_type=F32)
        before = [jnp.zeros((1, 128), F32)]
        for i in range(16):
            before.append(before[-1] + allowed[i:i + 1, :])
        rank = jnp.concatenate(before[:16], axis=0)
        pairs = jnp.broadcast_to(jnp.floor(before[16] * 0.5), (16, 128))
        single = jnp.broadcast_to(before[16], (16, 128)) - 2.0 * pairs
        alone = allowed * jnp.where(rank == 2.0 * pairs, 1.0, 0.0)
        allowed = allowed - alone
        earlier = (
            lax.broadcasted_iota(jnp.int32, (128, 128), 0) < lax.broadcasted_iota(jnp.int32, (128, 128), 1)
        ).astype(F32).astype(BF16)
        start = jnp.dot(pairs.astype(BF16), earlier, preferred_element_type=F32)
        total = jnp.sum(pairs[0:1, :], axis=1, keepdims=True)
        single_start = jnp.dot(single.astype(BF16), earlier, preferred_element_type=F32)
        singles = jnp.sum(single[0:1, :], axis=1, keepdims=True)
        rank = rank + 2.0 * start
        entry = 2.0 * lax.broadcasted_iota(jnp.int32, (16, 128), 1).astype(F32)
        number = lax.broadcasted_iota(jnp.int32, (16, 128), 0).astype(F32)
        block = jnp.zeros((16, 128), F32)
        single_block = jnp.zeros((16, 128), F32)
        single_picked = jnp.zeros((16, 128), F32)
        single_found = jnp.zeros((16, 128), F32)
        picked = [jnp.zeros((16, 128), F32)] * 2
        found = [jnp.zeros((16, 128), F32)] * 2
        for k in range(16):
            at = jnp.broadcast_to(rank[:, k:k + 1], (16, 128))
            here = jnp.broadcast_to(allowed[:, k:k + 1], (16, 128))
            for side in range(2):
                hit = jnp.where(at == entry + side, here, 0.0)
                found[side] = found[side] + hit
                picked[side] = picked[side] + hit * number
                if side == 0:
                    block = block + hit * k
            at = jnp.broadcast_to(single_start[:, k:k + 1], (16, 128))
            here = jnp.broadcast_to(alone[:, k:k + 1], (16, 128))
            hit = jnp.where(2.0 * at == entry, here, 0.0)
            single_found = single_found + hit
            single_picked = single_picked + hit * number
            single_block = single_block + hit * k
        rows = [jnp.sum(block, axis=0, keepdims=True)]
        for side in range(2):
            missing = 1.0 - jnp.sum(found[side], axis=0, keepdims=True)
            rows.append(jnp.sum(picked[side], axis=0, keepdims=True) + (16.0 + side) * missing)
        rows.append(jnp.broadcast_to(total, (1, 128)))
        missing = 1.0 - jnp.sum(single_found, axis=0, keepdims=True)
        rows.append(jnp.sum(single_block, axis=0, keepdims=True))
        rows.append(jnp.sum(single_picked, axis=0, keepdims=True) + 16.0 * missing)
        rows.append(jnp.broadcast_to(singles, (1, 128)))
        rows.append(jnp.zeros((1, 128), F32))
        lists_ref[...] = jnp.concatenate(rows, axis=0).astype(jnp.int32)

    own_cols.wait()
    project(0)
    make_lists()
    own.wait()
    for k, step in enumerate((-2, 2, -1, 1)):
        z_arrive(k, chunk(step))
    z_push(4, chunk(-2), chunk(-3), 1)
    z_push(5, chunk(2), chunk(3), -1)
    z_push(6, chunk(-2, 0, 1), chunk(4, 0, 1), 2)
    z_push(7, chunk(2, 1, 1), chunk(4, 1, 1), -2)

    def far_bias():
        z_arrive(4, chunk(-3))
        z_arrive(5, chunk(3))
        z_arrive(6, chunk(4, 0, 1))
        z_arrive(7, chunk(4, 1, 1))

    def node(run, a, b):
        return (a, b) if run == 0 else (b, a)

    first = (x, y)
    second = (y, x)

    def whole_of(span):
        return span[0], span[2] - span[0]

    def halves_of(span):
        return (span[0], span[1] - span[0]), (span[1], span[2] - span[1])

    def shipment(far, run, index, a, b, rows, to_a, to_b):
        k = far * 40 + run * 20 + index
        ref = unit(*node(run, a, b), run, *rows)
        push(ref, ref, g_send.at[k], g_recv.at[k], place(*node(run, to_a, to_b)))

    def receive(far, run, index, a, b, rows):
        k = far * 40 + run * 20 + index
        arrive(unit(*node(run, a, b), run, *rows), g_send.at[k], g_recv.at[k])

    def to_sibling(run, u, v):
        k = run * 16 + u * 4 + v
        a, b = ring(first[run] + (0, -1, 1, 2)[u], 4), ring(second[run] + (0, -1, 1, 2)[v], 4)
        ref = unit(*node(run, a, b), run, 0, 8)
        push(ref, ref, s_send.at[k], s_recv.at[k], place(x, y, 1 - core))

    def begin(far, run):
        a, b, rows = first[run], second[run], whole_of(spans[far])
        shipment(far, run, 0, a, b, rows, ring(a + 1, 4), b)
        shipment(far, run, 1, a, b, rows, ring(a - 1, 4), b)

    def across(far, run, u):
        a, b, rows = ring(first[run] + (0, -1, 1, 2)[u], 4), second[run], whole_of(spans[far])
        shipment(far, run, 4 + 4 * u, a, b, rows, first[run], ring(b + 1, 4))
        shipment(far, run, 5 + 4 * u, a, b, rows, first[run], ring(b - 1, 4))

    def pass_first(far, run):
        a, b, rows = first[run], second[run], whole_of(spans[far])
        low, high = halves_of(spans[far])
        receive(far, run, 0, ring(a - 1, 4), b, rows)
        shipment(far, run, 2, ring(a - 1, 4), b, low, ring(a + 1, 4), b)
        receive(far, run, 1, ring(a + 1, 4), b, rows)
        shipment(far, run, 3, ring(a + 1, 4), b, high, ring(a - 1, 4), b)

    def end_first(far, run):
        a, b = ring(first[run] + 2, 4), second[run]
        low, high = halves_of(spans[far])
        receive(far, run, 2, a, b, low)
        receive(far, run, 3, a, b, high)

    def pass_second(far, run, u):
        a, b, rows = ring(first[run] + (0, -1, 1, 2)[u], 4), second[run], whole_of(spans[far])
        low, high = halves_of(spans[far])
        receive(far, run, 4 + 4 * u, a, ring(b - 1, 4), rows)
        shipment(far, run, 6 + 4 * u, a, ring(b - 1, 4), low, first[run], ring(b + 1, 4))
        receive(far, run, 5 + 4 * u, a, ring(b + 1, 4), rows)
        shipment(far, run, 7 + 4 * u, a, ring(b + 1, 4), high, first[run], ring(b - 1, 4))

    def end_second(far, run, u):
        a, b = ring(first[run] + (0, -1, 1, 2)[u], 4), ring(second[run] + 2, 4)
        low, high = halves_of(spans[far])
        receive(far, run, 6 + 4 * u, a, b, low)
        receive(far, run, 7 + 4 * u, a, b, high)

    for run in range(2):
        begin(0, run)
    for run in range(2):
        across(0, run, 0)
    for step in (4, 3, 5, 2, 6):
        col_push(step)
    take(1)
    take(-1)
    far_bias()
    for run in range(2):
        begin(1, run)
    for run in range(2):
        across(1, run, 0)
    for run in range(2):
        to_sibling(run, 0, 0)
    for far in range(2):
        for run in range(2):
            pass_first(far, run)
        for run in range(2):
            across(far, run, 1)
            across(far, run, 2)
    for run in range(2):
        to_sibling(run, 1, 0)
        to_sibling(run, 2, 0)
    for far in range(2):
        for run in range(2):
            end_first(far, run)
            across(far, run, 3)
    for run in range(2):
        to_sibling(run, 3, 0)
    take(4)
    for u in range(4):
        for far in range(2):
            for run in range(2):
                pass_second(far, run, u)
        for run in range(2):
            to_sibling(run, u, 1)
            to_sibling(run, u, 2)
        if u == 1:
            take(3)
        if u == 3:
            take(-3)
    for u in range(4):
        for run in range(2):
            for far in range(2):
                end_second(far, run, u)
            to_sibling(run, u, 3)
        if u == 2:
            take(2)
    take(-2)
    bound_ref[0:8, :] = tops[...]
    bound_ref[8:24, :] = jnp.broadcast_to(jnp.sum(weighted * weighted, axis=1, keepdims=True), (16, 128))
    for run in range(2):
        for u in range(4):
            for v in range(4):
                a = ring(first[run] + (0, -1, 1, 2)[u], 4)
                b = ring(second[run] + (0, -1, 1, 2)[v], 4)
                k = run * 16 + u * 4 + v
                arrive(unit(*node(run, a, b), run, 0, 8, 1 - core), s_send.at[k], s_recv.at[k])
    for copy in sent:
        copy.wait_send()


def spread(*operands):
    whole = pl.BlockSpec(memory_space=VMEM)
    return pl.pallas_call(
        spread_kernel,
        out_shape=(
            jax.ShapeDtypeStruct((2, 4, 1024, 128), BF16),
            jax.ShapeDtypeStruct((4, 16, 128, 256), BF16),
            jax.ShapeDtypeStruct((4, 16, 256, 128), BF16),
            jax.ShapeDtypeStruct((2, 2, 4, 2, 2, 8, 32, 256), BF16),
            jax.ShapeDtypeStruct((24, 128), F32),
            jax.ShapeDtypeStruct((128, 128), BF16),
            jax.ShapeDtypeStruct((8, 128), jnp.int32),
        ),
        in_specs=[pl.BlockSpec(memory_space=pltpu.HBM)] * len(operands),
        out_specs=(whole,) * 7,
        scratch_shapes=[
            VMEM((128, 32, 128), BF16),
            VMEM((1, 128), F32),
            VMEM((2, 128), BF16),
            VMEM((8, 128), jnp.int32),
            VMEM((128, 128), BF16),
            VMEM((16, 16), jnp.int32),
            VMEM((4096, 128), F32),
            VMEM((8, 4, 128, 128), BF16),
            VMEM((4, 1024, 128), BF16),
            VMEM((2, 272, 128), BF16),
            VMEM((512, 128), BF16),
            VMEM((256, 128), F32),
            VMEM((2, 32, 256), BF16),
            VMEM((8, 128), F32),
            DMA((10,)), DMA((8,)), DMA((8,)), DMA((8,)), DMA((8,)), DMA, DMA,
            DMA((80,)), DMA((80,)), DMA((32,)), DMA((32,)), DMA((2,)),
        ],
        compiler_params=pltpu.CompilerParams(
            collective_id=0, has_side_effects=True, vmem_limit_bytes=32 * 1024 * 1024
        ),
        name="spread",
    )(*operands)


def attend_kernel(
    lists_ref, qg_ref, kbd, vbd, bias, bound_ref,
    acc0, acc1, acc2, acc3,
    peak,
):
    accs = (acc0, acc1, acc2, acc3)
    for acc in accs:
        acc[...] = jnp.zeros_like(acc)
    same = (
        lax.div(lax.broadcasted_iota(jnp.int32, (256, 128), 0), 64)
        == lax.div(lax.broadcasted_iota(jnp.int32, (256, 128), 1), 32)
    ).astype(F32).astype(BF16)

    reach = jnp.sqrt(jnp.max(bound_ref[0:1, :])) * jnp.sqrt(jnp.max(bound_ref[1:2, :]))
    bias_reach = jnp.sqrt(jnp.max(bound_ref[8:24, :])) * (math.sqrt(128) * LOG2E)
    safe = (reach + bias_reach) * 1.03 <= SAFE

    def query(j, i):
        return qg_ref[0, j, pl.ds(pl.multiple_of(jnp.minimum(i, 15) * 64, 64), 64), :]

    def values_of(j, block):
        return jnp.concatenate([vbd[j, block], same], axis=1)

    def offset_of(i, block):
        at = (lax.rem(block, 2), jnp.minimum(i, 15))
        n = lax.div(block, 2)
        return [bias[at[0], at[1], half, n].astype(F32) for half in range(2)]

    total_pairs = lists_ref[3, 0]

    @pl.when(safe)
    def _():
        def pairs_from(first, count):
            work = []
            for side in range(count):
                e = first + side
                block = lists_ref[0, e]
                ids = (lists_ref[1, e], lists_ref[2, e])
                offset = jnp.concatenate(offset_of(ids[0], block) + offset_of(ids[1], block), axis=0)
                work.append((block, ids, offset))
            for j in range(4):
                for block, ids, offset in work:
                    queries = jnp.concatenate([query(j, i) for i in ids], axis=0)
                    score = jnp.dot(queries, kbd[j, block], preferred_element_type=F32)
                    weights = jnp.exp2(score + offset).astype(BF16)
                    total = jnp.dot(weights, values_of(j, block), preferred_element_type=F32)
                    olds = [accs[j][i] for i in ids]
                    for n in range(2):
                        accs[j][ids[n]] = olds[n] + total[n * 64:(n + 1) * 64, :]

        def four_step(t, carry):
            pairs_from(4 * t, 4)
            return carry

        def two_step(t, carry):
            pairs_from(2 * t, 2)
            return carry

        def single_step(t, carry):
            for j in range(4):
                for side in range(4):
                    e = 4 * t + side
                    block = lists_ref[4, e]
                    i = lists_ref[5, e]
                    offset = jnp.concatenate(offset_of(i, block), axis=0)
                    score = jnp.dot(query(j, i), kbd[j, block], preferred_element_type=F32)
                    weights = jnp.exp2(score + offset).astype(BF16)
                    total = jnp.dot(weights, values_of(j, block), preferred_element_type=F32)
                    accs[j][i] = accs[j][i] + total
            return carry

        fours = lax.div(total_pairs, 4)
        lax.fori_loop(0, fours, four_step, 0)
        lax.fori_loop(2 * fours, lax.div(total_pairs + 1, 2), two_step, 0)
        lax.fori_loop(0, lax.div(lists_ref[6, 0] + 3, 4), single_step, 0)

    @pl.when(jnp.logical_not(safe))
    def _():
        peak[...] = jnp.full_like(peak, -1e30)

        def step(n, carry):
            e = jnp.where(n < 2 * total_pairs, lax.div(n, 2), n - 2 * total_pairs)
            line = jnp.where(n < 2 * total_pairs, lax.rem(n, 2), 4)
            block = lists_ref[jnp.where(line == 4, 4, 0), e]
            i = lists_ref[1 + line, e]
            offset = jnp.concatenate(offset_of(i, block), axis=0)
            for j in range(4):
                score = jnp.dot(query(j, i), kbd[j, block], preferred_element_type=F32) + offset
                old = peak[j, i]
                tops = [
                    jnp.maximum(
                        jnp.max(score[:, h * 64:(h + 1) * 64], axis=1, keepdims=True),
                        old[:, h * 32:h * 32 + 1],
                    )
                    for h in range(4)
                ]
                shift = jnp.concatenate([jnp.broadcast_to(top, (64, 64)) for top in tops], axis=1)
                fresh = jnp.concatenate([jnp.broadcast_to(top, (64, 32)) for top in tops], axis=1)
                decay = jnp.exp2(old - fresh)
                weights = jnp.exp2(score - shift).astype(BF16)
                total = jnp.dot(weights, values_of(j, block), preferred_element_type=F32)
                accs[j][i] = accs[j][i] * jnp.concatenate([decay, decay], axis=1) + total
                peak[j, i] = fresh
            return carry

        lax.fori_loop(0, 2 * total_pairs + lists_ref[6, 0], step, 0)


def attend(lists, qg, kbd, vbd, bias, bound):
    whole = pl.BlockSpec(memory_space=VMEM)
    return pl.pallas_call(
        attend_kernel,
        out_shape=[jax.ShapeDtypeStruct((18, 64, 256), F32)] * 4,
        in_specs=[pl.BlockSpec(memory_space=pltpu.SMEM)] + [whole] * 5,
        out_specs=[whole] * 4,
        scratch_shapes=[VMEM((4, 18, 64, 128), F32)],
        compiler_params=pltpu.CompilerParams(vmem_limit_bytes=24 * 1024 * 1024),
        name="attend",
    )(lists, qg, kbd, vbd, bias, bound)


def deliver_kernel(
    acc0, acc1, acc2, acc3, qg_ref, mixing_ref, out_ref,
    update_ref, relay, send_sem, recv_sem, own_sem,
):
    row = lax.axis_index("row")
    col = lax.axis_index("col")
    head = lax.axis_index("head")

    def other(flip):
        return (1 - head) if flip else head

    def device(step, flip):
        return (ring(row + step, 8), col, other(flip))

    steps = (4, 3, 5, 2, 6, 1, 7, 0)
    partner = device(0, 1)
    peers = [partner] + [device(step, 0) for step in steps if step]
    barrier = pltpu.get_barrier_semaphore()
    for peer in peers:
        pl.semaphore_signal(barrier, inc=1, device_id=peer, device_id_type=MESH)

    def spot(step, flip):
        return out_ref.at[pl.ds((other(flip) * 8 + ring(row + step, 8)) * 4, 4)]

    def part(step, flip):
        return update_ref.at[other(flip), ring(row + step, 8)]

    def finish(step):
        target = ring(row + step, 8)
        rows = pl.ds(pl.multiple_of(target * 128, 128), 128)
        for j, acc in enumerate((acc0, acc1, acc2, acc3)):
            sums = acc[pl.ds(target * 2, 2)].reshape(128, 256)
            attention = sums[:, :128] / sums[:, 128:]
            gated = (attention * qg_ref[1, j, rows, :].astype(F32)).astype(BF16)
            update = lax.dot_general(mixing_ref[...], gated, NT, preferred_element_type=F32).astype(BF16)
            update_ref[0, target, j] = update[:64, :]
            update_ref[1, target, j] = update[64:, :]

    copies = []

    def push(k, src, dst, target):
        copy = pltpu.make_async_remote_copy(
            src_ref=src, dst_ref=dst, send_sem=send_sem.at[k], recv_sem=recv_sem.at[k],
            device_id=target, device_id_type=MESH,
        )
        copy.start()
        copies.append(copy)

    def arrive(k, ref):
        pltpu.make_async_remote_copy(
            src_ref=ref, dst_ref=ref, send_sem=send_sem.at[k], recv_sem=recv_sem.at[k],
            device_id=partner, device_id_type=MESH,
        ).wait_recv()

    for step in (4, 3, 5):
        finish(step)
    pl.semaphore_wait(barrier, len(peers))
    for step in steps:
        if step not in (4, 3, 5):
            finish(step)
        if step:
            push(step, part(step, 1), relay.at[step - 1], partner)
            push(8 + step, part(step, 0), spot(0, 0), device(step, 0))
        else:
            push(0, part(0, 1), spot(0, 0), partner)
    own = pltpu.make_async_copy(part(0, 0), spot(0, 0), own_sem)
    own.start()
    for step in steps[:-1]:
        arrive(step, relay.at[step - 1])
        push(16 + step, relay.at[step - 1], spot(0, 1), device(step, 0))
    own.wait()
    arrive(0, spot(0, 1))
    for step in steps[:-1]:
        arrive(8 + step, spot(-step, 0))
    for step in steps[:-1]:
        arrive(16 + step, spot(-step, 1))
    for copy in copies:
        copy.wait_send()


def deliver(accs, qg, mixing):
    whole = pl.BlockSpec(memory_space=VMEM)
    return pl.pallas_call(
        deliver_kernel,
        out_shape=jax.ShapeDtypeStruct((64, 64, 128), BF16),
        in_specs=[whole] * 6,
        out_specs=whole,
        scratch_shapes=[VMEM((2, 8, 4, 64, 128), BF16), VMEM((7, 4, 64, 128), BF16), DMA((24,)), DMA((24,)), DMA],
        compiler_params=pltpu.CompilerParams(
            collective_id=1, has_side_effects=True, vmem_limit_bytes=16 * 1024 * 1024
        ),
        name="deliver",
    )(*accs, qg, mixing)


def per_device(
    pair_field, ln_gain, w_query, w_key, w_value, w_gate, w_bias, w_out, tile_mask, type_ids
):
    weights = [w.T for w in (w_query, w_key, w_value, w_gate)]
    weights.append(w_bias.T)
    operands = (pair_field, ln_gain.reshape(1, 128), *weights, type_ids.reshape(8, 128), w_out, tile_mask)
    qg, kbd, vbd, bias, bound, mixing, lists = spread(
        *[pltpu.with_memory_space_constraint(operand, pltpu.HBM) for operand in operands]
    )
    accs = attend(lists, qg, kbd, vbd, bias.reshape(2, 16, 2, 8, 32, 256), bound)
    return jnp.transpose(deliver(accs, qg, mixing), (2, 0, 1))


def solution(mesh):
    return jax.shard_map(
        per_device,
        mesh=mesh,
        in_specs=(
            P("row", "col", None),
            P(),
            P(None, "head"),
            P(None, "head"),
            P(None, "head"),
            P(None, "head"),
            P(None, "head"),
            P(),
            P(),
            P(),
        ),
        out_specs=P("row", "col", "head"),
        check_vma=False,
    )
```

```python
import math

import jax
import jax.numpy as jnp
from jax import lax
from jax.experimental import pallas as pl
from jax.experimental.pallas import tpu as pltpu
from jax.sharding import PartitionSpec as P

MESH = pl.DeviceIdType.MESH
F32 = jnp.float32
BF16 = jnp.bfloat16
VMEM = pltpu.VMEM
DMA = pltpu.SemaphoreType.DMA

epsilon = 1e-05
masked_score = -1000000000.0
LOG2E = math.log2(math.e)
SCALE = LOG2E / math.sqrt(32)
SAFE = 64.0
NT = (((1,), (1,)), ((), ()))


def ring(value, size):
    return lax.rem(value + size, size)


def spread_kernel(
    tile_ref, gain_in, wq_ref, wk_ref, wv_ref, wg_ref, wb_in, types_in, w_out_in, mask_in,
    qg_ref, kbd_ref, vbd_ref, bias_ref, bound_ref, mixing_ref, lists_ref,
    half, gain_ref, wb_ref, types_ref, w_out_ref, mask_ref, wide, send, strip, wbuf, wall, flat, bsend, tops,
    load_sem, col_send, col_recv, z_send, z_recv, w_send, w_recv,
    g_send, g_recv, s_send, s_recv, own_sem,
):
    row = lax.axis_index("row")
    col = lax.axis_index("col")
    head = lax.axis_index("head")
    core = lax.rem(col, 2)
    x = lax.rem(lax.div(col, 2), 4)
    y = head * 2 + lax.div(col, 8)

    def place(x_, y_, core_=None):
        return (row, lax.rem(y_, 2) * 8 + x_ * 2 + (core if core_ is None else core_), lax.div(y_, 2))

    def along_z(step):
        return (ring(row + step, 8), col, head)

    partner = place(x, ring(y + 2, 4))
    peers = [along_z(step) for step in range(1, 8)]
    peers += [place(ring(x + 1, 4), y), place(ring(x - 1, 4), y)]
    peers += [place(x, ring(y + 1, 4)), place(x, ring(y - 1, 4)), partner]
    peers += [place(x, y, 1 - core)]
    barrier = pltpu.get_barrier_semaphore()
    for peer in peers:
        pl.semaphore_signal(barrier, inc=1, device_id=peer, device_id_type=MESH)

    loads = [
        (tile_ref.at[:, pl.ds(pl.multiple_of(head * 32, 32), 32), :], half),
        (gain_in, gain_ref), (wb_in, wb_ref), (types_in, types_ref),
    ]
    loads += [
        (ref, wbuf.at[head, pl.ds(kind * 64, 64)]) for kind, ref in enumerate((wq_ref, wk_ref, wv_ref, wg_ref))
    ]
    loads += [(w_out_in, w_out_ref), (mask_in, mask_ref)]
    loads = [pltpu.make_async_copy(src, dst, load_sem.at[n]) for n, (src, dst) in enumerate(loads)]
    for load in loads:
        load.start()
    tops[...] = jnp.zeros_like(tops)
    loads[0].wait()

    def widen(block, carry):
        rows = half[pl.ds(block * 8, 8)].astype(F32).reshape(256, 128)
        wide[pl.ds(pl.multiple_of(block * 256, 256), 256), :] = rows
        return carry

    lax.fori_loop(0, 16, widen, 0)
    ones = jnp.ones((128, 128), BF16)
    loads[1].wait()
    gain = gain_ref[...]

    def norm_for(step):
        target = ring(row + step, 8)
        for jj in range(4):
            value = wide[pl.ds(4 * target + jj, 128, stride=32), :]
            mean = jnp.dot(value.astype(BF16), ones, preferred_element_type=F32) * (1.0 / 128)
            centred = value - mean
            squares = (centred * centred).astype(BF16)
            spread = jnp.dot(squares, ones, preferred_element_type=F32) * (1.0 / 128)
            normed = centred * lax.rsqrt(spread + epsilon) * gain
            send[target, jj] = normed.astype(BF16)

    def norm_near(n, carry):
        norm_for(n)
        norm_for(-n)
        return carry

    def norm_far(n, carry):
        norm_for(3 + n)
        norm_for(-3 * (1 - n))
        return carry

    lax.fori_loop(1, 3, norm_near, 0)
    for load in loads[2:]:
        load.wait()
    wbuf[head, 256:272, :] = jnp.concatenate(
        [wb_ref[...].astype(F32), jnp.zeros((14, 128), F32)], axis=0
    ).astype(BF16)
    pl.semaphore_wait(barrier, len(peers))
    w_copy = pltpu.make_async_remote_copy(
        src_ref=wbuf.at[head], dst_ref=wbuf.at[head], send_sem=w_send, recv_sem=w_recv,
        device_id=partner, device_id_type=MESH,
    )
    w_copy.start()
    sent = [w_copy]

    def push(src, dst, send_sem, recv_sem, device):
        copy = pltpu.make_async_remote_copy(
            src_ref=src, dst_ref=dst, send_sem=send_sem, recv_sem=recv_sem,
            device_id=device, device_id_type=MESH,
        )
        copy.start()
        sent.append(copy)

    def strip_rows(step):
        source = ring(row + step, 8)
        return strip.at[:, pl.ds(pl.multiple_of(source * 128, 128), 128), :]

    def col_push(step):
        target = ring(row + step, 8)
        push(send.at[target], strip_rows(0), col_send.at[step], col_recv.at[step], along_z(step))

    col_push(1)
    col_push(7)
    lax.fori_loop(0, 2, norm_far, 0)
    pltpu.make_async_remote_copy(
        src_ref=wbuf.at[1 - head], dst_ref=wbuf.at[1 - head], send_sem=w_send, recv_sem=w_recv,
        device_id=partner, device_id_type=MESH,
    ).wait_recv()

    wb = wbuf[0, 256:272, :].astype(F32) + pltpu.roll(wbuf[1, 256:272, :].astype(F32), 2, 0)
    weighted = wb * gain
    wbt = wb.astype(BF16)

    def bias_for(target, carry):
        part = lax.dot_general(wbt, send[target].reshape(512, 128), NT, preferred_element_type=F32)
        for jj in range(4):
            flat[pl.ds(pl.multiple_of((4 * target + jj) * 8, 8), 8), :] = part[0:8, jj * 128:jj * 128 + 128]
        return carry

    lax.fori_loop(0, 8, bias_for, 0, unroll=4)
    living = jnp.broadcast_to(types_ref[pl.ds(row, 1), :] != 0, (32, 128))
    by_head = [
        jnp.where(living, flat[pl.ds(h, 32, stride=8), :] * LOG2E, masked_score) for h in range(4)
    ]
    bsend[0] = jnp.concatenate([b[:, :64] for b in by_head], axis=1).astype(BF16)
    bsend[1] = jnp.concatenate([b[:, 64:] for b in by_head], axis=1).astype(BF16)

    def unit(x_, y_, run, low, count, core_=None):
        return bias_ref.at[
            run, lax.rem(y_, 2), x_, core if core_ is None else core_, lax.div(y_, 2), pl.ds(low, count)
        ]

    def arrive(dst, send_sem, recv_sem):
        pltpu.make_async_remote_copy(
            src_ref=dst, dst_ref=dst, send_sem=send_sem, recv_sem=recv_sem,
            device_id=partner, device_id_type=MESH,
        ).wait_recv()

    def slot(step):
        return 2 * step - 1 if step > 0 else -2 * step

    spans = ((0, 2, 5), (5, 7, 8))

    def chunk(step, low=0, count=2):
        return bias_ref.at[pl.ds(low, count), lax.rem(y, 2), x, core, lax.div(y, 2), slot(step)]

    def z_push(k, src, dst, step):
        push(src, dst, z_send.at[k], z_recv.at[k], along_z(step))

    def z_arrive(k, dst):
        arrive(dst, z_send.at[k], z_recv.at[k])

    own = pltpu.make_async_copy(bsend, chunk(0), own_sem.at[0])
    own.start()
    for k, step in enumerate((2, -2, 1, -1)):
        z_push(k, bsend, chunk(-step), step)

    own_cols = pltpu.make_async_copy(send.at[row], strip_rows(0), own_sem.at[1])
    own_cols.start()

    for kind, place_of in enumerate((1, 0, 2, 3)):
        for s in range(2):
            wall[place_of * 128 + s * 64:place_of * 128 + s * 64 + 64, :] = wbuf[s, kind * 64:kind * 64 + 64, :]
    together = (
        lax.div(lax.broadcasted_iota(jnp.int32, (128, 128), 0), 32)
        == lax.div(lax.broadcasted_iota(jnp.int32, (128, 128), 1), 32)
    ).astype(F32).astype(BF16)

    key_head = lax.div(lax.broadcasted_iota(jnp.int32, (128, 128), 0), 32)
    side_of = lax.div(lax.broadcasted_iota(jnp.int32, (128, 128), 1), 64)
    key_here = [(key_head == 2 * n + side_of).astype(F32).astype(BF16) for n in range(2)]
    lane_head = lax.div(lax.broadcasted_iota(jnp.int32, (64, 128), 1), 32)
    value_here = [(lane_head == h).astype(F32).astype(BF16) for h in range(4)]

    def project(step):
        source = ring(row + step, 8)
        first_block = 2 * slot(step)
        rows = pl.ds(pl.multiple_of(source * 128, 128), 128)

        def one(jj, carry):
            value = strip[jj, rows, :]
            keys = lax.dot_general(wall[0:128, :], value, NT, preferred_element_type=F32)
            left = lax.dot_general(value, wall[128:256, :], NT, preferred_element_type=F32)
            right = lax.dot_general(value, wall[256:512, :], NT, preferred_element_type=F32)
            query = left * SCALE
            qg_ref[0, jj, rows, :] = query.astype(BF16)
            qg_ref[1, jj, rows, :] = jax.nn.sigmoid(right[:, 128:]).astype(BF16)
            short = keys.astype(BF16)
            values = right[:, :128].astype(BF16)
            for odd in range(2):
                twice = jnp.concatenate([short[:, odd * 64:odd * 64 + 64]] * 2, axis=1)
                for n in range(2):
                    kbd_ref[jj, first_block + odd, :, n * 128:(n + 1) * 128] = twice * key_here[n]
                for h in range(4):
                    vbd_ref[jj, first_block + odd, h * 64:(h + 1) * 64, :] = (
                        values[odd * 64:odd * 64 + 64, :] * value_here[h]
                    )
            lengths = jnp.dot((query * query).astype(BF16), together, preferred_element_type=F32)
            tops[0:1, :] = jnp.maximum(tops[0:1, :], jnp.max(lengths, axis=0, keepdims=True))
            lengths = jnp.dot(together, (keys * keys).astype(BF16), preferred_element_type=F32)
            tops[1:2, :] = jnp.maximum(tops[1:2, :], jnp.max(lengths, axis=0, keepdims=True))
            return carry

        lax.fori_loop(0, 4, one, 0, unroll=True)

    def take(step):
        arrive(strip_rows(step), col_send.at[(8 - step) % 8], col_recv.at[(8 - step) % 8])
        project(step)

    def make_lists():
        mixing_ref[...] = w_out_ref[...].astype(F32).T.astype(BF16)
        part = mask_ref[...].astype(F32)
        place_ = lax.div(lax.broadcasted_iota(jnp.int32, (16, 128), 1), 2)
        away = lax.div(place_ + 1, 2) * (2 * lax.rem(place_, 2) - 1)
        there = 2 * lax.rem(row + away + 8, 8) + lax.rem(lax.broadcasted_iota(jnp.int32, (16, 128), 1), 2)
        inside = lax.broadcasted_iota(jnp.int32, (16, 128), 1) < 16
        turned = (inside & (lax.broadcasted_iota(jnp.int32, (16, 128), 0) == there)).astype(F32).astype(BF16)
        diagonal = lax.broadcasted_iota(jnp.int32, (16, 16), 0) == lax.broadcasted_iota(jnp.int32, (16, 16), 1)
        part = jnp.where((part == 1.0) | diagonal, 1.0, 0.0)
        allowed = jnp.dot(part.astype(BF16), turned, preferred_element_type=F32)
        before = [jnp.zeros((1, 128), F32)]
        for i in range(16):
            before.append(before[-1] + allowed[i:i + 1, :])
        rank = jnp.concatenate(before[:16], axis=0)
        pairs = jnp.broadcast_to(jnp.floor(before[16] * 0.5), (16, 128))
        single = jnp.broadcast_to(before[16], (16, 128)) - 2.0 * pairs
        alone = allowed * jnp.where(rank == 2.0 * pairs, 1.0, 0.0)
        allowed = allowed - alone
        earlier = (
            lax.broadcasted_iota(jnp.int32, (128, 128), 0) < lax.broadcasted_iota(jnp.int32, (128, 128), 1)
        ).astype(F32).astype(BF16)
        start = jnp.dot(pairs.astype(BF16), earlier, preferred_element_type=F32)
        total = jnp.sum(pairs[0:1, :], axis=1, keepdims=True)
        single_start = jnp.dot(single.astype(BF16), earlier, preferred_element_type=F32)
        singles = jnp.sum(single[0:1, :], axis=1, keepdims=True)
        rank = rank + 2.0 * start
        entry = 2.0 * lax.broadcasted_iota(jnp.int32, (16, 128), 1).astype(F32)
        number = lax.broadcasted_iota(jnp.int32, (16, 128), 0).astype(F32)
        block = jnp.zeros((16, 128), F32)
        single_block = jnp.zeros((16, 128), F32)
        single_picked = jnp.zeros((16, 128), F32)
        single_found = jnp.zeros((16, 128), F32)
        picked = [jnp.zeros((16, 128), F32)] * 2
        found = [jnp.zeros((16, 128), F32)] * 2
        for k in range(16):
            at = jnp.broadcast_to(rank[:, k:k + 1], (16, 128))
            here = jnp.broadcast_to(allowed[:, k:k + 1], (16, 128))
            for side in range(2):
                hit = jnp.where(at == entry + side, here, 0.0)
                found[side] = found[side] + hit
                picked[side] = picked[side] + hit * number
                if side == 0:
                    block = block + hit * k
            at = jnp.broadcast_to(single_start[:, k:k + 1], (16, 128))
            here = jnp.broadcast_to(alone[:, k:k + 1], (16, 128))
            hit = jnp.where(2.0 * at == entry, here, 0.0)
            single_found = single_found + hit
            single_picked = single_picked + hit * number
            single_block = single_block + hit * k
        rows = [jnp.sum(block, axis=0, keepdims=True)]
        for side in range(2):
            missing = 1.0 - jnp.sum(found[side], axis=0, keepdims=True)
            rows.append(jnp.sum(picked[side], axis=0, keepdims=True) + (16.0 + side) * missing)
        rows.append(jnp.broadcast_to(total, (1, 128)))
        missing = 1.0 - jnp.sum(single_found, axis=0, keepdims=True)
        rows.append(jnp.sum(single_block, axis=0, keepdims=True))
        rows.append(jnp.sum(single_picked, axis=0, keepdims=True) + 16.0 * missing)
        rows.append(jnp.broadcast_to(singles, (1, 128)))
        rows.append(jnp.zeros((1, 128), F32))
        lists_ref[...] = jnp.concatenate(rows, axis=0).astype(jnp.int32)

    own_cols.wait()
    project(0)
    make_lists()
    own.wait()
    for k, step in enumerate((-2, 2, -1, 1)):
        z_arrive(k, chunk(step))
    z_push(4, chunk(-2), chunk(-3), 1)
    z_push(5, chunk(2), chunk(3), -1)
    z_push(6, chunk(-2, 0, 1), chunk(4, 0, 1), 2)
    z_push(7, chunk(2, 1, 1), chunk(4, 1, 1), -2)

    def far_bias():
        z_arrive(4, chunk(-3))
        z_arrive(5, chunk(3))
        z_arrive(6, chunk(4, 0, 1))
        z_arrive(7, chunk(4, 1, 1))

    def node(run, a, b):
        return (a, b) if run == 0 else (b, a)

    first = (x, y)
    second = (y, x)

    def whole_of(span):
        return span[0], span[2] - span[0]

    def halves_of(span):
        return (span[0], span[1] - span[0]), (span[1], span[2] - span[1])

    def shipment(far, run, index, a, b, rows, to_a, to_b):
        k = far * 40 + run * 20 + index
        ref = unit(*node(run, a, b), run, *rows)
        push(ref, ref, g_send.at[k], g_recv.at[k], place(*node(run, to_a, to_b)))

    def receive(far, run, index, a, b, rows):
        k = far * 40 + run * 20 + index
        arrive(unit(*node(run, a, b), run, *rows), g_send.at[k], g_recv.at[k])

    def to_sibling(run, u, v):
        k = run * 16 + u * 4 + v
        a, b = ring(first[run] + (0, -1, 1, 2)[u], 4), ring(second[run] + (0, -1, 1, 2)[v], 4)
        ref = unit(*node(run, a, b), run, 0, 8)
        push(ref, ref, s_send.at[k], s_recv.at[k], place(x, y, 1 - core))

    def begin(far, run):
        a, b, rows = first[run], second[run], whole_of(spans[far])
        shipment(far, run, 0, a, b, rows, ring(a + 1, 4), b)
        shipment(far, run, 1, a, b, rows, ring(a - 1, 4), b)

    def across(far, run, u):
        a, b, rows = ring(first[run] + (0, -1, 1, 2)[u], 4), second[run], whole_of(spans[far])
        shipment(far, run, 4 + 4 * u, a, b, rows, first[run], ring(b + 1, 4))
        shipment(far, run, 5 + 4 * u, a, b, rows, first[run], ring(b - 1, 4))

    def pass_first(far, run):
        a, b, rows = first[run], second[run], whole_of(spans[far])
        low, high = halves_of(spans[far])
        receive(far, run, 0, ring(a - 1, 4), b, rows)
        shipment(far, run, 2, ring(a - 1, 4), b, low, ring(a + 1, 4), b)
        receive(far, run, 1, ring(a + 1, 4), b, rows)
        shipment(far, run, 3, ring(a + 1, 4), b, high, ring(a - 1, 4), b)

    def end_first(far, run):
        a, b = ring(first[run] + 2, 4), second[run]
        low, high = halves_of(spans[far])
        receive(far, run, 2, a, b, low)
        receive(far, run, 3, a, b, high)

    def pass_second(far, run, u):
        a, b, rows = ring(first[run] + (0, -1, 1, 2)[u], 4), second[run], whole_of(spans[far])
        low, high = halves_of(spans[far])
        receive(far, run, 4 + 4 * u, a, ring(b - 1, 4), rows)
        shipment(far, run, 6 + 4 * u, a, ring(b - 1, 4), low, first[run], ring(b + 1, 4))
        receive(far, run, 5 + 4 * u, a, ring(b + 1, 4), rows)
        shipment(far, run, 7 + 4 * u, a, ring(b + 1, 4), high, first[run], ring(b - 1, 4))

    def end_second(far, run, u):
        a, b = ring(first[run] + (0, -1, 1, 2)[u], 4), ring(second[run] + 2, 4)
        low, high = halves_of(spans[far])
        receive(far, run, 6 + 4 * u, a, b, low)
        receive(far, run, 7 + 4 * u, a, b, high)

    for run in range(2):
        begin(0, run)
    for run in range(2):
        across(0, run, 0)
    for step in (2, 6, 3, 5, 4):
        col_push(step)
    take(1)
    take(-1)
    far_bias()
    for run in range(2):
        begin(1, run)
    for run in range(2):
        across(1, run, 0)
    for run in range(2):
        to_sibling(run, 0, 0)
    for far in range(2):
        for run in range(2):
            pass_first(far, run)
        for run in range(2):
            across(far, run, 1)
            across(far, run, 2)
    for run in range(2):
        to_sibling(run, 1, 0)
        to_sibling(run, 2, 0)
    for far in range(2):
        for run in range(2):
            end_first(far, run)
            across(far, run, 3)
    for run in range(2):
        to_sibling(run, 3, 0)
    for u in range(4):
        for far in range(2):
            for run in range(2):
                pass_second(far, run, u)
        for run in range(2):
            to_sibling(run, u, 1)
            to_sibling(run, u, 2)
        if u == 1:
            take(2)
        if u == 3:
            take(-2)
    for u in range(4):
        for run in range(2):
            for far in range(2):
                end_second(far, run, u)
            to_sibling(run, u, 3)
        if u == 2:
            take(3)
    take(-3)
    take(4)
    bound_ref[0:8, :] = tops[...]
    bound_ref[8:24, :] = jnp.broadcast_to(jnp.sum(weighted * weighted, axis=1, keepdims=True), (16, 128))
    for run in range(2):
        for u in range(4):
            for v in range(4):
                a = ring(first[run] + (0, -1, 1, 2)[u], 4)
                b = ring(second[run] + (0, -1, 1, 2)[v], 4)
                k = run * 16 + u * 4 + v
                arrive(unit(*node(run, a, b), run, 0, 8, 1 - core), s_send.at[k], s_recv.at[k])
    for copy in sent:
        copy.wait_send()


def spread(*operands):
    whole = pl.BlockSpec(memory_space=VMEM)
    return pl.pallas_call(
        spread_kernel,
        out_shape=(
            jax.ShapeDtypeStruct((2, 4, 1024, 128), BF16),
            jax.ShapeDtypeStruct((4, 16, 128, 256), BF16),
            jax.ShapeDtypeStruct((4, 16, 256, 128), BF16),
            jax.ShapeDtypeStruct((2, 2, 4, 2, 2, 8, 32, 256), BF16),
            jax.ShapeDtypeStruct((24, 128), F32),
            jax.ShapeDtypeStruct((128, 128), BF16),
            jax.ShapeDtypeStruct((8, 128), jnp.int32),
        ),
        in_specs=[pl.BlockSpec(memory_space=pltpu.HBM)] * len(operands),
        out_specs=(whole,) * 7,
        scratch_shapes=[
            VMEM((128, 32, 128), BF16),
            VMEM((1, 128), F32),
            VMEM((2, 128), BF16),
            VMEM((8, 128), jnp.int32),
            VMEM((128, 128), BF16),
            VMEM((16, 16), jnp.int32),
            VMEM((4096, 128), F32),
            VMEM((8, 4, 128, 128), BF16),
            VMEM((4, 1024, 128), BF16),
            VMEM((2, 272, 128), BF16),
            VMEM((512, 128), BF16),
            VMEM((256, 128), F32),
            VMEM((2, 32, 256), BF16),
            VMEM((8, 128), F32),
            DMA((10,)), DMA((8,)), DMA((8,)), DMA((8,)), DMA((8,)), DMA, DMA,
            DMA((80,)), DMA((80,)), DMA((32,)), DMA((32,)), DMA((2,)),
        ],
        compiler_params=pltpu.CompilerParams(
            collective_id=0, has_side_effects=True, vmem_limit_bytes=32 * 1024 * 1024
        ),
        name="spread",
    )(*operands)


def attend_kernel(
    lists_ref, qg_ref, kbd, vbd, bias, bound_ref,
    acc0, acc1, acc2, acc3,
    peak,
):
    accs = (acc0, acc1, acc2, acc3)
    for acc in accs:
        acc[...] = jnp.zeros_like(acc)
    same = (
        lax.div(lax.broadcasted_iota(jnp.int32, (256, 128), 0), 64)
        == lax.div(lax.broadcasted_iota(jnp.int32, (256, 128), 1), 32)
    ).astype(F32).astype(BF16)

    reach = jnp.sqrt(jnp.max(bound_ref[0:1, :])) * jnp.sqrt(jnp.max(bound_ref[1:2, :]))
    bias_reach = jnp.sqrt(jnp.max(bound_ref[8:24, :])) * (math.sqrt(128) * LOG2E)
    safe = (reach + bias_reach) * 1.03 <= SAFE

    def query(j, i):
        return qg_ref[0, j, pl.ds(pl.multiple_of(jnp.minimum(i, 15) * 64, 64), 64), :]

    def values_of(j, block):
        return jnp.concatenate([vbd[j, block], same], axis=1)

    def offset_of(i, block):
        at = (lax.rem(block, 2), jnp.minimum(i, 15))
        n = lax.div(block, 2)
        return [bias[at[0], at[1], half, n].astype(F32) for half in range(2)]

    total_pairs = lists_ref[3, 0]

    @pl.when(safe)
    def _():
        def pairs_from(first, count):
            work = []
            for side in range(count):
                e = first + side
                block = lists_ref[0, e]
                ids = (lists_ref[1, e], lists_ref[2, e])
                offset = jnp.concatenate(offset_of(ids[0], block) + offset_of(ids[1], block), axis=0)
                work.append((block, ids, offset))
            for j in range(4):
                for block, ids, offset in work:
                    queries = jnp.concatenate([query(j, i) for i in ids], axis=0)
                    score = jnp.dot(queries, kbd[j, block], preferred_element_type=F32)
                    weights = jnp.exp2(score + offset).astype(BF16)
                    total = jnp.dot(weights, values_of(j, block), preferred_element_type=F32)
                    olds = [accs[j][i] for i in ids]
                    for n in range(2):
                        accs[j][ids[n]] = olds[n] + total[n * 64:(n + 1) * 64, :]

        def four_step(t, carry):
            pairs_from(4 * t, 4)
            return carry

        def two_step(t, carry):
            pairs_from(2 * t, 2)
            return carry

        def single_step(t, carry):
            for j in range(4):
                for side in range(4):
                    e = 4 * t + side
                    block = lists_ref[4, e]
                    i = lists_ref[5, e]
                    offset = jnp.concatenate(offset_of(i, block), axis=0)
                    score = jnp.dot(query(j, i), kbd[j, block], preferred_element_type=F32)
                    weights = jnp.exp2(score + offset).astype(BF16)
                    total = jnp.dot(weights, values_of(j, block), preferred_element_type=F32)
                    accs[j][i] = accs[j][i] + total
            return carry

        fours = lax.div(total_pairs, 4)
        lax.fori_loop(0, fours, four_step, 0)
        lax.fori_loop(2 * fours, lax.div(total_pairs + 1, 2), two_step, 0)
        lax.fori_loop(0, lax.div(lists_ref[6, 0] + 3, 4), single_step, 0)

    @pl.when(jnp.logical_not(safe))
    def _():
        peak[...] = jnp.full_like(peak, -1e30)

        def step(n, carry):
            e = jnp.where(n < 2 * total_pairs, lax.div(n, 2), n - 2 * total_pairs)
            line = jnp.where(n < 2 * total_pairs, lax.rem(n, 2), 4)
            block = lists_ref[jnp.where(line == 4, 4, 0), e]
            i = lists_ref[1 + line, e]
            offset = jnp.concatenate(offset_of(i, block), axis=0)
            for j in range(4):
                score = jnp.dot(query(j, i), kbd[j, block], preferred_element_type=F32) + offset
                old = peak[j, i]
                tops = [
                    jnp.maximum(
                        jnp.max(score[:, h * 64:(h + 1) * 64], axis=1, keepdims=True),
                        old[:, h * 32:h * 32 + 1],
                    )
                    for h in range(4)
                ]
                shift = jnp.concatenate([jnp.broadcast_to(top, (64, 64)) for top in tops], axis=1)
                fresh = jnp.concatenate([jnp.broadcast_to(top, (64, 32)) for top in tops], axis=1)
                decay = jnp.exp2(old - fresh)
                weights = jnp.exp2(score - shift).astype(BF16)
                total = jnp.dot(weights, values_of(j, block), preferred_element_type=F32)
                accs[j][i] = accs[j][i] * jnp.concatenate([decay, decay], axis=1) + total
                peak[j, i] = fresh
            return carry

        lax.fori_loop(0, 2 * total_pairs + lists_ref[6, 0], step, 0)


def attend(lists, qg, kbd, vbd, bias, bound):
    whole = pl.BlockSpec(memory_space=VMEM)
    return pl.pallas_call(
        attend_kernel,
        out_shape=[jax.ShapeDtypeStruct((18, 64, 256), F32)] * 4,
        in_specs=[pl.BlockSpec(memory_space=pltpu.SMEM)] + [whole] * 5,
        out_specs=[whole] * 4,
        scratch_shapes=[VMEM((4, 18, 64, 128), F32)],
        compiler_params=pltpu.CompilerParams(vmem_limit_bytes=24 * 1024 * 1024),
        name="attend",
    )(lists, qg, kbd, vbd, bias, bound)


def deliver_kernel(
    acc0, acc1, acc2, acc3, qg_ref, mixing_ref, out_ref,
    update_ref, relay, send_sem, recv_sem, own_sem,
):
    row = lax.axis_index("row")
    col = lax.axis_index("col")
    head = lax.axis_index("head")

    def other(flip):
        return (1 - head) if flip else head

    def device(step, flip):
        return (ring(row + step, 8), col, other(flip))

    steps = (4, 3, 5, 2, 6, 1, 7, 0)
    partner = device(0, 1)
    peers = [partner] + [device(step, 0) for step in steps if step]
    barrier = pltpu.get_barrier_semaphore()
    for peer in peers:
        pl.semaphore_signal(barrier, inc=1, device_id=peer, device_id_type=MESH)

    def spot(step, flip):
        return out_ref.at[pl.ds((other(flip) * 8 + ring(row + step, 8)) * 4, 4)]

    def part(step, flip):
        return update_ref.at[other(flip), ring(row + step, 8)]

    def finish(step):
        target = ring(row + step, 8)
        rows = pl.ds(pl.multiple_of(target * 128, 128), 128)
        for j, acc in enumerate((acc0, acc1, acc2, acc3)):
            sums = acc[pl.ds(target * 2, 2)].reshape(128, 256)
            attention = sums[:, :128] / sums[:, 128:]
            gated = (attention * qg_ref[1, j, rows, :].astype(F32)).astype(BF16)
            update = lax.dot_general(mixing_ref[...], gated, NT, preferred_element_type=F32).astype(BF16)
            update_ref[0, target, j] = update[:64, :]
            update_ref[1, target, j] = update[64:, :]

    copies = []

    def push(k, src, dst, target):
        copy = pltpu.make_async_remote_copy(
            src_ref=src, dst_ref=dst, send_sem=send_sem.at[k], recv_sem=recv_sem.at[k],
            device_id=target, device_id_type=MESH,
        )
        copy.start()
        copies.append(copy)

    def arrive(k, ref):
        pltpu.make_async_remote_copy(
            src_ref=ref, dst_ref=ref, send_sem=send_sem.at[k], recv_sem=recv_sem.at[k],
            device_id=partner, device_id_type=MESH,
        ).wait_recv()

    for step in (4, 3, 5):
        finish(step)
    pl.semaphore_wait(barrier, len(peers))
    for step in steps:
        if step not in (4, 3, 5):
            finish(step)
        if step:
            push(step, part(step, 1), relay.at[step - 1], partner)
            push(8 + step, part(step, 0), spot(0, 0), device(step, 0))
        else:
            push(0, part(0, 1), spot(0, 0), partner)
    own = pltpu.make_async_copy(part(0, 0), spot(0, 0), own_sem)
    own.start()
    for step in steps[:-1]:
        arrive(step, relay.at[step - 1])
        push(16 + step, relay.at[step - 1], spot(0, 1), device(step, 0))
    own.wait()
    arrive(0, spot(0, 1))
    for step in steps[:-1]:
        arrive(8 + step, spot(-step, 0))
    for step in steps[:-1]:
        arrive(16 + step, spot(-step, 1))
    for copy in copies:
        copy.wait_send()


def deliver(accs, qg, mixing):
    whole = pl.BlockSpec(memory_space=VMEM)
    return pl.pallas_call(
        deliver_kernel,
        out_shape=jax.ShapeDtypeStruct((64, 64, 128), BF16),
        in_specs=[whole] * 6,
        out_specs=whole,
        scratch_shapes=[VMEM((2, 8, 4, 64, 128), BF16), VMEM((7, 4, 64, 128), BF16), DMA((24,)), DMA((24,)), DMA],
        compiler_params=pltpu.CompilerParams(
            collective_id=1, has_side_effects=True, vmem_limit_bytes=16 * 1024 * 1024
        ),
        name="deliver",
    )(*accs, qg, mixing)


def per_device(
    pair_field, ln_gain, w_query, w_key, w_value, w_gate, w_bias, w_out, tile_mask, type_ids
):
    weights = [w.T for w in (w_query, w_key, w_value, w_gate)]
    weights.append(w_bias.T)
    operands = (pair_field, ln_gain.reshape(1, 128), *weights, type_ids.reshape(8, 128), w_out, tile_mask)
    qg, kbd, vbd, bias, bound, mixing, lists = spread(
        *[pltpu.with_memory_space_constraint(operand, pltpu.HBM) for operand in operands]
    )
    accs = attend(lists, qg, kbd, vbd, bias.reshape(2, 16, 2, 8, 32, 256), bound)
    return jnp.transpose(deliver(accs, qg, mixing), (2, 0, 1))


def solution(mesh):
    return jax.shard_map(
        per_device,
        mesh=mesh,
        in_specs=(
            P("row", "col", None),
            P(),
            P(None, "head"),
            P(None, "head"),
            P(None, "head"),
            P(None, "head"),
            P(None, "head"),
            P(),
            P(),
            P(),
        ),
        out_specs=P("row", "col", "head"),
        check_vma=False,
    )
```

```python
import math

import jax
import jax.numpy as jnp
from jax import lax
from jax.experimental import pallas as pl
from jax.experimental.pallas import tpu as pltpu
from jax.sharding import PartitionSpec as P

MESH = pl.DeviceIdType.MESH
F32 = jnp.float32
BF16 = jnp.bfloat16
VMEM = pltpu.VMEM
DMA = pltpu.SemaphoreType.DMA

epsilon = 1e-05
masked_score = -1000000000.0
LOG2E = math.log2(math.e)
SCALE = LOG2E / math.sqrt(32)
SAFE = 64.0
NT = (((1,), (1,)), ((), ()))


def ring(value, size):
    return lax.rem(value + size, size)


def spread_kernel(
    tile_ref, gain_in, wq_ref, wk_ref, wv_ref, wg_ref, wb_in, types_in, w_out_in, mask_in,
    qg_ref, kbd_ref, vbd_ref, bias_ref, bound_ref, mixing_ref, lists_ref,
    half, gain_ref, wb_ref, types_ref, w_out_ref, mask_ref, wide, send, strip, wbuf, wall, flat, bsend, tops,
    load_sem, col_send, col_recv, z_send, z_recv, w_send, w_recv,
    g_send, g_recv, s_send, s_recv, own_sem,
):
    row = lax.axis_index("row")
    col = lax.axis_index("col")
    head = lax.axis_index("head")
    core = lax.rem(col, 2)
    x = lax.rem(lax.div(col, 2), 4)
    y = head * 2 + lax.div(col, 8)

    def place(x_, y_, core_=None):
        return (row, lax.rem(y_, 2) * 8 + x_ * 2 + (core if core_ is None else core_), lax.div(y_, 2))

    def along_z(step):
        return (ring(row + step, 8), col, head)

    partner = place(x, ring(y + 2, 4))
    peers = [along_z(step) for step in range(1, 8)]
    peers += [place(ring(x + 1, 4), y), place(ring(x - 1, 4), y)]
    peers += [place(x, ring(y + 1, 4)), place(x, ring(y - 1, 4)), partner]
    peers += [place(x, y, 1 - core)]
    barrier = pltpu.get_barrier_semaphore()
    for peer in peers:
        pl.semaphore_signal(barrier, inc=1, device_id=peer, device_id_type=MESH)

    loads = [
        (tile_ref.at[:, pl.ds(pl.multiple_of(head * 32, 32), 32), :], half),
        (gain_in, gain_ref), (wb_in, wb_ref), (types_in, types_ref),
    ]
    loads += [
        (ref, wbuf.at[head, pl.ds(kind * 64, 64)]) for kind, ref in enumerate((wq_ref, wk_ref, wv_ref, wg_ref))
    ]
    loads += [(w_out_in, w_out_ref), (mask_in, mask_ref)]
    loads = [pltpu.make_async_copy(src, dst, load_sem.at[n]) for n, (src, dst) in enumerate(loads)]
    for load in loads:
        load.start()
    tops[...] = jnp.zeros_like(tops)
    loads[0].wait()

    def widen(block, carry):
        rows = half[pl.ds(block * 8, 8)].astype(F32).reshape(256, 128)
        wide[pl.ds(pl.multiple_of(block * 256, 256), 256), :] = rows
        return carry

    lax.fori_loop(0, 16, widen, 0)
    ones = jnp.ones((128, 128), BF16)
    loads[1].wait()
    gain = gain_ref[...]

    def norm_for(step):
        target = ring(row + step, 8)
        for jj in range(4):
            value = wide[pl.ds(4 * target + jj, 128, stride=32), :]
            mean = jnp.dot(value.astype(BF16), ones, preferred_element_type=F32) * (1.0 / 128)
            centred = value - mean
            squares = (centred * centred).astype(BF16)
            spread = jnp.dot(squares, ones, preferred_element_type=F32) * (1.0 / 128)
            normed = centred * lax.rsqrt(spread + epsilon) * gain
            send[target, jj] = normed.astype(BF16)

    def norm_near(n, carry):
        norm_for(n)
        norm_for(-n)
        return carry

    def norm_far(n, carry):
        norm_for(3 + n)
        norm_for(-3 * (1 - n))
        return carry

    lax.fori_loop(1, 3, norm_near, 0)
    for load in loads[2:]:
        load.wait()
    wbuf[head, 256:272, :] = jnp.concatenate(
        [wb_ref[...].astype(F32), jnp.zeros((14, 128), F32)], axis=0
    ).astype(BF16)
    pl.semaphore_wait(barrier, len(peers))
    w_copy = pltpu.make_async_remote_copy(
        src_ref=wbuf.at[head], dst_ref=wbuf.at[head], send_sem=w_send, recv_sem=w_recv,
        device_id=partner, device_id_type=MESH,
    )
    w_copy.start()
    sent = [w_copy]

    def push(src, dst, send_sem, recv_sem, device):
        copy = pltpu.make_async_remote_copy(
            src_ref=src, dst_ref=dst, send_sem=send_sem, recv_sem=recv_sem,
            device_id=device, device_id_type=MESH,
        )
        copy.start()
        sent.append(copy)

    def strip_rows(step):
        source = ring(row + step, 8)
        return strip.at[:, pl.ds(pl.multiple_of(source * 128, 128), 128), :]

    def col_push(step):
        target = ring(row + step, 8)
        push(send.at[target], strip_rows(0), col_send.at[step], col_recv.at[step], along_z(step))

    col_push(1)
    col_push(7)
    lax.fori_loop(0, 2, norm_far, 0)
    pltpu.make_async_remote_copy(
        src_ref=wbuf.at[1 - head], dst_ref=wbuf.at[1 - head], send_sem=w_send, recv_sem=w_recv,
        device_id=partner, device_id_type=MESH,
    ).wait_recv()

    wb = wbuf[0, 256:272, :].astype(F32) + pltpu.roll(wbuf[1, 256:272, :].astype(F32), 2, 0)
    weighted = wb * gain
    wbt = wb.astype(BF16)

    def bias_for(target, carry):
        part = lax.dot_general(wbt, send[target].reshape(512, 128), NT, preferred_element_type=F32)
        for jj in range(4):
            flat[pl.ds(pl.multiple_of((4 * target + jj) * 8, 8), 8), :] = part[0:8, jj * 128:jj * 128 + 128]
        return carry

    lax.fori_loop(0, 8, bias_for, 0, unroll=4)
    living = jnp.broadcast_to(types_ref[pl.ds(row, 1), :] != 0, (32, 128))
    by_head = [
        jnp.where(living, flat[pl.ds(h, 32, stride=8), :] * LOG2E, masked_score) for h in range(4)
    ]
    bsend[0] = jnp.concatenate([b[:, :64] for b in by_head], axis=1).astype(BF16)
    bsend[1] = jnp.concatenate([b[:, 64:] for b in by_head], axis=1).astype(BF16)

    def unit(x_, y_, run, low, count, core_=None):
        return bias_ref.at[
            run, lax.rem(y_, 2), x_, core if core_ is None else core_, lax.div(y_, 2), pl.ds(low, count)
        ]

    def arrive(dst, send_sem, recv_sem):
        pltpu.make_async_remote_copy(
            src_ref=dst, dst_ref=dst, send_sem=send_sem, recv_sem=recv_sem,
            device_id=partner, device_id_type=MESH,
        ).wait_recv()

    def slot(step):
        return 2 * step - 1 if step > 0 else -2 * step

    spans = ((0, 2, 5), (5, 7, 8))

    def chunk(step, low=0, count=2):
        return bias_ref.at[pl.ds(low, count), lax.rem(y, 2), x, core, lax.div(y, 2), slot(step)]

    def z_push(k, src, dst, step):
        push(src, dst, z_send.at[k], z_recv.at[k], along_z(step))

    def z_arrive(k, dst):
        arrive(dst, z_send.at[k], z_recv.at[k])

    own = pltpu.make_async_copy(bsend, chunk(0), own_sem.at[0])
    own.start()
    for k, step in enumerate((2, -2, 1, -1)):
        z_push(k, bsend, chunk(-step), step)

    own_cols = pltpu.make_async_copy(send.at[row], strip_rows(0), own_sem.at[1])
    own_cols.start()

    for kind, place_of in enumerate((1, 0, 2, 3)):
        for s in range(2):
            wall[place_of * 128 + s * 64:place_of * 128 + s * 64 + 64, :] = wbuf[s, kind * 64:kind * 64 + 64, :]
    together = (
        lax.div(lax.broadcasted_iota(jnp.int32, (128, 128), 0), 32)
        == lax.div(lax.broadcasted_iota(jnp.int32, (128, 128), 1), 32)
    ).astype(F32).astype(BF16)

    key_head = lax.div(lax.broadcasted_iota(jnp.int32, (128, 128), 0), 32)
    side_of = lax.div(lax.broadcasted_iota(jnp.int32, (128, 128), 1), 64)
    key_here = [(key_head == 2 * n + side_of).astype(F32).astype(BF16) for n in range(2)]
    lane_head = lax.div(lax.broadcasted_iota(jnp.int32, (64, 128), 1), 32)
    value_here = [(lane_head == h).astype(F32).astype(BF16) for h in range(4)]

    def project(step):
        source = ring(row + step, 8)
        first_block = 2 * slot(step)
        rows = pl.ds(pl.multiple_of(source * 128, 128), 128)

        def one(jj, carry):
            value = strip[jj, rows, :]
            keys = lax.dot_general(wall[0:128, :], value, NT, preferred_element_type=F32)
            left = lax.dot_general(value, wall[128:256, :], NT, preferred_element_type=F32)
            right = lax.dot_general(value, wall[256:512, :], NT, preferred_element_type=F32)
            query = left * SCALE
            qg_ref[0, jj, rows, :] = query.astype(BF16)
            qg_ref[1, jj, rows, :] = jax.nn.sigmoid(right[:, 128:]).astype(BF16)
            short = keys.astype(BF16)
            values = right[:, :128].astype(BF16)
            for odd in range(2):
                twice = jnp.concatenate([short[:, odd * 64:odd * 64 + 64]] * 2, axis=1)
                for n in range(2):
                    kbd_ref[jj, first_block + odd, :, n * 128:(n + 1) * 128] = twice * key_here[n]
                for h in range(4):
                    vbd_ref[jj, first_block + odd, h * 64:(h + 1) * 64, :] = (
                        values[odd * 64:odd * 64 + 64, :] * value_here[h]
                    )
            lengths = jnp.dot((query * query).astype(BF16), together, preferred_element_type=F32)
            tops[0:1, :] = jnp.maximum(tops[0:1, :], jnp.max(lengths, axis=0, keepdims=True))
            lengths = jnp.dot(together, (keys * keys).astype(BF16), preferred_element_type=F32)
            tops[1:2, :] = jnp.maximum(tops[1:2, :], jnp.max(lengths, axis=0, keepdims=True))
            return carry

        lax.fori_loop(0, 4, one, 0, unroll=True)

    def take(step):
        arrive(strip_rows(step), col_send.at[(8 - step) % 8], col_recv.at[(8 - step) % 8])
        project(step)

    def make_lists():
        mixing_ref[...] = w_out_ref[...].astype(F32).T.astype(BF16)
        part = mask_ref[...].astype(F32)
        place_ = lax.div(lax.broadcasted_iota(jnp.int32, (16, 128), 1), 2)
        away = lax.div(place_ + 1, 2) * (2 * lax.rem(place_, 2) - 1)
        there = 2 * lax.rem(row + away + 8, 8) + lax.rem(lax.broadcasted_iota(jnp.int32, (16, 128), 1), 2)
        inside = lax.broadcasted_iota(jnp.int32, (16, 128), 1) < 16
        turned = (inside & (lax.broadcasted_iota(jnp.int32, (16, 128), 0) == there)).astype(F32).astype(BF16)
        diagonal = lax.broadcasted_iota(jnp.int32, (16, 16), 0) == lax.broadcasted_iota(jnp.int32, (16, 16), 1)
        part = jnp.where((part == 1.0) | diagonal, 1.0, 0.0)
        allowed = jnp.dot(part.astype(BF16), turned, preferred_element_type=F32)
        before = [jnp.zeros((1, 128), F32)]
        for i in range(16):
            before.append(before[-1] + allowed[i:i + 1, :])
        rank = jnp.concatenate(before[:16], axis=0)
        pairs = jnp.broadcast_to(jnp.floor(before[16] * 0.5), (16, 128))
        single = jnp.broadcast_to(before[16], (16, 128)) - 2.0 * pairs
        alone = allowed * jnp.where(rank == 2.0 * pairs, 1.0, 0.0)
        allowed = allowed - alone
        earlier = (
            lax.broadcasted_iota(jnp.int32, (128, 128), 0) < lax.broadcasted_iota(jnp.int32, (128, 128), 1)
        ).astype(F32).astype(BF16)
        start = jnp.dot(pairs.astype(BF16), earlier, preferred_element_type=F32)
        total = jnp.sum(pairs[0:1, :], axis=1, keepdims=True)
        single_start = jnp.dot(single.astype(BF16), earlier, preferred_element_type=F32)
        singles = jnp.sum(single[0:1, :], axis=1, keepdims=True)
        rank = rank + 2.0 * start
        entry = 2.0 * lax.broadcasted_iota(jnp.int32, (16, 128), 1).astype(F32)
        number = lax.broadcasted_iota(jnp.int32, (16, 128), 0).astype(F32)
        block = jnp.zeros((16, 128), F32)
        single_block = jnp.zeros((16, 128), F32)
        single_picked = jnp.zeros((16, 128), F32)
        single_found = jnp.zeros((16, 128), F32)
        picked = [jnp.zeros((16, 128), F32)] * 2
        found = [jnp.zeros((16, 128), F32)] * 2
        for k in range(16):
            at = jnp.broadcast_to(rank[:, k:k + 1], (16, 128))
            here = jnp.broadcast_to(allowed[:, k:k + 1], (16, 128))
            for side in range(2):
                hit = jnp.where(at == entry + side, here, 0.0)
                found[side] = found[side] + hit
                picked[side] = picked[side] + hit * number
                if side == 0:
                    block = block + hit * k
            at = jnp.broadcast_to(single_start[:, k:k + 1], (16, 128))
            here = jnp.broadcast_to(alone[:, k:k + 1], (16, 128))
            hit = jnp.where(2.0 * at == entry, here, 0.0)
            single_found = single_found + hit
            single_picked = single_picked + hit * number
            single_block = single_block + hit * k
        rows = [jnp.sum(block, axis=0, keepdims=True)]
        for side in range(2):
            missing = 1.0 - jnp.sum(found[side], axis=0, keepdims=True)
            rows.append(jnp.sum(picked[side], axis=0, keepdims=True) + (16.0 + side) * missing)
        rows.append(jnp.broadcast_to(total, (1, 128)))
        missing = 1.0 - jnp.sum(single_found, axis=0, keepdims=True)
        rows.append(jnp.sum(single_block, axis=0, keepdims=True))
        rows.append(jnp.sum(single_picked, axis=0, keepdims=True) + 16.0 * missing)
        rows.append(jnp.broadcast_to(singles, (1, 128)))
        rows.append(jnp.zeros((1, 128), F32))
        lists_ref[...] = jnp.concatenate(rows, axis=0).astype(jnp.int32)

    own_cols.wait()
    project(0)
    make_lists()
    own.wait()
    for k, step in enumerate((-2, 2, -1, 1)):
        z_arrive(k, chunk(step))
    z_push(4, chunk(-2), chunk(-3), 1)
    z_push(5, chunk(2), chunk(3), -1)
    z_push(6, chunk(-2, 0, 1), chunk(4, 0, 1), 2)
    z_push(7, chunk(2, 1, 1), chunk(4, 1, 1), -2)

    def far_bias():
        z_arrive(4, chunk(-3))
        z_arrive(5, chunk(3))
        z_arrive(6, chunk(4, 0, 1))
        z_arrive(7, chunk(4, 1, 1))

    def node(run, a, b):
        return (a, b) if run == 0 else (b, a)

    first = (x, y)
    second = (y, x)

    def whole_of(span):
        return span[0], span[2] - span[0]

    def halves_of(span):
        return (span[0], span[1] - span[0]), (span[1], span[2] - span[1])

    def shipment(far, run, index, a, b, rows, to_a, to_b):
        k = far * 40 + run * 20 + index
        ref = unit(*node(run, a, b), run, *rows)
        push(ref, ref, g_send.at[k], g_recv.at[k], place(*node(run, to_a, to_b)))

    def receive(far, run, index, a, b, rows):
        k = far * 40 + run * 20 + index
        arrive(unit(*node(run, a, b), run, *rows), g_send.at[k], g_recv.at[k])

    def to_sibling(run, u, v):
        k = run * 16 + u * 4 + v
        a, b = ring(first[run] + (0, -1, 1, 2)[u], 4), ring(second[run] + (0, -1, 1, 2)[v], 4)
        ref = unit(*node(run, a, b), run, 0, 8)
        push(ref, ref, s_send.at[k], s_recv.at[k], place(x, y, 1 - core))

    def begin(far, run):
        a, b, rows = first[run], second[run], whole_of(spans[far])
        shipment(far, run, 0, a, b, rows, ring(a + 1, 4), b)
        shipment(far, run, 1, a, b, rows, ring(a - 1, 4), b)

    def across(far, run, u):
        a, b, rows = ring(first[run] + (0, -1, 1, 2)[u], 4), second[run], whole_of(spans[far])
        shipment(far, run, 4 + 4 * u, a, b, rows, first[run], ring(b + 1, 4))
        shipment(far, run, 5 + 4 * u, a, b, rows, first[run], ring(b - 1, 4))

    def pass_first(far, run):
        a, b, rows = first[run], second[run], whole_of(spans[far])
        low, high = halves_of(spans[far])
        receive(far, run, 0, ring(a - 1, 4), b, rows)
        shipment(far, run, 2, ring(a - 1, 4), b, low, ring(a + 1, 4), b)
        receive(far, run, 1, ring(a + 1, 4), b, rows)
        shipment(far, run, 3, ring(a + 1, 4), b, high, ring(a - 1, 4), b)

    def end_first(far, run):
        a, b = ring(first[run] + 2, 4), second[run]
        low, high = halves_of(spans[far])
        receive(far, run, 2, a, b, low)
        receive(far, run, 3, a, b, high)

    def pass_second(far, run, u):
        a, b, rows = ring(first[run] + (0, -1, 1, 2)[u], 4), second[run], whole_of(spans[far])
        low, high = halves_of(spans[far])
        receive(far, run, 4 + 4 * u, a, ring(b - 1, 4), rows)
        shipment(far, run, 6 + 4 * u, a, ring(b - 1, 4), low, first[run], ring(b + 1, 4))
        receive(far, run, 5 + 4 * u, a, ring(b + 1, 4), rows)
        shipment(far, run, 7 + 4 * u, a, ring(b + 1, 4), high, first[run], ring(b - 1, 4))

    def end_second(far, run, u):
        a, b = ring(first[run] + (0, -1, 1, 2)[u], 4), ring(second[run] + 2, 4)
        low, high = halves_of(spans[far])
        receive(far, run, 6 + 4 * u, a, b, low)
        receive(far, run, 7 + 4 * u, a, b, high)

    for run in range(2):
        begin(0, run)
    for run in range(2):
        across(0, run, 0)
    for step in (2, 6, 3, 5, 4):
        col_push(step)
    take(1)
    take(-1)
    far_bias()
    for run in range(2):
        begin(1, run)
    for run in range(2):
        across(1, run, 0)
    for run in range(2):
        to_sibling(run, 0, 0)
    for far in range(2):
        for run in range(2):
            pass_first(far, run)
        for run in range(2):
            across(far, run, 1)
            across(far, run, 2)
    for run in range(2):
        to_sibling(run, 1, 0)
        to_sibling(run, 2, 0)
    for far in range(2):
        for run in range(2):
            end_first(far, run)
            across(far, run, 3)
    for run in range(2):
        to_sibling(run, 3, 0)
    take(2)
    for u in range(4):
        for far in range(2):
            for run in range(2):
                pass_second(far, run, u)
        for run in range(2):
            to_sibling(run, u, 1)
            to_sibling(run, u, 2)
        if u == 1:
            take(-2)
        if u == 3:
            take(3)
    for u in range(4):
        for run in range(2):
            for far in range(2):
                end_second(far, run, u)
            to_sibling(run, u, 3)
        if u == 2:
            take(-3)
    take(4)
    bound_ref[0:8, :] = tops[...]
    bound_ref[8:24, :] = jnp.broadcast_to(jnp.sum(weighted * weighted, axis=1, keepdims=True), (16, 128))
    for run in range(2):
        for u in range(4):
            for v in range(4):
                a = ring(first[run] + (0, -1, 1, 2)[u], 4)
                b = ring(second[run] + (0, -1, 1, 2)[v], 4)
                k = run * 16 + u * 4 + v
                arrive(unit(*node(run, a, b), run, 0, 8, 1 - core), s_send.at[k], s_recv.at[k])
    for copy in sent:
        copy.wait_send()


def spread(*operands):
    whole = pl.BlockSpec(memory_space=VMEM)
    return pl.pallas_call(
        spread_kernel,
        out_shape=(
            jax.ShapeDtypeStruct((2, 4, 1024, 128), BF16),
            jax.ShapeDtypeStruct((4, 16, 128, 256), BF16),
            jax.ShapeDtypeStruct((4, 16, 256, 128), BF16),
            jax.ShapeDtypeStruct((2, 2, 4, 2, 2, 8, 32, 256), BF16),
            jax.ShapeDtypeStruct((24, 128), F32),
            jax.ShapeDtypeStruct((128, 128), BF16),
            jax.ShapeDtypeStruct((8, 128), jnp.int32),
        ),
        in_specs=[pl.BlockSpec(memory_space=pltpu.HBM)] * len(operands),
        out_specs=(whole,) * 7,
        scratch_shapes=[
            VMEM((128, 32, 128), BF16),
            VMEM((1, 128), F32),
            VMEM((2, 128), BF16),
            VMEM((8, 128), jnp.int32),
            VMEM((128, 128), BF16),
            VMEM((16, 16), jnp.int32),
            VMEM((4096, 128), F32),
            VMEM((8, 4, 128, 128), BF16),
            VMEM((4, 1024, 128), BF16),
            VMEM((2, 272, 128), BF16),
            VMEM((512, 128), BF16),
            VMEM((256, 128), F32),
            VMEM((2, 32, 256), BF16),
            VMEM((8, 128), F32),
            DMA((10,)), DMA((8,)), DMA((8,)), DMA((8,)), DMA((8,)), DMA, DMA,
            DMA((80,)), DMA((80,)), DMA((32,)), DMA((32,)), DMA((2,)),
        ],
        compiler_params=pltpu.CompilerParams(
            collective_id=0, has_side_effects=True, vmem_limit_bytes=32 * 1024 * 1024
        ),
        name="spread",
    )(*operands)


def attend_kernel(
    lists_ref, qg_ref, kbd, vbd, bias, bound_ref,
    acc0, acc1, acc2, acc3,
    peak,
):
    accs = (acc0, acc1, acc2, acc3)
    for acc in accs:
        acc[...] = jnp.zeros_like(acc)
    same = (
        lax.div(lax.broadcasted_iota(jnp.int32, (256, 128), 0), 64)
        == lax.div(lax.broadcasted_iota(jnp.int32, (256, 128), 1), 32)
    ).astype(F32).astype(BF16)

    reach = jnp.sqrt(jnp.max(bound_ref[0:1, :])) * jnp.sqrt(jnp.max(bound_ref[1:2, :]))
    bias_reach = jnp.sqrt(jnp.max(bound_ref[8:24, :])) * (math.sqrt(128) * LOG2E)
    safe = (reach + bias_reach) * 1.03 <= SAFE

    def query(j, i):
        return qg_ref[0, j, pl.ds(pl.multiple_of(jnp.minimum(i, 15) * 64, 64), 64), :]

    def values_of(j, block):
        return jnp.concatenate([vbd[j, block], same], axis=1)

    def offset_of(i, block):
        at = (lax.rem(block, 2), jnp.minimum(i, 15))
        n = lax.div(block, 2)
        return [bias[at[0], at[1], half, n].astype(F32) for half in range(2)]

    total_pairs = lists_ref[3, 0]

    @pl.when(safe)
    def _():
        def pairs_from(first, count):
            work = []
            for side in range(count):
                e = first + side
                block = lists_ref[0, e]
                ids = (lists_ref[1, e], lists_ref[2, e])
                offset = jnp.concatenate(offset_of(ids[0], block) + offset_of(ids[1], block), axis=0)
                work.append((block, ids, offset))
            for j in range(4):
                for block, ids, offset in work:
                    queries = jnp.concatenate([query(j, i) for i in ids], axis=0)
                    score = jnp.dot(queries, kbd[j, block], preferred_element_type=F32)
                    weights = jnp.exp2(score + offset).astype(BF16)
                    total = jnp.dot(weights, values_of(j, block), preferred_element_type=F32)
                    olds = [accs[j][i] for i in ids]
                    for n in range(2):
                        accs[j][ids[n]] = olds[n] + total[n * 64:(n + 1) * 64, :]

        def four_step(t, carry):
            pairs_from(4 * t, 4)
            return carry

        def two_step(t, carry):
            pairs_from(2 * t, 2)
            return carry

        def single_step(t, carry):
            for j in range(4):
                for side in range(4):
                    e = 4 * t + side
                    block = lists_ref[4, e]
                    i = lists_ref[5, e]
                    offset = jnp.concatenate(offset_of(i, block), axis=0)
                    score = jnp.dot(query(j, i), kbd[j, block], preferred_element_type=F32)
                    weights = jnp.exp2(score + offset).astype(BF16)
                    total = jnp.dot(weights, values_of(j, block), preferred_element_type=F32)
                    accs[j][i] = accs[j][i] + total
            return carry

        fours = lax.div(total_pairs, 4)
        lax.fori_loop(0, fours, four_step, 0)
        lax.fori_loop(2 * fours, lax.div(total_pairs + 1, 2), two_step, 0)
        lax.fori_loop(0, lax.div(lists_ref[6, 0] + 3, 4), single_step, 0)

    @pl.when(jnp.logical_not(safe))
    def _():
        peak[...] = jnp.full_like(peak, -1e30)

        def step(n, carry):
            e = jnp.where(n < 2 * total_pairs, lax.div(n, 2), n - 2 * total_pairs)
            line = jnp.where(n < 2 * total_pairs, lax.rem(n, 2), 4)
            block = lists_ref[jnp.where(line == 4, 4, 0), e]
            i = lists_ref[1 + line, e]
            offset = jnp.concatenate(offset_of(i, block), axis=0)
            for j in range(4):
                score = jnp.dot(query(j, i), kbd[j, block], preferred_element_type=F32) + offset
                old = peak[j, i]
                tops = [
                    jnp.maximum(
                        jnp.max(score[:, h * 64:(h + 1) * 64], axis=1, keepdims=True),
                        old[:, h * 32:h * 32 + 1],
                    )
                    for h in range(4)
                ]
                shift = jnp.concatenate([jnp.broadcast_to(top, (64, 64)) for top in tops], axis=1)
                fresh = jnp.concatenate([jnp.broadcast_to(top, (64, 32)) for top in tops], axis=1)
                decay = jnp.exp2(old - fresh)
                weights = jnp.exp2(score - shift).astype(BF16)
                total = jnp.dot(weights, values_of(j, block), preferred_element_type=F32)
                accs[j][i] = accs[j][i] * jnp.concatenate([decay, decay], axis=1) + total
                peak[j, i] = fresh
            return carry

        lax.fori_loop(0, 2 * total_pairs + lists_ref[6, 0], step, 0)


def attend(lists, qg, kbd, vbd, bias, bound):
    whole = pl.BlockSpec(memory_space=VMEM)
    return pl.pallas_call(
        attend_kernel,
        out_shape=[jax.ShapeDtypeStruct((18, 64, 256), F32)] * 4,
        in_specs=[pl.BlockSpec(memory_space=pltpu.SMEM)] + [whole] * 5,
        out_specs=[whole] * 4,
        scratch_shapes=[VMEM((4, 18, 64, 128), F32)],
        compiler_params=pltpu.CompilerParams(vmem_limit_bytes=24 * 1024 * 1024),
        name="attend",
    )(lists, qg, kbd, vbd, bias, bound)


def deliver_kernel(
    acc0, acc1, acc2, acc3, qg_ref, mixing_ref, out_ref,
    update_ref, relay, send_sem, recv_sem, own_sem,
):
    row = lax.axis_index("row")
    col = lax.axis_index("col")
    head = lax.axis_index("head")

    def other(flip):
        return (1 - head) if flip else head

    def device(step, flip):
        return (ring(row + step, 8), col, other(flip))

    steps = (1, 7, 2, 6, 3, 5, 4, 0)
    partner = device(0, 1)
    peers = [partner] + [device(step, 0) for step in steps if step]
    barrier = pltpu.get_barrier_semaphore()
    for peer in peers:
        pl.semaphore_signal(barrier, inc=1, device_id=peer, device_id_type=MESH)

    def spot(step, flip):
        return out_ref.at[pl.ds((other(flip) * 8 + ring(row + step, 8)) * 4, 4)]

    def part(step, flip):
        return update_ref.at[other(flip), ring(row + step, 8)]

    def finish(step):
        target = ring(row + step, 8)
        rows = pl.ds(pl.multiple_of(target * 128, 128), 128)
        for j, acc in enumerate((acc0, acc1, acc2, acc3)):
            sums = acc[pl.ds(target * 2, 2)].reshape(128, 256)
            attention = sums[:, :128] / sums[:, 128:]
            gated = (attention * qg_ref[1, j, rows, :].astype(F32)).astype(BF16)
            update = lax.dot_general(mixing_ref[...], gated, NT, preferred_element_type=F32).astype(BF16)
            update_ref[0, target, j] = update[:64, :]
            update_ref[1, target, j] = update[64:, :]

    copies = []

    def push(k, src, dst, target):
        copy = pltpu.make_async_remote_copy(
            src_ref=src, dst_ref=dst, send_sem=send_sem.at[k], recv_sem=recv_sem.at[k],
            device_id=target, device_id_type=MESH,
        )
        copy.start()
        copies.append(copy)

    def arrive(k, ref):
        pltpu.make_async_remote_copy(
            src_ref=ref, dst_ref=ref, send_sem=send_sem.at[k], recv_sem=recv_sem.at[k],
            device_id=partner, device_id_type=MESH,
        ).wait_recv()

    for step in (1, 7, 2):
        finish(step)
    pl.semaphore_wait(barrier, len(peers))
    for step in steps:
        if step not in (1, 7, 2):
            finish(step)
        if step:
            push(step, part(step, 1), relay.at[step - 1], partner)
            push(8 + step, part(step, 0), spot(0, 0), device(step, 0))
        else:
            push(0, part(0, 1), spot(0, 0), partner)
    own = pltpu.make_async_copy(part(0, 0), spot(0, 0), own_sem)
    own.start()
    for step in steps[:-1]:
        arrive(step, relay.at[step - 1])
        push(16 + step, relay.at[step - 1], spot(0, 1), device(step, 0))
    own.wait()
    arrive(0, spot(0, 1))
    for step in steps[:-1]:
        arrive(8 + step, spot(-step, 0))
    for step in steps[:-1]:
        arrive(16 + step, spot(-step, 1))
    for copy in copies:
        copy.wait_send()


def deliver(accs, qg, mixing):
    whole = pl.BlockSpec(memory_space=VMEM)
    return pl.pallas_call(
        deliver_kernel,
        out_shape=jax.ShapeDtypeStruct((64, 64, 128), BF16),
        in_specs=[whole] * 6,
        out_specs=whole,
        scratch_shapes=[VMEM((2, 8, 4, 64, 128), BF16), VMEM((7, 4, 64, 128), BF16), DMA((24,)), DMA((24,)), DMA],
        compiler_params=pltpu.CompilerParams(
            collective_id=1, has_side_effects=True, vmem_limit_bytes=16 * 1024 * 1024
        ),
        name="deliver",
    )(*accs, qg, mixing)


def per_device(
    pair_field, ln_gain, w_query, w_key, w_value, w_gate, w_bias, w_out, tile_mask, type_ids
):
    weights = [w.T for w in (w_query, w_key, w_value, w_gate)]
    weights.append(w_bias.T)
    operands = (pair_field, ln_gain.reshape(1, 128), *weights, type_ids.reshape(8, 128), w_out, tile_mask)
    qg, kbd, vbd, bias, bound, mixing, lists = spread(
        *[pltpu.with_memory_space_constraint(operand, pltpu.HBM) for operand in operands]
    )
    accs = attend(lists, qg, kbd, vbd, bias.reshape(2, 16, 2, 8, 32, 256), bound)
    return jnp.transpose(deliver(accs, qg, mixing), (2, 0, 1))


def solution(mesh):
    return jax.shard_map(
        per_device,
        mesh=mesh,
        in_specs=(
            P("row", "col", None),
            P(),
            P(None, "head"),
            P(None, "head"),
            P(None, "head"),
            P(None, "head"),
            P(None, "head"),
            P(),
            P(),
            P(),
        ),
        out_specs=P("row", "col", "head"),
        check_vma=False,
    )
```

```python
import math

import jax
import jax.numpy as jnp
from jax import lax
from jax.experimental import pallas as pl
from jax.experimental.pallas import tpu as pltpu
from jax.sharding import PartitionSpec as P

MESH = pl.DeviceIdType.MESH
F32 = jnp.float32
BF16 = jnp.bfloat16
VMEM = pltpu.VMEM
DMA = pltpu.SemaphoreType.DMA

epsilon = 1e-05
masked_score = -1000000000.0
LOG2E = math.log2(math.e)
SCALE = LOG2E / math.sqrt(32)
SAFE = 64.0
NT = (((1,), (1,)), ((), ()))


def ring(value, size):
    return lax.rem(value + size, size)


def spread_kernel(
    tile_ref, gain_in, wq_ref, wk_ref, wv_ref, wg_ref, wb_in, types_in, w_out_in, mask_in,
    qg_ref, kbd_ref, vbd_ref, bias_ref, bound_ref, mixing_ref, lists_ref,
    half, gain_ref, wb_ref, types_ref, w_out_ref, mask_ref, wide, send, strip, wbuf, wall, flat, bsend, tops,
    load_sem, col_send, col_recv, z_send, z_recv, w_send, w_recv,
    g_send, g_recv, s_send, s_recv, own_sem,
):
    row = lax.axis_index("row")
    col = lax.axis_index("col")
    head = lax.axis_index("head")
    core = lax.rem(col, 2)
    x = lax.rem(lax.div(col, 2), 4)
    y = head * 2 + lax.div(col, 8)

    def place(x_, y_, core_=None):
        return (row, lax.rem(y_, 2) * 8 + x_ * 2 + (core if core_ is None else core_), lax.div(y_, 2))

    def along_z(step):
        return (ring(row + step, 8), col, head)

    partner = place(x, ring(y + 2, 4))
    peers = [along_z(step) for step in range(1, 8)]
    peers += [place(ring(x + 1, 4), y), place(ring(x - 1, 4), y)]
    peers += [place(x, ring(y + 1, 4)), place(x, ring(y - 1, 4)), partner]
    peers += [place(x, y, 1 - core)]
    barrier = pltpu.get_barrier_semaphore()
    for peer in peers:
        pl.semaphore_signal(barrier, inc=1, device_id=peer, device_id_type=MESH)

    loads = [
        (tile_ref.at[:, pl.ds(pl.multiple_of(head * 32, 32), 32), :], half),
        (gain_in, gain_ref), (wb_in, wb_ref), (types_in, types_ref),
    ]
    loads += [
        (ref, wbuf.at[head, pl.ds(kind * 64, 64)]) for kind, ref in enumerate((wq_ref, wk_ref, wv_ref, wg_ref))
    ]
    loads += [(w_out_in, w_out_ref), (mask_in, mask_ref)]
    loads = [pltpu.make_async_copy(src, dst, load_sem.at[n]) for n, (src, dst) in enumerate(loads)]
    for load in loads:
        load.start()
    tops[...] = jnp.zeros_like(tops)
    loads[0].wait()

    def widen(block, carry):
        rows = half[pl.ds(block * 8, 8)].astype(F32).reshape(256, 128)
        wide[pl.ds(pl.multiple_of(block * 256, 256), 256), :] = rows
        return carry

    lax.fori_loop(0, 16, widen, 0)
    ones = jnp.ones((128, 128), BF16)
    loads[1].wait()
    gain = gain_ref[...]

    def norm_for(step):
        target = ring(row + step, 8)
        for jj in range(4):
            value = wide[pl.ds(4 * target + jj, 128, stride=32), :]
            mean = jnp.dot(value.astype(BF16), ones, preferred_element_type=F32) * (1.0 / 128)
            centred = value - mean
            squares = (centred * centred).astype(BF16)
            spread = jnp.dot(squares, ones, preferred_element_type=F32) * (1.0 / 128)
            normed = centred * lax.rsqrt(spread + epsilon) * gain
            send[target, jj] = normed.astype(BF16)

    def norm_near(n, carry):
        norm_for(n)
        norm_for(-n)
        return carry

    def norm_far(n, carry):
        norm_for(3 + n)
        norm_for(-3 * (1 - n))
        return carry

    lax.fori_loop(1, 3, norm_near, 0)
    for load in loads[2:]:
        load.wait()
    wbuf[head, 256:272, :] = jnp.concatenate(
        [wb_ref[...].astype(F32), jnp.zeros((14, 128), F32)], axis=0
    ).astype(BF16)
    pl.semaphore_wait(barrier, len(peers))
    w_copy = pltpu.make_async_remote_copy(
        src_ref=wbuf.at[head], dst_ref=wbuf.at[head], send_sem=w_send, recv_sem=w_recv,
        device_id=partner, device_id_type=MESH,
    )
    w_copy.start()
    sent = [w_copy]

    def push(src, dst, send_sem, recv_sem, device):
        copy = pltpu.make_async_remote_copy(
            src_ref=src, dst_ref=dst, send_sem=send_sem, recv_sem=recv_sem,
            device_id=device, device_id_type=MESH,
        )
        copy.start()
        sent.append(copy)

    def strip_rows(step):
        source = ring(row + step, 8)
        return strip.at[:, pl.ds(pl.multiple_of(source * 128, 128), 128), :]

    def col_push(step):
        target = ring(row + step, 8)
        push(send.at[target], strip_rows(0), col_send.at[step], col_recv.at[step], along_z(step))

    col_push(1)
    col_push(7)
    lax.fori_loop(0, 2, norm_far, 0)
    pltpu.make_async_remote_copy(
        src_ref=wbuf.at[1 - head], dst_ref=wbuf.at[1 - head], send_sem=w_send, recv_sem=w_recv,
        device_id=partner, device_id_type=MESH,
    ).wait_recv()

    wb = wbuf[0, 256:272, :].astype(F32) + pltpu.roll(wbuf[1, 256:272, :].astype(F32), 2, 0)
    weighted = wb * gain
    wbt = wb.astype(BF16)

    def bias_for(target, carry):
        part = lax.dot_general(wbt, send[target].reshape(512, 128), NT, preferred_element_type=F32)
        for jj in range(4):
            flat[pl.ds(pl.multiple_of((4 * target + jj) * 8, 8), 8), :] = part[0:8, jj * 128:jj * 128 + 128]
        return carry

    lax.fori_loop(0, 8, bias_for, 0, unroll=4)
    living = jnp.broadcast_to(types_ref[pl.ds(row, 1), :] != 0, (32, 128))
    by_head = [
        jnp.where(living, flat[pl.ds(h, 32, stride=8), :] * LOG2E, masked_score) for h in range(4)
    ]
    bsend[0] = jnp.concatenate([b[:, :64] for b in by_head], axis=1).astype(BF16)
    bsend[1] = jnp.concatenate([b[:, 64:] for b in by_head], axis=1).astype(BF16)

    def unit(x_, y_, run, low, count, core_=None):
        return bias_ref.at[
            run, lax.rem(y_, 2), x_, core if core_ is None else core_, lax.div(y_, 2), pl.ds(low, count)
        ]

    def arrive(dst, send_sem, recv_sem):
        pltpu.make_async_remote_copy(
            src_ref=dst, dst_ref=dst, send_sem=send_sem, recv_sem=recv_sem,
            device_id=partner, device_id_type=MESH,
        ).wait_recv()

    def slot(step):
        return 2 * step - 1 if step > 0 else -2 * step

    spans = ((0, 2, 5), (5, 7, 8))

    def chunk(step, low=0, count=2):
        return bias_ref.at[pl.ds(low, count), lax.rem(y, 2), x, core, lax.div(y, 2), slot(step)]

    def z_push(k, src, dst, step):
        push(src, dst, z_send.at[k], z_recv.at[k], along_z(step))

    def z_arrive(k, dst):
        arrive(dst, z_send.at[k], z_recv.at[k])

    own = pltpu.make_async_copy(bsend, chunk(0), own_sem.at[0])
    own.start()
    for k, step in enumerate((2, -2, 1, -1)):
        z_push(k, bsend, chunk(-step), step)

    own_cols = pltpu.make_async_copy(send.at[row], strip_rows(0), own_sem.at[1])
    own_cols.start()

    for kind, place_of in enumerate((1, 0, 2, 3)):
        for s in range(2):
            wall[place_of * 128 + s * 64:place_of * 128 + s * 64 + 64, :] = wbuf[s, kind * 64:kind * 64 + 64, :]
    together = (
        lax.div(lax.broadcasted_iota(jnp.int32, (128, 128), 0), 32)
        == lax.div(lax.broadcasted_iota(jnp.int32, (128, 128), 1), 32)
    ).astype(F32).astype(BF16)

    key_head = lax.div(lax.broadcasted_iota(jnp.int32, (128, 128), 0), 32)
    side_of = lax.div(lax.broadcasted_iota(jnp.int32, (128, 128), 1), 64)
    key_here = [(key_head == 2 * n + side_of).astype(F32).astype(BF16) for n in range(2)]
    lane_head = lax.div(lax.broadcasted_iota(jnp.int32, (64, 128), 1), 32)
    value_here = [(lane_head == h).astype(F32).astype(BF16) for h in range(4)]

    def project(step):
        source = ring(row + step, 8)
        first_block = 2 * slot(step)
        rows = pl.ds(pl.multiple_of(source * 128, 128), 128)

        def one(jj, carry):
            value = strip[jj, rows, :]
            keys = lax.dot_general(wall[0:128, :], value, NT, preferred_element_type=F32)
            left = lax.dot_general(value, wall[128:256, :], NT, preferred_element_type=F32)
            right = lax.dot_general(value, wall[256:512, :], NT, preferred_element_type=F32)
            query = left * SCALE
            qg_ref[0, jj, rows, :] = query.astype(BF16)
            qg_ref[1, jj, rows, :] = jax.nn.sigmoid(right[:, 128:]).astype(BF16)
            short = keys.astype(BF16)
            values = right[:, :128].astype(BF16)
            for odd in range(2):
                twice = jnp.concatenate([short[:, odd * 64:odd * 64 + 64]] * 2, axis=1)
                for n in range(2):
                    kbd_ref[jj, first_block + odd, :, n * 128:(n + 1) * 128] = twice * key_here[n]
                for h in range(4):
                    vbd_ref[jj, first_block + odd, h * 64:(h + 1) * 64, :] = (
                        values[odd * 64:odd * 64 + 64, :] * value_here[h]
                    )
            lengths = jnp.dot((query * query).astype(BF16), together, preferred_element_type=F32)
            tops[0:1, :] = jnp.maximum(tops[0:1, :], jnp.max(lengths, axis=0, keepdims=True))
            lengths = jnp.dot(together, (keys * keys).astype(BF16), preferred_element_type=F32)
            tops[1:2, :] = jnp.maximum(tops[1:2, :], jnp.max(lengths, axis=0, keepdims=True))
            return carry

        lax.fori_loop(0, 4, one, 0, unroll=True)

    def take(step):
        arrive(strip_rows(step), col_send.at[(8 - step) % 8], col_recv.at[(8 - step) % 8])
        project(step)

    def make_lists():
        mixing_ref[...] = w_out_ref[...].astype(F32).T.astype(BF16)
        part = mask_ref[...].astype(F32)
        place_ = lax.div(lax.broadcasted_iota(jnp.int32, (16, 128), 1), 2)
        away = lax.div(place_ + 1, 2) * (2 * lax.rem(place_, 2) - 1)
        there = 2 * lax.rem(row + away + 8, 8) + lax.rem(lax.broadcasted_iota(jnp.int32, (16, 128), 1), 2)
        inside = lax.broadcasted_iota(jnp.int32, (16, 128), 1) < 16
        turned = (inside & (lax.broadcasted_iota(jnp.int32, (16, 128), 0) == there)).astype(F32).astype(BF16)
        diagonal = lax.broadcasted_iota(jnp.int32, (16, 16), 0) == lax.broadcasted_iota(jnp.int32, (16, 16), 1)
        part = jnp.where((part == 1.0) | diagonal, 1.0, 0.0)
        allowed = jnp.dot(part.astype(BF16), turned, preferred_element_type=F32)
        before = [jnp.zeros((1, 128), F32)]
        for i in range(16):
            before.append(before[-1] + allowed[i:i + 1, :])
        rank = jnp.concatenate(before[:16], axis=0)
        pairs = jnp.broadcast_to(jnp.floor(before[16] * 0.5), (16, 128))
        single = jnp.broadcast_to(before[16], (16, 128)) - 2.0 * pairs
        alone = allowed * jnp.where(rank == 2.0 * pairs, 1.0, 0.0)
        allowed = allowed - alone
        earlier = (
            lax.broadcasted_iota(jnp.int32, (128, 128), 0) < lax.broadcasted_iota(jnp.int32, (128, 128), 1)
        ).astype(F32).astype(BF16)
        start = jnp.dot(pairs.astype(BF16), earlier, preferred_element_type=F32)
        total = jnp.sum(pairs[0:1, :], axis=1, keepdims=True)
        single_start = jnp.dot(single.astype(BF16), earlier, preferred_element_type=F32)
        singles = jnp.sum(single[0:1, :], axis=1, keepdims=True)
        rank = rank + 2.0 * start
        entry = 2.0 * lax.broadcasted_iota(jnp.int32, (16, 128), 1).astype(F32)
        number = lax.broadcasted_iota(jnp.int32, (16, 128), 0).astype(F32)
        block = jnp.zeros((16, 128), F32)
        single_block = jnp.zeros((16, 128), F32)
        single_picked = jnp.zeros((16, 128), F32)
        single_found = jnp.zeros((16, 128), F32)
        picked = [jnp.zeros((16, 128), F32)] * 2
        found = [jnp.zeros((16, 128), F32)] * 2
        for k in range(16):
            at = jnp.broadcast_to(rank[:, k:k + 1], (16, 128))
            here = jnp.broadcast_to(allowed[:, k:k + 1], (16, 128))
            for side in range(2):
                hit = jnp.where(at == entry + side, here, 0.0)
                found[side] = found[side] + hit
                picked[side] = picked[side] + hit * number
                if side == 0:
                    block = block + hit * k
            at = jnp.broadcast_to(single_start[:, k:k + 1], (16, 128))
            here = jnp.broadcast_to(alone[:, k:k + 1], (16, 128))
            hit = jnp.where(2.0 * at == entry, here, 0.0)
            single_found = single_found + hit
            single_picked = single_picked + hit * number
            single_block = single_block + hit * k
        rows = [jnp.sum(block, axis=0, keepdims=True)]
        for side in range(2):
            missing = 1.0 - jnp.sum(found[side], axis=0, keepdims=True)
            rows.append(jnp.sum(picked[side], axis=0, keepdims=True) + (16.0 + side) * missing)
        rows.append(jnp.broadcast_to(total, (1, 128)))
        missing = 1.0 - jnp.sum(single_found, axis=0, keepdims=True)
        rows.append(jnp.sum(single_block, axis=0, keepdims=True))
        rows.append(jnp.sum(single_picked, axis=0, keepdims=True) + 16.0 * missing)
        rows.append(jnp.broadcast_to(singles, (1, 128)))
        rows.append(jnp.zeros((1, 128), F32))
        lists_ref[...] = jnp.concatenate(rows, axis=0).astype(jnp.int32)

    own_cols.wait()
    project(0)
    make_lists()
    own.wait()
    for k, step in enumerate((-2, 2, -1, 1)):
        z_arrive(k, chunk(step))
    z_push(4, chunk(-2), chunk(-3), 1)
    z_push(5, chunk(2), chunk(3), -1)
    z_push(6, chunk(-2, 0, 1), chunk(4, 0, 1), 2)
    z_push(7, chunk(2, 1, 1), chunk(4, 1, 1), -2)

    def far_bias():
        z_arrive(4, chunk(-3))
        z_arrive(5, chunk(3))
        z_arrive(6, chunk(4, 0, 1))
        z_arrive(7, chunk(4, 1, 1))

    def node(run, a, b):
        return (a, b) if run == 0 else (b, a)

    first = (x, y)
    second = (y, x)

    def whole_of(span):
        return span[0], span[2] - span[0]

    def halves_of(span):
        return (span[0], span[1] - span[0]), (span[1], span[2] - span[1])

    def shipment(far, run, index, a, b, rows, to_a, to_b):
        k = far * 40 + run * 20 + index
        ref = unit(*node(run, a, b), run, *rows)
        push(ref, ref, g_send.at[k], g_recv.at[k], place(*node(run, to_a, to_b)))

    def receive(far, run, index, a, b, rows):
        k = far * 40 + run * 20 + index
        arrive(unit(*node(run, a, b), run, *rows), g_send.at[k], g_recv.at[k])

    def to_sibling(run, u, v):
        k = run * 16 + u * 4 + v
        a, b = ring(first[run] + (0, -1, 1, 2)[u], 4), ring(second[run] + (0, -1, 1, 2)[v], 4)
        ref = unit(*node(run, a, b), run, 0, 8)
        push(ref, ref, s_send.at[k], s_recv.at[k], place(x, y, 1 - core))

    def begin(far, run):
        a, b, rows = first[run], second[run], whole_of(spans[far])
        shipment(far, run, 0, a, b, rows, ring(a + 1, 4), b)
        shipment(far, run, 1, a, b, rows, ring(a - 1, 4), b)

    def across(far, run, u):
        a, b, rows = ring(first[run] + (0, -1, 1, 2)[u], 4), second[run], whole_of(spans[far])
        shipment(far, run, 4 + 4 * u, a, b, rows, first[run], ring(b + 1, 4))
        shipment(far, run, 5 + 4 * u, a, b, rows, first[run], ring(b - 1, 4))

    def pass_first(far, run):
        a, b, rows = first[run], second[run], whole_of(spans[far])
        low, high = halves_of(spans[far])
        receive(far, run, 0, ring(a - 1, 4), b, rows)
        shipment(far, run, 2, ring(a - 1, 4), b, low, ring(a + 1, 4), b)
        receive(far, run, 1, ring(a + 1, 4), b, rows)
        shipment(far, run, 3, ring(a + 1, 4), b, high, ring(a - 1, 4), b)

    def end_first(far, run):
        a, b = ring(first[run] + 2, 4), second[run]
        low, high = halves_of(spans[far])
        receive(far, run, 2, a, b, low)
        receive(far, run, 3, a, b, high)

    def pass_second(far, run, u):
        a, b, rows = ring(first[run] + (0, -1, 1, 2)[u], 4), second[run], whole_of(spans[far])
        low, high = halves_of(spans[far])
        receive(far, run, 4 + 4 * u, a, ring(b - 1, 4), rows)
        shipment(far, run, 6 + 4 * u, a, ring(b - 1, 4), low, first[run], ring(b + 1, 4))
        receive(far, run, 5 + 4 * u, a, ring(b + 1, 4), rows)
        shipment(far, run, 7 + 4 * u, a, ring(b + 1, 4), high, first[run], ring(b - 1, 4))

    def end_second(far, run, u):
        a, b = ring(first[run] + (0, -1, 1, 2)[u], 4), ring(second[run] + 2, 4)
        low, high = halves_of(spans[far])
        receive(far, run, 6 + 4 * u, a, b, low)
        receive(far, run, 7 + 4 * u, a, b, high)

    for run in range(2):
        begin(0, run)
    for run in range(2):
        across(0, run, 0)
    for step in (2, 6, 3, 5, 4):
        col_push(step)
    take(1)
    take(-1)
    far_bias()
    for run in range(2):
        begin(1, run)
    for run in range(2):
        across(1, run, 0)
    for run in range(2):
        to_sibling(run, 0, 0)
    for far in range(2):
        for run in range(2):
            pass_first(far, run)
        for run in range(2):
            across(far, run, 1)
            across(far, run, 2)
    for run in range(2):
        to_sibling(run, 1, 0)
        to_sibling(run, 2, 0)
    for far in range(2):
        for run in range(2):
            end_first(far, run)
            across(far, run, 3)
    for run in range(2):
        to_sibling(run, 3, 0)
    for u in range(4):
        for far in range(2):
            for run in range(2):
                pass_second(far, run, u)
        for run in range(2):
            to_sibling(run, u, 1)
            to_sibling(run, u, 2)
        if u == 1:
            take(2)
        if u == 3:
            take(-2)
    for u in range(4):
        for run in range(2):
            for far in range(2):
                end_second(far, run, u)
            to_sibling(run, u, 3)
        if u == 2:
            take(3)
    take(-3)
    take(4)
    bound_ref[0:8, :] = tops[...]
    bound_ref[8:24, :] = jnp.broadcast_to(jnp.sum(weighted * weighted, axis=1, keepdims=True), (16, 128))
    for run in range(2):
        for u in range(4):
            for v in range(4):
                a = ring(first[run] + (0, -1, 1, 2)[u], 4)
                b = ring(second[run] + (0, -1, 1, 2)[v], 4)
                k = run * 16 + u * 4 + v
                arrive(unit(*node(run, a, b), run, 0, 8, 1 - core), s_send.at[k], s_recv.at[k])
    for copy in sent:
        copy.wait_send()


def spread(*operands):
    whole = pl.BlockSpec(memory_space=VMEM)
    return pl.pallas_call(
        spread_kernel,
        out_shape=(
            jax.ShapeDtypeStruct((2, 4, 1024, 128), BF16),
            jax.ShapeDtypeStruct((4, 16, 128, 256), BF16),
            jax.ShapeDtypeStruct((4, 16, 256, 128), BF16),
            jax.ShapeDtypeStruct((2, 2, 4, 2, 2, 8, 32, 256), BF16),
            jax.ShapeDtypeStruct((24, 128), F32),
            jax.ShapeDtypeStruct((128, 128), BF16),
            jax.ShapeDtypeStruct((8, 128), jnp.int32),
        ),
        in_specs=[pl.BlockSpec(memory_space=pltpu.HBM)] * len(operands),
        out_specs=(whole,) * 7,
        scratch_shapes=[
            VMEM((128, 32, 128), BF16),
            VMEM((1, 128), F32),
            VMEM((2, 128), BF16),
            VMEM((8, 128), jnp.int32),
            VMEM((128, 128), BF16),
            VMEM((16, 16), jnp.int32),
            VMEM((4096, 128), F32),
            VMEM((8, 4, 128, 128), BF16),
            VMEM((4, 1024, 128), BF16),
            VMEM((2, 272, 128), BF16),
            VMEM((512, 128), BF16),
            VMEM((256, 128), F32),
            VMEM((2, 32, 256), BF16),
            VMEM((8, 128), F32),
            DMA((10,)), DMA((8,)), DMA((8,)), DMA((8,)), DMA((8,)), DMA, DMA,
            DMA((80,)), DMA((80,)), DMA((32,)), DMA((32,)), DMA((2,)),
        ],
        compiler_params=pltpu.CompilerParams(
            collective_id=0, has_side_effects=True, vmem_limit_bytes=32 * 1024 * 1024
        ),
        name="spread",
    )(*operands)


def attend_kernel(
    lists_ref, qg_ref, kbd, vbd, bias, bound_ref,
    acc0, acc1, acc2, acc3,
    peak,
):
    accs = (acc0, acc1, acc2, acc3)
    for acc in accs:
        acc[...] = jnp.zeros_like(acc)
    same = (
        lax.div(lax.broadcasted_iota(jnp.int32, (256, 128), 0), 64)
        == lax.div(lax.broadcasted_iota(jnp.int32, (256, 128), 1), 32)
    ).astype(F32).astype(BF16)

    reach = jnp.sqrt(jnp.max(bound_ref[0:1, :])) * jnp.sqrt(jnp.max(bound_ref[1:2, :]))
    bias_reach = jnp.sqrt(jnp.max(bound_ref[8:24, :])) * (math.sqrt(128) * LOG2E)
    safe = (reach + bias_reach) * 1.03 <= SAFE

    def query(j, i):
        return qg_ref[0, j, pl.ds(pl.multiple_of(jnp.minimum(i, 15) * 64, 64), 64), :]

    def values_of(j, block):
        return jnp.concatenate([vbd[j, block], same], axis=1)

    def offset_of(i, block):
        at = (lax.rem(block, 2), jnp.minimum(i, 15))
        n = lax.div(block, 2)
        return [bias[at[0], at[1], half, n].astype(F32) for half in range(2)]

    total_pairs = lists_ref[3, 0]

    @pl.when(safe)
    def _():
        def pairs_from(first, count):
            work = []
            for side in range(count):
                e = first + side
                block = lists_ref[0, e]
                ids = (lists_ref[1, e], lists_ref[2, e])
                offset = jnp.concatenate(offset_of(ids[0], block) + offset_of(ids[1], block), axis=0)
                work.append((block, ids, offset))
            for j in range(4):
                for block, ids, offset in work:
                    queries = jnp.concatenate([query(j, i) for i in ids], axis=0)
                    score = jnp.dot(queries, kbd[j, block], preferred_element_type=F32)
                    weights = jnp.exp2(score + offset).astype(BF16)
                    total = jnp.dot(weights, values_of(j, block), preferred_element_type=F32)
                    olds = [accs[j][i] for i in ids]
                    for n in range(2):
                        accs[j][ids[n]] = olds[n] + total[n * 64:(n + 1) * 64, :]

        def four_step(t, carry):
            pairs_from(4 * t, 4)
            return carry

        def two_step(t, carry):
            pairs_from(2 * t, 2)
            return carry

        def single_step(t, carry):
            for j in range(4):
                for side in range(4):
                    e = 4 * t + side
                    block = lists_ref[4, e]
                    i = lists_ref[5, e]
                    offset = jnp.concatenate(offset_of(i, block), axis=0)
                    score = jnp.dot(query(j, i), kbd[j, block], preferred_element_type=F32)
                    weights = jnp.exp2(score + offset).astype(BF16)
                    total = jnp.dot(weights, values_of(j, block), preferred_element_type=F32)
                    accs[j][i] = accs[j][i] + total
            return carry

        fours = lax.div(total_pairs, 4)
        lax.fori_loop(0, fours, four_step, 0)
        lax.fori_loop(2 * fours, lax.div(total_pairs + 1, 2), two_step, 0)
        lax.fori_loop(0, lax.div(lists_ref[6, 0] + 3, 4), single_step, 0)

    @pl.when(jnp.logical_not(safe))
    def _():
        peak[...] = jnp.full_like(peak, -1e30)

        def step(n, carry):
            e = jnp.where(n < 2 * total_pairs, lax.div(n, 2), n - 2 * total_pairs)
            line = jnp.where(n < 2 * total_pairs, lax.rem(n, 2), 4)
            block = lists_ref[jnp.where(line == 4, 4, 0), e]
            i = lists_ref[1 + line, e]
            offset = jnp.concatenate(offset_of(i, block), axis=0)
            for j in range(4):
                score = jnp.dot(query(j, i), kbd[j, block], preferred_element_type=F32) + offset
                old = peak[j, i]
                tops = [
                    jnp.maximum(
                        jnp.max(score[:, h * 64:(h + 1) * 64], axis=1, keepdims=True),
                        old[:, h * 32:h * 32 + 1],
                    )
                    for h in range(4)
                ]
                shift = jnp.concatenate([jnp.broadcast_to(top, (64, 64)) for top in tops], axis=1)
                fresh = jnp.concatenate([jnp.broadcast_to(top, (64, 32)) for top in tops], axis=1)
                decay = jnp.exp2(old - fresh)
                weights = jnp.exp2(score - shift).astype(BF16)
                total = jnp.dot(weights, values_of(j, block), preferred_element_type=F32)
                accs[j][i] = accs[j][i] * jnp.concatenate([decay, decay], axis=1) + total
                peak[j, i] = fresh
            return carry

        lax.fori_loop(0, 2 * total_pairs + lists_ref[6, 0], step, 0)


def attend(lists, qg, kbd, vbd, bias, bound):
    whole = pl.BlockSpec(memory_space=VMEM)
    return pl.pallas_call(
        attend_kernel,
        out_shape=[jax.ShapeDtypeStruct((18, 64, 256), F32)] * 4,
        in_specs=[pl.BlockSpec(memory_space=pltpu.SMEM)] + [whole] * 5,
        out_specs=[whole] * 4,
        scratch_shapes=[VMEM((4, 18, 64, 128), F32)],
        compiler_params=pltpu.CompilerParams(vmem_limit_bytes=24 * 1024 * 1024),
        name="attend",
    )(lists, qg, kbd, vbd, bias, bound)


def deliver_kernel(
    acc0, acc1, acc2, acc3, qg_ref, mixing_ref, out_ref,
    update_ref, relay, send_sem, recv_sem, own_sem,
):
    row = lax.axis_index("row")
    col = lax.axis_index("col")
    head = lax.axis_index("head")

    def other(flip):
        return (1 - head) if flip else head

    def device(step, flip):
        return (ring(row + step, 8), col, other(flip))

    steps = (1, 7, 2, 6, 3, 5, 4, 0)
    partner = device(0, 1)
    peers = [partner] + [device(step, 0) for step in steps if step]
    barrier = pltpu.get_barrier_semaphore()
    for peer in peers:
        pl.semaphore_signal(barrier, inc=1, device_id=peer, device_id_type=MESH)

    def spot(step, flip):
        return out_ref.at[pl.ds((other(flip) * 8 + ring(row + step, 8)) * 4, 4)]

    def part(step, flip):
        return update_ref.at[other(flip), ring(row + step, 8)]

    def finish(step):
        target = ring(row + step, 8)
        rows = pl.ds(pl.multiple_of(target * 128, 128), 128)
        for j, acc in enumerate((acc0, acc1, acc2, acc3)):
            sums = acc[pl.ds(target * 2, 2)].reshape(128, 256)
            attention = sums[:, :128] / sums[:, 128:]
            gated = (attention * qg_ref[1, j, rows, :].astype(F32)).astype(BF16)
            update = lax.dot_general(mixing_ref[...], gated, NT, preferred_element_type=F32).astype(BF16)
            update_ref[0, target, j] = update[:64, :]
            update_ref[1, target, j] = update[64:, :]

    copies = []

    def push(k, src, dst, target):
        copy = pltpu.make_async_remote_copy(
            src_ref=src, dst_ref=dst, send_sem=send_sem.at[k], recv_sem=recv_sem.at[k],
            device_id=target, device_id_type=MESH,
        )
        copy.start()
        copies.append(copy)

    def arrive(k, ref):
        pltpu.make_async_remote_copy(
            src_ref=ref, dst_ref=ref, send_sem=send_sem.at[k], recv_sem=recv_sem.at[k],
            device_id=partner, device_id_type=MESH,
        ).wait_recv()

    for step in (1, 7, 2):
        finish(step)
    pl.semaphore_wait(barrier, len(peers))
    for step in steps:
        if step not in (1, 7, 2):
            finish(step)
        if step:
            push(step, part(step, 1), relay.at[step - 1], partner)
            push(8 + step, part(step, 0), spot(0, 0), device(step, 0))
        else:
            push(0, part(0, 1), spot(0, 0), partner)
    own = pltpu.make_async_copy(part(0, 0), spot(0, 0), own_sem)
    own.start()
    for step in steps[:-1]:
        arrive(step, relay.at[step - 1])
        push(16 + step, relay.at[step - 1], spot(0, 1), device(step, 0))
    own.wait()
    arrive(0, spot(0, 1))
    for step in steps[:-1]:
        arrive(8 + step, spot(-step, 0))
    for step in steps[:-1]:
        arrive(16 + step, spot(-step, 1))
    for copy in copies:
        copy.wait_send()


def deliver(accs, qg, mixing):
    whole = pl.BlockSpec(memory_space=VMEM)
    return pl.pallas_call(
        deliver_kernel,
        out_shape=jax.ShapeDtypeStruct((64, 64, 128), BF16),
        in_specs=[whole] * 6,
        out_specs=whole,
        scratch_shapes=[VMEM((2, 8, 4, 64, 128), BF16), VMEM((7, 4, 64, 128), BF16), DMA((24,)), DMA((24,)), DMA],
        compiler_params=pltpu.CompilerParams(
            collective_id=1, has_side_effects=True, vmem_limit_bytes=16 * 1024 * 1024
        ),
        name="deliver",
    )(*accs, qg, mixing)


def per_device(
    pair_field, ln_gain, w_query, w_key, w_value, w_gate, w_bias, w_out, tile_mask, type_ids
):
    weights = [w.T for w in (w_query, w_key, w_value, w_gate)]
    weights.append(w_bias.T)
    operands = (pair_field, ln_gain.reshape(1, 128), *weights, type_ids.reshape(8, 128), w_out, tile_mask)
    qg, kbd, vbd, bias, bound, mixing, lists = spread(
        *[pltpu.with_memory_space_constraint(operand, pltpu.HBM) for operand in operands]
    )
    accs = attend(lists, qg, kbd, vbd, bias.reshape(2, 16, 2, 8, 32, 256), bound)
    return jnp.transpose(deliver(accs, qg, mixing), (2, 0, 1))


def solution(mesh):
    return jax.shard_map(
        per_device,
        mesh=mesh,
        in_specs=(
            P("row", "col", None),
            P(),
            P(None, "head"),
            P(None, "head"),
            P(None, "head"),
            P(None, "head"),
            P(None, "head"),
            P(),
            P(),
            P(),
        ),
        out_specs=P("row", "col", "head"),
        check_vma=False,
    )
```
